32 devices in a mesh: dp: 16 (over z, y, x), seq: 2 (over core).
Axes of the slice: x: 2, y: 2, z: 4, core: 2. Of those that a mesh axis runs over, the one named last changes fastest.
Arguments:
- layer_input: bfloat16 [16, 512, 768], P('dp', 'seq'), may hold values from -6 to 6
- encoder_states: bfloat16 [16, 3, 1500, 768], P('dp', None, 'seq'), may hold values from -6 to 6
- clip_lengths: int32 [16, 3], P('dp'), may hold values from 1 to 448, as said below
- out_grad: bfloat16 [16, 512, 768], P('dp', 'seq'), may hold values from -6 to 6
- self_weights: bfloat16 [768, 3072], P(('dp', 'seq')), may hold values from -2 to 2
- cross_weights: bfloat16 [768, 3072], P(('dp', 'seq')), may hold values from -2 to 2
- up_weights: bfloat16 [768, 3072], P(('dp', 'seq')), may hold values from -0.21875 to 0.21875
- down_weights: bfloat16 [3072, 768], P(('dp', 'seq')), may hold values from -0.15625 to 0.15625
- up_bias: bfloat16 [3072], P(('dp', 'seq')), may hold values from -3 to 3
- down_bias: bfloat16 [768], P(('dp', 'seq')), may hold values from -3 to 3
- vectors: bfloat16 [768, 12], P(('dp', 'seq')), may hold values from -2 to 2
Outputs:
- layer_output: bfloat16 [16, 512, 768], P('dp', 'seq')
- input_grad: float32 [16, 512, 768], P('dp', 'seq')
- encoder_grad: float32 [16, 3, 1500, 768], P('dp', None, 'seq')
- self_weights_grad: float32 [768, 3072], P(('dp', 'seq'))
- cross_weights_grad: float32 [768, 3072], P(('dp', 'seq'))
- up_weights_grad: float32 [768, 3072], P(('dp', 'seq'))
- down_weights_grad: float32 [3072, 768], P(('dp', 'seq'))
- up_bias_grad: float32 [3072], P(('dp', 'seq'))
- down_bias_grad: float32 [768], P(('dp', 'seq'))
- vectors_grad: float32 [768, 12], P(('dp', 'seq'))
The draws below stay inside these ranges and needn't reach their ends.
Inputs may be any that keep to these rules, and one draw needn't show every extreme that they name: `clip_lengths`: each row's 3 clips lie end to end from the row's first token, in order, and take at most 512 tokens together; the rest of the row is padding. Every row has a clip of exactly 448 tokens.
All inputs are finite; a program needn't handle non-finite values.
Results may differ from the reference program's by a relative error of at most 0.019.
Values may be sent and summed in bfloat16 or wider, within the bound.
A program may use at most 192 MiB of HBM per device.

```python
import jax
import jax.numpy as jnp
from jax import lax

D = 768
HEAD_DIM = 64
HEADS = 12
FF = 3072
FRAMES = 1500
MAX_LEN = 448
CLIPS = 3
TOK_DEV = 256
ROW = 512
N_DP = 16


def block_weights(key, gain_list):
    gauss_noise = jax.random.truncated_normal(key, -3.0, 3.0, (D, 4 * D), jnp.float32)
    block_scale = jnp.repeat(jnp.sqrt(jnp.array(gain_list, jnp.float32) / D), D)
    return (gauss_noise * block_scale[None, :]).astype(jnp.bfloat16)


def draw_self_weights(key, part):
    key = jax.random.fold_in(key, 5)
    return block_weights(key, (2.0, 1.0, 1.0, 16.0))


def draw_cross_weights(key, part):
    key = jax.random.fold_in(key, 6)
    return block_weights(key, (2.0, 1.0, 1.0, 64.0))


def draw_vectors(key, part):
    key = jax.random.fold_in(key, 7)
    first_key, second_key = jax.random.split(key)
    gains = jax.random.uniform(first_key, (12, D), jnp.float32, 0.5, 1.5)
    shifts = 0.5 * jax.random.truncated_normal(second_key, -3.0, 3.0, (12, D), jnp.float32)
    row_index = jnp.arange(12)[:, None]
    is_gain = (row_index < 6) & (row_index % 2 == 0)
    return jnp.where(is_gain, gains, shifts).T.astype(jnp.bfloat16)


def draw_clip_lengths(key, part):
    key = jax.random.fold_in(key, 11)
    first_key, second_key = jax.random.split(key)
    low_gap = max(1, max(TOK_DEV - MAX_LEN, MAX_LEN - TOK_DEV + 1))
    high_gap = min(MAX_LEN - 1, TOK_DEV - 1)
    gap = jax.random.randint(first_key, (N_DP,), low_gap, high_gap + 1)
    first_len = TOK_DEV - gap
    room = jnp.minimum(MAX_LEN, TOK_DEV + gap - MAX_LEN)
    third_len = jax.random.randint(second_key, (N_DP,), 1, room + 1)
    second_len = jnp.full((N_DP,), MAX_LEN, jnp.int32)
    return jnp.stack([first_len, second_len, third_len], 1).astype(jnp.int32)


def raised(entries, own_key, source, target, blocks, factor):
    owner, partner = [(jnp.arange(entries.shape[dim]) // (entries.shape[dim] // blocks)).reshape([-1 if axis == dim else 1 for axis in range(entries.ndim)]) for dim in (source, target)]
    chosen = jax.random.permutation(own_key, blocks)[partner]
    strong = (owner == chosen) | (owner == (partner + blocks // 2) % blocks)
    return jnp.where(strong, factor * entries, entries)


def shard_levels(rng, extent, pieces, smallest, top_value):
    level = 1.0
    for axis_at, blocks in pieces:
        heights = jax.random.uniform(jax.random.fold_in(jax.random.fold_in(rng, 6), axis_at), (blocks,), jnp.float32, smallest / len(pieces), top_value / len(pieces))
        level = level * jnp.repeat(jnp.exp(heights), extent[axis_at] // blocks).reshape((-1,) + (1,) * (len(extent) - 1 - axis_at))
    return level


def gaussian(key, extent, deviation, limit, cuts=(), kind=jnp.bfloat16):
    values = jax.random.normal(key, extent, jnp.float32) * deviation
    if len(cuts) > 0:
        values = shard_levels(key, extent, cuts, -0.22, 0.18) * values
    return jnp.clip(values, min=-limit, max=limit).astype(kind)


def noise_with(stream_key, shape, scale, most, shards, heavy, kind=jnp.bfloat16):
    values = scale * jax.random.normal(stream_key, shape, jnp.float32)
    if shards:
        values = values * shard_levels(stream_key, shape, shards, -0.22, 0.18)
    return jnp.clip(raised(values, jax.random.fold_in(stream_key, 3), *heavy), -most, most).astype(kind)


def setup_inputs(seed: int = 0) -> dict:
    arg_keys = jax.random.split(jax.random.key(seed), 12)
    return {
        "layer_input": gaussian(arg_keys[0], (N_DP, ROW, D), 1.0, 6.0, ((0, 16), (1, 2))),
        "encoder_states": gaussian(arg_keys[1], (N_DP, CLIPS, FRAMES, D), 1.0, 6.0, ((0, 16), (2, 2))),
        "clip_lengths": draw_clip_lengths(jax.random.fold_in(arg_keys[11], 71), 0),
        "out_grad": noise_with(arg_keys[3], (N_DP, ROW, D), 1.0, 6.0, ((0, 16), (1, 2)), (0, 2, 16, 2.0)),
        "self_weights": draw_self_weights(jax.random.fold_in(arg_keys[11], 71), 0),
        "cross_weights": draw_cross_weights(jax.random.fold_in(arg_keys[11], 71), 0),
        "up_weights": gaussian(arg_keys[6], (D, FF), D ** -0.5, 0.21875, ((0, 32),)),
        "down_weights": gaussian(arg_keys[7], (FF, D), (FF // 2) ** -0.5, 0.15625, ((0, 32),)),
        "up_bias": gaussian(arg_keys[8], (FF,), 0.5, 3.0, ((0, 32),)),
        "down_bias": gaussian(arg_keys[9], (D,), 0.5, 3.0, ((0, 32),)),
        "vectors": draw_vectors(jax.random.fold_in(arg_keys[11], 71), 0),
    }


@jax.custom_vjp
def low(v):
    return lax.optimization_barrier(v.astype(jnp.bfloat16)).astype(jnp.float32)

@jax.custom_vjp
def low_back(v):
    return v

def low_keep(v):
    return (low(v), None)

def low_pass(kept, grad):
    return (grad,)

def back_keep(v):
    return (v, None)

def back_low(kept, grad):
    return (low(grad),)
low.defvjp(low_keep, low_pass)
low_back.defvjp(back_keep, back_low)
EXACT_MODE = lax.Precision.HIGHEST

def layer_norm(values, gain, shift):
    average = lax.optimization_barrier(jnp.mean(values, -1, keepdims=True))
    centred = values - average
    spread = lax.optimization_barrier(jnp.mean(centred * centred, -1, keepdims=True))
    return centred * lax.rsqrt(spread + 1e-05) * gain + shift

def matmul(left, right):
    return jnp.dot(left, right, precision=EXACT_MODE)

def attend(queries, key_rows, value_rows, allowed):
    row_count = queries.shape[0]
    head_query = queries.reshape(row_count, HEADS, HEAD_DIM)
    head_key = key_rows.reshape(key_rows.shape[0], HEADS, HEAD_DIM)
    head_value = value_rows.reshape(value_rows.shape[0], HEADS, HEAD_DIM)
    scores = low_back(jnp.einsum('qhd,khd->hqk', head_query, head_key, precision=EXACT_MODE) * 0.125)
    scores = jnp.where(allowed[None], scores, -1e+30)
    row_peak = lax.optimization_barrier(jnp.max(scores, -1, keepdims=True))
    exp_terms = jnp.exp(scores - row_peak)
    weights = low(exp_terms / lax.optimization_barrier(jnp.sum(exp_terms, -1, keepdims=True)))
    result = jnp.einsum('hqk,khd->qhd', weights, head_value, precision=EXACT_MODE)
    return result.reshape(row_count, -1)

def layer_row(params, row_input, row_frames, row_lengths):
    self_full, cross_full, up_full, down_full, bias_full, out_bias_full, vector_cols = params
    vector_full = vector_cols.T
    model_width = row_input.shape[1]
    row_span = row_input.shape[0]
    position = jnp.arange(row_span, dtype=jnp.int32)
    clip_ends = jnp.cumsum(row_lengths).astype(jnp.int32)
    segment = lax.optimization_barrier(jnp.sum((position[:, None] >= clip_ends[None, :]).astype(jnp.int32), 1))
    allowed = (segment[:, None] == segment[None, :]) & (position[None, :] <= position[:, None])
    normed_one = low(layer_norm(row_input, vector_full[0], vector_full[1]))
    query = low(low_back(matmul(normed_one, self_full[:, :model_width]) + vector_full[6]))
    key_own = low(low_back(matmul(normed_one, self_full[:, model_width:2 * model_width])))
    value_own = low(low_back(matmul(normed_one, self_full[:, 2 * model_width:3 * model_width]) + vector_full[7]))
    attended = low(low_back(attend(query, key_own, value_own, allowed)))
    after_self = row_input + low_back(matmul(attended, self_full[:, 3 * model_width:]) + vector_full[8])
    normed_two = low(layer_norm(after_self, vector_full[2], vector_full[3]))
    cross_query = low(low_back(matmul(normed_two, cross_full[:, :model_width]) + vector_full[9]))
    cross_key = low(low_back(jnp.einsum('cfd,de->cfe', row_frames, cross_full[:, model_width:2 * model_width], precision=EXACT_MODE)))
    cross_value = low(low_back(jnp.einsum('cfd,de->cfe', row_frames, cross_full[:, 2 * model_width:3 * model_width], precision=EXACT_MODE) + vector_full[10]))
    full_rows = jnp.ones((row_span, row_frames.shape[1]), bool)
    mixed = jnp.zeros((row_span, model_width), jnp.float32)
    for clip_index in range(CLIPS):
        result = attend(cross_query, cross_key[clip_index], cross_value[clip_index], full_rows)
        mixed = mixed + jnp.where((segment == clip_index)[:, None], result, 0.0)
    mixed = low(low_back(mixed))
    after_cross = after_self + low_back(matmul(mixed, cross_full[:, 3 * model_width:]) + vector_full[11])
    normed_three = low(layer_norm(after_cross, vector_full[4], vector_full[5]))
    pre_act = low_back(matmul(normed_three, up_full) + bias_full)
    activated = low(low_back(jax.nn.gelu(pre_act, approximate=False)))
    return after_cross + low_back(matmul(activated, down_full) + out_bias_full)

def reference(layer_input, encoder_states, clip_lengths, out_grad, self_weights, cross_weights, up_weights, down_weights, up_bias, down_bias, vectors):
    params = (self_weights.astype(jnp.float32), cross_weights.astype(jnp.float32), up_weights.astype(jnp.float32), down_weights.astype(jnp.float32), up_bias.astype(jnp.float32), down_bias.astype(jnp.float32), vectors.astype(jnp.float32))
    inputs = layer_input.astype(jnp.float32)
    frames = encoder_states.astype(jnp.float32)

    def forward(weights_all, inputs_all, frames_all):
        row_step = jax.checkpoint(layer_row)

        def scan_row(state_carry, row_item):
            return (state_carry, row_step(weights_all, row_item[0], row_item[1], row_item[2]))
        _, rows_out = lax.scan(scan_row, jnp.zeros((), jnp.float32), (inputs_all, frames_all, clip_lengths))
        return rows_out
    output, pullback = jax.vjp(forward, params, inputs, frames)
    grad_params, grad_input, grad_frames = pullback(out_grad.astype(jnp.float32))
    return (output.astype(jnp.bfloat16), grad_input, grad_frames, grad_params[0], grad_params[1], grad_params[2], grad_params[3], grad_params[4], grad_params[5], grad_params[6])
```

```python
import functools

import jax
import jax.numpy as jnp
from jax import lax
from jax.experimental import pallas as pl
from jax.experimental.pallas import tpu as pltpu
from jax.sharding import PartitionSpec as P

HEAD_DIM = 64
GROUP_HEADS = 4
CLIPS = 3
MESH = pl.DeviceIdType.MESH
Z = 4


class Place:
    def __init__(self):
        self.dp = lax.axis_index("dp")
        self.core = lax.axis_index("seq")
        self.z = self.dp // 4
        self.p = self.dp % 4
        x, y = self.p % 2, self.p // 2
        px, py = self.p + 1 - 2 * x, self.p + 2 - 4 * y
        self.p_first = px * (1 - self.core) + py * self.core
        self.p_second = py * (1 - self.core) + px * self.core
        self.p_diag = 3 - self.p
        base = self.z * 4
        self.first = (base + self.p_first, self.core)
        self.second = (base + self.p_second, self.core)
        self.up = (lax.rem(self.dp + 4, 16), self.core)
        self.down = (lax.rem(self.dp + 12, 16), self.core)
        self.mate = (self.dp, 1 - self.core)
        self.has_up = self.z < Z - 1
        self.has_down = self.z > 0

    def greet(self):
        barrier = pltpu.get_barrier_semaphore()
        for target in (self.mate, self.first, self.second):
            pl.semaphore_signal(barrier, inc=1, device_id=target, device_id_type=MESH)

        @pl.when(self.has_up)
        def _():
            pl.semaphore_signal(barrier, inc=1, device_id=self.up, device_id_type=MESH)

        @pl.when(self.has_down)
        def _():
            pl.semaphore_signal(barrier, inc=1, device_id=self.down, device_id_type=MESH)

        pl.semaphore_wait(barrier, 3 + (self.z + 3) // 4 + (6 - self.z) // 4)


def when(cond, fn):
    if cond is None:
        fn()
    else:
        pl.when(cond)(fn)


def both(a, b):
    if a is None:
        return b
    if b is None:
        return a
    return jnp.logical_and(a, b)


def gather_kernel(count, plane_first, *refs):
    ins, outs = refs[:count], refs[count:2 * count]
    send_sem, recv_sem, own_sem = refs[2 * count:]
    me = Place()
    me.greet()
    sends = []

    def block(z, p):
        return (z * 4 + p) * 2 + me.core

    def send(m, src, index, target, cond):
        slot = len(sends)
        copy = pltpu.make_async_remote_copy(
            src_ref=src, dst_ref=outs[m].at[index], send_sem=send_sem.at[slot],
            recv_sem=recv_sem.at[m, index], device_id=target, device_id_type=MESH)
        sends.append((cond, copy))
        when(cond, copy.start)

    def arrive(m, index, cond):
        def go():
            pltpu.make_async_remote_copy(
                src_ref=ins[m], dst_ref=outs[m].at[index], send_sem=send_sem.at[0],
                recv_sem=recv_sem.at[m, index], device_id=me.mate, device_id_type=MESH).wait_recv()
        when(cond, go)

    def forward(m, z, p, targets, cond=None):
        index = block(z, p)
        arrive(m, index, cond)
        for target, extra in targets:
            send(m, outs[m].at[index], index, target, both(cond, extra))

    own = block(me.z, me.p)
    for m in range(count):
        targets = [(me.up, me.has_up), (me.down, me.has_down), (me.first, None), (me.second, None), (me.mate, None)]
        if m in plane_first:
            targets = targets[2:4] + targets[:2] + targets[4:]
        for target, cond in targets:
            send(m, ins[m], own, target, cond)
    for m in range(count):
        pltpu.make_async_copy(ins[m], outs[m].at[own], own_sem.at[m]).start()

    up = [(me.up, me.has_up)]
    down = [(me.down, me.has_down)]
    mate = [(me.mate, None)]
    for m in plane_first:
        forward(m, me.z, me.p_first, [(me.second, None)] + up + down + mate)
        forward(m, me.z, me.p_second, up + down + mate)
        forward(m, me.z, me.p_diag, up + down + mate)
    line_first = [m for m in range(count) if m not in plane_first]
    for d in range(1, Z + 1):
        for m in range(count):
            below, above = me.z - d, me.z + d
            if d < Z:
                if m in plane_first:
                    for p in (me.p, me.p_first, me.p_second, me.p_diag):
                        forward(m, below, p, up + mate, below >= 0)
                        forward(m, above, p, down + mate, above < Z)
                else:
                    plane = [(me.first, None), (me.second, None)] + mate
                    forward(m, below, me.p, up + plane, below >= 0)
                    forward(m, above, me.p, down + plane, above < Z)
            if m not in plane_first:
                if d == 1:
                    forward(m, me.z, me.p_first, [(me.second, None)] + mate)
                else:
                    forward(m, below + 1, me.p_first, [(me.second, None)] + mate, below + 1 >= 0)
                    forward(m, above - 1, me.p_first, [(me.second, None)] + mate, above - 1 < Z)
    for p in (me.p_second, me.p_diag):
        for m in line_first:
            for d in range(Z):
                if d == 0:
                    forward(m, me.z, p, mate)
                else:
                    forward(m, me.z - d, p, mate, me.z - d >= 0)
                    forward(m, me.z + d, p, mate, me.z + d < Z)
    for m in range(count):
        pltpu.make_async_copy(ins[m], outs[m].at[own], own_sem.at[m]).wait()
        for q in range(16):
            arrive(m, q * 2 + 1 - me.core, None)
    for cond, copy in sends:
        when(cond, copy.wait_send)


def gather_all(shards, plane_first):
    count = len(shards)
    any_spec = pl.BlockSpec(memory_space=pl.ANY)
    return pl.pallas_call(
        functools.partial(gather_kernel, count, plane_first),
        out_shape=tuple(jax.ShapeDtypeStruct((32,) + s.shape, s.dtype) for s in shards),
        in_specs=[any_spec] * count,
        out_specs=tuple([any_spec] * count),
        scratch_shapes=[
            pltpu.SemaphoreType.DMA((80 * count,)),
            pltpu.SemaphoreType.DMA((count, 32)),
            pltpu.SemaphoreType.DMA((count,)),
        ],
        compiler_params=pltpu.CompilerParams(collective_id=0, has_side_effects=True),
        name="gather_all",
    )(*shards)


def scatter_kernel(count, *refs):
    grads, outs = refs[:count], refs[count:2 * count]
    scratch = refs[2 * count:]
    owns, pairs, plane_as, plane_bs, plane_cs, lines = (scratch[k * count:(k + 1) * count] for k in range(6))
    send_sem, own_sem, pair_sem, plane_sem, line_sem = scratch[6 * count:]
    me = Place()
    half = me.z // 2
    near = me.z + half * (3 - 2 * me.z)

    def far(k):
        base = (3, 2, 1 - near, near)[k]
        return base + half * (3 - 2 * base)

    order = [far(k) for k in range(4)]
    plane = [me.p_diag, me.p_first, me.p_second, me.p]
    mate_plane = [me.p_diag, me.p_second, me.p_first, me.p]
    for k in range(4):
        for m in range(count):
            pltpu.make_async_copy(grads[m].at[:, plane[k], me.core], owns[m].at[:, plane[k]], own_sem.at[m, plane[k]]).start()
    me.greet()
    sends = []

    def send(src, dst, sem, target, cond=None):
        slot = len(sends)
        copy = pltpu.make_async_remote_copy(src_ref=src, dst_ref=dst, send_sem=send_sem.at[slot], recv_sem=sem, device_id=target, device_id_type=MESH)
        sends.append((cond, copy))
        when(cond, copy.start)

    def arrive(dst, sem, cond=None):
        when(cond, pltpu.make_async_remote_copy(src_ref=dst, dst_ref=dst, send_sem=send_sem.at[0], recv_sem=sem, device_id=me.mate, device_id_type=MESH).wait_recv)

    for k in range(4):
        for m in range(count):
            p = mate_plane[k]
            send(grads[m].at[:, p, 1 - me.core], pairs[m].at[:, p], pair_sem.at[m, p], me.mate)

    def paired(m, p):
        pltpu.make_async_copy(grads[m].at[:, p, me.core], owns[m].at[:, p], own_sem.at[m, p]).wait()
        arrive(pairs[m].at[:, p], pair_sem.at[m, p])

    def add(dst, *others):
        total = dst[...].astype(jnp.float32)
        for other in others:
            total = total + other[...].astype(jnp.float32)
        dst[...] = total.astype(dst.dtype)

    def steps(m):
        own = owns[m]
        paired(m, me.p_diag)
        for k in range(4):
            z = order[k]
            add(own.at[z, me.p_diag], pairs[m].at[z, me.p_diag])
            send(own.at[z, me.p_diag], plane_as[m].at[z], plane_sem.at[m, 0, z], me.second)
        yield
        paired(m, me.p_second)
        for k in range(4):
            z = order[k]
            add(own.at[z, me.p_second], pairs[m].at[z, me.p_second])
            send(own.at[z, me.p_second], plane_cs[m].at[z], plane_sem.at[m, 2, z], me.second)
        yield
        paired(m, me.p_first)
        for k in range(4):
            z = order[k]
            arrive(plane_as[m].at[z], plane_sem.at[m, 0, z])
            add(own.at[z, me.p_first], pairs[m].at[z, me.p_first], plane_as[m].at[z])
            send(own.at[z, me.p_first], plane_bs[m].at[z], plane_sem.at[m, 1, z], me.first)
        yield
        paired(m, me.p)
        for k in range(4):
            z = order[k]
            arrive(plane_bs[m].at[z], plane_sem.at[m, 1, z])
            arrive(plane_cs[m].at[z], plane_sem.at[m, 2, z])
            if k == 3:
                break
            add(own.at[z, me.p], pairs[m].at[z, me.p], plane_bs[m].at[z], plane_cs[m].at[z])
            upward = (z - me.z + 3) // 4
            source = me.z + 1 - 2 * upward
            came = jnp.logical_and(source >= 0, source < Z)

            def gather_in(z=z, upward=upward):
                slot = lines[m].at[upward, z]
                arrive(slot, line_sem.at[m, upward, z])
                add(own.at[z, me.p], slot)

            pl.when(came)(gather_in)
            target = (lax.rem(me.dp + 12 + 8 * upward, 16), me.core)
            send(own.at[z, me.p], lines[m].at[upward, z], line_sem.at[m, upward, z], target)
        yield
        z = me.z
        total = own[z, me.p].astype(jnp.float32) + pairs[m][z, me.p].astype(jnp.float32)
        total = total + plane_bs[m][z].astype(jnp.float32) + plane_cs[m][z].astype(jnp.float32)
        outs[m][...] = total
        for upward, cond in ((0, me.has_up), (1, me.has_down)):

            def last(upward=upward):
                arrive(lines[m].at[upward, z], line_sem.at[m, upward, z])
                outs[m][...] += lines[m][upward, z].astype(jnp.float32)

            pl.when(cond)(last)

    running = [steps(m) for m in range(count)]
    while running:
        still = []
        for step in running:
            try:
                next(step)
                still.append(step)
            except StopIteration:
                pass
        running = still
    for cond, copy in sends:
        when(cond, copy.wait_send)


def scatter_all(grads):
    count = len(grads)
    shapes = [g.shape[1:] for g in grads]
    views = [g.reshape((4, 4, 2) + s) for g, s in zip(grads, shapes)]

    def vmem(*lead):
        return [pltpu.VMEM(lead + s, g.dtype) for g, s in zip(grads, shapes)]

    return pl.pallas_call(
        functools.partial(scatter_kernel, count),
        out_shape=tuple(jax.ShapeDtypeStruct(s, jnp.float32) for s in shapes),
        in_specs=[pl.BlockSpec(memory_space=pl.ANY)] * count,
        out_specs=tuple([pl.BlockSpec(memory_space=pltpu.VMEM)] * count),
        scratch_shapes=vmem(4, 4) + vmem(4, 4) + vmem(4) + vmem(4) + vmem(4) + vmem(2, 4) + [
            pltpu.SemaphoreType.DMA((20 * count,)),
            pltpu.SemaphoreType.DMA((count, 4)),
            pltpu.SemaphoreType.DMA((count, 4)),
            pltpu.SemaphoreType.DMA((count, 3, 4)),
            pltpu.SemaphoreType.DMA((count, 2, 4)),
        ],
        compiler_params=pltpu.CompilerParams(collective_id=1, has_side_effects=True, vmem_limit_bytes=60 * 2**20),
        name="scatter_all",
    )(*views)


def pack_rows(up_bias, down_bias, vectors, size):
    rows = jnp.concatenate([up_bias, down_bias, vectors], 1)
    return jnp.pad(rows, ((0, 0), (0, size - rows.shape[1])))


def gather_weights(self_weights, cross_weights, up_weights, down_weights, up_bias, down_bias, vectors):
    if lax.axis_size("dp") != 16:
        return tuple(
            lax.all_gather(part, ("dp", "seq"), axis=0, tiled=True)
            for part in (self_weights, cross_weights, up_weights, down_weights, up_bias, down_bias, vectors)
        )
    small = pack_rows(up_bias[None], down_bias[None], vectors.reshape(1, -1), 2048).reshape(16, 128)
    whole = gather_all((self_weights, cross_weights, up_weights, down_weights, small), ())
    rows = whole[4].reshape(32, 2048)
    n_up, n_down = up_bias.shape[0], down_bias.shape[0]
    n_all = n_up + n_down + vectors.size
    return tuple(w.reshape(-1, w.shape[2]) for w in whole[:4]) + (
        rows[:, :n_up].reshape(-1),
        rows[:, n_up:n_up + n_down].reshape(-1),
        rows[:, n_up + n_down:n_all].reshape(-1, vectors.shape[1]),
    )


def scatter_grads(grads_self, grads_cross, grad_up, grad_down, grad_up_bias, grad_out_bias, vector_grads):
    parts = (grads_self, grads_cross, grad_up, grad_down, grad_up_bias, grad_out_bias, vector_grads)
    if lax.axis_size("dp") != 16:
        return tuple(lax.psum_scatter(part, ("dp", "seq"), scatter_dimension=0, tiled=True) for part in parts)
    small = pack_rows(
        grad_up_bias.reshape(32, -1), grad_out_bias.reshape(32, -1), vector_grads.reshape(32, -1), 1024
    ).reshape(32, 8, 128)
    large = tuple(g.astype(jnp.bfloat16).reshape(32, -1, g.shape[1]) for g in parts[:4])
    whole = scatter_all(large + (small,))
    row = whole[4].reshape(-1)
    n_up, n_down, n_vec = (g.size // 32 for g in parts[4:])
    return tuple(whole[:4]) + (
        row[:n_up],
        row[n_up:n_up + n_down],
        row[n_up + n_down:n_up + n_down + n_vec].reshape(-1, vector_grads.shape[1]),
    )


def seq_scatter(value):
    span = value.shape[0] // 2
    half = lax.axis_index("seq")
    mine = lax.dynamic_slice_in_dim(value, half * span, span, 0)
    other = lax.dynamic_slice_in_dim(value, (1 - half) * span, span, 0).astype(jnp.bfloat16)
    came = lax.ppermute(other, "seq", [(0, 1), (1, 0)])
    return mine + came.astype(value.dtype)


def from_behind(value, axis, steps):
    count = lax.axis_size(axis)
    leading, last = (max(0, -steps), min(count, count - steps))
    return lax.ppermute(value, axis, [(source, source + steps) for source in range(leading, last)])


def joined(array, axis, combine):
    everything = jax.tree.map(lambda part: lax.all_gather(part, axis), array)
    leading = jax.tree.map(lambda part: part[0], everything)

    def lap(k, so_far):
        return combine(so_far, jax.tree.map(lambda part: part[k], everything))

    return lax.fori_loop(1, lax.axis_size(axis), lap, leading)


def layer_norm(values, gain, shift):
    average = jnp.mean(values, -1, keepdims=True)
    centred = values - average
    spread = jnp.mean(centred * centred, -1, keepdims=True)
    return centred * lax.rsqrt(spread + 1e-05) * gain + shift


def exact_gelu(values):
    return jax.nn.gelu(values, approximate=False)


def matmul(left, right):
    return jnp.dot(left, right, preferred_element_type=jnp.float32)


def split_heads(values):
    return values.reshape(values.shape[0], -1, GROUP_HEADS, HEAD_DIM).transpose(1, 0, 2, 3)


def join_heads(values):
    return values.transpose(1, 0, 2, 3).reshape(values.shape[1], -1)


def group_scores(query_part, key_part, allowed):
    scores = (
        jnp.einsum("qhd,khd->hqk", query_part, key_part, preferred_element_type=jnp.float32) * 0.125
    )
    return jnp.where(allowed[None], scores, -1e30)


def plain_scores(query_part, key_part):
    return (
        jnp.einsum("qhd,khd->hqk", query_part, key_part, preferred_element_type=jnp.float32) * 0.125
    )


def attend_forward(queries, key_rows, value_rows, allowed):

    def one_group(operands):
        query_part, key_part, value_part = operands
        scores = group_scores(query_part, key_part, allowed)
        row_peak = jnp.max(scores, -1, keepdims=True)
        exp_terms = jnp.exp(scores - row_peak)
        row_total = jnp.sum(exp_terms, -1, keepdims=True)
        weights_low = (exp_terms / row_total).astype(jnp.bfloat16)
        result = jnp.einsum(
            "hqk,khd->qhd", weights_low, value_part, preferred_element_type=jnp.float32
        )
        return (result, (row_peak + jnp.log(row_total))[..., 0])

    return lax.map(one_group, (queries, key_rows, value_rows))


def attend_backward(queries, key_rows, value_rows, allowed, log_totals, grad_out):

    def one_group(operands):
        query_part, key_part, value_part, log_total, grad_part = operands
        scores = group_scores(query_part, key_part, allowed)
        weights = jnp.where(allowed[None], jnp.exp(scores - log_total[..., None]), 0.0)
        weights_low = weights.astype(jnp.bfloat16)
        grad_value = jnp.einsum(
            "hqk,qhd->khd", weights_low, grad_part, preferred_element_type=jnp.float32
        )
        grad_weights = jnp.einsum(
            "qhd,khd->hqk", grad_part, value_part, preferred_element_type=jnp.float32
        )
        inner = jnp.sum(grad_weights * weights, -1, keepdims=True)
        grad_scores = (weights * (grad_weights - inner)).astype(jnp.bfloat16)
        grad_query = (
            jnp.einsum("hqk,khd->qhd", grad_scores, key_part, preferred_element_type=jnp.float32)
            * 0.125
        )
        grad_key = (
            jnp.einsum("hqk,qhd->khd", grad_scores, query_part, preferred_element_type=jnp.float32)
            * 0.125
        )
        return (grad_query, grad_key, grad_value)

    return lax.map(one_group, (queries, key_rows, value_rows, log_totals, grad_out))


def local_totals(queries, key_rows):

    def one_group(operands):
        query_part, key_part = operands
        scores = plain_scores(query_part, key_part)
        row_peak = jnp.max(scores, -1)
        row_total = jnp.sum(jnp.exp(scores - row_peak[..., None]), -1)
        return (row_peak, row_total)

    return lax.map(one_group, (queries, key_rows))


def combine_totals(first, second):
    peak = jnp.maximum(first[0], second[0])
    total = first[1] * jnp.exp(first[0] - peak) + second[1] * jnp.exp(second[0] - peak)
    return (peak, total)


def partial_forward(queries, key_rows, value_rows, log_totals):

    def one_group(operands):
        query_part, key_part, value_part, log_total = operands
        scores = plain_scores(query_part, key_part)
        weights_low = jnp.exp(scores - log_total[..., None]).astype(jnp.bfloat16)
        return jnp.einsum(
            "hqk,khd->qhd", weights_low, value_part, preferred_element_type=jnp.float32
        )

    return lax.map(one_group, (queries, key_rows, value_rows, log_totals))


def partial_inner(queries, key_rows, value_rows, log_totals, grad_out):

    def one_group(operands):
        query_part, key_part, value_part, log_total, grad_part = operands
        scores = plain_scores(query_part, key_part)
        weights = jnp.exp(scores - log_total[..., None])
        grad_weights = jnp.einsum(
            "qhd,khd->hqk", grad_part, value_part, preferred_element_type=jnp.float32
        )
        return jnp.sum(grad_weights * weights, -1)

    return lax.map(one_group, (queries, key_rows, value_rows, log_totals, grad_out))


def partial_backward(queries, key_rows, value_rows, log_totals, inner_sums, grad_out):

    def one_group(operands):
        query_part, key_part, value_part, log_total, inner, grad_part = operands
        scores = plain_scores(query_part, key_part)
        weights = jnp.exp(scores - log_total[..., None])
        weights_low = weights.astype(jnp.bfloat16)
        grad_value = jnp.einsum(
            "hqk,qhd->khd", weights_low, grad_part, preferred_element_type=jnp.float32
        )
        grad_weights = jnp.einsum(
            "qhd,khd->hqk", grad_part, value_part, preferred_element_type=jnp.float32
        )
        grad_scores = (weights * (grad_weights - inner[..., None])).astype(jnp.bfloat16)
        grad_query = (
            jnp.einsum("hqk,khd->qhd", grad_scores, key_part, preferred_element_type=jnp.float32)
            * 0.125
        )
        grad_key = (
            jnp.einsum("hqk,qhd->khd", grad_scores, query_part, preferred_element_type=jnp.float32)
            * 0.125
        )
        return (grad_query, grad_key, grad_value)

    return lax.map(one_group, (queries, key_rows, value_rows, log_totals, inner_sums, grad_out))


def unpack(gathered):
    self_full, cross_full, up_full, down_full, bias_full, out_bias_full, vector_full = gathered
    return (
        self_full,
        cross_full,
        up_full,
        down_full,
        bias_full.astype(jnp.float32),
        out_bias_full.astype(jnp.float32),
        vector_full.astype(jnp.float32).T,
    )


def per_device(
    layer_input,
    encoder_states,
    clip_lengths,
    out_grad,
    self_weights,
    cross_weights,
    up_weights,
    down_weights,
    up_bias,
    down_bias,
    vectors,
):
    model_width = layer_input.shape[2]
    tok_span = layer_input.shape[1]
    seq_half = lax.axis_index("seq")
    gathered = gather_weights(
        self_weights, cross_weights, up_weights, down_weights, up_bias, down_bias, vectors
    )
    self_full, cross_full, up_full, down_full, bias_full, out_bias_full, vector_full = gathered
    return (
        self_full,
        cross_full,
        up_full,
        down_full,
        bias_full.astype(jnp.float32),
        out_bias_full.astype(jnp.float32),
        vector_full.astype(jnp.float32).T,
    )


def per_device(
    layer_input,
    encoder_states,
    clip_lengths,
    out_grad,
    self_weights,
    cross_weights,
    up_weights,
    down_weights,
    up_bias,
    down_bias,
    vectors,
):
    model_width = layer_input.shape[2]
    tok_span = layer_input.shape[1]
    seq_half = lax.axis_index("seq")
    gathered = (
        lax.all_gather(self_weights, ("dp", "seq"), axis=0, tiled=True),
        lax.all_gather(cross_weights, ("dp", "seq"), axis=0, tiled=True),
        lax.all_gather(up_weights, ("dp", "seq"), axis=0, tiled=True),
        lax.all_gather(down_weights, ("dp", "seq"), axis=0, tiled=True),
        lax.all_gather(up_bias, ("dp", "seq"), axis=0, tiled=True),
        lax.all_gather(down_bias, ("dp", "seq"), axis=0, tiled=True),
        lax.all_gather(vectors, ("dp", "seq"), axis=0, tiled=True),
    )
    self_full, cross_full, up_full, down_full, bias_full, out_bias_full, vector_full = unpack(
        gathered
    )
    source = layer_input[0].astype(jnp.float32)
    position = seq_half * tok_span + jnp.arange(tok_span, dtype=jnp.int32)
    clip_ends = jnp.cumsum(clip_lengths[0])
    segment = jnp.sum((position[:, None] >= clip_ends[None, :]).astype(jnp.int32), 1)
    key_position = jnp.concatenate([position - tok_span, position])
    key_segment = jnp.sum((key_position[:, None] >= clip_ends[None, :]).astype(jnp.int32), 1)
    allowed = (
        (key_segment[None, :] == segment[:, None])
        & (key_position[None, :] <= position[:, None])
        & (key_position[None, :] >= 0)
    )
    row_position = jnp.arange(2 * tok_span, dtype=jnp.int32)
    row_segment = jnp.sum((row_position[:, None] >= clip_ends[None, :]).astype(jnp.int32), 1)
    normed_one = layer_norm(source, vector_full[0], vector_full[1]).astype(jnp.bfloat16)
    proj_bias = jnp.concatenate([vector_full[6], jnp.zeros_like(vector_full[6]), vector_full[7]])
    qkv_low = (matmul(normed_one, self_full[:, : 3 * model_width]) + proj_bias).astype(jnp.bfloat16)
    query = qkv_low[:, :model_width]
    key_own = qkv_low[:, model_width : 2 * model_width]
    value_own = qkv_low[:, 2 * model_width :]
    key_prev, value_prev = from_behind((key_own, value_own), "seq", 1)
    key_heads = split_heads(jnp.concatenate([key_prev, key_own]))
    value_heads = split_heads(jnp.concatenate([value_prev, value_own]))
    query_heads = split_heads(query)
    attended, self_stats = attend_forward(query_heads, key_heads, value_heads, allowed)
    attended_low = join_heads(attended).astype(jnp.bfloat16)
    after_self = source + matmul(attended_low, self_full[:, 3 * model_width :]) + vector_full[8]
    normed_two = layer_norm(after_self, vector_full[2], vector_full[3]).astype(jnp.bfloat16)
    cross_query = (matmul(normed_two, cross_full[:, :model_width]) + vector_full[9]).astype(
        jnp.bfloat16
    )
    frames = encoder_states[0]
    clip_count = frames.shape[0]
    frames_here = frames.shape[1]
    flat_frames = frames.reshape(-1, model_width)
    cross_kv = matmul(flat_frames, cross_full[:, model_width : 3 * model_width])
    cross_key = (
        cross_kv[:, :model_width].astype(jnp.bfloat16).reshape(clip_count, frames_here, model_width)
    )
    cross_value = (
        (cross_kv[:, model_width:] + vector_full[10])
        .astype(jnp.bfloat16)
        .reshape(clip_count, frames_here, model_width)
    )
    cross_stats = []
    clip_keys = []
    clip_values = []
    row_query = lax.all_gather(cross_query, "seq", axis=0, tiled=True)
    cross_heads = split_heads(row_query)
    peak_list = []
    total_list = []
    for clip_index in range(CLIPS):
        clip_keys.append(split_heads(cross_key[clip_index]))
        clip_values.append(split_heads(cross_value[clip_index]))
        row_peak, row_total = local_totals(cross_heads, clip_keys[clip_index])
        peak_list.append(row_peak)
        total_list.append(row_total)
    all_peak, all_total = joined(
        (jnp.stack(peak_list), jnp.stack(total_list)), "seq", combine_totals
    )
    log_sums = all_peak + jnp.log(all_total)
    partial_value = jnp.zeros((2 * tok_span, model_width), jnp.float32)
    for clip_index in range(CLIPS):
        cross_stats.append(log_sums[clip_index])
        result = partial_forward(
            cross_heads, clip_keys[clip_index], clip_values[clip_index], log_sums[clip_index]
        )
        partial_value = partial_value + jnp.where(
            (row_segment == clip_index)[:, None], join_heads(result), 0.0
        )
    mixed = seq_scatter(partial_value).astype(jnp.bfloat16)
    after_cross = after_self + matmul(mixed, cross_full[:, 3 * model_width :]) + vector_full[11]
    normed_three = layer_norm(after_cross, vector_full[4], vector_full[5]).astype(jnp.bfloat16)
    pre_act = matmul(normed_three, up_full) + bias_full
    activated_low = exact_gelu(pre_act).astype(jnp.bfloat16)
    result_rows = after_cross + matmul(activated_low, down_full) + out_bias_full
    layer_output = result_rows.astype(jnp.bfloat16)[None]
    self_back, cross_back, up_back, down_back, vector_back = (
        self_full,
        cross_full,
        up_full,
        down_full,
        vector_full,
    )
    grad_low = out_grad[0]
    grad_rows = grad_low.astype(jnp.float32)
    grad_down = matmul(activated_low.T, grad_low)
    grad_out_bias = jnp.sum(grad_rows, 0)
    grad_act = matmul(grad_low, down_back.T).astype(jnp.bfloat16)
    _, gelu_pull = jax.vjp(exact_gelu, pre_act)
    grad_pre = gelu_pull(grad_act.astype(jnp.float32))[0].astype(jnp.bfloat16)
    grad_up = matmul(normed_three.T, grad_pre)
    grad_up_bias = jnp.sum(grad_pre, 0, dtype=jnp.float32)
    grad_normed_three = matmul(grad_pre, up_back.T)
    _, norm_pull_three = jax.vjp(layer_norm, after_cross, vector_back[4], vector_back[5])
    grad_part, grad_gain_three, grad_shift_three = norm_pull_three(grad_normed_three)
    grad_after_cross = grad_rows + grad_part
    grad_cross_low = grad_after_cross.astype(jnp.bfloat16)
    grad_cross_out = matmul(mixed.T, grad_cross_low)
    grad_cross_bias = jnp.sum(grad_cross_low, 0, dtype=jnp.float32)
    grad_mixed = matmul(grad_cross_low, cross_back[:, 3 * model_width :].T).astype(jnp.bfloat16)
    grad_keys = []
    grad_values = []
    row_grad = lax.all_gather(grad_mixed, "seq", axis=0, tiled=True)
    grad_pieces = []
    inner_list = []
    for clip_index in range(CLIPS):
        row_mask = (row_segment == clip_index)[:, None]
        grad_piece = split_heads(jnp.where(row_mask, row_grad, jnp.zeros_like(row_grad)))
        grad_pieces.append(grad_piece)
        inner_list.append(
            partial_inner(
                cross_heads,
                clip_keys[clip_index],
                clip_values[clip_index],
                cross_stats[clip_index],
                grad_piece,
            )
        )
    inner_all = lax.psum(jnp.stack(inner_list).astype(jnp.bfloat16), "seq").astype(jnp.float32)
    partial_query = jnp.zeros((2 * tok_span, model_width), jnp.float32)
    for clip_index in range(CLIPS):
        grad_query, grad_key, grad_value = partial_backward(
            cross_heads,
            clip_keys[clip_index],
            clip_values[clip_index],
            cross_stats[clip_index],
            inner_all[clip_index],
            grad_pieces[clip_index],
        )
        partial_query = partial_query + join_heads(grad_query)
        grad_keys.append(join_heads(grad_key))
        grad_values.append(join_heads(grad_value))
    grad_query_sum = seq_scatter(partial_query).astype(jnp.bfloat16)
    own_key_grad = jnp.stack(grad_keys)
    own_value_grad = jnp.stack(grad_values)
    grad_cq_weight = matmul(normed_two.T, grad_query_sum)
    grad_cq_bias = jnp.sum(grad_query_sum, 0, dtype=jnp.float32)
    grad_normed_two = matmul(grad_query_sum, cross_back[:, :model_width].T)
    own_kv_low = jnp.concatenate(
        [own_key_grad.reshape(-1, model_width), own_value_grad.reshape(-1, model_width)], 1
    ).astype(jnp.bfloat16)
    grad_ckv_weight = matmul(flat_frames.T, own_kv_low)
    grad_cv_bias = jnp.sum(own_kv_low[:, model_width:], 0, dtype=jnp.float32)
    encoder_grad = matmul(own_kv_low, cross_back[:, model_width : 3 * model_width].T).reshape(
        1, clip_count, frames_here, model_width
    )
    _, norm_pull_two = jax.vjp(layer_norm, after_self, vector_back[2], vector_back[3])
    grad_part, grad_gain_two, grad_shift_two = norm_pull_two(grad_normed_two)
    grad_after_self = grad_after_cross + grad_part
    grad_self_low = grad_after_self.astype(jnp.bfloat16)
    grad_self_out = matmul(attended_low.T, grad_self_low)
    grad_self_bias = jnp.sum(grad_self_low, 0, dtype=jnp.float32)
    grad_attended = matmul(grad_self_low, self_back[:, 3 * model_width :].T).astype(jnp.bfloat16)
    grad_query, grad_key, grad_value = attend_backward(
        query_heads, key_heads, value_heads, allowed, self_stats, split_heads(grad_attended)
    )
    grad_query = join_heads(grad_query)
    grad_key = join_heads(grad_key)
    grad_value = join_heads(grad_value)
    back_key, back_value = (
        from_behind(grad_key[:tok_span].astype(jnp.bfloat16), "seq", -1).astype(jnp.float32),
        from_behind(grad_value[:tok_span].astype(jnp.bfloat16), "seq", -1).astype(jnp.float32),
    )
    grad_qkv_low = jnp.concatenate(
        [grad_query, grad_key[tok_span:] + back_key, grad_value[tok_span:] + back_value], 1
    ).astype(jnp.bfloat16)
    grad_qkv_weight = matmul(normed_one.T, grad_qkv_low)
    grad_qkv_bias = jnp.sum(grad_qkv_low, 0, dtype=jnp.float32)
    grad_normed_one = matmul(grad_qkv_low, self_back[:, : 3 * model_width].T)
    _, norm_pull_one = jax.vjp(layer_norm, source, vector_back[0], vector_back[1])
    grad_part, grad_gain_one, grad_shift_one = norm_pull_one(grad_normed_one)
    input_grad = (grad_after_self + grad_part)[None]
    grads_self = jnp.concatenate([grad_qkv_weight, grad_self_out], 1)
    grads_cross = jnp.concatenate([grad_cq_weight, grad_ckv_weight, grad_cross_out], 1)
    vector_grads = jnp.stack(
        [
            grad_gain_one,
            grad_shift_one,
            grad_gain_two,
            grad_shift_two,
            grad_gain_three,
            grad_shift_three,
            grad_qkv_bias[:model_width],
            grad_qkv_bias[2 * model_width :],
            grad_self_bias,
            grad_cq_bias,
            grad_cv_bias,
            grad_cross_bias,
        ],
        1,
    )
    shares = scatter_grads(
        grads_self, grads_cross, grad_up, grad_down, grad_up_bias, grad_out_bias, vector_grads
    )
    return (
        layer_output,
        input_grad,
        encoder_grad,
        shares[0],
        shares[1],
        shares[2],
        shares[3],
        shares[4],
        shares[5],
        shares[6],
    )


def solution(mesh):
    return jax.shard_map(
        per_device,
        mesh=mesh,
        in_specs=(
            P("dp", "seq", None),
            P("dp", None, "seq", None),
            P("dp", None),
            P("dp", "seq", None),
            P(("dp", "seq"), None),
            P(("dp", "seq"), None),
            P(("dp", "seq"), None),
            P(("dp", "seq"), None),
            P(("dp", "seq")),
            P(("dp", "seq")),
            P(("dp", "seq"), None),
        ),
        out_specs=(
            P("dp", "seq", None),
            P("dp", "seq", None),
            P("dp", None, "seq", None),
            P(("dp", "seq"), None),
            P(("dp", "seq"), None),
            P(("dp", "seq"), None),
            P(("dp", "seq"), None),
            P(("dp", "seq")),
            P(("dp", "seq")),
            P(("dp", "seq"), None),
        ),
        check_vma=False,
    )
```

```python
import functools

import jax
import jax.numpy as jnp
from jax import lax
from jax.experimental import pallas as pl
from jax.experimental.pallas import tpu as pltpu
from jax.sharding import PartitionSpec as P

HEAD_DIM = 64
CLIPS = 3
MESH = pl.DeviceIdType.MESH
NT = (((1,), (1,)), ((), ()))
NN = (((1,), (0,)), ((), ()))


def dot(left, right, dims):
    return lax.dot_general(left, right, dims, preferred_element_type=jnp.float32)


def one_head(values, h):
    lane = lax.broadcasted_iota(jnp.int32, values.shape, 1)
    return jnp.where((lane >= 64) == (h == 1), values, jnp.zeros_like(values))


def self_forward_kernel(q_ref, k_ref, v_ref, bias_ref, out_ref, lse_ref):
    keys = k_ref[...]
    values_t = v_ref[...].T
    halves = []
    for h in range(2):
        scores = dot(keys, one_head(q_ref[...], h), NT) + bias_ref[...]
        peak = jnp.max(scores, 0, keepdims=True)
        terms = jnp.exp(scores - peak)
        total = jnp.sum(terms, 0, keepdims=True)
        result = dot(values_t[h * 64:(h + 1) * 64], terms.astype(jnp.bfloat16), NN)
        halves.append(result / total)
        lse_ref[0, h:h + 1] = peak + jnp.log(total)
    out_ref[...] = jnp.concatenate(halves, 0).T.astype(out_ref.dtype)


def self_forward(q, k, v, bias):
    toks, width = q.shape
    keys = k.shape[0]
    return pl.pallas_call(
        self_forward_kernel,
        grid=(width // 128,),
        in_specs=[
            pl.BlockSpec((toks, 128), lambda j: (0, j)),
            pl.BlockSpec((keys, 128), lambda j: (0, j)),
            pl.BlockSpec((keys, 128), lambda j: (0, j)),
            pl.BlockSpec((keys, toks), lambda j: (0, 0)),
        ],
        out_specs=[
            pl.BlockSpec((toks, 128), lambda j: (0, j)),
            pl.BlockSpec((1, 2, toks), lambda j: (j, 0, 0)),
        ],
        out_shape=[
            jax.ShapeDtypeStruct((toks, width), jnp.float32),
            jax.ShapeDtypeStruct((width // 128, 2, toks), jnp.float32),
        ],
        compiler_params=pltpu.CompilerParams(vmem_limit_bytes=48 * 2**20),
        name="self_forward",
    )(q, k, v, bias)


def self_backward_kernel(q_ref, k_ref, v_ref, bias_ref, lse_ref, inner_ref, g_ref, dq_ref, dk_ref, dv_ref):
    keys, values = k_ref[...], v_ref[...]
    keys_t = keys.T
    grad_k = grad_v = None
    halves = []
    for h in range(2):
        query, grad = one_head(q_ref[...], h), one_head(g_ref[...], h)
        weights = jnp.exp(dot(keys, query, NT) + bias_ref[...] - lse_ref[0, h:h + 1])
        part = dot(weights.astype(jnp.bfloat16), grad, NN)
        grad_v = part if grad_v is None else grad_v + part
        grad_s = (weights * (dot(values, grad, NT) - inner_ref[0, h:h + 1])).astype(jnp.bfloat16)
        part = dot(grad_s, query, NN)
        grad_k = part if grad_k is None else grad_k + part
        halves.append(dot(keys_t[h * 64:(h + 1) * 64], grad_s, NN))
    dq_ref[...] = (jnp.concatenate(halves, 0) * 0.125).T
    dk_ref[...] = grad_k
    dv_ref[...] = grad_v


def self_backward(q, k, v, bias, lse, inner, grad):
    toks, width = q.shape
    keys = k.shape[0]
    tok_spec = pl.BlockSpec((toks, 128), lambda j: (0, j))
    key_spec = pl.BlockSpec((keys, 128), lambda j: (0, j))
    row_spec = pl.BlockSpec((1, 2, toks), lambda j: (j, 0, 0))
    return pl.pallas_call(
        self_backward_kernel,
        grid=(width // 128,),
        in_specs=[tok_spec, key_spec, key_spec, pl.BlockSpec((keys, toks), lambda j: (0, 0)), row_spec, row_spec, tok_spec],
        out_specs=[tok_spec, key_spec, key_spec],
        out_shape=[
            jax.ShapeDtypeStruct((toks, width), jnp.float32),
            jax.ShapeDtypeStruct((keys, width), jnp.float32),
            jax.ShapeDtypeStruct((keys, width), jnp.float32),
        ],
        compiler_params=pltpu.CompilerParams(vmem_limit_bytes=48 * 2**20),
        name="self_backward",
    )(q, k, v, bias, lse, inner, grad)


def cross_forward_kernel(which, q_ref, k_ref, v_ref, seg_ref, out_ref, stat_ref, acc_ref):
    big = which[0]

    def attend(clip, values_t, query, h):
        scores = dot(k_ref[clip], query, NT)
        peak = jnp.max(scores, 0, keepdims=True)
        terms = jnp.exp(scores - peak)
        total = jnp.sum(terms, 0, keepdims=True)
        result = dot(values_t[h * 64:(h + 1) * 64], terms.astype(jnp.bfloat16), NN)
        return result / total, peak, total

    values_t = v_ref[big].T
    for h in range(2):
        mine = seg_ref[...] == big
        result, peak, total = attend(big, values_t, one_head(q_ref[...], h), h)
        acc_ref[h * 64:(h + 1) * 64] = jnp.where(mine, result, 0.0)
        stat_ref[0, h:h + 1] = jnp.where(mine, peak, 0.0)
        stat_ref[0, 2 + h:3 + h] = jnp.where(mine, total, 1.0)
    for k in (1, 2):
        clip = which[k]
        cols = pl.ds(pl.multiple_of(which[2 + k] * 128, 128), 128)
        values_t = v_ref[clip].T
        mine = seg_ref[:, cols] == clip
        for h in range(2):
            result, peak, total = attend(clip, values_t, one_head(q_ref[cols], h), h)
            rows = slice(h * 64, (h + 1) * 64)
            acc_ref[rows, cols] = jnp.where(mine, result, acc_ref[rows, cols])
            stat_ref[0, h:h + 1, cols] = jnp.where(mine, peak, stat_ref[0, h:h + 1, cols])
            stat_ref[0, 2 + h:3 + h, cols] = jnp.where(mine, total, stat_ref[0, 2 + h:3 + h, cols])
    out_ref[...] = acc_ref[...].T


def cross_forward(which, q, k, v, seg):
    toks, width = q.shape
    clips, frames = k.shape[:2]
    kv_spec = pl.BlockSpec((clips, frames, 128), lambda j, w: (0, 0, j))
    tok_spec = pl.BlockSpec((toks, 128), lambda j, w: (0, j))
    return pl.pallas_call(
        cross_forward_kernel,
        grid_spec=pltpu.PrefetchScalarGridSpec(
            num_scalar_prefetch=1,
            grid=(width // 128,),
            in_specs=[tok_spec, kv_spec, kv_spec, pl.BlockSpec((1, toks), lambda j, w: (0, 0))],
            out_specs=[tok_spec, pl.BlockSpec((1, 4, toks), lambda j, w: (j, 0, 0))],
            scratch_shapes=[pltpu.VMEM((128, toks), jnp.float32)],
        ),
        out_shape=[
            jax.ShapeDtypeStruct((toks, width), jnp.float32),
            jax.ShapeDtypeStruct((width // 128, 4, toks), jnp.float32),
        ],
        compiler_params=pltpu.CompilerParams(vmem_limit_bytes=48 * 2**20),
        name="cross_forward",
    )(which, q, k, v, seg)


def cross_backward_kernel(which, q_ref, k_ref, v_ref, seg_ref, lse_ref, inner_ref, g_ref, dq_ref, dk_ref, dv_ref, acc_ref):
    def back(clip, keys_t, cols, h):
        query, grad = one_head(q_ref[cols], h), one_head(g_ref[cols], h)
        lse = jnp.where(seg_ref[:, cols] == clip, lse_ref[0, h:h + 1, cols], 1e30)
        weights = jnp.exp(dot(k_ref[clip], query, NT) - lse)
        grad_v = dot(weights.astype(jnp.bfloat16), grad, NN)
        grad_s = (weights * (dot(v_ref[clip], grad, NT) - inner_ref[0, h:h + 1, cols])).astype(jnp.bfloat16)
        grad_k = dot(grad_s, query, NN)
        return dot(keys_t[h * 64:(h + 1) * 64], grad_s, NN), grad_k, grad_v

    for k in range(3):
        clip = which[k]
        cols = slice(None) if k == 0 else pl.ds(pl.multiple_of(which[2 + k] * 128, 128), 128)
        keys_t = k_ref[clip].T
        grad_q, grad_k, grad_v = zip(*(back(clip, keys_t, cols, h) for h in range(2)))
        grad_q = jnp.concatenate(grad_q, 0)
        if k == 0:
            acc_ref[...] = grad_q
        else:
            acc_ref[:, cols] += grad_q
        dk_ref[clip] = (grad_k[0] + grad_k[1]).astype(jnp.bfloat16)
        dv_ref[clip] = (grad_v[0] + grad_v[1]).astype(jnp.bfloat16)
    dq_ref[...] = (acc_ref[...] * 0.125).T


def cross_backward(which, q, k, v, seg, lse, inner, grad):
    toks, width = q.shape
    clips, frames = k.shape[:2]
    kv_spec = pl.BlockSpec((clips, frames, 128), lambda j, w: (0, 0, j))
    tok_spec = pl.BlockSpec((toks, 128), lambda j, w: (0, j))
    row_spec = pl.BlockSpec((1, 2, toks), lambda j, w: (j, 0, 0))
    return pl.pallas_call(
        cross_backward_kernel,
        grid_spec=pltpu.PrefetchScalarGridSpec(
            num_scalar_prefetch=1,
            grid=(width // 128,),
            in_specs=[tok_spec, kv_spec, kv_spec, pl.BlockSpec((1, toks), lambda j, w: (0, 0)), row_spec, row_spec, tok_spec],
            out_specs=[tok_spec, kv_spec, kv_spec],
            scratch_shapes=[pltpu.VMEM((128, toks), jnp.float32)],
        ),
        out_shape=[
            jax.ShapeDtypeStruct((toks, width), jnp.float32),
            jax.ShapeDtypeStruct(k.shape, jnp.bfloat16),
            jax.ShapeDtypeStruct(k.shape, jnp.bfloat16),
        ],
        compiler_params=pltpu.CompilerParams(vmem_limit_bytes=48 * 2**20),
        name="cross_backward",
    )(which, q, k, v, seg, lse, inner, grad)


Z = 4


class Place:
    def __init__(self):
        self.dp = lax.axis_index("dp")
        self.core = lax.axis_index("seq")
        self.z = self.dp // 4
        self.p = self.dp % 4
        x, y = self.p % 2, self.p // 2
        px, py = self.p + 1 - 2 * x, self.p + 2 - 4 * y
        self.p_first = px * (1 - self.core) + py * self.core
        self.p_second = py * (1 - self.core) + px * self.core
        self.p_diag = 3 - self.p
        base = self.z * 4
        self.first = (base + self.p_first, self.core)
        self.second = (base + self.p_second, self.core)
        self.up = (lax.rem(self.dp + 4, 16), self.core)
        self.down = (lax.rem(self.dp + 12, 16), self.core)
        self.mate = (self.dp, 1 - self.core)
        self.has_up = self.z < Z - 1
        self.has_down = self.z > 0

    def greet(self):
        barrier = pltpu.get_barrier_semaphore()
        for target in (self.mate, self.first, self.second):
            pl.semaphore_signal(barrier, inc=1, device_id=target, device_id_type=MESH)

        @pl.when(self.has_up)
        def _():
            pl.semaphore_signal(barrier, inc=1, device_id=self.up, device_id_type=MESH)

        @pl.when(self.has_down)
        def _():
            pl.semaphore_signal(barrier, inc=1, device_id=self.down, device_id_type=MESH)

        pl.semaphore_wait(barrier, 3 + (self.z + 3) // 4 + (6 - self.z) // 4)


def when(cond, fn):
    if cond is None:
        fn()
    else:
        pl.when(cond)(fn)


def both(a, b):
    if a is None:
        return b
    if b is None:
        return a
    return jnp.logical_and(a, b)


def gather_kernel(count, plane_first, *refs):
    ins, outs = refs[:count], refs[count:2 * count]
    send_sem, recv_sem, own_sem = refs[2 * count:]
    me = Place()
    me.greet()
    sends = []

    def block(z, p):
        return (z * 4 + p) * 2 + me.core

    def send(m, src, index, target, cond):
        slot = len(sends)
        copy = pltpu.make_async_remote_copy(
            src_ref=src, dst_ref=outs[m].at[index], send_sem=send_sem.at[slot],
            recv_sem=recv_sem.at[m, index], device_id=target, device_id_type=MESH)
        sends.append((cond, copy))
        when(cond, copy.start)

    def arrive(m, index, cond):
        def go():
            pltpu.make_async_remote_copy(
                src_ref=ins[m], dst_ref=outs[m].at[index], send_sem=send_sem.at[0],
                recv_sem=recv_sem.at[m, index], device_id=me.mate, device_id_type=MESH).wait_recv()
        when(cond, go)

    def forward(m, z, p, targets, cond=None):
        index = block(z, p)
        arrive(m, index, cond)
        for target, extra in targets:
            send(m, outs[m].at[index], index, target, both(cond, extra))

    own = block(me.z, me.p)
    for m in range(count):
        targets = [(me.up, me.has_up), (me.down, me.has_down), (me.first, None), (me.second, None), (me.mate, None)]
        if m in plane_first:
            targets = targets[2:4] + targets[:2] + targets[4:]
        for target, cond in targets:
            send(m, ins[m], own, target, cond)
    for m in range(count):
        pltpu.make_async_copy(ins[m], outs[m].at[own], own_sem.at[m]).start()

    up = [(me.up, me.has_up)]
    down = [(me.down, me.has_down)]
    mate = [(me.mate, None)]
    for m in plane_first:
        forward(m, me.z, me.p_first, [(me.second, None)] + up + down + mate)
        forward(m, me.z, me.p_second, up + down + mate)
        forward(m, me.z, me.p_diag, up + down + mate)
    line_first = [m for m in range(count) if m not in plane_first]
    for d in range(1, Z + 1):
        for m in range(count):
            below, above = me.z - d, me.z + d
            if d < Z:
                if m in plane_first:
                    for p in (me.p, me.p_first, me.p_second, me.p_diag):
                        forward(m, below, p, up + mate, below >= 0)
                        forward(m, above, p, down + mate, above < Z)
                else:
                    plane = [(me.first, None), (me.second, None)] + mate
                    forward(m, below, me.p, up + plane, below >= 0)
                    forward(m, above, me.p, down + plane, above < Z)
            if m not in plane_first:
                if d == 1:
                    forward(m, me.z, me.p_first, [(me.second, None)] + mate)
                else:
                    forward(m, below + 1, me.p_first, [(me.second, None)] + mate, below + 1 >= 0)
                    forward(m, above - 1, me.p_first, [(me.second, None)] + mate, above - 1 < Z)
    for p in (me.p_second, me.p_diag):
        for m in line_first:
            for d in range(Z):
                if d == 0:
                    forward(m, me.z, p, mate)
                else:
                    forward(m, me.z - d, p, mate, me.z - d >= 0)
                    forward(m, me.z + d, p, mate, me.z + d < Z)
    for m in range(count):
        pltpu.make_async_copy(ins[m], outs[m].at[own], own_sem.at[m]).wait()
        for q in range(16):
            arrive(m, q * 2 + 1 - me.core, None)
    for cond, copy in sends:
        when(cond, copy.wait_send)


def gather_all(shards, plane_first):
    count = len(shards)
    any_spec = pl.BlockSpec(memory_space=pl.ANY)
    return pl.pallas_call(
        functools.partial(gather_kernel, count, plane_first),
        out_shape=tuple(jax.ShapeDtypeStruct((32,) + s.shape, s.dtype) for s in shards),
        in_specs=[any_spec] * count,
        out_specs=tuple([any_spec] * count),
        scratch_shapes=[
            pltpu.SemaphoreType.DMA((80 * count,)),
            pltpu.SemaphoreType.DMA((count, 32)),
            pltpu.SemaphoreType.DMA((count,)),
        ],
        compiler_params=pltpu.CompilerParams(collective_id=0, has_side_effects=True),
        name="gather_all",
    )(*shards)


def scatter_kernel(count, *refs):
    grads, outs = refs[:count], refs[count:2 * count]
    scratch = refs[2 * count:]
    owns, pairs, plane_as, plane_bs, plane_cs, lines = (scratch[k * count:(k + 1) * count] for k in range(6))
    send_sem, own_sem, pair_sem, plane_sem, line_sem = scratch[6 * count:]
    me = Place()
    half = me.z // 2
    near = me.z + half * (3 - 2 * me.z)

    def far(k):
        base = (3, 2, 1 - near, near)[k]
        return base + half * (3 - 2 * base)

    order = [far(k) for k in range(4)]
    plane = [me.p_diag, me.p_first, me.p_second, me.p]
    mate_plane = [me.p_diag, me.p_second, me.p_first, me.p]
    for k in range(4):
        for m in range(count):
            pltpu.make_async_copy(grads[m].at[:, plane[k], me.core], owns[m].at[:, plane[k]], own_sem.at[m, plane[k]]).start()
    me.greet()
    sends = []

    def send(src, dst, sem, target, cond=None):
        slot = len(sends)
        copy = pltpu.make_async_remote_copy(src_ref=src, dst_ref=dst, send_sem=send_sem.at[slot], recv_sem=sem, device_id=target, device_id_type=MESH)
        sends.append((cond, copy))
        when(cond, copy.start)

    def arrive(dst, sem, cond=None):
        when(cond, pltpu.make_async_remote_copy(src_ref=dst, dst_ref=dst, send_sem=send_sem.at[0], recv_sem=sem, device_id=me.mate, device_id_type=MESH).wait_recv)

    for k in range(4):
        for m in range(count):
            p = mate_plane[k]
            send(grads[m].at[:, p, 1 - me.core], pairs[m].at[:, p], pair_sem.at[m, p], me.mate)

    def paired(m, p):
        pltpu.make_async_copy(grads[m].at[:, p, me.core], owns[m].at[:, p], own_sem.at[m, p]).wait()
        arrive(pairs[m].at[:, p], pair_sem.at[m, p])

    def add(dst, *others):
        total = dst[...].astype(jnp.float32)
        for other in others:
            total = total + other[...].astype(jnp.float32)
        dst[...] = total.astype(dst.dtype)

    def steps(m):
        own = owns[m]
        paired(m, me.p_diag)
        for k in range(4):
            z = order[k]
            add(own.at[z, me.p_diag], pairs[m].at[z, me.p_diag])
            send(own.at[z, me.p_diag], plane_as[m].at[z], plane_sem.at[m, 0, z], me.second)
        yield
        paired(m, me.p_second)
        for k in range(4):
            z = order[k]
            add(own.at[z, me.p_second], pairs[m].at[z, me.p_second])
            send(own.at[z, me.p_second], plane_cs[m].at[z], plane_sem.at[m, 2, z], me.second)
        yield
        paired(m, me.p_first)
        for k in range(4):
            z = order[k]
            arrive(plane_as[m].at[z], plane_sem.at[m, 0, z])
            add(own.at[z, me.p_first], pairs[m].at[z, me.p_first], plane_as[m].at[z])
            send(own.at[z, me.p_first], plane_bs[m].at[z], plane_sem.at[m, 1, z], me.first)
        yield
        paired(m, me.p)
        for k in range(4):
            z = order[k]
            arrive(plane_bs[m].at[z], plane_sem.at[m, 1, z])
            arrive(plane_cs[m].at[z], plane_sem.at[m, 2, z])
            if k == 3:
                break
            add(own.at[z, me.p], pairs[m].at[z, me.p], plane_bs[m].at[z], plane_cs[m].at[z])
            upward = (z - me.z + 3) // 4
            source = me.z + 1 - 2 * upward
            came = jnp.logical_and(source >= 0, source < Z)

            def gather_in(z=z, upward=upward):
                slot = lines[m].at[upward, z]
                arrive(slot, line_sem.at[m, upward, z])
                add(own.at[z, me.p], slot)

            pl.when(came)(gather_in)
            target = (lax.rem(me.dp + 12 + 8 * upward, 16), me.core)
            send(own.at[z, me.p], lines[m].at[upward, z], line_sem.at[m, upward, z], target)
        yield
        z = me.z
        total = own[z, me.p].astype(jnp.float32) + pairs[m][z, me.p].astype(jnp.float32)
        total = total + plane_bs[m][z].astype(jnp.float32) + plane_cs[m][z].astype(jnp.float32)
        outs[m][...] = total
        for upward, cond in ((0, me.has_up), (1, me.has_down)):

            def last(upward=upward):
                arrive(lines[m].at[upward, z], line_sem.at[m, upward, z])
                outs[m][...] += lines[m][upward, z].astype(jnp.float32)

            pl.when(cond)(last)

    running = [steps(m) for m in range(count)]
    while running:
        still = []
        for step in running:
            try:
                next(step)
                still.append(step)
            except StopIteration:
                pass
        running = still
    for cond, copy in sends:
        when(cond, copy.wait_send)


def scatter_all(grads):
    count = len(grads)
    shapes = [g.shape[1:] for g in grads]
    views = [g.reshape((4, 4, 2) + s) for g, s in zip(grads, shapes)]

    def vmem(*lead):
        return [pltpu.VMEM(lead + s, g.dtype) for g, s in zip(grads, shapes)]

    return pl.pallas_call(
        functools.partial(scatter_kernel, count),
        out_shape=tuple(jax.ShapeDtypeStruct(s, jnp.float32) for s in shapes),
        in_specs=[pl.BlockSpec(memory_space=pl.ANY)] * count,
        out_specs=tuple([pl.BlockSpec(memory_space=pltpu.VMEM)] * count),
        scratch_shapes=vmem(4, 4) + vmem(4, 4) + vmem(4) + vmem(4) + vmem(4) + vmem(2, 4) + [
            pltpu.SemaphoreType.DMA((20 * count,)),
            pltpu.SemaphoreType.DMA((count, 4)),
            pltpu.SemaphoreType.DMA((count, 4)),
            pltpu.SemaphoreType.DMA((count, 3, 4)),
            pltpu.SemaphoreType.DMA((count, 2, 4)),
        ],
        compiler_params=pltpu.CompilerParams(collective_id=1, has_side_effects=True, vmem_limit_bytes=60 * 2**20),
        name="scatter_all",
    )(*views)


def pack_rows(up_bias, down_bias, vectors, size):
    rows = jnp.concatenate([up_bias, down_bias, vectors], 1)
    return jnp.pad(rows, ((0, 0), (0, size - rows.shape[1])))


def gather_weights(self_weights, cross_weights, up_weights, down_weights, up_bias, down_bias, vectors):
    if lax.axis_size("dp") != 16:
        return tuple(
            lax.all_gather(part, ("dp", "seq"), axis=0, tiled=True)
            for part in (self_weights, cross_weights, up_weights, down_weights, up_bias, down_bias, vectors)
        )
    small = pack_rows(up_bias[None], down_bias[None], vectors.reshape(1, -1), 2048).reshape(16, 128)
    whole = gather_all((self_weights, cross_weights, up_weights, down_weights, small), ())
    rows = whole[4].reshape(32, 2048)
    n_up, n_down = up_bias.shape[0], down_bias.shape[0]
    n_all = n_up + n_down + vectors.size
    return tuple(w.reshape(-1, w.shape[2]) for w in whole[:4]) + (
        rows[:, :n_up].reshape(-1),
        rows[:, n_up:n_up + n_down].reshape(-1),
        rows[:, n_up + n_down:n_all].reshape(-1, vectors.shape[1]),
    )


def scatter_grads(grads_self, grads_cross, grad_up, grad_down, grad_up_bias, grad_out_bias, vector_grads):
    parts = (grads_self, grads_cross, grad_up, grad_down, grad_up_bias, grad_out_bias, vector_grads)
    if lax.axis_size("dp") != 16:
        return tuple(lax.psum_scatter(part, ("dp", "seq"), scatter_dimension=0, tiled=True) for part in parts)
    small = pack_rows(
        grad_up_bias.reshape(32, -1), grad_out_bias.reshape(32, -1), vector_grads.reshape(32, -1), 1024
    ).reshape(32, 8, 128)
    large = tuple(g.astype(jnp.bfloat16).reshape(32, -1, g.shape[1]) for g in parts[:4])
    whole = scatter_all(large + (small,))
    row = whole[4].reshape(-1)
    n_up, n_down, n_vec = (g.size // 32 for g in parts[4:])
    return tuple(whole[:4]) + (
        row[:n_up],
        row[n_up:n_up + n_down],
        row[n_up + n_down:n_up + n_down + n_vec].reshape(-1, vector_grads.shape[1]),
    )


def from_behind(value, axis, steps):
    count = lax.axis_size(axis)
    leading, last = (max(0, -steps), min(count, count - steps))
    return lax.ppermute(value, axis, [(source, source + steps) for source in range(leading, last)])


def layer_norm(values, gain, shift):
    average = jnp.mean(values, -1, keepdims=True)
    centred = values - average
    spread = jnp.mean(centred * centred, -1, keepdims=True)
    return centred * lax.rsqrt(spread + 1e-05) * gain + shift


def exact_gelu(values):
    return jax.nn.gelu(values, approximate=False)


def matmul(left, right):
    return jnp.dot(left, right, preferred_element_type=jnp.float32)


def swap_halves(value):
    return lax.ppermute(value, "seq", [(0, 1), (1, 0)])


def seq_halves(value, axis):
    span = value.shape[axis] // 2
    half = lax.axis_index("seq")
    mine = lax.dynamic_slice_in_dim(value, half * span, span, axis)
    other = lax.dynamic_slice_in_dim(value, (1 - half) * span, span, axis)
    return mine, other


def seq_scatter(value):
    mine, other = seq_halves(value, 0)
    return mine + swap_halves(other.astype(jnp.bfloat16)).astype(value.dtype)


def per_head(values):
    rows = values.reshape(-1, values.shape[2]).T
    return jnp.repeat(rows, HEAD_DIM, axis=1)


def head_sums(values):
    sums = jnp.sum(values.reshape(values.shape[0], -1, HEAD_DIM), -1)
    return sums.T.reshape(-1, 2, values.shape[0])


def per_device(
    layer_input,
    encoder_states,
    clip_lengths,
    out_grad,
    self_weights,
    cross_weights,
    up_weights,
    down_weights,
    up_bias,
    down_bias,
    vectors,
):
    model_width = layer_input.shape[2]
    tok_span = layer_input.shape[1]
    seq_half = lax.axis_index("seq")
    self_full, cross_full, up_full, down_full, bias_full, out_bias_full, vector_full = gather_weights(
        self_weights, cross_weights, up_weights, down_weights, up_bias, down_bias, vectors
    )
    bias_full = bias_full.astype(jnp.float32)
    out_bias_full = out_bias_full.astype(jnp.float32)
    vector_full = vector_full.astype(jnp.float32).T
    cross_in = [cross_full[:, k * model_width : (k + 1) * model_width] for k in range(4)]

    source = layer_input[0].astype(jnp.float32)
    position = seq_half * tok_span + jnp.arange(tok_span, dtype=jnp.int32)
    clip_ends = jnp.cumsum(clip_lengths[0])
    segment = jnp.sum((position[:, None] >= clip_ends[None, :]).astype(jnp.int32), 1)
    key_position = jnp.concatenate([position - tok_span, position])
    key_segment = jnp.sum((key_position[:, None] >= clip_ends[None, :]).astype(jnp.int32), 1)
    allowed = (
        (key_segment[:, None] == segment[None, :])
        & (key_position[:, None] <= position[None, :])
        & (key_position[:, None] >= 0)
    )
    mask_bias = jnp.where(allowed, 0.0, -1e30).astype(jnp.float32)
    row_position = jnp.arange(2 * tok_span, dtype=jnp.int32)
    row_segment = jnp.sum((row_position[:, None] >= clip_ends[None, :]).astype(jnp.int32), 1)[None]
    big = jnp.argmax(clip_lengths[0]).astype(jnp.int32)
    small_one = jnp.where(big == 0, 1, 0)
    small_two = jnp.where(big == 2, 1, 2)
    last_group = 2 * tok_span // 128 - 1
    which = jnp.stack(
        [
            big,
            small_one,
            small_two,
            jnp.where(small_one < big, 0, last_group),
            jnp.where(small_two < big, 0, last_group),
        ]
    ).astype(jnp.int32)

    normed_one = layer_norm(source, vector_full[0], vector_full[1]).astype(jnp.bfloat16)
    proj_bias = jnp.concatenate([vector_full[6], jnp.zeros_like(vector_full[6]), vector_full[7]])
    qkv_low = (matmul(normed_one, self_full[:, : 3 * model_width]) + proj_bias).astype(jnp.bfloat16)
    query = qkv_low[:, :model_width] * jnp.bfloat16(0.125)
    kv_own = qkv_low[:, model_width:]
    kv_row = jnp.concatenate([from_behind(kv_own, "seq", 1), kv_own])
    key_row, value_row = kv_row[:, :model_width], kv_row[:, model_width:]
    attended, self_lse = self_forward(query, key_row, value_row, mask_bias)
    attended_low = attended.astype(jnp.bfloat16)
    after_self = source + matmul(attended_low, self_full[:, 3 * model_width :]) + vector_full[8]
    normed_two = layer_norm(after_self, vector_full[2], vector_full[3]).astype(jnp.bfloat16)
    cross_query = (matmul(normed_two, cross_in[0]) + vector_full[9]).astype(jnp.bfloat16)
    frames = encoder_states[0]
    cross_key = jnp.einsum(
        "cfd,de->cfe", frames, cross_in[1], preferred_element_type=jnp.float32
    ).astype(jnp.bfloat16)
    cross_value = (
        jnp.einsum("cfd,de->cfe", frames, cross_in[2], preferred_element_type=jnp.float32)
        + vector_full[10]
    ).astype(jnp.bfloat16)
    row_query = lax.all_gather(cross_query * jnp.bfloat16(0.125), "seq", axis=0, tiled=True)
    part_mixed, part_stats = cross_forward(which, row_query, cross_key, cross_value, row_segment)
    mixed_mine, mixed_other = seq_halves(part_mixed, 0)
    stats_mine, stats_other = seq_halves(part_stats, 2)
    mixed_came = swap_halves(mixed_other.astype(jnp.bfloat16))
    stats_came = swap_halves(stats_other)
    peak = jnp.maximum(stats_mine[:, :2], stats_came[:, :2])
    share_mine = stats_mine[:, 2:] * jnp.exp(stats_mine[:, :2] - peak)
    share_came = stats_came[:, 2:] * jnp.exp(stats_came[:, :2] - peak)
    total = share_mine + share_came
    cross_lse = peak + jnp.log(total)
    mixed_full = mixed_mine * per_head(share_mine / total) + mixed_came.astype(
        jnp.float32
    ) * per_head(share_came / total)
    mixed = mixed_full.astype(jnp.bfloat16)
    after_cross = after_self + matmul(mixed, cross_in[3]) + vector_full[11]
    normed_three = layer_norm(after_cross, vector_full[4], vector_full[5]).astype(jnp.bfloat16)
    pre_act = matmul(normed_three, up_full) + bias_full
    activated_low = exact_gelu(pre_act).astype(jnp.bfloat16)
    result_rows = after_cross + matmul(activated_low, down_full) + out_bias_full
    layer_output = result_rows.astype(jnp.bfloat16)[None]

    grad_low = out_grad[0]
    grad_rows = grad_low.astype(jnp.float32)
    grad_down = matmul(activated_low.T, grad_low)
    grad_out_bias = jnp.sum(grad_rows, 0)
    grad_act = matmul(grad_low, down_full.T).astype(jnp.bfloat16)
    _, gelu_pull = jax.vjp(exact_gelu, pre_act)
    grad_pre = gelu_pull(grad_act.astype(jnp.float32))[0].astype(jnp.bfloat16)
    grad_up = matmul(normed_three.T, grad_pre)
    grad_up_bias = jnp.sum(grad_pre, 0, dtype=jnp.float32)
    grad_normed_three = matmul(grad_pre, up_full.T)
    _, norm_pull_three = jax.vjp(layer_norm, after_cross, vector_full[4], vector_full[5])
    grad_part, grad_gain_three, grad_shift_three = norm_pull_three(grad_normed_three)
    grad_after_cross = grad_rows + grad_part
    grad_cross_low = grad_after_cross.astype(jnp.bfloat16)
    grad_cross_out = matmul(mixed.T, grad_cross_low)
    grad_cross_bias = jnp.sum(grad_cross_low, 0, dtype=jnp.float32)
    grad_mixed = matmul(grad_cross_low, cross_in[3].T).astype(jnp.bfloat16)
    row_grad = lax.all_gather(grad_mixed, "seq", axis=0, tiled=True)
    cross_inner = head_sums(grad_mixed.astype(jnp.float32) * mixed_full)
    row_stats = lax.all_gather(jnp.stack([cross_lse, cross_inner]), "seq", axis=3, tiled=True)
    part_query, grad_key, grad_value = cross_backward(
        which, row_query, cross_key, cross_value, row_segment, row_stats[0], row_stats[1], row_grad
    )
    grad_query_sum = seq_scatter(part_query).astype(jnp.bfloat16)
    grad_cq_weight = matmul(normed_two.T, grad_query_sum)
    grad_cq_bias = jnp.sum(grad_query_sum, 0, dtype=jnp.float32)
    grad_normed_two = matmul(grad_query_sum, cross_in[0].T)
    grad_ck_weight = jnp.einsum(
        "cfd,cfe->de", frames, grad_key, preferred_element_type=jnp.float32
    )
    grad_cv_weight = jnp.einsum(
        "cfd,cfe->de", frames, grad_value, preferred_element_type=jnp.float32
    )
    grad_cv_bias = jnp.sum(grad_value, (0, 1), dtype=jnp.float32)
    encoder_grad = (
        jnp.einsum("cfe,de->cfd", grad_key, cross_in[1], preferred_element_type=jnp.float32)
        + jnp.einsum("cfe,de->cfd", grad_value, cross_in[2], preferred_element_type=jnp.float32)
    )[None]
    _, norm_pull_two = jax.vjp(layer_norm, after_self, vector_full[2], vector_full[3])
    grad_part, grad_gain_two, grad_shift_two = norm_pull_two(grad_normed_two)
    grad_after_self = grad_after_cross + grad_part
    grad_self_low = grad_after_self.astype(jnp.bfloat16)
    grad_self_out = matmul(attended_low.T, grad_self_low)
    grad_self_bias = jnp.sum(grad_self_low, 0, dtype=jnp.float32)
    grad_attended = matmul(grad_self_low, self_full[:, 3 * model_width :].T).astype(jnp.bfloat16)
    self_inner = head_sums(grad_attended.astype(jnp.float32) * attended)
    grad_query, grad_key_row, grad_value_row = self_backward(
        query, key_row, value_row, mask_bias, self_lse, self_inner, grad_attended
    )
    grad_kv = jnp.concatenate([grad_key_row, grad_value_row], 1)
    back_kv = from_behind(grad_kv[:tok_span].astype(jnp.bfloat16), "seq", -1)
    grad_qkv_low = jnp.concatenate(
        [grad_query, grad_kv[tok_span:] + back_kv.astype(jnp.float32)], 1
    ).astype(jnp.bfloat16)
    grad_qkv_weight = matmul(normed_one.T, grad_qkv_low)
    grad_qkv_bias = jnp.sum(grad_qkv_low, 0, dtype=jnp.float32)
    grad_normed_one = matmul(grad_qkv_low, self_full[:, : 3 * model_width].T)
    _, norm_pull_one = jax.vjp(layer_norm, source, vector_full[0], vector_full[1])
    grad_part, grad_gain_one, grad_shift_one = norm_pull_one(grad_normed_one)
    input_grad = (grad_after_self + grad_part)[None]
    grads_self = jnp.concatenate([grad_qkv_weight, grad_self_out], 1)
    grads_cross = jnp.concatenate(
        [grad_cq_weight, grad_ck_weight, grad_cv_weight, grad_cross_out], 1
    )
    vector_grads = jnp.stack(
        [
            grad_gain_one,
            grad_shift_one,
            grad_gain_two,
            grad_shift_two,
            grad_gain_three,
            grad_shift_three,
            grad_qkv_bias[:model_width],
            grad_qkv_bias[2 * model_width :],
            grad_self_bias,
            grad_cq_bias,
            grad_cv_bias,
            grad_cross_bias,
        ],
        1,
    )
    shares = scatter_grads(
        grads_self, grads_cross, grad_up, grad_down, grad_up_bias, grad_out_bias, vector_grads
    )
    return (layer_output, input_grad, encoder_grad) + shares


def solution(mesh):
    return jax.shard_map(
        per_device,
        mesh=mesh,
        in_specs=(
            P("dp", "seq", None),
            P("dp", None, "seq", None),
            P("dp", None),
            P("dp", "seq", None),
            P(("dp", "seq"), None),
            P(("dp", "seq"), None),
            P(("dp", "seq"), None),
            P(("dp", "seq"), None),
            P(("dp", "seq")),
            P(("dp", "seq")),
            P(("dp", "seq"), None),
        ),
        out_specs=(
            P("dp", "seq", None),
            P("dp", "seq", None),
            P("dp", None, "seq", None),
            P(("dp", "seq"), None),
            P(("dp", "seq"), None),
            P(("dp", "seq"), None),
            P(("dp", "seq"), None),
            P(("dp", "seq")),
            P(("dp", "seq")),
            P(("dp", "seq"), None),
        ),
        check_vma=False,
    )
```

```python
import functools

import jax
import jax.numpy as jnp
from jax import lax
from jax.experimental import pallas as pl
from jax.experimental.pallas import tpu as pltpu
from jax.sharding import PartitionSpec as P

HEAD_DIM = 64
CLIPS = 3
MESH = pl.DeviceIdType.MESH
NT = (((1,), (1,)), ((), ()))
NN = (((1,), (0,)), ((), ()))


def dot(left, right, dims):
    return lax.dot_general(left, right, dims, preferred_element_type=jnp.float32)


def one_head(values, h):
    lane = lax.broadcasted_iota(jnp.int32, values.shape, 1)
    return jnp.where((lane >= 64) == (h == 1), values, jnp.zeros_like(values))


def self_forward_kernel(q_ref, k_ref, v_ref, bias_ref, out_ref, lse_ref):
    keys = k_ref[...]
    values_t = v_ref[...].T
    halves = []
    for h in range(2):
        scores = dot(keys, one_head(q_ref[...], h), NT) + bias_ref[...]
        peak = jnp.max(scores, 0, keepdims=True)
        terms = jnp.exp(scores - peak)
        total = jnp.sum(terms, 0, keepdims=True)
        result = dot(values_t[h * 64:(h + 1) * 64], terms.astype(jnp.bfloat16), NN)
        halves.append(result / total)
        lse_ref[0, h:h + 1] = peak + jnp.log(total)
    out_ref[...] = jnp.concatenate(halves, 0).T.astype(out_ref.dtype)


def self_forward(q, kv, bias):
    toks, width = q.shape
    keys, pairs = kv.shape[0], width // 128
    return pl.pallas_call(
        self_forward_kernel,
        grid=(width // 128,),
        in_specs=[
            pl.BlockSpec((toks, 128), lambda j: (0, j)),
            pl.BlockSpec((keys, 128), lambda j: (0, j)),
            pl.BlockSpec((keys, 128), lambda j: (0, j + pairs)),
            pl.BlockSpec((keys, toks), lambda j: (0, 0)),
        ],
        out_specs=[
            pl.BlockSpec((toks, 128), lambda j: (0, j)),
            pl.BlockSpec((1, 2, toks), lambda j: (j, 0, 0)),
        ],
        out_shape=[
            jax.ShapeDtypeStruct((toks, width), jnp.float32),
            jax.ShapeDtypeStruct((width // 128, 2, toks), jnp.float32),
        ],
        compiler_params=pltpu.CompilerParams(vmem_limit_bytes=48 * 2**20),
        name="self_forward",
    )(q, kv, kv, bias)


def self_backward_kernel(q_ref, k_ref, v_ref, bias_ref, lse_ref, inner_ref, g_ref, dq_ref, dk_ref, dv_ref):
    keys, values = k_ref[...], v_ref[...]
    keys_t = keys.T
    grad_k = grad_v = None
    halves = []
    for h in range(2):
        query, grad = one_head(q_ref[...], h), one_head(g_ref[...], h)
        weights = jnp.exp(dot(keys, query, NT) + bias_ref[...] - lse_ref[0, h:h + 1])
        part = dot(weights.astype(jnp.bfloat16), grad, NN)
        grad_v = part if grad_v is None else grad_v + part
        grad_s = (weights * (dot(values, grad, NT) - inner_ref[0, h:h + 1])).astype(jnp.bfloat16)
        part = dot(grad_s, query, NN)
        grad_k = part if grad_k is None else grad_k + part
        halves.append(dot(keys_t[h * 64:(h + 1) * 64], grad_s, NN))
    dq_ref[...] = (jnp.concatenate(halves, 0) * 0.125).T
    dk_ref[...] = grad_k
    dv_ref[...] = grad_v


def self_backward(q, kv, bias, lse, inner, grad):
    toks, width = q.shape
    keys, pairs = kv.shape[0], width // 128
    tok_spec = pl.BlockSpec((toks, 128), lambda j: (0, j))
    key_spec = pl.BlockSpec((keys, 128), lambda j: (0, j))
    row_spec = pl.BlockSpec((1, 2, toks), lambda j: (j, 0, 0))
    return pl.pallas_call(
        self_backward_kernel,
        grid=(width // 128,),
        in_specs=[tok_spec, key_spec, pl.BlockSpec((keys, 128), lambda j: (0, j + pairs)), pl.BlockSpec((keys, toks), lambda j: (0, 0)), row_spec, row_spec, tok_spec],
        out_specs=[tok_spec, key_spec, key_spec],
        out_shape=[
            jax.ShapeDtypeStruct((toks, width), jnp.float32),
            jax.ShapeDtypeStruct((keys, width), jnp.float32),
            jax.ShapeDtypeStruct((keys, width), jnp.float32),
        ],
        compiler_params=pltpu.CompilerParams(vmem_limit_bytes=48 * 2**20),
        name="self_backward",
    )(q, kv, kv, bias, lse, inner, grad)


def cross_forward_kernel(which, q_ref, k_ref, v_ref, seg_ref, out_ref, stat_ref, acc_ref):
    def attend(clip, values_t, query, h):
        scores = dot(k_ref[clip], query, NT)
        peak = jnp.max(scores, 0, keepdims=True)
        terms = jnp.exp(scores - peak)
        total = jnp.sum(terms, 0, keepdims=True)
        result = dot(values_t[h * 64:(h + 1) * 64], terms.astype(jnp.bfloat16), NN)
        return result / total, peak, total

    values_t = v_ref[0].T
    for h in range(2):
        mine = seg_ref[...] == 0
        result, peak, total = attend(0, values_t, one_head(q_ref[...], h), h)
        acc_ref[h * 64:(h + 1) * 64] = jnp.where(mine, result, 0.0)
        stat_ref[0, h:h + 1] = jnp.where(mine, peak, 0.0)
        stat_ref[0, 2 + h:3 + h] = jnp.where(mine, total, 1.0)
    for clip in (1, 2):
        cols = pl.ds(pl.multiple_of(which[clip - 1] * 128, 128), 128)
        values_t = v_ref[clip].T
        mine = seg_ref[:, cols] == clip
        for h in range(2):
            result, peak, total = attend(clip, values_t, one_head(q_ref[cols], h), h)
            rows = slice(h * 64, (h + 1) * 64)
            acc_ref[rows, cols] = jnp.where(mine, result, acc_ref[rows, cols])
            stat_ref[0, h:h + 1, cols] = jnp.where(mine, peak, stat_ref[0, h:h + 1, cols])
            stat_ref[0, 2 + h:3 + h, cols] = jnp.where(mine, total, stat_ref[0, 2 + h:3 + h, cols])
    out_ref[...] = acc_ref[...].T


def cross_forward(which, q, kv, seg):
    toks, width = q.shape
    clips, frames = kv.shape[:2]
    pairs = width // 128
    kv_spec = pl.BlockSpec((clips, frames, 128), lambda j, w: (0, 0, j))
    v_spec = pl.BlockSpec((clips, frames, 128), lambda j, w: (0, 0, j + pairs))
    tok_spec = pl.BlockSpec((toks, 128), lambda j, w: (0, j))
    return pl.pallas_call(
        cross_forward_kernel,
        grid_spec=pltpu.PrefetchScalarGridSpec(
            num_scalar_prefetch=1,
            grid=(width // 128,),
            in_specs=[tok_spec, kv_spec, v_spec, pl.BlockSpec((1, toks), lambda j, w: (0, 0))],
            out_specs=[tok_spec, pl.BlockSpec((1, 4, toks), lambda j, w: (j, 0, 0))],
            scratch_shapes=[pltpu.VMEM((128, toks), jnp.float32)],
        ),
        out_shape=[
            jax.ShapeDtypeStruct((toks, width), jnp.float32),
            jax.ShapeDtypeStruct((width // 128, 4, toks), jnp.float32),
        ],
        compiler_params=pltpu.CompilerParams(vmem_limit_bytes=48 * 2**20),
        name="cross_forward",
    )(which, q, kv, kv, seg)


def cross_backward_kernel(which, q_ref, k_ref, v_ref, seg_ref, lse_ref, inner_ref, g_ref, dq_ref, dk_ref, dv_ref, acc_ref):
    def back(clip, keys_t, cols, h):
        query, grad = one_head(q_ref[cols], h), one_head(g_ref[cols], h)
        lse = jnp.where(seg_ref[:, cols] == clip, lse_ref[0, h:h + 1, cols], 1e30)
        weights = jnp.exp(dot(k_ref[clip], query, NT) - lse)
        grad_v = dot(weights.astype(jnp.bfloat16), grad, NN)
        grad_s = (weights * (dot(v_ref[clip], grad, NT) - inner_ref[0, h:h + 1, cols])).astype(jnp.bfloat16)
        grad_k = dot(grad_s, query, NN)
        return dot(keys_t[h * 64:(h + 1) * 64], grad_s, NN), grad_k, grad_v

    for clip in range(3):
        cols = slice(None) if clip == 0 else pl.ds(pl.multiple_of(which[clip - 1] * 128, 128), 128)
        keys_t = k_ref[clip].T
        grad_q, grad_k, grad_v = zip(*(back(clip, keys_t, cols, h) for h in range(2)))
        grad_q = jnp.concatenate(grad_q, 0)
        if clip == 0:
            acc_ref[...] = grad_q
        else:
            acc_ref[:, cols] += grad_q
        dk_ref[clip] = (grad_k[0] + grad_k[1]).astype(jnp.bfloat16)
        dv_ref[clip] = (grad_v[0] + grad_v[1]).astype(jnp.bfloat16)
    dq_ref[...] = (acc_ref[...] * 0.125).T


def cross_backward(which, q, kv, seg, lse, inner, grad):
    toks, width = q.shape
    clips, frames = kv.shape[:2]
    pairs = width // 128
    kv_spec = pl.BlockSpec((clips, frames, 128), lambda j, w: (0, 0, j))
    v_spec = pl.BlockSpec((clips, frames, 128), lambda j, w: (0, 0, j + pairs))
    tok_spec = pl.BlockSpec((toks, 128), lambda j, w: (0, j))
    row_spec = pl.BlockSpec((1, 2, toks), lambda j, w: (j, 0, 0))
    return pl.pallas_call(
        cross_backward_kernel,
        grid_spec=pltpu.PrefetchScalarGridSpec(
            num_scalar_prefetch=1,
            grid=(width // 128,),
            in_specs=[tok_spec, kv_spec, v_spec, pl.BlockSpec((1, toks), lambda j, w: (0, 0)), row_spec, row_spec, tok_spec],
            out_specs=[tok_spec, kv_spec, kv_spec],
            scratch_shapes=[pltpu.VMEM((128, toks), jnp.float32)],
        ),
        out_shape=[
            jax.ShapeDtypeStruct((toks, width), jnp.float32),
            jax.ShapeDtypeStruct((clips, frames, width), jnp.bfloat16),
            jax.ShapeDtypeStruct((clips, frames, width), jnp.bfloat16),
        ],
        compiler_params=pltpu.CompilerParams(vmem_limit_bytes=48 * 2**20),
        name="cross_backward",
    )(which, q, kv, kv, seg, lse, inner, grad)


Z = 4


class Place:
    def __init__(self):
        self.dp = lax.axis_index("dp")
        self.core = lax.axis_index("seq")
        self.z = self.dp // 4
        self.p = self.dp % 4
        x, y = self.p % 2, self.p // 2
        px, py = self.p + 1 - 2 * x, self.p + 2 - 4 * y
        self.p_first = px * (1 - self.core) + py * self.core
        self.p_second = py * (1 - self.core) + px * self.core
        self.p_diag = 3 - self.p
        base = self.z * 4
        self.first = (base + self.p_first, self.core)
        self.second = (base + self.p_second, self.core)
        self.up = (lax.rem(self.dp + 4, 16), self.core)
        self.down = (lax.rem(self.dp + 12, 16), self.core)
        self.mate = (self.dp, 1 - self.core)
        self.has_up = self.z < Z - 1
        self.has_down = self.z > 0

    def greet(self):
        barrier = pltpu.get_barrier_semaphore()
        for target in (self.mate, self.first, self.second):
            pl.semaphore_signal(barrier, inc=1, device_id=target, device_id_type=MESH)

        @pl.when(self.has_up)
        def _():
            pl.semaphore_signal(barrier, inc=1, device_id=self.up, device_id_type=MESH)

        @pl.when(self.has_down)
        def _():
            pl.semaphore_signal(barrier, inc=1, device_id=self.down, device_id_type=MESH)

        pl.semaphore_wait(barrier, 3 + (self.z + 3) // 4 + (6 - self.z) // 4)


def when(cond, fn):
    if cond is None:
        fn()
    else:
        pl.when(cond)(fn)


def both(a, b):
    if a is None:
        return b
    if b is None:
        return a
    return jnp.logical_and(a, b)


MATE_COLS = 1536


class Gather:
    def __init__(self, me, srcs, outs, send_sem, recv_sem, own_sem):
        self.me, self.srcs, self.outs = me, srcs, outs
        self.send_sem, self.recv_sem, self.own_sem = send_sem, recv_sem, own_sem
        self.sends = []
        self.tasks = []
        for m, (begin, step) in enumerate(GATHER_TIMES):
            for k, task in enumerate(self.steps(m)):
                self.tasks.append((begin + step * k, m, task))
        self.tasks.sort(key=lambda entry: entry[:2])

    def piece(self, m, chip, core):
        if m == 0:
            return self.outs[m].at[chip * 2 + core]
        if m == 4:
            return self.outs[m].at[pl.ds(pl.multiple_of(chip * 192 + core * 96, 96), 96)]
        rows = pl.ds(pl.multiple_of(chip * 48, 48), 48)
        return self.outs[m].at[rows, pl.ds(pl.multiple_of(core * MATE_COLS, MATE_COLS), MATE_COLS)]

    def sender(self, m, src, chip, target, cond):
        copy = pltpu.make_async_remote_copy(
            src_ref=src, dst_ref=self.piece(m, chip, self.me.core), send_sem=self.send_sem.at[len(self.sends)],
            recv_sem=self.recv_sem.at[m, chip * 2 + self.me.core], device_id=target, device_id_type=MESH)
        self.sends.append((cond, copy))
        return lambda: when(cond, copy.start)

    def arrival(self, m, chip, core, cond=None):
        piece = self.piece(m, chip, core)
        copy = pltpu.make_async_remote_copy(
            src_ref=piece, dst_ref=piece, send_sem=self.send_sem.at[0],
            recv_sem=self.recv_sem.at[m, chip * 2 + core], device_id=self.me.mate, device_id_type=MESH)
        return lambda: when(cond, copy.wait_recv)

    def forward(self, m, z, p, targets, cond=None):
        chip = z * 4 + p
        return [self.arrival(m, chip, self.me.core, cond)] + [
            self.sender(m, self.piece(m, chip, self.me.core), chip, target, both(cond, extra))
            for target, extra in targets
        ]

    def steps(self, m):
        me = self.me
        up, down, mate = (me.up, me.has_up), (me.down, me.has_down), (me.mate, None)
        first, second = (me.first, None), (me.second, None)

        def at(d, p, below_to, above_to):
            if d == 0:
                return self.forward(m, me.z, p, below_to)
            return self.forward(m, me.z - d, p, below_to, me.z - d >= 0) + self.forward(
                m, me.z + d, p, above_to, me.z + d < Z)

        begin = [self.sender(m, self.srcs[m], me.dp, *target) for target in (up, down, first, second, mate)]
        begin.append(pltpu.make_async_copy(self.srcs[m], self.piece(m, me.dp, me.core), self.own_sem.at[m]).start)
        steps = [begin]
        for d in range(1, Z + 1):
            line = at(d, me.p, [up, first, second, mate], [down, first, second, mate]) if d < Z else []
            steps.append(line + at(d - 1, me.p_first, [second, mate], [second, mate]))
        steps.append([act for p in (me.p_second, me.p_diag) for d in range(Z) for act in at(d, p, [mate], [mate])])
        return steps

    def run(self, entry):
        for act in entry[2]:
            act()

    def run_until(self, time):
        while self.tasks and self.tasks[0][0] <= time:
            self.run(self.tasks.pop(0))

    def take_until(self, time):
        taken = []
        while self.tasks and self.tasks[0][0] <= time:
            taken.append(self.tasks.pop(0))
        return taken

    def need(self, m):
        for entry in [e for e in self.tasks if e[1] == m]:
            self.run(entry)
        self.tasks = [e for e in self.tasks if e[1] != m]
        pltpu.make_async_copy(self.srcs[m], self.piece(m, self.me.dp, self.me.core), self.own_sem.at[m]).wait()
        for chip in range(16):
            self.arrival(m, chip, 1 - self.me.core)()

    def finish(self):
        for cond, copy in self.sends:
            when(cond, copy.wait_send)


GATHER_TIMES = ((3, 4), (2, 5), (14, 6), (34, 6), (52, 6))


def loop_with(gather, count, begin, length, body):
    due = [gather.take_until(begin + length * i) for i in range(count)]

    def turn(i, carry):
        for k, tasks in enumerate(due):
            if tasks:

                def run(tasks=tasks):
                    for task in tasks:
                        gather.run(task)

                pl.when(i == k)(run)
        body(i)
        return carry

    lax.fori_loop(0, count, turn, 0)


def norm_rows(values, gain, shift):
    average = jnp.mean(values, -1, keepdims=True)
    centred = values - average
    spread = jnp.mean(centred * centred, -1, keepdims=True)
    return centred * lax.rsqrt(spread + 1e-05) * gain + shift


def columns(j, size=128):
    return pl.ds(pl.multiple_of(j * size, size), size)


def forward_kernel(*refs):
    (group_ref, x_ref, frames_ref, bias_ref, seg_ref, small_in, self_in, cross_in, up_in, down_in) = refs[:10]
    (small_out, self_out, cross_out, up_out, down_out, kv_out, vec_ref, normed_one_ref, query_ref, kv_row_ref,
     attended_ref, self_lse_ref, after_self_ref, normed_two_ref, row_query_ref, cross_lse_ref, mixed_ref,
     after_cross_ref, normed_three_ref) = refs[10:29]
    (half_ref, pair_ref, small_vm, self_vm, cross_vm, kv_vm, acc_ref, stat_ref, part_ref, part_stat_ref, give_ref,
     give_stat_ref, take_ref, take_stat_ref, send_sem, recv_sem, own_sem, half_sems, mate_sems, load_sem) = refs[29:]
    me = Place()
    core = me.core
    width = x_ref.shape[1]
    toks = x_ref.shape[0]
    me.greet()

    def to_mate(src, dst, k):
        return pltpu.make_async_remote_copy(
            src_ref=src, dst_ref=dst, send_sem=mate_sems.at[0, k], recv_sem=mate_sems.at[1, k], device_id=me.mate,
            device_id_type=MESH)

    shards = (self_in, cross_in, up_in)
    halves = [
        pltpu.make_async_remote_copy(
            src_ref=shard.at[:, columns(1 - core, MATE_COLS)], dst_ref=half_ref.at[m], send_sem=half_sems.at[0, m],
            recv_sem=half_sems.at[1, m], device_id=me.mate, device_id_type=MESH)
        for m, shard in enumerate(shards)
    ]
    for copy in halves:
        copy.start()
    gather = Gather(me, (small_in, pair_ref.at[0], pair_ref.at[1], pair_ref.at[2], down_in),
                    (small_out, self_out, cross_out, up_out, down_out), send_sem, recv_sem, own_sem)
    for m, shard in enumerate(shards):
        halves[m].wait()
        own = shard[:, columns(core, MATE_COLS)].astype(jnp.float32)
        came = half_ref[m].astype(jnp.float32)
        is_first = core == 0
        pair_ref[m] = jnp.concatenate(
            [jnp.where(is_first, own, came), jnp.where(is_first, came, own)], 0).astype(jnp.bfloat16)
        if m == 0:
            gather.run_until(GATHER_TIMES[1][0])
    gather.run_until(GATHER_TIMES[1][0] + 3 * GATHER_TIMES[1][1])
    gather.need(0)
    copy = pltpu.make_async_copy(small_out, small_vm, load_sem.at[0])
    copy.start()
    copy.wait()
    row = lax.broadcasted_iota(jnp.int32, (128, width), 0)
    spot = lax.broadcasted_iota(jnp.int32, (128, width), 1) - row

    def place_small(d, total):
        chosen = jnp.where((spot == d * 24) & (row < 24), 1.0, 0.0).astype(jnp.bfloat16)
        return total + dot(small_vm[d], chosen, NN)

    vec_ref[...] = lax.fori_loop(0, 32, place_small, jnp.zeros(vec_ref.shape, jnp.float32))

    def vec(k):
        return vec_ref[k:k + 1]

    source = x_ref[...].astype(jnp.float32)
    normed_one_ref[...] = norm_rows(source, vec(0), vec(1)).astype(jnp.bfloat16)
    gather.run_until(GATHER_TIMES[1][0] + 5 * GATHER_TIMES[1][1])
    gather.need(1)
    copy = pltpu.make_async_copy(self_out, self_vm, load_sem.at[0])
    copy.start()
    copy.wait()

    normed = normed_one_ref[...]
    own_rows = slice(toks, 2 * toks)
    kv_row_ref[own_rows, :width] = dot(normed, self_vm[:, width:2 * width], NN).astype(jnp.bfloat16)
    kv_row_ref[own_rows, width:] = (dot(normed, self_vm[:, 2 * width:3 * width], NN) + vec(7)).astype(jnp.bfloat16)
    kv_copy = to_mate(kv_row_ref.at[own_rows], kv_row_ref.at[slice(0, toks)], 0)
    kv_copy.start()
    query = (dot(normed, self_vm[:, :width], NN) + vec(6)).astype(jnp.bfloat16)
    query_ref[...] = query * jnp.bfloat16(0.125)
    gather.run_until(33)
    kv_copy.wait()

    def self_pair(j):
        cols = columns(j)
        keys = kv_row_ref[:, cols]
        values_t = kv_row_ref[:, columns(j + 6)].T
        parts = []
        for h in range(2):
            scores = dot(keys, one_head(query_ref[:, cols], h), NT) + bias_ref[...]
            peak = jnp.max(scores, 0, keepdims=True)
            terms = jnp.exp(scores - peak)
            total = jnp.sum(terms, 0, keepdims=True)
            parts.append(dot(values_t[h * 64:(h + 1) * 64], terms.astype(jnp.bfloat16), NN) / total)
            self_lse_ref[j, h:h + 1] = peak + jnp.log(total)
        attended_ref[:, cols] = jnp.concatenate(parts, 0).T

    loop_with(gather, 6, 33, 1.2, self_pair)
    after_self = source + dot(attended_ref[...].astype(jnp.bfloat16), self_vm[:, 3 * width:], NN) + vec(8)
    after_self_ref[...] = after_self
    normed_two = norm_rows(after_self, vec(2), vec(3)).astype(jnp.bfloat16)
    normed_two_ref[...] = normed_two
    gather.run_until(44)
    gather.need(2)
    copy = pltpu.make_async_copy(cross_out, cross_vm, load_sem.at[0])
    copy.start()
    copy.wait()
    my_rows = pl.ds(pl.multiple_of(core * toks, toks), toks)
    cross_query = (dot(normed_two, cross_vm[:, :width], NN) + vec(9)).astype(jnp.bfloat16)
    row_query_ref[my_rows] = cross_query * jnp.bfloat16(0.125)
    query_copy = to_mate(row_query_ref.at[my_rows], row_query_ref.at[my_rows], 1)
    query_copy.start()

    clips = frames_ref.shape[0]
    tiles = 2 * width // 256

    def project(t):
        clip, tile = t // tiles, t % tiles
        result = dot(frames_ref[clip], cross_vm[:, columns(tile + 3, 256)], NN)
        is_value = (tile >= 3).astype(jnp.float32)
        shift = vec_ref[10:11, columns(tile % 3, 256)] * is_value
        kv_vm[clip, :, columns(tile, 256)] = (result + shift).astype(jnp.bfloat16)

    loop_with(gather, clips * tiles, 46, 0.7, project)
    kv_store = pltpu.make_async_copy(kv_vm, kv_out, load_sem.at[1])
    kv_store.start()
    query_copy.wait()

    def attend(clip, values_t, query, j, h):
        scores = dot(kv_vm[clip, :, columns(j)], query, NT)
        peak = jnp.max(scores, 0, keepdims=True)
        terms = jnp.exp(scores - peak)
        total = jnp.sum(terms, 0, keepdims=True)
        result = dot(values_t[h * 64:(h + 1) * 64], terms.astype(jnp.bfloat16), NN)
        return result / total, peak, total

    def cross_pair(j):
        values_t = kv_vm[0, :, columns(j + 6)].T
        mine = seg_ref[...] == 0
        for h in range(2):
            result, peak, total = attend(0, values_t, one_head(row_query_ref[:, columns(j)], h), j, h)
            acc_ref[h * 64:(h + 1) * 64] = jnp.where(mine, result, 0.0)
            stat_ref[h:h + 1] = jnp.where(mine, peak, 0.0)
            stat_ref[2 + h:3 + h] = jnp.where(mine, total, 1.0)
        for clip in (1, 2):
            values_t = kv_vm[clip, :, columns(j + 6)].T
            query_rows = jnp.where(
                group_ref[clip - 1:clip] == 0, row_query_ref[:128, columns(j)], row_query_ref[384:, columns(j)])
            for h in range(2):
                result, peak, total = attend(clip, values_t, one_head(query_rows, h), j, h)
                for spot in (0, 3):
                    cols = slice(spot * 128, (spot + 1) * 128)
                    mine = seg_ref[:, cols] == clip
                    rows = slice(h * 64, (h + 1) * 64)
                    acc_ref[rows, cols] = jnp.where(mine, result, acc_ref[rows, cols])
                    stat_ref[h:h + 1, cols] = jnp.where(mine, peak, stat_ref[h:h + 1, cols])
                    stat_ref[2 + h:3 + h, cols] = jnp.where(mine, total, stat_ref[2 + h:3 + h, cols])
        my_cols, mate_cols = columns(core, toks), columns(1 - core, toks)
        part_ref[j] = acc_ref[:, my_cols]
        part_stat_ref[j] = stat_ref[:, my_cols]
        give_ref[j] = acc_ref[:, mate_cols].astype(jnp.bfloat16)
        give_stat_ref[j] = stat_ref[:, mate_cols]

    loop_with(gather, 6, 60, 4, cross_pair)
    give_copy = to_mate(give_ref, take_ref, 2)
    give_copy.start()
    give_stat_copy = to_mate(give_stat_ref, take_stat_ref, 3)
    give_stat_copy.start()
    gather.run_until(1000)
    give_copy.wait()
    give_stat_copy.wait()

    def combine(j, carry):
        parts = []
        for h in range(2):
            rows = slice(h * 64, (h + 1) * 64)
            peak_a, peak_b = part_stat_ref[j, h:h + 1], take_stat_ref[j, h:h + 1]
            peak = jnp.maximum(peak_a, peak_b)
            share_a = part_stat_ref[j, 2 + h:3 + h] * jnp.exp(peak_a - peak)
            share_b = take_stat_ref[j, 2 + h:3 + h] * jnp.exp(peak_b - peak)
            total = share_a + share_b
            cross_lse_ref[j, h:h + 1] = peak + jnp.log(total)
            parts.append(part_ref[j, rows] * (share_a / total)
                         + take_ref[j, rows].astype(jnp.float32) * (share_b / total))
        mixed_ref[:, columns(j)] = jnp.concatenate(parts, 0).T
        return carry

    lax.fori_loop(0, 6, combine, 0)
    after_cross = after_self_ref[...] + dot(mixed_ref[...].astype(jnp.bfloat16), cross_vm[:, 3 * width:], NN) + vec(11)
    after_cross_ref[...] = after_cross
    normed_three_ref[...] = norm_rows(after_cross, vec(4), vec(5)).astype(jnp.bfloat16)
    gather.need(3)
    gather.need(4)
    kv_store.wait()
    gather.finish()


def fused_forward(group, x, frames, bias, seg, small, self_w, cross_w, up_w, down_w):
    toks, width = x.shape
    clips, count = frames.shape[:2]
    low, full = jnp.bfloat16, jnp.float32
    pairs = width // 128
    vmem, hbm = pl.BlockSpec(memory_space=pltpu.VMEM), pl.BlockSpec(memory_space=pl.ANY)
    shape = jax.ShapeDtypeStruct
    outs = [
        (hbm, shape((32, 16, 128), low)), (hbm, shape((width, 4 * width), low)), (hbm, shape((width, 4 * width), low)),
        (hbm, shape((width, 4 * width), low)), (hbm, shape((4 * width, width), low)),
        (hbm, shape((clips, count, 2 * width), low)),
        (vmem, shape((16, width), full)), (vmem, shape((toks, width), low)), (vmem, shape((toks, width), low)),
        (vmem, shape((2 * toks, 2 * width), low)), (vmem, shape((toks, width), full)),
        (vmem, shape((pairs, 2, toks), full)), (vmem, shape((toks, width), full)), (vmem, shape((toks, width), low)),
        (vmem, shape((2 * toks, width), low)), (vmem, shape((pairs, 2, toks), full)), (vmem, shape((toks, width), full)),
        (vmem, shape((toks, width), full)), (vmem, shape((toks, width), low)),
    ]
    return pl.pallas_call(
        forward_kernel,
        in_specs=[vmem] * 5 + [hbm] + [vmem] * 3 + [hbm],
        out_specs=tuple(spec for spec, _ in outs),
        out_shape=tuple(s for _, s in outs),
        scratch_shapes=[
            pltpu.VMEM((3, 24, MATE_COLS), low), pltpu.VMEM((3, 48, MATE_COLS), low), pltpu.VMEM((32, 16, 128), low),
            pltpu.VMEM((width, 4 * width), low), pltpu.VMEM((width, 4 * width), low),
            pltpu.VMEM((clips, count, 2 * width), low), pltpu.VMEM((128, 2 * toks), full), pltpu.VMEM((4, 2 * toks), full),
            pltpu.VMEM((pairs, 128, toks), full), pltpu.VMEM((pairs, 4, toks), full),
            pltpu.VMEM((pairs, 128, toks), low), pltpu.VMEM((pairs, 4, toks), full),
            pltpu.VMEM((pairs, 128, toks), low), pltpu.VMEM((pairs, 4, toks), full),
            pltpu.SemaphoreType.DMA((340,)), pltpu.SemaphoreType.DMA((5, 32)), pltpu.SemaphoreType.DMA((5,)),
            pltpu.SemaphoreType.DMA((2, 3)), pltpu.SemaphoreType.DMA((2, 4)), pltpu.SemaphoreType.DMA((2,)),
        ],
        compiler_params=pltpu.CompilerParams(collective_id=0, has_side_effects=True, vmem_limit_bytes=60 * 2**20),
        name="fused_forward",
    )(group, x, frames, bias, seg, small, self_w, cross_w, up_w, down_w)


def scatter_kernel(count, *refs):
    grads, outs = refs[:count], refs[count:2 * count]
    scratch = refs[2 * count:]
    owns, pairs, plane_as, plane_bs, plane_cs, lines = (scratch[k * count:(k + 1) * count] for k in range(6))
    send_sem, own_sem, pair_sem, plane_sem, line_sem = scratch[6 * count:]
    me = Place()
    half = me.z // 2
    near = me.z + half * (3 - 2 * me.z)

    def far(k):
        base = (3, 2, 1 - near, near)[k]
        return base + half * (3 - 2 * base)

    order = [far(k) for k in range(4)]
    plane = [me.p_diag, me.p_first, me.p_second, me.p]
    mate_plane = [me.p_diag, me.p_second, me.p_first, me.p]
    for k in range(4):
        for m in range(count):
            pltpu.make_async_copy(grads[m].at[:, plane[k], me.core], owns[m].at[:, plane[k]], own_sem.at[m, plane[k]]).start()
    me.greet()
    sends = []

    def send(src, dst, sem, target, cond=None):
        slot = len(sends)
        copy = pltpu.make_async_remote_copy(src_ref=src, dst_ref=dst, send_sem=send_sem.at[slot], recv_sem=sem, device_id=target, device_id_type=MESH)
        sends.append((cond, copy))
        when(cond, copy.start)

    def arrive(dst, sem, cond=None):
        when(cond, pltpu.make_async_remote_copy(src_ref=dst, dst_ref=dst, send_sem=send_sem.at[0], recv_sem=sem, device_id=me.mate, device_id_type=MESH).wait_recv)

    for k in range(4):
        for m in range(count):
            p = mate_plane[k]
            send(grads[m].at[:, p, 1 - me.core], pairs[m].at[:, p], pair_sem.at[m, p], me.mate)

    def paired(m, p):
        pltpu.make_async_copy(grads[m].at[:, p, me.core], owns[m].at[:, p], own_sem.at[m, p]).wait()
        arrive(pairs[m].at[:, p], pair_sem.at[m, p])

    def add(dst, *others):
        total = dst[...].astype(jnp.float32)
        for other in others:
            total = total + other[...].astype(jnp.float32)
        dst[...] = total.astype(dst.dtype)

    def steps(m):
        own = owns[m]
        paired(m, me.p_diag)
        for k in range(4):
            z = order[k]
            add(own.at[z, me.p_diag], pairs[m].at[z, me.p_diag])
            send(own.at[z, me.p_diag], plane_as[m].at[z], plane_sem.at[m, 0, z], me.second)
        yield
        paired(m, me.p_second)
        for k in range(4):
            z = order[k]
            add(own.at[z, me.p_second], pairs[m].at[z, me.p_second])
            send(own.at[z, me.p_second], plane_cs[m].at[z], plane_sem.at[m, 2, z], me.second)
        yield
        paired(m, me.p_first)
        for k in range(4):
            z = order[k]
            arrive(plane_as[m].at[z], plane_sem.at[m, 0, z])
            add(own.at[z, me.p_first], pairs[m].at[z, me.p_first], plane_as[m].at[z])
            send(own.at[z, me.p_first], plane_bs[m].at[z], plane_sem.at[m, 1, z], me.first)
        yield
        paired(m, me.p)
        for k in range(4):
            z = order[k]
            arrive(plane_bs[m].at[z], plane_sem.at[m, 1, z])
            arrive(plane_cs[m].at[z], plane_sem.at[m, 2, z])
            if k == 3:
                break
            add(own.at[z, me.p], pairs[m].at[z, me.p], plane_bs[m].at[z], plane_cs[m].at[z])
            upward = (z - me.z + 3) // 4
            source = me.z + 1 - 2 * upward
            came = jnp.logical_and(source >= 0, source < Z)

            def gather_in(z=z, upward=upward):
                slot = lines[m].at[upward, z]
                arrive(slot, line_sem.at[m, upward, z])
                add(own.at[z, me.p], slot)

            pl.when(came)(gather_in)
            target = (lax.rem(me.dp + 12 + 8 * upward, 16), me.core)
            send(own.at[z, me.p], lines[m].at[upward, z], line_sem.at[m, upward, z], target)
        yield
        z = me.z
        total = own[z, me.p].astype(jnp.float32) + pairs[m][z, me.p].astype(jnp.float32)
        total = total + plane_bs[m][z].astype(jnp.float32) + plane_cs[m][z].astype(jnp.float32)
        outs[m][...] = total
        for upward, cond in ((0, me.has_up), (1, me.has_down)):

            def last(upward=upward):
                arrive(lines[m].at[upward, z], line_sem.at[m, upward, z])
                outs[m][...] += lines[m][upward, z].astype(jnp.float32)

            pl.when(cond)(last)

    running = [steps(m) for m in range(count)]
    while running:
        still = []
        for step in running:
            try:
                next(step)
                still.append(step)
            except StopIteration:
                pass
        running = still
    for cond, copy in sends:
        when(cond, copy.wait_send)


def scatter_all(grads):
    count = len(grads)
    shapes = [g.shape[1:] for g in grads]
    views = [g.reshape((4, 4, 2) + s) for g, s in zip(grads, shapes)]

    def vmem(*lead):
        return [pltpu.VMEM(lead + s, g.dtype) for g, s in zip(grads, shapes)]

    return pl.pallas_call(
        functools.partial(scatter_kernel, count),
        out_shape=tuple(jax.ShapeDtypeStruct(s, jnp.float32) for s in shapes),
        in_specs=[pl.BlockSpec(memory_space=pl.ANY)] * count,
        out_specs=tuple([pl.BlockSpec(memory_space=pltpu.VMEM)] * count),
        scratch_shapes=vmem(4, 4) + vmem(4, 4) + vmem(4) + vmem(4) + vmem(4) + vmem(2, 4) + [
            pltpu.SemaphoreType.DMA((20 * count,)),
            pltpu.SemaphoreType.DMA((count, 4)),
            pltpu.SemaphoreType.DMA((count, 4)),
            pltpu.SemaphoreType.DMA((count, 3, 4)),
            pltpu.SemaphoreType.DMA((count, 2, 4)),
        ],
        compiler_params=pltpu.CompilerParams(collective_id=1, has_side_effects=True, vmem_limit_bytes=60 * 2**20),
        name="scatter_all",
    )(*views)


def pack_rows(up_bias, down_bias, vectors, size):
    rows = jnp.concatenate([up_bias, down_bias, vectors], 1)
    return jnp.pad(rows, ((0, 0), (0, size - rows.shape[1])))


def scatter_grads(grads_self, grads_cross, grad_up, grad_down, grad_up_bias, grad_out_bias, vector_grads):
    parts = (grads_self, grads_cross, grad_up, grad_down, grad_up_bias, grad_out_bias, vector_grads)
    if lax.axis_size("dp") != 16:
        return tuple(lax.psum_scatter(part, ("dp", "seq"), scatter_dimension=0, tiled=True) for part in parts)
    small = pack_rows(
        grad_up_bias.reshape(32, -1), grad_out_bias.reshape(32, -1), vector_grads.reshape(32, -1), 1024
    ).reshape(32, 8, 128)
    large = tuple(g.astype(jnp.bfloat16).reshape(32, -1, g.shape[1]) for g in parts[:4])
    whole = scatter_all(large + (small,))
    row = whole[4].reshape(-1)
    n_up, n_down, n_vec = (g.size // 32 for g in parts[4:])
    return tuple(whole[:4]) + (
        row[:n_up],
        row[n_up:n_up + n_down],
        row[n_up + n_down:n_up + n_down + n_vec].reshape(-1, vector_grads.shape[1]),
    )


def from_behind(value, axis, steps):
    count = lax.axis_size(axis)
    leading, last = (max(0, -steps), min(count, count - steps))
    return lax.ppermute(value, axis, [(source, source + steps) for source in range(leading, last)])


def layer_norm(values, gain, shift):
    average = jnp.mean(values, -1, keepdims=True)
    centred = values - average
    spread = jnp.mean(centred * centred, -1, keepdims=True)
    return centred * lax.rsqrt(spread + 1e-05) * gain + shift


def exact_gelu(values):
    return jax.nn.gelu(values, approximate=False)


def matmul(left, right):
    return jnp.dot(left, right, preferred_element_type=jnp.float32)


def swap_halves(value):
    return lax.ppermute(value, "seq", [(0, 1), (1, 0)])


def seq_halves(value, axis):
    span = value.shape[axis] // 2
    half = lax.axis_index("seq")
    mine = lax.dynamic_slice_in_dim(value, half * span, span, axis)
    other = lax.dynamic_slice_in_dim(value, (1 - half) * span, span, axis)
    return mine, other


def seq_scatter(value):
    mine, other = seq_halves(value, 0)
    return mine + swap_halves(other.astype(jnp.bfloat16)).astype(value.dtype)


def per_head(values):
    rows = values.reshape(-1, values.shape[2]).T
    return jnp.repeat(rows, HEAD_DIM, axis=1)


def head_sums(values):
    sums = jnp.sum(values.reshape(values.shape[0], -1, HEAD_DIM), -1)
    return sums.T.reshape(-1, 2, values.shape[0])


def plain_forward(
    which, layer_input, frames, mask_bias, row_segment, weights
):
    self_full, cross_full, up_full, down_full, bias_full, out_bias_full, vectors = (
        lax.all_gather(part, ("dp", "seq"), axis=0, tiled=True) for part in weights
    )
    vec = jnp.pad(
        jnp.concatenate([vectors.T, out_bias_full[None]]).astype(jnp.float32), ((0, 3), (0, 0))
    )
    model_width = layer_input.shape[1]
    cross_in = [cross_full[:, k * model_width : (k + 1) * model_width] for k in range(4)]
    source = layer_input.astype(jnp.float32)
    normed_one = layer_norm(source, vec[0], vec[1]).astype(jnp.bfloat16)
    proj_bias = jnp.concatenate([vec[6], jnp.zeros_like(vec[6]), vec[7]])
    qkv_low = (matmul(normed_one, self_full[:, : 3 * model_width]) + proj_bias).astype(jnp.bfloat16)
    query = qkv_low[:, :model_width] * jnp.bfloat16(0.125)
    kv_own = qkv_low[:, model_width:]
    kv_row = jnp.concatenate([from_behind(kv_own, "seq", 1), kv_own])
    attended, self_lse = self_forward(query, kv_row, mask_bias)
    attended_low = attended.astype(jnp.bfloat16)
    after_self = source + matmul(attended_low, self_full[:, 3 * model_width :]) + vec[8]
    normed_two = layer_norm(after_self, vec[2], vec[3]).astype(jnp.bfloat16)
    cross_query = (matmul(normed_two, cross_in[0]) + vec[9]).astype(jnp.bfloat16)
    cross_key = jnp.einsum(
        "cfd,de->cfe", frames, cross_in[1], preferred_element_type=jnp.float32
    ).astype(jnp.bfloat16)
    cross_value = (
        jnp.einsum("cfd,de->cfe", frames, cross_in[2], preferred_element_type=jnp.float32)
        + vec[10]
    ).astype(jnp.bfloat16)
    row_query = lax.all_gather(cross_query * jnp.bfloat16(0.125), "seq", axis=0, tiled=True)
    cross_kv = jnp.concatenate([cross_key, cross_value], 2)
    part_mixed, part_stats = cross_forward(which, row_query, cross_kv, row_segment)
    mixed_mine, mixed_other = seq_halves(part_mixed, 0)
    stats_mine, stats_other = seq_halves(part_stats, 2)
    mixed_came = swap_halves(mixed_other.astype(jnp.bfloat16))
    stats_came = swap_halves(stats_other)
    peak = jnp.maximum(stats_mine[:, :2], stats_came[:, :2])
    share_mine = stats_mine[:, 2:] * jnp.exp(stats_mine[:, :2] - peak)
    share_came = stats_came[:, 2:] * jnp.exp(stats_came[:, :2] - peak)
    total = share_mine + share_came
    cross_lse = peak + jnp.log(total)
    mixed_full = mixed_mine * per_head(share_mine / total) + mixed_came.astype(
        jnp.float32
    ) * per_head(share_came / total)
    mixed = mixed_full.astype(jnp.bfloat16)
    after_cross = after_self + matmul(mixed, cross_in[3]) + vec[11]
    normed_three = layer_norm(after_cross, vec[4], vec[5]).astype(jnp.bfloat16)
    return (
        bias_full, self_full, cross_full, up_full, down_full, cross_kv, vec, normed_one, query, kv_row, attended,
        self_lse, after_self, normed_two, row_query, cross_lse, mixed_full, after_cross, normed_three,
    )


def forward(which, layer_input, frames, mask_bias, row_segment, weights):
    if lax.axis_size("dp") != 16:
        return plain_forward(which, layer_input, frames, mask_bias, row_segment, weights)
    self_weights, cross_weights, up_weights, down_weights, up_bias, down_bias, vectors = weights

    def as_row(values):
        return jnp.pad(values, ((0, 0), (0, 128 - values.shape[1])))

    small = jnp.concatenate(
        [as_row(vectors.T), as_row(down_bias[None]), as_row(up_bias[None]), jnp.zeros((2, 128), vectors.dtype)]
    )
    group = jnp.broadcast_to(which[:, None], (2, 128))
    whole = fused_forward(
        group, layer_input, frames, mask_bias, row_segment, small, self_weights, cross_weights, up_weights,
        down_weights,
    )
    return (whole[0][:, 13, : up_bias.shape[0]].reshape(-1),) + tuple(whole[1:])


def per_device(
    layer_input,
    encoder_states,
    clip_lengths,
    out_grad,
    self_weights,
    cross_weights,
    up_weights,
    down_weights,
    up_bias,
    down_bias,
    vectors,
):
    model_width = layer_input.shape[2]
    tok_span = layer_input.shape[1]
    seq_half = lax.axis_index("seq")
    source = layer_input[0].astype(jnp.float32)
    position = seq_half * tok_span + jnp.arange(tok_span, dtype=jnp.int32)
    clip_ends = jnp.cumsum(clip_lengths[0])
    segment = jnp.sum((position[:, None] >= clip_ends[None, :]).astype(jnp.int32), 1)
    key_position = jnp.concatenate([position - tok_span, position])
    key_segment = jnp.sum((key_position[:, None] >= clip_ends[None, :]).astype(jnp.int32), 1)
    allowed = (
        (key_segment[:, None] == segment[None, :])
        & (key_position[:, None] <= position[None, :])
        & (key_position[:, None] >= 0)
    )
    mask_bias = jnp.where(allowed, 0.0, -1e30).astype(jnp.float32)
    row_position = jnp.arange(2 * tok_span, dtype=jnp.int32)
    row_segment = jnp.sum((row_position[:, None] >= clip_ends[None, :]).astype(jnp.int32), 1)[None]
    big = jnp.argmax(clip_lengths[0]).astype(jnp.int32)
    small_one = jnp.where(big == 0, 1, 0)
    small_two = jnp.where(big == 2, 1, 2)
    last_group = 2 * tok_span // 128 - 1
    order = jnp.stack([big, small_one, small_two]).astype(jnp.int32)
    row_segment = jnp.where(
        row_segment == order[0], 0, jnp.where(row_segment == order[1], 1, jnp.where(row_segment == order[2], 2, 3))
    )
    place_of = jnp.stack([jnp.sum(jnp.where(order == clip, jnp.arange(CLIPS), 0)) for clip in range(CLIPS)])
    which = jnp.where(order[1:] < big, 0, last_group).astype(jnp.int32)

    frames = jnp.take(encoder_states[0], order, axis=0, mode="clip")
    (
        bias_full, self_full, cross_full, up_full, down_full, cross_kv, vec, normed_one, query, kv_row, attended,
        self_lse, after_self, normed_two, row_query, cross_lse, mixed_full, after_cross, normed_three,
    ) = forward(
        which, layer_input[0], frames, mask_bias, row_segment,
        (self_weights, cross_weights, up_weights, down_weights, up_bias, down_bias, vectors),
    )
    bias_full = bias_full.astype(jnp.float32)
    out_bias_full = vec[12]
    attended_low = attended.astype(jnp.bfloat16)
    mixed = mixed_full.astype(jnp.bfloat16)
    cross_in = [cross_full[:, k * model_width : (k + 1) * model_width] for k in range(4)]
    pre_act = matmul(normed_three, up_full) + bias_full
    activated_low = exact_gelu(pre_act).astype(jnp.bfloat16)
    result_rows = after_cross + matmul(activated_low, down_full) + out_bias_full
    layer_output = result_rows.astype(jnp.bfloat16)[None]

    grad_low = out_grad[0]
    grad_rows = grad_low.astype(jnp.float32)
    grad_down = matmul(activated_low.T, grad_low)
    grad_out_bias = jnp.sum(grad_rows, 0)
    grad_act = matmul(grad_low, down_full.T).astype(jnp.bfloat16)
    _, gelu_pull = jax.vjp(exact_gelu, pre_act)
    grad_pre = gelu_pull(grad_act.astype(jnp.float32))[0].astype(jnp.bfloat16)
    grad_up = matmul(normed_three.T, grad_pre)
    grad_up_bias = jnp.sum(grad_pre, 0, dtype=jnp.float32)
    grad_normed_three = matmul(grad_pre, up_full.T)
    _, norm_pull_three = jax.vjp(layer_norm, after_cross, vec[4], vec[5])
    grad_part, grad_gain_three, grad_shift_three = norm_pull_three(grad_normed_three)
    grad_after_cross = grad_rows + grad_part
    grad_cross_low = grad_after_cross.astype(jnp.bfloat16)
    grad_cross_out = matmul(mixed.T, grad_cross_low)
    grad_cross_bias = jnp.sum(grad_cross_low, 0, dtype=jnp.float32)
    grad_mixed = matmul(grad_cross_low, cross_in[3].T).astype(jnp.bfloat16)
    row_grad = lax.all_gather(grad_mixed, "seq", axis=0, tiled=True)
    cross_inner = head_sums(grad_mixed.astype(jnp.float32) * mixed_full)
    row_stats = lax.all_gather(jnp.stack([cross_lse, cross_inner]), "seq", axis=3, tiled=True)
    part_query, grad_key, grad_value = cross_backward(
        which, row_query, cross_kv, row_segment, row_stats[0], row_stats[1], row_grad
    )
    grad_query_sum = seq_scatter(part_query).astype(jnp.bfloat16)
    grad_cq_weight = matmul(normed_two.T, grad_query_sum)
    grad_cq_bias = jnp.sum(grad_query_sum, 0, dtype=jnp.float32)
    grad_normed_two = matmul(grad_query_sum, cross_in[0].T)
    grad_ck_weight = jnp.einsum(
        "cfd,cfe->de", frames, grad_key, preferred_element_type=jnp.float32
    )
    grad_cv_weight = jnp.einsum(
        "cfd,cfe->de", frames, grad_value, preferred_element_type=jnp.float32
    )
    grad_cv_bias = jnp.sum(grad_value, (0, 1), dtype=jnp.float32)
    clip_key, clip_value = (jnp.take(g, place_of, axis=0, mode="clip") for g in (grad_key, grad_value))
    encoder_grad = (
        jnp.einsum("cfe,de->cfd", clip_key, cross_in[1], preferred_element_type=jnp.float32)
        + jnp.einsum("cfe,de->cfd", clip_value, cross_in[2], preferred_element_type=jnp.float32)
    )[None]
    _, norm_pull_two = jax.vjp(layer_norm, after_self, vec[2], vec[3])
    grad_part, grad_gain_two, grad_shift_two = norm_pull_two(grad_normed_two)
    grad_after_self = grad_after_cross + grad_part
    grad_self_low = grad_after_self.astype(jnp.bfloat16)
    grad_self_out = matmul(attended_low.T, grad_self_low)
    grad_self_bias = jnp.sum(grad_self_low, 0, dtype=jnp.float32)
    grad_attended = matmul(grad_self_low, self_full[:, 3 * model_width :].T).astype(jnp.bfloat16)
    self_inner = head_sums(grad_attended.astype(jnp.float32) * attended)
    grad_query, grad_key_row, grad_value_row = self_backward(
        query, kv_row, mask_bias, self_lse, self_inner, grad_attended
    )
    grad_kv = jnp.concatenate([grad_key_row, grad_value_row], 1)
    back_kv = from_behind(grad_kv[:tok_span].astype(jnp.bfloat16), "seq", -1)
    grad_qkv_low = jnp.concatenate(
        [grad_query, grad_kv[tok_span:] + back_kv.astype(jnp.float32)], 1
    ).astype(jnp.bfloat16)
    grad_qkv_weight = matmul(normed_one.T, grad_qkv_low)
    grad_qkv_bias = jnp.sum(grad_qkv_low, 0, dtype=jnp.float32)
    grad_normed_one = matmul(grad_qkv_low, self_full[:, : 3 * model_width].T)
    _, norm_pull_one = jax.vjp(layer_norm, source, vec[0], vec[1])
    grad_part, grad_gain_one, grad_shift_one = norm_pull_one(grad_normed_one)
    input_grad = (grad_after_self + grad_part)[None]
    grads_self = jnp.concatenate([grad_qkv_weight, grad_self_out], 1)
    grads_cross = jnp.concatenate(
        [grad_cq_weight, grad_ck_weight, grad_cv_weight, grad_cross_out], 1
    )
    vector_grads = jnp.stack(
        [
            grad_gain_one,
            grad_shift_one,
            grad_gain_two,
            grad_shift_two,
            grad_gain_three,
            grad_shift_three,
            grad_qkv_bias[:model_width],
            grad_qkv_bias[2 * model_width :],
            grad_self_bias,
            grad_cq_bias,
            grad_cv_bias,
            grad_cross_bias,
        ],
        1,
    )
    shares = scatter_grads(
        grads_self, grads_cross, grad_up, grad_down, grad_up_bias, grad_out_bias, vector_grads
    )
    return (layer_output, input_grad, encoder_grad) + shares


def solution(mesh):
    return jax.shard_map(
        per_device,
        mesh=mesh,
        in_specs=(
            P("dp", "seq", None),
            P("dp", None, "seq", None),
            P("dp", None),
            P("dp", "seq", None),
            P(("dp", "seq"), None),
            P(("dp", "seq"), None),
            P(("dp", "seq"), None),
            P(("dp", "seq"), None),
            P(("dp", "seq")),
            P(("dp", "seq")),
            P(("dp", "seq"), None),
        ),
        out_specs=(
            P("dp", "seq", None),
            P("dp", "seq", None),
            P("dp", None, "seq", None),
            P(("dp", "seq"), None),
            P(("dp", "seq"), None),
            P(("dp", "seq"), None),
            P(("dp", "seq"), None),
            P(("dp", "seq")),
            P(("dp", "seq")),
            P(("dp", "seq"), None),
        ),
        check_vma=False,
    )
```

```python
import functools

import jax
import jax.numpy as jnp
from jax import lax
from jax.experimental import pallas as pl
from jax.experimental.pallas import tpu as pltpu
from jax.sharding import PartitionSpec as P

HEAD_DIM = 64
CLIPS = 3
MESH = pl.DeviceIdType.MESH
NT = (((1,), (1,)), ((), ()))
NN = (((1,), (0,)), ((), ()))


def dot(left, right, dims):
    return lax.dot_general(left, right, dims, preferred_element_type=jnp.float32)


def one_head(values, h):
    lane = lax.broadcasted_iota(jnp.int32, values.shape, 1)
    return jnp.where((lane >= 64) == (h == 1), values, jnp.zeros_like(values))


def self_forward_kernel(q_ref, k_ref, v_ref, bias_ref, out_ref, lse_ref):
    keys = k_ref[...]
    values_t = v_ref[...].T
    halves = []
    for h in range(2):
        scores = dot(keys, one_head(q_ref[...], h), NT) + bias_ref[...]
        peak = jnp.max(scores, 0, keepdims=True)
        terms = jnp.exp(scores - peak)
        total = jnp.sum(terms, 0, keepdims=True)
        result = dot(values_t[h * 64:(h + 1) * 64], terms.astype(jnp.bfloat16), NN)
        halves.append(result / total)
        lse_ref[0, h:h + 1] = peak + jnp.log(total)
    out_ref[...] = jnp.concatenate(halves, 0).T.astype(out_ref.dtype)


def self_forward(q, kv, bias):
    toks, width = q.shape
    keys, pairs = kv.shape[0], width // 128
    return pl.pallas_call(
        self_forward_kernel,
        grid=(width // 128,),
        in_specs=[
            pl.BlockSpec((toks, 128), lambda j: (0, j)),
            pl.BlockSpec((keys, 128), lambda j: (0, j)),
            pl.BlockSpec((keys, 128), lambda j: (0, j + pairs)),
            pl.BlockSpec((keys, toks), lambda j: (0, 0)),
        ],
        out_specs=[
            pl.BlockSpec((toks, 128), lambda j: (0, j)),
            pl.BlockSpec((1, 2, toks), lambda j: (j, 0, 0)),
        ],
        out_shape=[
            jax.ShapeDtypeStruct((toks, width), jnp.float32),
            jax.ShapeDtypeStruct((width // 128, 2, toks), jnp.float32),
        ],
        compiler_params=pltpu.CompilerParams(vmem_limit_bytes=48 * 2**20),
        name="self_forward",
    )(q, kv, kv, bias)


def self_backward_kernel(q_ref, k_ref, v_ref, bias_ref, lse_ref, inner_ref, g_ref, dq_ref, dk_ref, dv_ref):
    keys, values = k_ref[...], v_ref[...]
    keys_t = keys.T
    grad_k = grad_v = None
    halves = []
    for h in range(2):
        query, grad = one_head(q_ref[...], h), one_head(g_ref[...], h)
        weights = jnp.exp(dot(keys, query, NT) + bias_ref[...] - lse_ref[0, h:h + 1])
        part = dot(weights.astype(jnp.bfloat16), grad, NN)
        grad_v = part if grad_v is None else grad_v + part
        grad_s = (weights * (dot(values, grad, NT) - inner_ref[0, h:h + 1])).astype(jnp.bfloat16)
        part = dot(grad_s, query, NN)
        grad_k = part if grad_k is None else grad_k + part
        halves.append(dot(keys_t[h * 64:(h + 1) * 64], grad_s, NN))
    dq_ref[...] = (jnp.concatenate(halves, 0) * 0.125).T
    dk_ref[...] = grad_k
    dv_ref[...] = grad_v


def self_backward(q, kv, bias, lse, inner, grad):
    toks, width = q.shape
    keys, pairs = kv.shape[0], width // 128
    tok_spec = pl.BlockSpec((toks, 128), lambda j: (0, j))
    key_spec = pl.BlockSpec((keys, 128), lambda j: (0, j))
    row_spec = pl.BlockSpec((1, 2, toks), lambda j: (j, 0, 0))
    return pl.pallas_call(
        self_backward_kernel,
        grid=(width // 128,),
        in_specs=[tok_spec, key_spec, pl.BlockSpec((keys, 128), lambda j: (0, j + pairs)), pl.BlockSpec((keys, toks), lambda j: (0, 0)), row_spec, row_spec, tok_spec],
        out_specs=[tok_spec, key_spec, key_spec],
        out_shape=[
            jax.ShapeDtypeStruct((toks, width), jnp.float32),
            jax.ShapeDtypeStruct((keys, width), jnp.float32),
            jax.ShapeDtypeStruct((keys, width), jnp.float32),
        ],
        compiler_params=pltpu.CompilerParams(vmem_limit_bytes=48 * 2**20),
        name="self_backward",
    )(q, kv, kv, bias, lse, inner, grad)


def cross_forward_kernel(which, q_ref, k_ref, v_ref, seg_ref, out_ref, stat_ref, acc_ref):
    def attend(clip, values_t, query, h):
        scores = dot(k_ref[clip], query, NT)
        peak = jnp.max(scores, 0, keepdims=True)
        terms = jnp.exp(scores - peak)
        total = jnp.sum(terms, 0, keepdims=True)
        result = dot(values_t[h * 64:(h + 1) * 64], terms.astype(jnp.bfloat16), NN)
        return result / total, peak, total

    values_t = v_ref[0].T
    for h in range(2):
        mine = seg_ref[...] == 0
        result, peak, total = attend(0, values_t, one_head(q_ref[...], h), h)
        acc_ref[h * 64:(h + 1) * 64] = jnp.where(mine, result, 0.0)
        stat_ref[0, h:h + 1] = jnp.where(mine, peak, 0.0)
        stat_ref[0, 2 + h:3 + h] = jnp.where(mine, total, 1.0)
    for clip in (1, 2):
        cols = pl.ds(pl.multiple_of(which[clip - 1] * 128, 128), 128)
        values_t = v_ref[clip].T
        mine = seg_ref[:, cols] == clip
        for h in range(2):
            result, peak, total = attend(clip, values_t, one_head(q_ref[cols], h), h)
            rows = slice(h * 64, (h + 1) * 64)
            acc_ref[rows, cols] = jnp.where(mine, result, acc_ref[rows, cols])
            stat_ref[0, h:h + 1, cols] = jnp.where(mine, peak, stat_ref[0, h:h + 1, cols])
            stat_ref[0, 2 + h:3 + h, cols] = jnp.where(mine, total, stat_ref[0, 2 + h:3 + h, cols])
    out_ref[...] = acc_ref[...].T


def cross_forward(which, q, kv, seg):
    toks, width = q.shape
    clips, frames = kv.shape[:2]
    pairs = width // 128
    kv_spec = pl.BlockSpec((clips, frames, 128), lambda j, w: (0, 0, j))
    v_spec = pl.BlockSpec((clips, frames, 128), lambda j, w: (0, 0, j + pairs))
    tok_spec = pl.BlockSpec((toks, 128), lambda j, w: (0, j))
    return pl.pallas_call(
        cross_forward_kernel,
        grid_spec=pltpu.PrefetchScalarGridSpec(
            num_scalar_prefetch=1,
            grid=(width // 128,),
            in_specs=[tok_spec, kv_spec, v_spec, pl.BlockSpec((1, toks), lambda j, w: (0, 0))],
            out_specs=[tok_spec, pl.BlockSpec((1, 4, toks), lambda j, w: (j, 0, 0))],
            scratch_shapes=[pltpu.VMEM((128, toks), jnp.float32)],
        ),
        out_shape=[
            jax.ShapeDtypeStruct((toks, width), jnp.float32),
            jax.ShapeDtypeStruct((width // 128, 4, toks), jnp.float32),
        ],
        compiler_params=pltpu.CompilerParams(vmem_limit_bytes=48 * 2**20),
        name="cross_forward",
    )(which, q, kv, kv, seg)


def cross_backward_kernel(which, q_ref, k_ref, v_ref, seg_ref, lse_ref, inner_ref, g_ref, dq_ref, dk_ref, dv_ref, acc_ref):
    def back(clip, keys_t, cols, h):
        query, grad = one_head(q_ref[cols], h), one_head(g_ref[cols], h)
        lse = jnp.where(seg_ref[:, cols] == clip, lse_ref[0, h:h + 1, cols], 1e30)
        weights = jnp.exp(dot(k_ref[clip], query, NT) - lse)
        grad_v = dot(weights.astype(jnp.bfloat16), grad, NN)
        grad_s = (weights * (dot(v_ref[clip], grad, NT) - inner_ref[0, h:h + 1, cols])).astype(jnp.bfloat16)
        grad_k = dot(grad_s, query, NN)
        return dot(keys_t[h * 64:(h + 1) * 64], grad_s, NN), grad_k, grad_v

    for clip in range(3):
        cols = slice(None) if clip == 0 else pl.ds(pl.multiple_of(which[clip - 1] * 128, 128), 128)
        keys_t = k_ref[clip].T
        grad_q, grad_k, grad_v = zip(*(back(clip, keys_t, cols, h) for h in range(2)))
        grad_q = jnp.concatenate(grad_q, 0)
        if clip == 0:
            acc_ref[...] = grad_q
        else:
            acc_ref[:, cols] += grad_q
        dk_ref[clip] = (grad_k[0] + grad_k[1]).astype(jnp.bfloat16)
        dv_ref[clip] = (grad_v[0] + grad_v[1]).astype(jnp.bfloat16)
    dq_ref[...] = (acc_ref[...] * 0.125).T


def cross_backward(which, q, kv, seg, lse, inner, grad):
    toks, width = q.shape
    clips, frames = kv.shape[:2]
    pairs = width // 128
    kv_spec = pl.BlockSpec((clips, frames, 128), lambda j, w: (0, 0, j))
    v_spec = pl.BlockSpec((clips, frames, 128), lambda j, w: (0, 0, j + pairs))
    tok_spec = pl.BlockSpec((toks, 128), lambda j, w: (0, j))
    row_spec = pl.BlockSpec((1, 2, toks), lambda j, w: (j, 0, 0))
    return pl.pallas_call(
        cross_backward_kernel,
        grid_spec=pltpu.PrefetchScalarGridSpec(
            num_scalar_prefetch=1,
            grid=(width // 128,),
            in_specs=[tok_spec, kv_spec, v_spec, pl.BlockSpec((1, toks), lambda j, w: (0, 0)), row_spec, row_spec, tok_spec],
            out_specs=[tok_spec, kv_spec, kv_spec],
            scratch_shapes=[pltpu.VMEM((128, toks), jnp.float32)],
        ),
        out_shape=[
            jax.ShapeDtypeStruct((toks, width), jnp.float32),
            jax.ShapeDtypeStruct((clips, frames, width), jnp.bfloat16),
            jax.ShapeDtypeStruct((clips, frames, width), jnp.bfloat16),
        ],
        compiler_params=pltpu.CompilerParams(vmem_limit_bytes=48 * 2**20),
        name="cross_backward",
    )(which, q, kv, kv, seg, lse, inner, grad)


Z = 4


class Place:
    def __init__(self):
        self.dp = lax.axis_index("dp")
        self.core = lax.axis_index("seq")
        self.z = self.dp // 4
        self.p = self.dp % 4
        x, y = self.p % 2, self.p // 2
        px, py = self.p + 1 - 2 * x, self.p + 2 - 4 * y
        self.p_first = px * (1 - self.core) + py * self.core
        self.p_second = py * (1 - self.core) + px * self.core
        self.p_diag = 3 - self.p
        base = self.z * 4
        self.first = (base + self.p_first, self.core)
        self.second = (base + self.p_second, self.core)
        self.up = (lax.rem(self.dp + 4, 16), self.core)
        self.down = (lax.rem(self.dp + 12, 16), self.core)
        self.mate = (self.dp, 1 - self.core)
        self.has_up = self.z < Z - 1
        self.has_down = self.z > 0

    def greet(self):
        barrier = pltpu.get_barrier_semaphore()
        for target in (self.mate, self.first, self.second):
            pl.semaphore_signal(barrier, inc=1, device_id=target, device_id_type=MESH)

        @pl.when(self.has_up)
        def _():
            pl.semaphore_signal(barrier, inc=1, device_id=self.up, device_id_type=MESH)

        @pl.when(self.has_down)
        def _():
            pl.semaphore_signal(barrier, inc=1, device_id=self.down, device_id_type=MESH)

        pl.semaphore_wait(barrier, 3 + (self.z + 3) // 4 + (6 - self.z) // 4)


def when(cond, fn):
    if cond is None:
        fn()
    else:
        pl.when(cond)(fn)


def both(a, b):
    if a is None:
        return b
    if b is None:
        return a
    return jnp.logical_and(a, b)


MATE_COLS = 1536


class Gather:
    def __init__(self, me, srcs, outs, send_sem, recv_sem, own_sem):
        self.me, self.srcs, self.outs = me, srcs, outs
        self.send_sem, self.recv_sem, self.own_sem = send_sem, recv_sem, own_sem
        self.sends = []
        self.tasks = []
        for m, (begin, step) in enumerate(GATHER_TIMES):
            for k, task in enumerate(self.steps(m)):
                self.tasks.append((begin + step * k, m, task))
        self.tasks.sort(key=lambda entry: entry[:2])

    def piece(self, m, chip, core):
        if m == 0:
            return self.outs[m].at[chip * 2 + core]
        if m == 4:
            return self.outs[m].at[pl.ds(pl.multiple_of(chip * 192 + core * 96, 96), 96)]
        rows = pl.ds(pl.multiple_of(chip * 48, 48), 48)
        return self.outs[m].at[rows, pl.ds(pl.multiple_of(core * MATE_COLS, MATE_COLS), MATE_COLS)]

    def sender(self, m, src, chip, target, cond):
        copy = pltpu.make_async_remote_copy(
            src_ref=src, dst_ref=self.piece(m, chip, self.me.core), send_sem=self.send_sem.at[len(self.sends)],
            recv_sem=self.recv_sem.at[m, chip * 2 + self.me.core], device_id=target, device_id_type=MESH)
        self.sends.append((cond, copy))
        return lambda: when(cond, copy.start)

    def arrival(self, m, chip, core, cond=None):
        piece = self.piece(m, chip, core)
        copy = pltpu.make_async_remote_copy(
            src_ref=piece, dst_ref=piece, send_sem=self.send_sem.at[0],
            recv_sem=self.recv_sem.at[m, chip * 2 + core], device_id=self.me.mate, device_id_type=MESH)
        return lambda: when(cond, copy.wait_recv)

    def forward(self, m, z, p, targets, cond=None):
        chip = z * 4 + p
        return [self.arrival(m, chip, self.me.core, cond)] + [
            self.sender(m, self.piece(m, chip, self.me.core), chip, target, both(cond, extra))
            for target, extra in targets
        ]

    def steps(self, m):
        me = self.me
        up, down, mate = (me.up, me.has_up), (me.down, me.has_down), (me.mate, None)
        first, second = (me.first, None), (me.second, None)

        def at(d, p, below_to, above_to):
            if d == 0:
                return self.forward(m, me.z, p, below_to)
            return self.forward(m, me.z - d, p, below_to, me.z - d >= 0) + self.forward(
                m, me.z + d, p, above_to, me.z + d < Z)

        begin = [self.sender(m, self.srcs[m], me.dp, *target) for target in (up, down, first, second, mate)]
        begin.append(pltpu.make_async_copy(self.srcs[m], self.piece(m, me.dp, me.core), self.own_sem.at[m]).start)
        steps = [begin]
        for d in range(1, Z + 1):
            line = at(d, me.p, [up, first, second, mate], [down, first, second, mate]) if d < Z else []
            steps.append(line + at(d - 1, me.p_first, [second, mate], [second, mate]))
        steps.append([act for p in (me.p_second, me.p_diag) for d in range(Z) for act in at(d, p, [mate], [mate])])
        return steps

    def run(self, entry):
        for act in entry[2]:
            act()

    def run_until(self, time):
        while self.tasks and self.tasks[0][0] <= time:
            self.run(self.tasks.pop(0))

    def take_until(self, time):
        taken = []
        while self.tasks and self.tasks[0][0] <= time:
            taken.append(self.tasks.pop(0))
        return taken

    def need(self, m):
        for entry in [e for e in self.tasks if e[1] == m]:
            self.run(entry)
        self.tasks = [e for e in self.tasks if e[1] != m]
        pltpu.make_async_copy(self.srcs[m], self.piece(m, self.me.dp, self.me.core), self.own_sem.at[m]).wait()
        for chip in range(16):
            self.arrival(m, chip, 1 - self.me.core)()

    def finish(self):
        for cond, copy in self.sends:
            when(cond, copy.wait_send)


GATHER_TIMES = ((3, 4), (2, 5), (14, 6), (34, 6), (52, 6))


def loop_with(gather, count, begin, length, body):
    due = [gather.take_until(begin + length * i) for i in range(count)]

    def turn(i, carry):
        for k, tasks in enumerate(due):
            if tasks:

                def run(tasks=tasks):
                    for task in tasks:
                        gather.run(task)

                pl.when(i == k)(run)
        body(i)
        return carry

    lax.fori_loop(0, count, turn, 0)


def norm_rows(values, gain, shift):
    average = jnp.mean(values, -1, keepdims=True)
    centred = values - average
    spread = jnp.mean(centred * centred, -1, keepdims=True)
    return centred * lax.rsqrt(spread + 1e-05) * gain + shift


def columns(j, size=128):
    return pl.ds(pl.multiple_of(j * size, size), size)


def forward_kernel(*refs):
    (group_ref, x_ref, frames_ref, bias_ref, seg_ref, small_in, self_in, cross_in, up_in, down_in) = refs[:10]
    (small_out, self_out, cross_out, up_out, down_out, kv_out, vec_ref, normed_one_ref, query_ref, kv_row_ref,
     attended_ref, self_lse_ref, after_self_ref, normed_two_ref, row_query_ref, cross_lse_ref, mixed_ref,
     after_cross_ref, normed_three_ref) = refs[10:29]
    (half_ref, pair_ref, small_vm, self_vm, cross_vm, kv_vm, acc_ref, stat_ref, part_ref, part_stat_ref, give_ref,
     give_stat_ref, take_ref, take_stat_ref, send_sem, recv_sem, own_sem, half_sems, mate_sems, load_sem) = refs[29:]
    me = Place()
    core = me.core
    width = x_ref.shape[1]
    toks = x_ref.shape[0]
    me.greet()

    def to_mate(src, dst, k):
        return pltpu.make_async_remote_copy(
            src_ref=src, dst_ref=dst, send_sem=mate_sems.at[0, k], recv_sem=mate_sems.at[1, k], device_id=me.mate,
            device_id_type=MESH)

    shards = (self_in, cross_in, up_in)
    halves = [
        pltpu.make_async_remote_copy(
            src_ref=shard.at[:, columns(1 - core, MATE_COLS)], dst_ref=half_ref.at[m], send_sem=half_sems.at[0, m],
            recv_sem=half_sems.at[1, m], device_id=me.mate, device_id_type=MESH)
        for m, shard in enumerate(shards)
    ]
    for copy in halves:
        copy.start()
    gather = Gather(me, (small_in, pair_ref.at[0], pair_ref.at[1], pair_ref.at[2], down_in),
                    (small_out, self_out, cross_out, up_out, down_out), send_sem, recv_sem, own_sem)
    for m, shard in enumerate(shards):
        halves[m].wait()
        own = shard[:, columns(core, MATE_COLS)].astype(jnp.float32)
        came = half_ref[m].astype(jnp.float32)
        is_first = core == 0
        pair_ref[m] = jnp.concatenate(
            [jnp.where(is_first, own, came), jnp.where(is_first, came, own)], 0).astype(jnp.bfloat16)
        if m == 0:
            gather.run_until(GATHER_TIMES[1][0])
    gather.run_until(GATHER_TIMES[1][0] + 3 * GATHER_TIMES[1][1])
    gather.need(0)
    copy = pltpu.make_async_copy(small_out, small_vm, load_sem.at[0])
    copy.start()
    copy.wait()
    row = lax.broadcasted_iota(jnp.int32, (128, width), 0)
    spot = lax.broadcasted_iota(jnp.int32, (128, width), 1) - row

    def place_small(d, total):
        chosen = jnp.where((spot == d * 24) & (row < 24), 1.0, 0.0).astype(jnp.bfloat16)
        return total + dot(small_vm[d], chosen, NN)

    vec_ref[...] = lax.fori_loop(0, 32, place_small, jnp.zeros(vec_ref.shape, jnp.float32))

    def vec(k):
        return vec_ref[k:k + 1]

    source = x_ref[...].astype(jnp.float32)
    normed_one_ref[...] = norm_rows(source, vec(0), vec(1)).astype(jnp.bfloat16)
    gather.run_until(GATHER_TIMES[1][0] + 5 * GATHER_TIMES[1][1])
    gather.need(1)
    copy = pltpu.make_async_copy(self_out, self_vm, load_sem.at[0])
    copy.start()
    copy.wait()

    normed = normed_one_ref[...]
    own_rows = slice(toks, 2 * toks)
    kv_row_ref[own_rows, :width] = dot(normed, self_vm[:, width:2 * width], NN).astype(jnp.bfloat16)
    kv_row_ref[own_rows, width:] = (dot(normed, self_vm[:, 2 * width:3 * width], NN) + vec(7)).astype(jnp.bfloat16)
    kv_copy = to_mate(kv_row_ref.at[own_rows], kv_row_ref.at[slice(0, toks)], 0)
    kv_copy.start()
    query = (dot(normed, self_vm[:, :width], NN) + vec(6)).astype(jnp.bfloat16)
    query_ref[...] = query * jnp.bfloat16(0.125)
    gather.run_until(33)
    kv_copy.wait()

    def self_pair(j):
        cols = columns(j)
        keys = kv_row_ref[:, cols]
        values_t = kv_row_ref[:, columns(j + 6)].T
        parts = []
        for h in range(2):
            scores = dot(keys, one_head(query_ref[:, cols], h), NT) + bias_ref[...]
            peak = jnp.max(scores, 0, keepdims=True)
            terms = jnp.exp(scores - peak)
            total = jnp.sum(terms, 0, keepdims=True)
            parts.append(dot(values_t[h * 64:(h + 1) * 64], terms.astype(jnp.bfloat16), NN) / total)
            self_lse_ref[j, h:h + 1] = peak + jnp.log(total)
        attended_ref[:, cols] = jnp.concatenate(parts, 0).T

    loop_with(gather, 6, 33, 1.2, self_pair)
    after_self = source + dot(attended_ref[...].astype(jnp.bfloat16), self_vm[:, 3 * width:], NN) + vec(8)
    after_self_ref[...] = after_self
    normed_two = norm_rows(after_self, vec(2), vec(3)).astype(jnp.bfloat16)
    normed_two_ref[...] = normed_two
    gather.run_until(44)
    gather.need(2)
    copy = pltpu.make_async_copy(cross_out, cross_vm, load_sem.at[0])
    copy.start()
    copy.wait()
    my_rows = pl.ds(pl.multiple_of(core * toks, toks), toks)
    cross_query = (dot(normed_two, cross_vm[:, :width], NN) + vec(9)).astype(jnp.bfloat16)
    row_query_ref[my_rows] = cross_query * jnp.bfloat16(0.125)
    query_copy = to_mate(row_query_ref.at[my_rows], row_query_ref.at[my_rows], 1)
    query_copy.start()

    clips = frames_ref.shape[0]
    tiles = 2 * width // 256

    def project(t):
        clip, tile = t // tiles, t % tiles
        result = dot(frames_ref[clip], cross_vm[:, columns(tile + 3, 256)], NN)
        is_value = (tile >= 3).astype(jnp.float32)
        shift = vec_ref[10:11, columns(tile % 3, 256)] * is_value
        kv_vm[clip, :, columns(tile, 256)] = (result + shift).astype(jnp.bfloat16)

    loop_with(gather, clips * tiles, 46, 0.7, project)
    kv_store = pltpu.make_async_copy(kv_vm, kv_out, load_sem.at[1])
    kv_store.start()
    query_copy.wait()

    def attend(clip, values_t, query, j, h):
        scores = dot(kv_vm[clip, :, columns(j)], query, NT)
        peak = jnp.max(scores, 0, keepdims=True)
        terms = jnp.exp(scores - peak)
        total = jnp.sum(terms, 0, keepdims=True)
        result = dot(values_t[h * 64:(h + 1) * 64], terms.astype(jnp.bfloat16), NN)
        return result / total, peak, total

    def cross_pair(j):
        values_t = kv_vm[0, :, columns(j + 6)].T
        mine = seg_ref[...] == 0
        for h in range(2):
            result, peak, total = attend(0, values_t, one_head(row_query_ref[:, columns(j)], h), j, h)
            acc_ref[h * 64:(h + 1) * 64] = jnp.where(mine, result, 0.0)
            stat_ref[h:h + 1] = jnp.where(mine, peak, 0.0)
            stat_ref[2 + h:3 + h] = jnp.where(mine, total, 1.0)
        for clip in (1, 2):
            values_t = kv_vm[clip, :, columns(j + 6)].T
            query_rows = jnp.where(
                group_ref[clip - 1:clip] == 0, row_query_ref[:128, columns(j)], row_query_ref[384:, columns(j)])
            for h in range(2):
                result, peak, total = attend(clip, values_t, one_head(query_rows, h), j, h)
                for spot in (0, 3):
                    cols = slice(spot * 128, (spot + 1) * 128)
                    mine = seg_ref[:, cols] == clip
                    rows = slice(h * 64, (h + 1) * 64)
                    acc_ref[rows, cols] = jnp.where(mine, result, acc_ref[rows, cols])
                    stat_ref[h:h + 1, cols] = jnp.where(mine, peak, stat_ref[h:h + 1, cols])
                    stat_ref[2 + h:3 + h, cols] = jnp.where(mine, total, stat_ref[2 + h:3 + h, cols])
        my_cols, mate_cols = columns(core, toks), columns(1 - core, toks)
        part_ref[j] = acc_ref[:, my_cols]
        part_stat_ref[j] = stat_ref[:, my_cols]
        give_ref[j] = acc_ref[:, mate_cols].astype(jnp.bfloat16)
        give_stat_ref[j] = stat_ref[:, mate_cols]

    loop_with(gather, 6, 60, 4, cross_pair)
    give_copy = to_mate(give_ref, take_ref, 2)
    give_copy.start()
    give_stat_copy = to_mate(give_stat_ref, take_stat_ref, 3)
    give_stat_copy.start()
    gather.run_until(1000)
    give_copy.wait()
    give_stat_copy.wait()

    def combine(j, carry):
        parts = []
        for h in range(2):
            rows = slice(h * 64, (h + 1) * 64)
            peak_a, peak_b = part_stat_ref[j, h:h + 1], take_stat_ref[j, h:h + 1]
            peak = jnp.maximum(peak_a, peak_b)
            share_a = part_stat_ref[j, 2 + h:3 + h] * jnp.exp(peak_a - peak)
            share_b = take_stat_ref[j, 2 + h:3 + h] * jnp.exp(peak_b - peak)
            total = share_a + share_b
            cross_lse_ref[j, h:h + 1] = peak + jnp.log(total)
            parts.append(part_ref[j, rows] * (share_a / total)
                         + take_ref[j, rows].astype(jnp.float32) * (share_b / total))
        mixed_ref[:, columns(j)] = jnp.concatenate(parts, 0).T
        return carry

    lax.fori_loop(0, 6, combine, 0)
    after_cross = after_self_ref[...] + dot(mixed_ref[...].astype(jnp.bfloat16), cross_vm[:, 3 * width:], NN) + vec(11)
    after_cross_ref[...] = after_cross
    normed_three_ref[...] = norm_rows(after_cross, vec(4), vec(5)).astype(jnp.bfloat16)
    gather.need(3)
    gather.need(4)
    kv_store.wait()
    gather.finish()


def fused_forward(group, x, frames, bias, seg, small, self_w, cross_w, up_w, down_w):
    toks, width = x.shape
    clips, count = frames.shape[:2]
    low, full = jnp.bfloat16, jnp.float32
    pairs = width // 128
    vmem, hbm = pl.BlockSpec(memory_space=pltpu.VMEM), pl.BlockSpec(memory_space=pl.ANY)
    shape = jax.ShapeDtypeStruct
    outs = [
        (hbm, shape((32, 16, 128), low)), (hbm, shape((width, 4 * width), low)), (hbm, shape((width, 4 * width), low)),
        (hbm, shape((width, 4 * width), low)), (hbm, shape((4 * width, width), low)),
        (hbm, shape((clips, count, 2 * width), low)),
        (vmem, shape((16, width), full)), (vmem, shape((toks, width), low)), (vmem, shape((toks, width), low)),
        (vmem, shape((2 * toks, 2 * width), low)), (vmem, shape((toks, width), full)),
        (vmem, shape((pairs, 2, toks), full)), (vmem, shape((toks, width), full)), (vmem, shape((toks, width), low)),
        (vmem, shape((2 * toks, width), low)), (vmem, shape((pairs, 2, toks), full)), (vmem, shape((toks, width), full)),
        (vmem, shape((toks, width), full)), (vmem, shape((toks, width), low)),
    ]
    return pl.pallas_call(
        forward_kernel,
        in_specs=[vmem] * 5 + [hbm] + [vmem] * 3 + [hbm],
        out_specs=tuple(spec for spec, _ in outs),
        out_shape=tuple(s for _, s in outs),
        scratch_shapes=[
            pltpu.VMEM((3, 24, MATE_COLS), low), pltpu.VMEM((3, 48, MATE_COLS), low), pltpu.VMEM((32, 16, 128), low),
            pltpu.VMEM((width, 4 * width), low), pltpu.VMEM((width, 4 * width), low),
            pltpu.VMEM((clips, count, 2 * width), low), pltpu.VMEM((128, 2 * toks), full), pltpu.VMEM((4, 2 * toks), full),
            pltpu.VMEM((pairs, 128, toks), full), pltpu.VMEM((pairs, 4, toks), full),
            pltpu.VMEM((pairs, 128, toks), low), pltpu.VMEM((pairs, 4, toks), full),
            pltpu.VMEM((pairs, 128, toks), low), pltpu.VMEM((pairs, 4, toks), full),
            pltpu.SemaphoreType.DMA((340,)), pltpu.SemaphoreType.DMA((5, 32)), pltpu.SemaphoreType.DMA((5,)),
            pltpu.SemaphoreType.DMA((2, 3)), pltpu.SemaphoreType.DMA((2, 4)), pltpu.SemaphoreType.DMA((2,)),
        ],
        compiler_params=pltpu.CompilerParams(collective_id=0, has_side_effects=True, vmem_limit_bytes=60 * 2**20),
        name="fused_forward",
    )(group, x, frames, bias, seg, small, self_w, cross_w, up_w, down_w)


class Scatter:
    def __init__(self, me, grads, outs, buffers, sems, times):
        self.me, self.grads, self.outs = me, grads, outs
        self.buffers = buffers
        self.send_sem, self.own_sem, self.pair_sem, self.plane_sem, self.line_sem = sems
        self.sends = []
        half = me.z // 2
        near = me.z + half * (3 - 2 * me.z)
        self.order = [base + half * (3 - 2 * base) for base in (3, 2, 1 - near, near)]
        self.tasks = []
        for m, (begin, ats) in enumerate(times):
            for at, acts in zip(ats, self.steps(m)):
                self.tasks.append((begin + at, m, acts))
        self.tasks.sort(key=lambda entry: entry[:2])

    def sender(self, src, dst, sem, target):
        copy = pltpu.make_async_remote_copy(
            src_ref=src, dst_ref=dst, send_sem=self.send_sem.at[len(self.sends)], recv_sem=sem, device_id=target,
            device_id_type=MESH)
        self.sends.append(copy)
        return copy.start

    def arrival(self, dst, sem):
        return pltpu.make_async_remote_copy(
            src_ref=dst, dst_ref=dst, send_sem=self.send_sem.at[0], recv_sem=sem, device_id=self.me.mate,
            device_id_type=MESH).wait_recv

    def steps(self, m):
        me, order = self.me, self.order
        grad, out = self.grads[m], self.outs[m]
        own, pair, plane_a, plane_b, plane_c, line = self.buffers[m]
        own_sem, pair_sem, plane_sem, line_sem = self.own_sem, self.pair_sem, self.plane_sem, self.line_sem

        def adder(dst, *others):
            def act():
                total = dst[...].astype(jnp.float32)
                for other in others:
                    total = total + other[...].astype(jnp.float32)
                dst[...] = total.astype(dst.dtype)
            return act

        loads = {}
        begin = []
        for k, p in enumerate((me.p_diag, me.p_second, me.p_first, me.p)):
            loads[k] = pltpu.make_async_copy(grad.at[:, p, me.core], own.at[:, p], own_sem.at[m, p])
            begin.append(loads[k].start)
        for p in (me.p_diag, me.p_first, me.p_second, me.p):
            begin.append(self.sender(grad.at[:, p, 1 - me.core], pair.at[:, p], pair_sem.at[m, p], me.mate))

        def paired(k, p):
            return [loads[k].wait, self.arrival(pair.at[:, p], pair_sem.at[m, p])]

        diag = paired(0, me.p_diag)
        second = paired(1, me.p_second)
        first = paired(2, me.p_first)
        for z in order:
            diag += [adder(own.at[z, me.p_diag], pair.at[z, me.p_diag]),
                     self.sender(own.at[z, me.p_diag], plane_a.at[z], plane_sem.at[m, 0, z], me.second)]
            second += [adder(own.at[z, me.p_second], pair.at[z, me.p_second]),
                       self.sender(own.at[z, me.p_second], plane_c.at[z], plane_sem.at[m, 2, z], me.second)]
            first += [self.arrival(plane_a.at[z], plane_sem.at[m, 0, z]),
                      adder(own.at[z, me.p_first], pair.at[z, me.p_first], plane_a.at[z]),
                      self.sender(own.at[z, me.p_first], plane_b.at[z], plane_sem.at[m, 1, z], me.first)]
        steps = [begin, diag, second, first]
        for k, z in enumerate(order):
            acts = paired(3, me.p) if k == 0 else []
            acts += [self.arrival(plane_b.at[z], plane_sem.at[m, 1, z]),
                     self.arrival(plane_c.at[z], plane_sem.at[m, 2, z])]
            if k < 3:
                acts.append(adder(own.at[z, me.p], pair.at[z, me.p], plane_b.at[z], plane_c.at[z]))
                upward = (z - me.z + 3) // 4
                source = me.z + 1 - 2 * upward
                came = jnp.logical_and(source >= 0, source < Z)
                slot = line.at[upward, z]
                arrival, add = self.arrival(slot, line_sem.at[m, upward, z]), adder(own.at[z, me.p], slot)

                def join(came=came, arrival=arrival, add=add):
                    def go():
                        arrival()
                        add()
                    pl.when(came)(go)

                target = (lax.rem(me.dp + 12 + 8 * upward, 16), me.core)
                acts += [join, self.sender(own.at[z, me.p], slot, line_sem.at[m, upward, z], target)]
            else:
                def total():
                    part = own[me.z, me.p].astype(jnp.float32) + pair[me.z, me.p].astype(jnp.float32)
                    out[...] = part + plane_b[me.z].astype(jnp.float32) + plane_c[me.z].astype(jnp.float32)

                acts.append(total)
                for upward, cond in ((0, me.has_up), (1, me.has_down)):
                    arrival = self.arrival(line.at[upward, me.z], line_sem.at[m, upward, me.z])

                    def last(upward=upward, cond=cond, arrival=arrival):
                        def go():
                            arrival()
                            out[...] += line[upward, me.z].astype(jnp.float32)
                        pl.when(cond)(go)

                    acts.append(last)
            steps.append(acts)
        return steps

    def run(self, entry):
        for act in entry[2]:
            act()

    def run_until(self, time):
        while self.tasks and self.tasks[0][0] <= time:
            self.run(self.tasks.pop(0))

    def take_until(self, time):
        taken = []
        while self.tasks and self.tasks[0][0] <= time:
            taken.append(self.tasks.pop(0))
        return taken

    def finish(self):
        self.run_until(10**6)
        for copy in self.sends:
            copy.wait_send()


def scatter_scratch(grads):
    shapes = []
    for g in grads:
        for lead in ((4, 4), (4, 4), (4,), (4,), (4,), (2, 4)):
            shapes.append(pltpu.VMEM(lead + g.shape[1:], g.dtype))
    count = len(grads)
    return shapes + [
        pltpu.SemaphoreType.DMA((20 * count,)),
        pltpu.SemaphoreType.DMA((count, 4)),
        pltpu.SemaphoreType.DMA((count, 4)),
        pltpu.SemaphoreType.DMA((count, 3, 4)),
        pltpu.SemaphoreType.DMA((count, 2, 4)),
    ]


def scatter_view(grad):
    return grad.reshape((4, 4, 2) + grad.shape[1:])


BACK_TIMES = ((0, (0, 4, 6, 12, 22, 27, 32, 38)), (1, (0, 14, 16, 22, 34, 39, 44, 50)))


def norm_rows_back(values, gain, grad):
    average = jnp.mean(values, -1, keepdims=True)
    centred = values - average
    scale = lax.rsqrt(jnp.mean(centred * centred, -1, keepdims=True) + 1e-05)
    normed = centred * scale
    inner = grad * gain
    mean_inner = jnp.mean(inner, -1, keepdims=True)
    mean_both = jnp.mean(inner * normed, -1, keepdims=True)
    result = scale * (inner - mean_inner - normed * mean_both)
    return result, jnp.sum(grad * normed, 0, keepdims=True), jnp.sum(grad, 0, keepdims=True)


def backward_kernel(*refs):
    (group_ref, x_ref, bias_ref, seg_ref, vec_ref, gac_ref, mixed_ref, cross_lse_ref, row_query_ref, after_self_ref,
     attended_ref, self_lse_ref, query_ref, kv_row_ref, cross_hbm, self_hbm, kv_hbm, up_hbm, down_hbm) = refs[:19]
    (input_grad_ref, cq_ref, self_low_ref, qkv_ref, vec_grad_ref, dkv_hbm, up_out, down_out) = refs[19:27]
    scratch = refs[27:]
    scatter_refs, scratch = scratch[:17], scratch[17:]
    (cross_vm, self_vm, kv_vm, row_grad_ref, row_stat_ref, acc_ref, own_ref, give_ref, take_ref,
     take_query_ref, load_sem, mate_sems) = scratch
    me = Place()
    core = me.core
    toks, width = x_ref.shape
    loads = [
        pltpu.make_async_copy(cross_hbm.at[:, pl.ds(0, width)], cross_vm.at[0], load_sem.at[0]),
        pltpu.make_async_copy(cross_hbm.at[:, pl.ds(3 * width, width)], cross_vm.at[1], load_sem.at[1]),
        pltpu.make_async_copy(kv_hbm, kv_vm, load_sem.at[2]),
        pltpu.make_async_copy(self_hbm, self_vm, load_sem.at[3]),
    ]
    for copy in (loads[1], loads[0], loads[2], loads[3]):
        copy.start()
    me.greet()
    scatter = Scatter(me, (up_hbm, down_hbm), (up_out, down_out), (scatter_refs[:6], scatter_refs[6:12]),
                      scatter_refs[12:], BACK_TIMES)
    scatter.run_until(1)

    def to_mate(src, dst, k):
        return pltpu.make_async_remote_copy(
            src_ref=src, dst_ref=dst, send_sem=mate_sems.at[0, k], recv_sem=mate_sems.at[1, k], device_id=me.mate,
            device_id_type=MESH)

    my_rows = pl.ds(pl.multiple_of(core * toks, toks), toks)
    my_cols = columns(core, toks)

    def head_rows(product, store):
        turned = product.T
        for h in range(2):
            store(h, jnp.sum(turned[h * 64:(h + 1) * 64], 0, keepdims=True))

    loads[1].wait()
    grad_mixed = dot(gac_ref[...].astype(jnp.bfloat16), cross_vm[1], NT).astype(jnp.bfloat16)
    row_grad_ref[my_rows] = grad_mixed
    grad_copy = to_mate(row_grad_ref.at[my_rows], row_grad_ref.at[my_rows], 0)
    grad_copy.start()
    for j in range(6):
        cols = slice(j * 128, (j + 1) * 128)
        product = grad_mixed[:, cols].astype(jnp.float32) * mixed_ref[:, cols]
        row_stat_ref[j, 0:2, my_cols] = cross_lse_ref[j]

        def keep(h, row, j=j):
            row_stat_ref[j, 2 + h:3 + h, my_cols] = row

        head_rows(product, keep)
    stat_copy = to_mate(row_stat_ref.at[:, :, my_cols], row_stat_ref.at[:, :, my_cols], 1)
    stat_copy.start()
    loads[2].wait()
    scatter.run_until(5)
    grad_copy.wait()
    stat_copy.wait()

    def cross_pair(j):
        def back(clip, keys_t, query, grad, lse, inner, h):
            weights = jnp.exp(dot(kv_vm[clip, :, columns(j)], query, NT) - lse)
            grad_v = dot(weights.astype(jnp.bfloat16), grad, NN)
            grad_s = (weights * (dot(kv_vm[clip, :, columns(j + 6)], grad, NT) - inner)).astype(jnp.bfloat16)
            return dot(keys_t[h * 64:(h + 1) * 64], grad_s, NN), dot(grad_s, query, NN), grad_v

        for clip in range(3):
            keys_t = kv_vm[clip, :, columns(j)].T
            grads = []
            for h in range(2):
                if clip == 0:
                    query, grad = row_query_ref[:, columns(j)], row_grad_ref[:, columns(j)]
                    mine = seg_ref[...] == 0
                    lse, inner = row_stat_ref[j, h:h + 1], row_stat_ref[j, 2 + h:3 + h]
                else:
                    low = group_ref[clip - 1:clip] == 0

                    def chosen(ref):
                        return jnp.where(low, ref[:128, columns(j)], ref[384:, columns(j)])

                    def chosen_row(row):
                        return jnp.where(low, row_stat_ref[j, row:row + 1, :128], row_stat_ref[j, row:row + 1, 384:])

                    query, grad = chosen(row_query_ref), chosen(row_grad_ref)
                    mine = jnp.where(low, seg_ref[:, :128], seg_ref[:, 384:]) == clip
                    lse, inner = chosen_row(h), chosen_row(2 + h)
                grads.append(back(clip, keys_t, one_head(query, h), one_head(grad, h), jnp.where(mine, lse, 1e30),
                                  inner, h))
            grad_q, grad_k, grad_v = zip(*grads)
            grad_q = jnp.concatenate(grad_q, 0)
            if clip == 0:
                acc_ref[...] = grad_q
            else:
                for spot in (0, 3):
                    cols = slice(spot * 128, (spot + 1) * 128)
                    acc_ref[:, cols] += jnp.where(low == (spot == 0), grad_q, 0.0)
            kv_vm[clip, :, columns(j)] = (grad_k[0] + grad_k[1]).astype(jnp.bfloat16)
            kv_vm[clip, :, columns(j + 6)] = (grad_v[0] + grad_v[1]).astype(jnp.bfloat16)
        own_ref[:, columns(j)] = (acc_ref[:, my_cols] * 0.125).T
        give_ref[:, columns(j)] = (acc_ref[:, columns(1 - core, toks)] * 0.125).T.astype(jnp.bfloat16)

    loop_with(scatter, 6, 6, 4.7, cross_pair)
    query_copy = to_mate(give_ref.at[:, pl.ds(0, width)], take_query_ref, 2)
    query_copy.start()
    dkv_store = pltpu.make_async_copy(kv_vm, dkv_hbm, load_sem.at[2])
    dkv_store.start()
    vec_grad_ref[...] = jnp.zeros_like(vec_grad_ref)
    cv_bias = sum(jnp.sum(kv_vm[clip, :, width:].astype(jnp.float32), 0, keepdims=True) for clip in range(3))
    vec_grad_ref[10:11] = cv_bias
    loads[0].wait()
    loads[3].wait()
    scatter.run_until(35)
    query_copy.wait()
    grad_query = (own_ref[:, :width] + take_query_ref[...].astype(jnp.float32)).astype(jnp.bfloat16)
    cq_ref[...] = grad_query
    vec_grad_ref[9:10] = jnp.sum(grad_query.astype(jnp.float32), 0, keepdims=True)
    grad_part, gain, shift = norm_rows_back(after_self_ref[...], vec_ref[2:3], dot(grad_query, cross_vm[0], NT))
    vec_grad_ref[2:3] = gain
    vec_grad_ref[3:4] = shift
    grad_after_self = gac_ref[...] + grad_part
    input_grad_ref[...] = grad_after_self
    grad_low = grad_after_self.astype(jnp.bfloat16)
    self_low_ref[...] = grad_low
    vec_grad_ref[8:9] = jnp.sum(grad_low.astype(jnp.float32), 0, keepdims=True)
    grad_attended = dot(grad_low, self_vm[:, 3 * width:], NT).astype(jnp.bfloat16)
    row_grad_ref[:toks] = grad_attended
    for j in range(6):
        cols = slice(j * 128, (j + 1) * 128)

        def keep_self(h, row, j=j):
            row_stat_ref[j, h:h + 1, :toks] = row

        head_rows(grad_attended[:, cols].astype(jnp.float32) * attended_ref[:, cols], keep_self)

    def self_pair(j):
        cols, value_cols = columns(j), columns(j + 6)
        keys, values = kv_row_ref[:, cols], kv_row_ref[:, value_cols]
        keys_t = keys.T
        grad_k = grad_v = None
        parts = []
        for h in range(2):
            query, grad = one_head(query_ref[:, cols], h), one_head(row_grad_ref[:toks, cols], h)
            weights = jnp.exp(dot(keys, query, NT) + bias_ref[...] - self_lse_ref[j, h:h + 1])
            part = dot(weights.astype(jnp.bfloat16), grad, NN)
            grad_v = part if grad_v is None else grad_v + part
            inner = row_stat_ref[j, h:h + 1, :toks]
            grad_s = (weights * (dot(values, grad, NT) - inner)).astype(jnp.bfloat16)
            part = dot(grad_s, query, NN)
            grad_k = part if grad_k is None else grad_k + part
            parts.append(dot(keys_t[h * 64:(h + 1) * 64], grad_s, NN))
        qkv_ref[:, cols] = (jnp.concatenate(parts, 0) * 0.125).T.astype(jnp.bfloat16)
        own_ref[:, cols] = grad_k[toks:]
        own_ref[:, value_cols] = grad_v[toks:]
        give_ref[:, cols] = grad_k[:toks].astype(jnp.bfloat16)
        give_ref[:, value_cols] = grad_v[:toks].astype(jnp.bfloat16)

    loop_with(scatter, 6, 42, 1.3, self_pair)
    row_copy = to_mate(give_ref, take_ref, 3)
    row_copy.start()
    scatter.run_until(51)
    row_copy.wait()
    qkv_ref[:, width:] = (own_ref[...] + take_ref[...].astype(jnp.float32)).astype(jnp.bfloat16)
    sums = jnp.sum(qkv_ref[...].astype(jnp.float32), 0, keepdims=True)
    vec_grad_ref[6:7] = sums[:, :width]
    vec_grad_ref[7:8] = sums[:, 2 * width:]
    grad_normed = dot(qkv_ref[...], self_vm[:, :3 * width], NT)
    grad_part, gain, shift = norm_rows_back(x_ref[...].astype(jnp.float32), vec_ref[0:1], grad_normed)
    vec_grad_ref[0:1] = gain
    vec_grad_ref[1:2] = shift
    input_grad_ref[...] += grad_part
    scatter.finish()
    dkv_store.wait()


def fused_backward(group, x, bias, seg, vec, gac, mixed, cross_lse, row_query, after_self, attended, self_lse, query,
                   kv_row, cross_full, self_full, kv, grad_up, grad_down):
    toks, width = x.shape
    low, full = jnp.bfloat16, jnp.float32
    pairs = width // 128
    vmem, hbm = pl.BlockSpec(memory_space=pltpu.VMEM), pl.BlockSpec(memory_space=pl.ANY)
    shape = jax.ShapeDtypeStruct
    outs = [
        (vmem, shape((toks, width), full)), (vmem, shape((toks, width), low)), (vmem, shape((toks, width), low)),
        (vmem, shape((toks, 3 * width), low)), (vmem, shape((16, width), full)), (hbm, shape(kv.shape, low)),
        (vmem, shape(grad_up.shape[1:], full)), (vmem, shape(grad_down.shape[1:], full)),
    ]
    return pl.pallas_call(
        backward_kernel,
        in_specs=[vmem] * 14 + [hbm] * 5,
        out_specs=tuple(spec for spec, _ in outs),
        out_shape=tuple(s for _, s in outs),
        scratch_shapes=scatter_scratch((grad_up, grad_down)) + [
            pltpu.VMEM((2, width, width), low), pltpu.VMEM((width, 4 * width), low), pltpu.VMEM(kv.shape, low),
            pltpu.VMEM((2 * toks, width), low), pltpu.VMEM((pairs, 4, 2 * toks), full),
            pltpu.VMEM((128, 2 * toks), full), pltpu.VMEM((toks, 2 * width), full), pltpu.VMEM((toks, 2 * width), low),
            pltpu.VMEM((toks, 2 * width), low), pltpu.VMEM((toks, width), low), pltpu.SemaphoreType.DMA((4,)), pltpu.SemaphoreType.DMA((2, 4)),
        ],
        compiler_params=pltpu.CompilerParams(collective_id=2, has_side_effects=True, vmem_limit_bytes=63 * 2**20),
        name="fused_backward",
    )(group, x, bias, seg, vec, gac, mixed, cross_lse, row_query, after_self, attended, self_lse, query, kv_row,
      cross_full, self_full, kv, scatter_view(grad_up), scatter_view(grad_down))


def scatter_kernel(count, *refs):
    grads, outs = refs[:count], refs[count:2 * count]
    scratch = refs[2 * count:]
    owns, pairs, plane_as, plane_bs, plane_cs, lines = (scratch[k * count:(k + 1) * count] for k in range(6))
    send_sem, own_sem, pair_sem, plane_sem, line_sem = scratch[6 * count:]
    me = Place()
    half = me.z // 2
    near = me.z + half * (3 - 2 * me.z)

    def far(k):
        base = (3, 2, 1 - near, near)[k]
        return base + half * (3 - 2 * base)

    order = [far(k) for k in range(4)]
    plane = [me.p_diag, me.p_first, me.p_second, me.p]
    mate_plane = [me.p_diag, me.p_second, me.p_first, me.p]
    for k in range(4):
        for m in range(count):
            pltpu.make_async_copy(grads[m].at[:, plane[k], me.core], owns[m].at[:, plane[k]], own_sem.at[m, plane[k]]).start()
    me.greet()
    sends = []

    def send(src, dst, sem, target, cond=None):
        slot = len(sends)
        copy = pltpu.make_async_remote_copy(src_ref=src, dst_ref=dst, send_sem=send_sem.at[slot], recv_sem=sem, device_id=target, device_id_type=MESH)
        sends.append((cond, copy))
        when(cond, copy.start)

    def arrive(dst, sem, cond=None):
        when(cond, pltpu.make_async_remote_copy(src_ref=dst, dst_ref=dst, send_sem=send_sem.at[0], recv_sem=sem, device_id=me.mate, device_id_type=MESH).wait_recv)

    for k in range(4):
        for m in range(count):
            p = mate_plane[k]
            send(grads[m].at[:, p, 1 - me.core], pairs[m].at[:, p], pair_sem.at[m, p], me.mate)

    def paired(m, p):
        pltpu.make_async_copy(grads[m].at[:, p, me.core], owns[m].at[:, p], own_sem.at[m, p]).wait()
        arrive(pairs[m].at[:, p], pair_sem.at[m, p])

    def add(dst, *others):
        total = dst[...].astype(jnp.float32)
        for other in others:
            total = total + other[...].astype(jnp.float32)
        dst[...] = total.astype(dst.dtype)

    def steps(m):
        own = owns[m]
        paired(m, me.p_diag)
        for k in range(4):
            z = order[k]
            add(own.at[z, me.p_diag], pairs[m].at[z, me.p_diag])
            send(own.at[z, me.p_diag], plane_as[m].at[z], plane_sem.at[m, 0, z], me.second)
        yield
        paired(m, me.p_second)
        for k in range(4):
            z = order[k]
            add(own.at[z, me.p_second], pairs[m].at[z, me.p_second])
            send(own.at[z, me.p_second], plane_cs[m].at[z], plane_sem.at[m, 2, z], me.second)
        yield
        paired(m, me.p_first)
        for k in range(4):
            z = order[k]
            arrive(plane_as[m].at[z], plane_sem.at[m, 0, z])
            add(own.at[z, me.p_first], pairs[m].at[z, me.p_first], plane_as[m].at[z])
            send(own.at[z, me.p_first], plane_bs[m].at[z], plane_sem.at[m, 1, z], me.first)
        yield
        paired(m, me.p)
        for k in range(4):
            z = order[k]
            arrive(plane_bs[m].at[z], plane_sem.at[m, 1, z])
            arrive(plane_cs[m].at[z], plane_sem.at[m, 2, z])
            if k == 3:
                break
            add(own.at[z, me.p], pairs[m].at[z, me.p], plane_bs[m].at[z], plane_cs[m].at[z])
            upward = (z - me.z + 3) // 4
            source = me.z + 1 - 2 * upward
            came = jnp.logical_and(source >= 0, source < Z)

            def gather_in(z=z, upward=upward):
                slot = lines[m].at[upward, z]
                arrive(slot, line_sem.at[m, upward, z])
                add(own.at[z, me.p], slot)

            pl.when(came)(gather_in)
            target = (lax.rem(me.dp + 12 + 8 * upward, 16), me.core)
            send(own.at[z, me.p], lines[m].at[upward, z], line_sem.at[m, upward, z], target)
        yield
        z = me.z
        total = own[z, me.p].astype(jnp.float32) + pairs[m][z, me.p].astype(jnp.float32)
        total = total + plane_bs[m][z].astype(jnp.float32) + plane_cs[m][z].astype(jnp.float32)
        outs[m][...] = total
        for upward, cond in ((0, me.has_up), (1, me.has_down)):

            def last(upward=upward):
                arrive(lines[m].at[upward, z], line_sem.at[m, upward, z])
                outs[m][...] += lines[m][upward, z].astype(jnp.float32)

            pl.when(cond)(last)

    running = [steps(m) for m in range(count)]
    while running:
        still = []
        for step in running:
            try:
                next(step)
                still.append(step)
            except StopIteration:
                pass
        running = still
    for cond, copy in sends:
        when(cond, copy.wait_send)


def scatter_all(grads):
    count = len(grads)
    shapes = [g.shape[1:] for g in grads]
    views = [g.reshape((4, 4, 2) + s) for g, s in zip(grads, shapes)]

    def vmem(*lead):
        return [pltpu.VMEM(lead + s, g.dtype) for g, s in zip(grads, shapes)]

    return pl.pallas_call(
        functools.partial(scatter_kernel, count),
        out_shape=tuple(jax.ShapeDtypeStruct(s, jnp.float32) for s in shapes),
        in_specs=[pl.BlockSpec(memory_space=pl.ANY)] * count,
        out_specs=tuple([pl.BlockSpec(memory_space=pltpu.VMEM)] * count),
        scratch_shapes=vmem(4, 4) + vmem(4, 4) + vmem(4) + vmem(4) + vmem(4) + vmem(2, 4) + [
            pltpu.SemaphoreType.DMA((20 * count,)),
            pltpu.SemaphoreType.DMA((count, 4)),
            pltpu.SemaphoreType.DMA((count, 4)),
            pltpu.SemaphoreType.DMA((count, 3, 4)),
            pltpu.SemaphoreType.DMA((count, 2, 4)),
        ],
        compiler_params=pltpu.CompilerParams(collective_id=1, has_side_effects=True, vmem_limit_bytes=60 * 2**20),
        name="scatter_all",
    )(*views)


def pack_rows(up_bias, down_bias, vectors, size):
    rows = jnp.concatenate([up_bias, down_bias, vectors], 1)
    return jnp.pad(rows, ((0, 0), (0, size - rows.shape[1])))


def scatter_grads(large, small):
    rows = pack_rows(*(part.reshape(32, -1) for part in small), 1024).reshape(32, 8, 128)
    whole = scatter_all(tuple(g.astype(jnp.bfloat16).reshape(32, -1, g.shape[1]) for g in large) + (rows,))
    row = whole[-1].reshape(-1)
    n_up, n_down, n_vec = (part.size // 32 for part in small)
    return tuple(whole[:-1]) + (
        row[:n_up],
        row[n_up : n_up + n_down],
        row[n_up + n_down : n_up + n_down + n_vec].reshape(-1, small[2].shape[1]),
    )


def from_behind(value, axis, steps):
    count = lax.axis_size(axis)
    leading, last = (max(0, -steps), min(count, count - steps))
    return lax.ppermute(value, axis, [(source, source + steps) for source in range(leading, last)])


def layer_norm(values, gain, shift):
    average = jnp.mean(values, -1, keepdims=True)
    centred = values - average
    spread = jnp.mean(centred * centred, -1, keepdims=True)
    return centred * lax.rsqrt(spread + 1e-05) * gain + shift


def exact_gelu(values):
    return jax.nn.gelu(values, approximate=False)


def matmul(left, right):
    return jnp.dot(left, right, preferred_element_type=jnp.float32)


def swap_halves(value):
    return lax.ppermute(value, "seq", [(0, 1), (1, 0)])


def seq_halves(value, axis):
    span = value.shape[axis] // 2
    half = lax.axis_index("seq")
    mine = lax.dynamic_slice_in_dim(value, half * span, span, axis)
    other = lax.dynamic_slice_in_dim(value, (1 - half) * span, span, axis)
    return mine, other


def seq_scatter(value):
    mine, other = seq_halves(value, 0)
    return mine + swap_halves(other.astype(jnp.bfloat16)).astype(value.dtype)


def per_head(values):
    rows = values.reshape(-1, values.shape[2]).T
    return jnp.repeat(rows, HEAD_DIM, axis=1)


def head_sums(values):
    sums = jnp.sum(values.reshape(values.shape[0], -1, HEAD_DIM), -1)
    return sums.T.reshape(-1, 2, values.shape[0])


def plain_forward(
    which, layer_input, frames, mask_bias, row_segment, weights
):
    self_full, cross_full, up_full, down_full, bias_full, out_bias_full, vectors = (
        lax.all_gather(part, ("dp", "seq"), axis=0, tiled=True) for part in weights
    )
    vec = jnp.pad(
        jnp.concatenate([vectors.T, out_bias_full[None]]).astype(jnp.float32), ((0, 3), (0, 0))
    )
    model_width = layer_input.shape[1]
    cross_in = [cross_full[:, k * model_width : (k + 1) * model_width] for k in range(4)]
    source = layer_input.astype(jnp.float32)
    normed_one = layer_norm(source, vec[0], vec[1]).astype(jnp.bfloat16)
    proj_bias = jnp.concatenate([vec[6], jnp.zeros_like(vec[6]), vec[7]])
    qkv_low = (matmul(normed_one, self_full[:, : 3 * model_width]) + proj_bias).astype(jnp.bfloat16)
    query = qkv_low[:, :model_width] * jnp.bfloat16(0.125)
    kv_own = qkv_low[:, model_width:]
    kv_row = jnp.concatenate([from_behind(kv_own, "seq", 1), kv_own])
    attended, self_lse = self_forward(query, kv_row, mask_bias)
    attended_low = attended.astype(jnp.bfloat16)
    after_self = source + matmul(attended_low, self_full[:, 3 * model_width :]) + vec[8]
    normed_two = layer_norm(after_self, vec[2], vec[3]).astype(jnp.bfloat16)
    cross_query = (matmul(normed_two, cross_in[0]) + vec[9]).astype(jnp.bfloat16)
    cross_key = jnp.einsum(
        "cfd,de->cfe", frames, cross_in[1], preferred_element_type=jnp.float32
    ).astype(jnp.bfloat16)
    cross_value = (
        jnp.einsum("cfd,de->cfe", frames, cross_in[2], preferred_element_type=jnp.float32)
        + vec[10]
    ).astype(jnp.bfloat16)
    row_query = lax.all_gather(cross_query * jnp.bfloat16(0.125), "seq", axis=0, tiled=True)
    cross_kv = jnp.concatenate([cross_key, cross_value], 2)
    part_mixed, part_stats = cross_forward(which, row_query, cross_kv, row_segment)
    mixed_mine, mixed_other = seq_halves(part_mixed, 0)
    stats_mine, stats_other = seq_halves(part_stats, 2)
    mixed_came = swap_halves(mixed_other.astype(jnp.bfloat16))
    stats_came = swap_halves(stats_other)
    peak = jnp.maximum(stats_mine[:, :2], stats_came[:, :2])
    share_mine = stats_mine[:, 2:] * jnp.exp(stats_mine[:, :2] - peak)
    share_came = stats_came[:, 2:] * jnp.exp(stats_came[:, :2] - peak)
    total = share_mine + share_came
    cross_lse = peak + jnp.log(total)
    mixed_full = mixed_mine * per_head(share_mine / total) + mixed_came.astype(
        jnp.float32
    ) * per_head(share_came / total)
    mixed = mixed_full.astype(jnp.bfloat16)
    after_cross = after_self + matmul(mixed, cross_in[3]) + vec[11]
    normed_three = layer_norm(after_cross, vec[4], vec[5]).astype(jnp.bfloat16)
    return (
        bias_full, self_full, cross_full, up_full, down_full, cross_kv, vec, normed_one, query, kv_row, attended,
        self_lse, after_self, normed_two, row_query, cross_lse, mixed_full, after_cross, normed_three,
    )


def forward(which, layer_input, frames, mask_bias, row_segment, weights):
    if lax.axis_size("dp") != 16:
        return plain_forward(which, layer_input, frames, mask_bias, row_segment, weights)
    self_weights, cross_weights, up_weights, down_weights, up_bias, down_bias, vectors = weights

    def as_row(values):
        return jnp.pad(values, ((0, 0), (0, 128 - values.shape[1])))

    small = jnp.concatenate(
        [as_row(vectors.T), as_row(down_bias[None]), as_row(up_bias[None]), jnp.zeros((2, 128), vectors.dtype)]
    )
    group = jnp.broadcast_to(which[:, None], (2, 128))
    whole = fused_forward(
        group, layer_input, frames, mask_bias, row_segment, small, self_weights, cross_weights, up_weights,
        down_weights,
    )
    return (whole[0][:, 13, : up_bias.shape[0]].reshape(-1),) + tuple(whole[1:])


def plain_backward(
    which, layer_input, mask_bias, row_segment, vec, grad_after_cross, mixed_full, cross_lse, row_query, after_self,
    attended, self_lse, query, kv_row, cross_full, self_full, cross_kv
):
    tok_span, model_width = layer_input.shape
    source = layer_input.astype(jnp.float32)
    cross_in = [cross_full[:, k * model_width : (k + 1) * model_width] for k in range(4)]
    grad_cross_low = grad_after_cross.astype(jnp.bfloat16)
    grad_mixed = matmul(grad_cross_low, cross_in[3].T).astype(jnp.bfloat16)
    row_grad = lax.all_gather(grad_mixed, "seq", axis=0, tiled=True)
    cross_inner = head_sums(grad_mixed.astype(jnp.float32) * mixed_full)
    row_stats = lax.all_gather(jnp.stack([cross_lse, cross_inner]), "seq", axis=3, tiled=True)
    part_query, grad_key, grad_value = cross_backward(
        which, row_query, cross_kv, row_segment, row_stats[0], row_stats[1], row_grad
    )
    grad_query_sum = seq_scatter(part_query).astype(jnp.bfloat16)
    grad_cq_bias = jnp.sum(grad_query_sum, 0, dtype=jnp.float32)
    grad_normed_two = matmul(grad_query_sum, cross_in[0].T)
    grad_cv_bias = jnp.sum(grad_value, (0, 1), dtype=jnp.float32)
    _, norm_pull_two = jax.vjp(layer_norm, after_self, vec[2], vec[3])
    grad_part, grad_gain_two, grad_shift_two = norm_pull_two(grad_normed_two)
    grad_after_self = grad_after_cross + grad_part
    grad_self_low = grad_after_self.astype(jnp.bfloat16)
    grad_self_bias = jnp.sum(grad_self_low, 0, dtype=jnp.float32)
    grad_attended = matmul(grad_self_low, self_full[:, 3 * model_width :].T).astype(jnp.bfloat16)
    self_inner = head_sums(grad_attended.astype(jnp.float32) * attended)
    grad_query, grad_key_row, grad_value_row = self_backward(
        query, kv_row, mask_bias, self_lse, self_inner, grad_attended
    )
    grad_kv = jnp.concatenate([grad_key_row, grad_value_row], 1)
    back_kv = from_behind(grad_kv[:tok_span].astype(jnp.bfloat16), "seq", -1)
    grad_qkv_low = jnp.concatenate(
        [grad_query, grad_kv[tok_span:] + back_kv.astype(jnp.float32)], 1
    ).astype(jnp.bfloat16)
    grad_qkv_bias = jnp.sum(grad_qkv_low, 0, dtype=jnp.float32)
    grad_normed_one = matmul(grad_qkv_low, self_full[:, : 3 * model_width].T)
    _, norm_pull_one = jax.vjp(layer_norm, source, vec[0], vec[1])
    grad_part, grad_gain_one, grad_shift_one = norm_pull_one(grad_normed_one)
    input_grad = grad_after_self + grad_part
    nothing = jnp.zeros_like(grad_cq_bias)
    vec_grads = jnp.stack(
        [
            grad_gain_one,
            grad_shift_one,
            grad_gain_two,
            grad_shift_two,
            nothing,
            nothing,
            grad_qkv_bias[:model_width],
            grad_qkv_bias[2 * model_width :],
            grad_self_bias,
            grad_cq_bias,
            grad_cv_bias,
        ]
        + [nothing] * 5
    )
    return (
        input_grad, grad_query_sum, grad_self_low, grad_qkv_low, vec_grads,
        jnp.concatenate([grad_key, grad_value], 2),
    )


def per_device(
    layer_input,
    encoder_states,
    clip_lengths,
    out_grad,
    self_weights,
    cross_weights,
    up_weights,
    down_weights,
    up_bias,
    down_bias,
    vectors,
):
    model_width = layer_input.shape[2]
    tok_span = layer_input.shape[1]
    seq_half = lax.axis_index("seq")
    source = layer_input[0].astype(jnp.float32)
    position = seq_half * tok_span + jnp.arange(tok_span, dtype=jnp.int32)
    clip_ends = jnp.cumsum(clip_lengths[0])
    segment = jnp.sum((position[:, None] >= clip_ends[None, :]).astype(jnp.int32), 1)
    key_position = jnp.concatenate([position - tok_span, position])
    key_segment = jnp.sum((key_position[:, None] >= clip_ends[None, :]).astype(jnp.int32), 1)
    allowed = (
        (key_segment[:, None] == segment[None, :])
        & (key_position[:, None] <= position[None, :])
        & (key_position[:, None] >= 0)
    )
    mask_bias = jnp.where(allowed, 0.0, -1e30).astype(jnp.float32)
    row_position = jnp.arange(2 * tok_span, dtype=jnp.int32)
    row_segment = jnp.sum((row_position[:, None] >= clip_ends[None, :]).astype(jnp.int32), 1)[None]
    big = jnp.argmax(clip_lengths[0]).astype(jnp.int32)
    small_one = jnp.where(big == 0, 1, 0)
    small_two = jnp.where(big == 2, 1, 2)
    last_group = 2 * tok_span // 128 - 1
    order = jnp.stack([big, small_one, small_two]).astype(jnp.int32)
    row_segment = jnp.where(
        row_segment == order[0], 0, jnp.where(row_segment == order[1], 1, jnp.where(row_segment == order[2], 2, 3))
    )
    place_of = jnp.stack([jnp.sum(jnp.where(order == clip, jnp.arange(CLIPS), 0)) for clip in range(CLIPS)])
    which = jnp.where(order[1:] < big, 0, last_group).astype(jnp.int32)

    frames = jnp.take(encoder_states[0], order, axis=0, mode="clip")
    (
        bias_full, self_full, cross_full, up_full, down_full, cross_kv, vec, normed_one, query, kv_row, attended,
        self_lse, after_self, normed_two, row_query, cross_lse, mixed_full, after_cross, normed_three,
    ) = forward(
        which, layer_input[0], frames, mask_bias, row_segment,
        (self_weights, cross_weights, up_weights, down_weights, up_bias, down_bias, vectors),
    )
    bias_full = bias_full.astype(jnp.float32)
    out_bias_full = vec[12]
    attended_low = attended.astype(jnp.bfloat16)
    mixed = mixed_full.astype(jnp.bfloat16)
    pre_act = matmul(normed_three, up_full) + bias_full
    activated_low = exact_gelu(pre_act).astype(jnp.bfloat16)
    result_rows = after_cross + matmul(activated_low, down_full) + out_bias_full
    layer_output = result_rows.astype(jnp.bfloat16)[None]

    grad_low = out_grad[0]
    grad_rows = grad_low.astype(jnp.float32)
    grad_down = matmul(activated_low.T, grad_low)
    grad_out_bias = jnp.sum(grad_rows, 0)
    grad_act = matmul(grad_low, down_full.T).astype(jnp.bfloat16)
    _, gelu_pull = jax.vjp(exact_gelu, pre_act)
    grad_pre = gelu_pull(grad_act.astype(jnp.float32))[0].astype(jnp.bfloat16)
    grad_up = matmul(normed_three.T, grad_pre)
    grad_up_bias = jnp.sum(grad_pre, 0, dtype=jnp.float32)
    grad_normed_three = matmul(grad_pre, up_full.T)
    _, norm_pull_three = jax.vjp(layer_norm, after_cross, vec[4], vec[5])
    grad_part, grad_gain_three, grad_shift_three = norm_pull_three(grad_normed_three)
    grad_after_cross = grad_rows + grad_part
    grad_cross_low = grad_after_cross.astype(jnp.bfloat16)
    grad_cross_out = matmul(mixed.T, grad_cross_low)
    grad_cross_bias = jnp.sum(grad_cross_low, 0, dtype=jnp.float32)
    operands = (
        layer_input[0], mask_bias, row_segment, vec, grad_after_cross, mixed_full, cross_lse, row_query, after_self,
        attended, self_lse, query, kv_row, cross_full, self_full, cross_kv,
    )
    fused = lax.axis_size("dp") == 16
    if fused:
        group = jnp.broadcast_to(which[:, None], (2, 128))
        large = [g.astype(jnp.bfloat16).reshape(32, -1, g.shape[1]) for g in (grad_up, grad_down)]
        *results, up_share, down_share = fused_backward(group, *operands, *large)
    else:
        results = plain_backward(which, *operands)
    input_grad, grad_query_sum, grad_self_low, grad_qkv_low, vec_grads, cross_kv_grad = results
    grad_cq_weight = matmul(normed_two.T, grad_query_sum)
    grad_self_out = matmul(attended_low.T, grad_self_low)
    grad_qkv_weight = matmul(normed_one.T, grad_qkv_low)
    grad_ckv_weight = jnp.einsum(
        "cfd,cfe->de", frames, cross_kv_grad, preferred_element_type=jnp.float32
    )
    encoder_grad = jnp.einsum(
        "cfe,de->cfd",
        jnp.take(cross_kv_grad, place_of, axis=0, mode="clip"),
        cross_full[:, model_width : 3 * model_width],
        preferred_element_type=jnp.float32,
    )[None]
    grads_self = jnp.concatenate([grad_qkv_weight, grad_self_out], 1)
    grads_cross = jnp.concatenate([grad_cq_weight, grad_ckv_weight, grad_cross_out], 1)
    vector_grads = jnp.concatenate(
        [vec_grads[:4], grad_gain_three[None], grad_shift_three[None], vec_grads[6:11], grad_cross_bias[None]]
    ).T
    small_grads = (grad_up_bias, grad_out_bias, vector_grads)
    if fused:
        shares = scatter_grads((grads_self, grads_cross), small_grads)
        shares = shares[:2] + (up_share, down_share) + shares[2:]
    else:
        shares = tuple(
            lax.psum_scatter(part, ("dp", "seq"), scatter_dimension=0, tiled=True)
            for part in (grads_self, grads_cross, grad_up, grad_down) + small_grads
        )
    return (layer_output, input_grad[None], encoder_grad) + shares


def solution(mesh):
    return jax.shard_map(
        per_device,
        mesh=mesh,
        in_specs=(
            P("dp", "seq", None),
            P("dp", None, "seq", None),
            P("dp", None),
            P("dp", "seq", None),
            P(("dp", "seq"), None),
            P(("dp", "seq"), None),
            P(("dp", "seq"), None),
            P(("dp", "seq"), None),
            P(("dp", "seq")),
            P(("dp", "seq")),
            P(("dp", "seq"), None),
        ),
        out_specs=(
            P("dp", "seq", None),
            P("dp", "seq", None),
            P("dp", None, "seq", None),
            P(("dp", "seq"), None),
            P(("dp", "seq"), None),
            P(("dp", "seq"), None),
            P(("dp", "seq"), None),
            P(("dp", "seq")),
            P(("dp", "seq")),
            P(("dp", "seq"), None),
        ),
        check_vma=False,
    )
```

```python
import functools

import jax
import jax.numpy as jnp
from jax import lax
from jax.experimental import pallas as pl
from jax.experimental.pallas import tpu as pltpu
from jax.sharding import PartitionSpec as P

HEAD_DIM = 64
CLIPS = 3
MESH = pl.DeviceIdType.MESH
NT = (((1,), (1,)), ((), ()))
NN = (((1,), (0,)), ((), ()))


def dot(left, right, dims):
    return lax.dot_general(left, right, dims, preferred_element_type=jnp.float32)


def one_head(values, h):
    lane = lax.broadcasted_iota(jnp.int32, values.shape, 1)
    return jnp.where((lane >= 64) == (h == 1), values, jnp.zeros_like(values))


def self_forward_kernel(q_ref, k_ref, v_ref, bias_ref, out_ref, lse_ref):
    keys = k_ref[...]
    values_t = v_ref[...].T
    halves = []
    for h in range(2):
        scores = dot(keys, one_head(q_ref[...], h), NT) + bias_ref[...]
        peak = jnp.max(scores, 0, keepdims=True)
        terms = jnp.exp(scores - peak)
        total = jnp.sum(terms, 0, keepdims=True)
        result = dot(values_t[h * 64:(h + 1) * 64], terms.astype(jnp.bfloat16), NN)
        halves.append(result / total)
        lse_ref[0, h:h + 1] = peak + jnp.log(total)
    out_ref[...] = jnp.concatenate(halves, 0).T.astype(out_ref.dtype)


def self_forward(q, kv, bias):
    toks, width = q.shape
    keys, pairs = kv.shape[0], width // 128
    return pl.pallas_call(
        self_forward_kernel,
        grid=(width // 128,),
        in_specs=[
            pl.BlockSpec((toks, 128), lambda j: (0, j)),
            pl.BlockSpec((keys, 128), lambda j: (0, j)),
            pl.BlockSpec((keys, 128), lambda j: (0, j + pairs)),
            pl.BlockSpec((keys, toks), lambda j: (0, 0)),
        ],
        out_specs=[
            pl.BlockSpec((toks, 128), lambda j: (0, j)),
            pl.BlockSpec((1, 2, toks), lambda j: (j, 0, 0)),
        ],
        out_shape=[
            jax.ShapeDtypeStruct((toks, width), jnp.float32),
            jax.ShapeDtypeStruct((width // 128, 2, toks), jnp.float32),
        ],
        compiler_params=pltpu.CompilerParams(vmem_limit_bytes=48 * 2**20),
        name="self_forward",
    )(q, kv, kv, bias)


def self_backward_kernel(q_ref, k_ref, v_ref, bias_ref, lse_ref, inner_ref, g_ref, dq_ref, dk_ref, dv_ref):
    keys, values = k_ref[...], v_ref[...]
    keys_t = keys.T
    grad_k = grad_v = None
    halves = []
    for h in range(2):
        query, grad = one_head(q_ref[...], h), one_head(g_ref[...], h)
        weights = jnp.exp(dot(keys, query, NT) + bias_ref[...] - lse_ref[0, h:h + 1])
        part = dot(weights.astype(jnp.bfloat16), grad, NN)
        grad_v = part if grad_v is None else grad_v + part
        grad_s = (weights * (dot(values, grad, NT) - inner_ref[0, h:h + 1])).astype(jnp.bfloat16)
        part = dot(grad_s, query, NN)
        grad_k = part if grad_k is None else grad_k + part
        halves.append(dot(keys_t[h * 64:(h + 1) * 64], grad_s, NN))
    dq_ref[...] = (jnp.concatenate(halves, 0) * 0.125).T
    dk_ref[...] = grad_k
    dv_ref[...] = grad_v


def self_backward(q, kv, bias, lse, inner, grad):
    toks, width = q.shape
    keys, pairs = kv.shape[0], width // 128
    tok_spec = pl.BlockSpec((toks, 128), lambda j: (0, j))
    key_spec = pl.BlockSpec((keys, 128), lambda j: (0, j))
    row_spec = pl.BlockSpec((1, 2, toks), lambda j: (j, 0, 0))
    return pl.pallas_call(
        self_backward_kernel,
        grid=(width // 128,),
        in_specs=[tok_spec, key_spec, pl.BlockSpec((keys, 128), lambda j: (0, j + pairs)), pl.BlockSpec((keys, toks), lambda j: (0, 0)), row_spec, row_spec, tok_spec],
        out_specs=[tok_spec, key_spec, key_spec],
        out_shape=[
            jax.ShapeDtypeStruct((toks, width), jnp.float32),
            jax.ShapeDtypeStruct((keys, width), jnp.float32),
            jax.ShapeDtypeStruct((keys, width), jnp.float32),
        ],
        compiler_params=pltpu.CompilerParams(vmem_limit_bytes=48 * 2**20),
        name="self_backward",
    )(q, kv, kv, bias, lse, inner, grad)


def cross_forward_kernel(which, q_ref, k_ref, v_ref, seg_ref, out_ref, stat_ref, acc_ref):
    def attend(clip, values_t, query, h):
        scores = dot(k_ref[clip], query, NT)
        peak = jnp.max(scores, 0, keepdims=True)
        terms = jnp.exp(scores - peak)
        total = jnp.sum(terms, 0, keepdims=True)
        result = dot(values_t[h * 64:(h + 1) * 64], terms.astype(jnp.bfloat16), NN)
        return result / total, peak, total

    values_t = v_ref[0].T
    for h in range(2):
        mine = seg_ref[...] == 0
        result, peak, total = attend(0, values_t, one_head(q_ref[...], h), h)
        acc_ref[h * 64:(h + 1) * 64] = jnp.where(mine, result, 0.0)
        stat_ref[0, h:h + 1] = jnp.where(mine, peak, 0.0)
        stat_ref[0, 2 + h:3 + h] = jnp.where(mine, total, 1.0)
    for clip in (1, 2):
        cols = pl.ds(pl.multiple_of(which[clip - 1] * 128, 128), 128)
        values_t = v_ref[clip].T
        mine = seg_ref[:, cols] == clip
        for h in range(2):
            result, peak, total = attend(clip, values_t, one_head(q_ref[cols], h), h)
            rows = slice(h * 64, (h + 1) * 64)
            acc_ref[rows, cols] = jnp.where(mine, result, acc_ref[rows, cols])
            stat_ref[0, h:h + 1, cols] = jnp.where(mine, peak, stat_ref[0, h:h + 1, cols])
            stat_ref[0, 2 + h:3 + h, cols] = jnp.where(mine, total, stat_ref[0, 2 + h:3 + h, cols])
    out_ref[...] = acc_ref[...].T


def cross_forward(which, q, kv, seg):
    toks, width = q.shape
    clips, frames = kv.shape[:2]
    pairs = width // 128
    kv_spec = pl.BlockSpec((clips, frames, 128), lambda j, w: (0, 0, j))
    v_spec = pl.BlockSpec((clips, frames, 128), lambda j, w: (0, 0, j + pairs))
    tok_spec = pl.BlockSpec((toks, 128), lambda j, w: (0, j))
    return pl.pallas_call(
        cross_forward_kernel,
        grid_spec=pltpu.PrefetchScalarGridSpec(
            num_scalar_prefetch=1,
            grid=(width // 128,),
            in_specs=[tok_spec, kv_spec, v_spec, pl.BlockSpec((1, toks), lambda j, w: (0, 0))],
            out_specs=[tok_spec, pl.BlockSpec((1, 4, toks), lambda j, w: (j, 0, 0))],
            scratch_shapes=[pltpu.VMEM((128, toks), jnp.float32)],
        ),
        out_shape=[
            jax.ShapeDtypeStruct((toks, width), jnp.float32),
            jax.ShapeDtypeStruct((width // 128, 4, toks), jnp.float32),
        ],
        compiler_params=pltpu.CompilerParams(vmem_limit_bytes=48 * 2**20),
        name="cross_forward",
    )(which, q, kv, kv, seg)


def cross_backward_kernel(which, q_ref, k_ref, v_ref, seg_ref, lse_ref, inner_ref, g_ref, dq_ref, dk_ref, dv_ref, acc_ref):
    def back(clip, keys_t, cols, h):
        query, grad = one_head(q_ref[cols], h), one_head(g_ref[cols], h)
        lse = jnp.where(seg_ref[:, cols] == clip, lse_ref[0, h:h + 1, cols], 1e30)
        weights = jnp.exp(dot(k_ref[clip], query, NT) - lse)
        grad_v = dot(weights.astype(jnp.bfloat16), grad, NN)
        grad_s = (weights * (dot(v_ref[clip], grad, NT) - inner_ref[0, h:h + 1, cols])).astype(jnp.bfloat16)
        grad_k = dot(grad_s, query, NN)
        return dot(keys_t[h * 64:(h + 1) * 64], grad_s, NN), grad_k, grad_v

    for clip in range(3):
        cols = slice(None) if clip == 0 else pl.ds(pl.multiple_of(which[clip - 1] * 128, 128), 128)
        keys_t = k_ref[clip].T
        grad_q, grad_k, grad_v = zip(*(back(clip, keys_t, cols, h) for h in range(2)))
        grad_q = jnp.concatenate(grad_q, 0)
        if clip == 0:
            acc_ref[...] = grad_q
        else:
            acc_ref[:, cols] += grad_q
        dk_ref[clip] = (grad_k[0] + grad_k[1]).astype(jnp.bfloat16)
        dv_ref[clip] = (grad_v[0] + grad_v[1]).astype(jnp.bfloat16)
    dq_ref[...] = (acc_ref[...] * 0.125).T


def cross_backward(which, q, kv, seg, lse, inner, grad):
    toks, width = q.shape
    clips, frames = kv.shape[:2]
    pairs = width // 128
    kv_spec = pl.BlockSpec((clips, frames, 128), lambda j, w: (0, 0, j))
    v_spec = pl.BlockSpec((clips, frames, 128), lambda j, w: (0, 0, j + pairs))
    tok_spec = pl.BlockSpec((toks, 128), lambda j, w: (0, j))
    row_spec = pl.BlockSpec((1, 2, toks), lambda j, w: (j, 0, 0))
    return pl.pallas_call(
        cross_backward_kernel,
        grid_spec=pltpu.PrefetchScalarGridSpec(
            num_scalar_prefetch=1,
            grid=(width // 128,),
            in_specs=[tok_spec, kv_spec, v_spec, pl.BlockSpec((1, toks), lambda j, w: (0, 0)), row_spec, row_spec, tok_spec],
            out_specs=[tok_spec, kv_spec, kv_spec],
            scratch_shapes=[pltpu.VMEM((128, toks), jnp.float32)],
        ),
        out_shape=[
            jax.ShapeDtypeStruct((toks, width), jnp.float32),
            jax.ShapeDtypeStruct((clips, frames, width), jnp.bfloat16),
            jax.ShapeDtypeStruct((clips, frames, width), jnp.bfloat16),
        ],
        compiler_params=pltpu.CompilerParams(vmem_limit_bytes=48 * 2**20),
        name="cross_backward",
    )(which, q, kv, kv, seg, lse, inner, grad)


Z = 4


class Place:
    def __init__(self):
        self.dp = lax.axis_index("dp")
        self.core = lax.axis_index("seq")
        self.z = self.dp // 4
        self.p = self.dp % 4
        x, y = self.p % 2, self.p // 2
        px, py = self.p + 1 - 2 * x, self.p + 2 - 4 * y
        self.p_first = px * (1 - self.core) + py * self.core
        self.p_second = py * (1 - self.core) + px * self.core
        self.p_diag = 3 - self.p
        base = self.z * 4
        self.first = (base + self.p_first, self.core)
        self.second = (base + self.p_second, self.core)
        self.up = (lax.rem(self.dp + 4, 16), self.core)
        self.down = (lax.rem(self.dp + 12, 16), self.core)
        self.mate = (self.dp, 1 - self.core)
        self.has_up = self.z < Z - 1
        self.has_down = self.z > 0

    def greet(self):
        barrier = pltpu.get_barrier_semaphore()
        for target in (self.mate, self.first, self.second):
            pl.semaphore_signal(barrier, inc=1, device_id=target, device_id_type=MESH)

        @pl.when(self.has_up)
        def _():
            pl.semaphore_signal(barrier, inc=1, device_id=self.up, device_id_type=MESH)

        @pl.when(self.has_down)
        def _():
            pl.semaphore_signal(barrier, inc=1, device_id=self.down, device_id_type=MESH)

        pl.semaphore_wait(barrier, 3 + (self.z + 3) // 4 + (6 - self.z) // 4)


def when(cond, fn):
    if cond is None:
        fn()
    else:
        pl.when(cond)(fn)


def both(a, b):
    if a is None:
        return b
    if b is None:
        return a
    return jnp.logical_and(a, b)


HALF_COLS = {1: 768, 2: 1536, 3: 768, 4: 1536}


class Gather:
    def __init__(self, me, srcs, outs, send_sem, recv_sem, own_sem):
        self.me, self.srcs, self.outs = me, srcs, outs
        self.send_sem, self.recv_sem, self.own_sem = send_sem, recv_sem, own_sem
        self.sends = []
        self.tasks = []
        for m, times in enumerate(GATHER_TIMES):
            for time, task in zip(times, self.steps(m)):
                self.tasks.append((time, m, task))
        self.tasks.sort(key=lambda entry: entry[:2])

    def piece(self, m, chip, core):
        if m == 0:
            return self.outs[m].at[chip * 2 + core]
        if m == 5:
            return self.outs[m].at[pl.ds(pl.multiple_of(chip * 192 + core * 96, 96), 96)]
        rows = pl.ds(pl.multiple_of(chip * 48, 48), 48)
        return self.outs[m].at[rows, columns(core, HALF_COLS[m])]

    def sender(self, m, src, chip, target, cond):
        copy = pltpu.make_async_remote_copy(
            src_ref=src, dst_ref=self.piece(m, chip, self.me.core), send_sem=self.send_sem.at[len(self.sends)],
            recv_sem=self.recv_sem.at[m, chip * 2 + self.me.core], device_id=target, device_id_type=MESH)
        self.sends.append((cond, copy))
        return lambda: when(cond, copy.start)

    def arrival(self, m, chip, core, cond=None):
        piece = self.piece(m, chip, core)
        copy = pltpu.make_async_remote_copy(
            src_ref=piece, dst_ref=piece, send_sem=self.send_sem.at[0],
            recv_sem=self.recv_sem.at[m, chip * 2 + core], device_id=self.me.mate, device_id_type=MESH)
        return lambda: when(cond, copy.wait_recv)

    def forward(self, m, z, p, targets, cond=None):
        chip = z * 4 + p
        return [self.arrival(m, chip, self.me.core, cond)] + [
            self.sender(m, self.piece(m, chip, self.me.core), chip, target, both(cond, extra))
            for target, extra in targets
        ]

    def steps(self, m):
        me = self.me
        up, down, mate = (me.up, me.has_up), (me.down, me.has_down), (me.mate, None)
        first, second = (me.first, None), (me.second, None)

        def at(d, p, below_to, above_to):
            if d == 0:
                return self.forward(m, me.z, p, below_to)
            return self.forward(m, me.z - d, p, below_to, me.z - d >= 0) + self.forward(
                m, me.z + d, p, above_to, me.z + d < Z)

        begin = [self.sender(m, self.srcs[m], me.dp, *target) for target in (up, down, first, second, mate)]
        begin.append(pltpu.make_async_copy(self.srcs[m], self.piece(m, me.dp, me.core), self.own_sem.at[m]).start)
        steps = [begin]
        for d in range(1, Z + 1):
            line = at(d, me.p, [up, first, second, mate], [down, first, second, mate]) if d < Z else []
            steps.append(line + at(d - 1, me.p_first, [second, mate], [second, mate]))
        steps.append([act for p in (me.p_second, me.p_diag) for d in range(Z) for act in at(d, p, [mate], [mate])])
        return steps

    def run(self, entry):
        for act in entry[2]:
            act()

    def run_until(self, time):
        while self.tasks and self.tasks[0][0] <= time:
            self.run(self.tasks.pop(0))

    def take_until(self, time):
        taken = []
        while self.tasks and self.tasks[0][0] <= time:
            taken.append(self.tasks.pop(0))
        return taken

    def need(self, m):
        for entry in [e for e in self.tasks if e[1] == m]:
            self.run(entry)
        self.tasks = [e for e in self.tasks if e[1] != m]
        pltpu.make_async_copy(self.srcs[m], self.piece(m, self.me.dp, self.me.core), self.own_sem.at[m]).wait()
        for chip in range(16):
            self.arrival(m, chip, 1 - self.me.core)()

    def finish(self):
        for cond, copy in self.sends:
            when(cond, copy.wait_send)


GATHER_TIMES = (
    (1, 4.5, 8.5, 12.5, 16.5, 18.5),
    (0, 4, 8, 12, 16, 18),
    (2, 9, 14, 19, 24, 27),
    (10, 20, 25, 29, 33, 36),
    (20, 31, 38, 45, 51, 55),
    (32, 50, 58, 66, 73, 78),
)


def loop_with(gather, count, begin, length, body):
    due = [gather.take_until(begin + length * i) for i in range(count)]

    def turn(i, carry):
        for k, tasks in enumerate(due):
            if tasks:

                def run(tasks=tasks):
                    for task in tasks:
                        gather.run(task)

                pl.when(i == k)(run)
        body(i)
        return carry

    lax.fori_loop(0, count, turn, 0)


def norm_rows(values, gain, shift):
    average = jnp.mean(values, -1, keepdims=True)
    centred = values - average
    spread = jnp.mean(centred * centred, -1, keepdims=True)
    return centred * lax.rsqrt(spread + 1e-05) * gain + shift


def columns(j, size=128):
    return pl.ds(pl.multiple_of(j * size, size), size)


def forward_kernel(*refs):
    (group_ref, x_ref, frames_ref, bias_ref, seg_ref, small_in, self_in, cross_in, up_in, down_in) = refs[:10]
    (small_out, ckv_out, self_out, cqo_out, up_out, down_out, kv_out, vec_ref, normed_one_ref, query_ref, kv_row_ref,
     attended_ref, self_lse_ref, after_self_ref, normed_two_ref, row_query_ref, cross_lse_ref, mixed_ref,
     after_cross_ref, normed_three_ref) = refs[10:30]
    (half_wide, half_narrow, pair_wide, pair_narrow, small_vm, ckv_vm, self_vm, cqo_vm, kv_vm, acc_ref, stat_ref, part_ref, part_stat_ref, give_ref,
     give_stat_ref, take_ref, take_stat_ref, send_sem, recv_sem, own_sem, half_sems, mate_sems, load_sem) = refs[30:]
    me = Place()
    core = me.core
    width = x_ref.shape[1]
    toks = x_ref.shape[0]
    me.greet()

    def to_mate(src, dst, k):
        return pltpu.make_async_remote_copy(
            src_ref=src, dst_ref=dst, send_sem=mate_sems.at[0, k], recv_sem=mate_sems.at[1, k], device_id=me.mate,
            device_id_type=MESH)

    def half_of(m, which):
        shard = (None, cross_in, self_in, cross_in, up_in)[m]
        size = HALF_COLS[m]
        begin = (0, width, 0, 0, 0)[m] + which * (0, width, size, 3 * width, size)[m]
        return shard.at[:, pl.ds(pl.multiple_of(begin, size), size)]

    buffers = {1: (half_narrow.at[0], pair_narrow.at[0]), 2: (half_wide.at[0], pair_wide.at[0]),
               3: (half_narrow.at[1], pair_narrow.at[1]), 4: (half_wide.at[1], pair_wide.at[1])}
    halves = {
        m: pltpu.make_async_remote_copy(
            src_ref=half_of(m, 1 - core), dst_ref=buffers[m][0], send_sem=half_sems.at[0, m],
            recv_sem=half_sems.at[1, m], device_id=me.mate, device_id_type=MESH)
        for m in buffers
    }
    for copy in halves.values():
        copy.start()
    sources = (small_in,) + tuple(buffers[m][1] for m in buffers) + (down_in,)
    gather = Gather(me, sources, (small_out, ckv_out, self_out, cqo_out, up_out, down_out), send_sem, recv_sem, own_sem)
    for m, (came_ref, both_ref) in buffers.items():
        halves[m].wait()
        own = half_of(m, core)[...].astype(jnp.float32)
        came = came_ref[...].astype(jnp.float32)
        both_ref[...] = jnp.concatenate(
            [jnp.where(core == 0, own, came), jnp.where(core == 0, came, own)], 0).astype(jnp.bfloat16)
        gather.run_until((0, 1, 2, 2, 4.5)[m])

    def fetch(src, dst, k):
        copy = pltpu.make_async_copy(src, dst, load_sem.at[k])
        copy.start()
        copy.wait()

    gather.run_until(18.5)
    gather.need(0)
    fetch(small_out, small_vm, 0)
    row = lax.broadcasted_iota(jnp.int32, (128, width), 0)
    spot = lax.broadcasted_iota(jnp.int32, (128, width), 1) - row

    def place_small(d, total):
        chosen = jnp.where((spot == d * 24) & (row < 24), 1.0, 0.0).astype(jnp.bfloat16)
        return total + dot(small_vm[d], chosen, NN)

    vec_ref[...] = lax.fori_loop(0, 32, place_small, jnp.zeros(vec_ref.shape, jnp.float32))

    def vec(k):
        return vec_ref[k:k + 1]

    source = x_ref[...].astype(jnp.float32)
    normed_one_ref[...] = norm_rows(source, vec(0), vec(1)).astype(jnp.bfloat16)
    gather.need(1)
    fetch(ckv_out, ckv_vm, 0)
    clips = frames_ref.shape[0]
    tiles = 2 * width // 256

    def project(t):
        clip, tile = t // tiles, t % tiles
        result = dot(frames_ref[clip], ckv_vm[:, columns(tile, 256)], NN)
        is_value = (tile >= 3).astype(jnp.float32)
        shift = vec_ref[10:11, columns(tile % 3, 256)] * is_value
        kv_vm[clip, :, columns(tile, 256)] = (result + shift).astype(jnp.bfloat16)

    loop_with(gather, clips * tiles, 20, 0.65, project)
    kv_store = pltpu.make_async_copy(kv_vm, kv_out, load_sem.at[1])
    kv_store.start()
    gather.run_until(31)
    gather.need(2)
    fetch(self_out, self_vm, 0)

    normed = normed_one_ref[...]
    own_rows = slice(toks, 2 * toks)
    kv_row_ref[own_rows, :width] = dot(normed, self_vm[:, width:2 * width], NN).astype(jnp.bfloat16)
    kv_row_ref[own_rows, width:] = (dot(normed, self_vm[:, 2 * width:3 * width], NN) + vec(7)).astype(jnp.bfloat16)
    kv_copy = to_mate(kv_row_ref.at[own_rows], kv_row_ref.at[slice(0, toks)], 0)
    kv_copy.start()
    query = (dot(normed, self_vm[:, :width], NN) + vec(6)).astype(jnp.bfloat16)
    query_ref[...] = query * jnp.bfloat16(0.125)
    gather.run_until(35)
    kv_copy.wait()

    def self_pair(j):
        cols = columns(j)
        keys = kv_row_ref[:, cols]
        values_t = kv_row_ref[:, columns(j + 6)].T
        parts = []
        for h in range(2):
            scores = dot(keys, one_head(query_ref[:, cols], h), NT) + bias_ref[...]
            peak = jnp.max(scores, 0, keepdims=True)
            terms = jnp.exp(scores - peak)
            total = jnp.sum(terms, 0, keepdims=True)
            parts.append(dot(values_t[h * 64:(h + 1) * 64], terms.astype(jnp.bfloat16), NN) / total)
            self_lse_ref[j, h:h + 1] = peak + jnp.log(total)
        attended_ref[:, cols] = jnp.concatenate(parts, 0).T

    loop_with(gather, 6, 35, 1.2, self_pair)
    after_self = source + dot(attended_ref[...].astype(jnp.bfloat16), self_vm[:, 3 * width:], NN) + vec(8)
    after_self_ref[...] = after_self
    normed_two = norm_rows(after_self, vec(2), vec(3)).astype(jnp.bfloat16)
    normed_two_ref[...] = normed_two
    gather.run_until(44)
    gather.need(3)
    fetch(cqo_out, cqo_vm, 0)
    my_rows = pl.ds(pl.multiple_of(core * toks, toks), toks)
    cross_query = (dot(normed_two, cqo_vm[:, :width], NN) + vec(9)).astype(jnp.bfloat16)
    row_query_ref[my_rows] = cross_query * jnp.bfloat16(0.125)
    query_copy = to_mate(row_query_ref.at[my_rows], row_query_ref.at[my_rows], 1)
    query_copy.start()
    gather.run_until(48)
    query_copy.wait()

    def attend(clip, values_t, query, j, h):
        scores = dot(kv_vm[clip, :, columns(j)], query, NT)
        peak = jnp.max(scores, 0, keepdims=True)
        terms = jnp.exp(scores - peak)
        total = jnp.sum(terms, 0, keepdims=True)
        result = dot(values_t[h * 64:(h + 1) * 64], terms.astype(jnp.bfloat16), NN)
        return result / total, peak, total

    def cross_pair(j):
        values_t = kv_vm[0, :, columns(j + 6)].T
        mine = seg_ref[...] == 0
        for h in range(2):
            result, peak, total = attend(0, values_t, one_head(row_query_ref[:, columns(j)], h), j, h)
            acc_ref[h * 64:(h + 1) * 64] = jnp.where(mine, result, 0.0)
            stat_ref[h:h + 1] = jnp.where(mine, peak, 0.0)
            stat_ref[2 + h:3 + h] = jnp.where(mine, total, 1.0)
        for clip in (1, 2):
            values_t = kv_vm[clip, :, columns(j + 6)].T
            query_rows = jnp.where(
                group_ref[clip - 1:clip] == 0, row_query_ref[:128, columns(j)], row_query_ref[384:, columns(j)])
            for h in range(2):
                result, peak, total = attend(clip, values_t, one_head(query_rows, h), j, h)
                for spot in (0, 3):
                    cols = slice(spot * 128, (spot + 1) * 128)
                    mine = seg_ref[:, cols] == clip
                    rows = slice(h * 64, (h + 1) * 64)
                    acc_ref[rows, cols] = jnp.where(mine, result, acc_ref[rows, cols])
                    stat_ref[h:h + 1, cols] = jnp.where(mine, peak, stat_ref[h:h + 1, cols])
                    stat_ref[2 + h:3 + h, cols] = jnp.where(mine, total, stat_ref[2 + h:3 + h, cols])
        my_cols, mate_cols = columns(core, toks), columns(1 - core, toks)
        part_ref[j] = acc_ref[:, my_cols]
        part_stat_ref[j] = stat_ref[:, my_cols]
        give_ref[j] = acc_ref[:, mate_cols].astype(jnp.bfloat16)
        give_stat_ref[j] = stat_ref[:, mate_cols]

    loop_with(gather, 6, 48, 3.8, cross_pair)
    give_copy = to_mate(give_ref, take_ref, 2)
    give_copy.start()
    give_stat_copy = to_mate(give_stat_ref, take_stat_ref, 3)
    give_stat_copy.start()
    gather.run_until(1000)
    give_copy.wait()
    give_stat_copy.wait()

    def combine(j, carry):
        parts = []
        for h in range(2):
            rows = slice(h * 64, (h + 1) * 64)
            peak_a, peak_b = part_stat_ref[j, h:h + 1], take_stat_ref[j, h:h + 1]
            peak = jnp.maximum(peak_a, peak_b)
            share_a = part_stat_ref[j, 2 + h:3 + h] * jnp.exp(peak_a - peak)
            share_b = take_stat_ref[j, 2 + h:3 + h] * jnp.exp(peak_b - peak)
            total = share_a + share_b
            cross_lse_ref[j, h:h + 1] = peak + jnp.log(total)
            parts.append(part_ref[j, rows] * (share_a / total)
                         + take_ref[j, rows].astype(jnp.float32) * (share_b / total))
        mixed_ref[:, columns(j)] = jnp.concatenate(parts, 0).T
        return carry

    lax.fori_loop(0, 6, combine, 0)
    after_cross = after_self_ref[...] + dot(mixed_ref[...].astype(jnp.bfloat16), cqo_vm[:, width:], NN) + vec(11)
    after_cross_ref[...] = after_cross
    normed_three_ref[...] = norm_rows(after_cross, vec(4), vec(5)).astype(jnp.bfloat16)
    gather.need(4)
    gather.need(5)
    kv_store.wait()
    gather.finish()


def fused_forward(group, x, frames, bias, seg, small, self_w, cross_w, up_w, down_w):
    toks, width = x.shape
    clips, count = frames.shape[:2]
    low, full = jnp.bfloat16, jnp.float32
    pairs = width // 128
    vmem, hbm = pl.BlockSpec(memory_space=pltpu.VMEM), pl.BlockSpec(memory_space=pl.ANY)
    shape = jax.ShapeDtypeStruct
    outs = [
        (hbm, shape((32, 16, 128), low)), (hbm, shape((width, 2 * width), low)), (hbm, shape((width, 4 * width), low)),
        (hbm, shape((width, 2 * width), low)), (hbm, shape((width, 4 * width), low)),
        (hbm, shape((4 * width, width), low)),
        (hbm, shape((clips, count, 2 * width), low)),
        (vmem, shape((16, width), full)), (vmem, shape((toks, width), low)), (vmem, shape((toks, width), low)),
        (vmem, shape((2 * toks, 2 * width), low)), (vmem, shape((toks, width), full)),
        (vmem, shape((pairs, 2, toks), full)), (vmem, shape((toks, width), full)), (vmem, shape((toks, width), low)),
        (vmem, shape((2 * toks, width), low)), (vmem, shape((pairs, 2, toks), full)), (vmem, shape((toks, width), full)),
        (vmem, shape((toks, width), full)), (vmem, shape((toks, width), low)),
    ]
    return pl.pallas_call(
        forward_kernel,
        in_specs=[vmem] * 5 + [hbm] + [vmem] * 3 + [hbm],
        out_specs=tuple(spec for spec, _ in outs),
        out_shape=tuple(s for _, s in outs),
        scratch_shapes=[
            pltpu.VMEM((2, 24, 2 * width), low), pltpu.VMEM((2, 24, width), low), pltpu.VMEM((2, 48, 2 * width), low),
            pltpu.VMEM((2, 48, width), low), pltpu.VMEM((32, 16, 128), low),
            pltpu.VMEM((width, 2 * width), low), pltpu.VMEM((width, 4 * width), low), pltpu.VMEM((width, 2 * width), low),
            pltpu.VMEM((clips, count, 2 * width), low), pltpu.VMEM((128, 2 * toks), full), pltpu.VMEM((4, 2 * toks), full),
            pltpu.VMEM((pairs, 128, toks), full), pltpu.VMEM((pairs, 4, toks), full),
            pltpu.VMEM((pairs, 128, toks), low), pltpu.VMEM((pairs, 4, toks), full),
            pltpu.VMEM((pairs, 128, toks), low), pltpu.VMEM((pairs, 4, toks), full),
            pltpu.SemaphoreType.DMA((400,)), pltpu.SemaphoreType.DMA((6, 32)), pltpu.SemaphoreType.DMA((6,)),
            pltpu.SemaphoreType.DMA((2, 5)), pltpu.SemaphoreType.DMA((2, 4)), pltpu.SemaphoreType.DMA((2,)),
        ],
        compiler_params=pltpu.CompilerParams(collective_id=0, has_side_effects=True, vmem_limit_bytes=60 * 2**20),
        name="fused_forward",
    )(group, x, frames, bias, seg, small, self_w, cross_w, up_w, down_w)


class Scatter:
    def __init__(self, me, grads, outs, buffers, sems, times):
        self.me, self.grads, self.outs = me, grads, outs
        self.buffers = buffers
        self.send_sem, self.own_sem, self.pair_sem, self.plane_sem, self.line_sem = sems
        self.sends = []
        half = me.z // 2
        near = me.z + half * (3 - 2 * me.z)
        self.order = [base + half * (3 - 2 * base) for base in (3, 2, 1 - near, near)]
        self.tasks = []
        for m, (begin, ats) in enumerate(times):
            for at, acts in zip(ats, self.steps(m)):
                self.tasks.append((begin + at, m, acts))
        self.tasks.sort(key=lambda entry: entry[:2])

    def sender(self, src, dst, sem, target):
        copy = pltpu.make_async_remote_copy(
            src_ref=src, dst_ref=dst, send_sem=self.send_sem.at[len(self.sends)], recv_sem=sem, device_id=target,
            device_id_type=MESH)
        self.sends.append(copy)
        return copy.start

    def arrival(self, dst, sem):
        return pltpu.make_async_remote_copy(
            src_ref=dst, dst_ref=dst, send_sem=self.send_sem.at[0], recv_sem=sem, device_id=self.me.mate,
            device_id_type=MESH).wait_recv

    def steps(self, m):
        me, order = self.me, self.order
        grad, out = self.grads[m], self.outs[m]
        own, pair, plane_a, plane_b, plane_c, line = self.buffers[m]

        def own_at(z, p):
            return grad.at[z, p, me.core] if own is None else own.at[z, p]

        own_sem, pair_sem, plane_sem, line_sem = self.own_sem, self.pair_sem, self.plane_sem, self.line_sem

        def adder(dst, *others):
            def act():
                total = dst[...].astype(jnp.float32)
                for other in others:
                    total = total + other[...].astype(jnp.float32)
                dst[...] = total.astype(dst.dtype)
            return act

        loads = {}
        begin = []
        for k, p in enumerate((me.p_diag, me.p_second, me.p_first, me.p)):
            if own is not None:
                loads[k] = pltpu.make_async_copy(grad.at[:, p, me.core], own.at[:, p], own_sem.at[m, p])
                begin.append(loads[k].start)
        for p in (me.p_diag, me.p_first, me.p_second, me.p):
            begin.append(self.sender(grad.at[:, p, 1 - me.core], pair.at[:, p], pair_sem.at[m, p], me.mate))

        def paired(k, p):
            return ([loads[k].wait] if loads else []) + [self.arrival(pair.at[:, p], pair_sem.at[m, p])]

        diag = paired(0, me.p_diag)
        second = paired(1, me.p_second)
        first = paired(2, me.p_first)
        for z in order:
            diag += [adder(own_at(z, me.p_diag), pair.at[z, me.p_diag]),
                     self.sender(own_at(z, me.p_diag), plane_a.at[z], plane_sem.at[m, 0, z], me.second)]
            second += [adder(own_at(z, me.p_second), pair.at[z, me.p_second]),
                       self.sender(own_at(z, me.p_second), plane_c.at[z], plane_sem.at[m, 2, z], me.second)]
            first += [self.arrival(plane_a.at[z], plane_sem.at[m, 0, z]),
                      adder(own_at(z, me.p_first), pair.at[z, me.p_first], plane_a.at[z]),
                      self.sender(own_at(z, me.p_first), plane_b.at[z], plane_sem.at[m, 1, z], me.first)]
        steps = [begin, diag, second, first]
        for k, z in enumerate(order):
            acts = paired(3, me.p) if k == 0 else []
            acts += [self.arrival(plane_b.at[z], plane_sem.at[m, 1, z]),
                     self.arrival(plane_c.at[z], plane_sem.at[m, 2, z])]
            if k < 3:
                acts.append(adder(own_at(z, me.p), pair.at[z, me.p], plane_b.at[z], plane_c.at[z]))
                upward = (z - me.z + 3) // 4
                source = me.z + 1 - 2 * upward
                came = jnp.logical_and(source >= 0, source < Z)
                slot = line.at[upward, z]
                arrival, add = self.arrival(slot, line_sem.at[m, upward, z]), adder(own_at(z, me.p), slot)

                def join(came=came, arrival=arrival, add=add):
                    def go():
                        arrival()
                        add()
                    pl.when(came)(go)

                target = (lax.rem(me.dp + 12 + 8 * upward, 16), me.core)
                acts += [join, self.sender(own_at(z, me.p), slot, line_sem.at[m, upward, z], target)]
            else:
                def total():
                    part = own_at(me.z, me.p)[...].astype(jnp.float32) + pair[me.z, me.p].astype(jnp.float32)
                    out[...] = part + plane_b[me.z].astype(jnp.float32) + plane_c[me.z].astype(jnp.float32)

                acts.append(total)
                for upward, cond in ((0, me.has_up), (1, me.has_down)):
                    arrival = self.arrival(line.at[upward, me.z], line_sem.at[m, upward, me.z])

                    def last(upward=upward, cond=cond, arrival=arrival):
                        def go():
                            arrival()
                            out[...] += line[upward, me.z].astype(jnp.float32)
                        pl.when(cond)(go)

                    acts.append(last)
            steps.append(acts)
        return steps

    def run(self, entry):
        for act in entry[2]:
            act()

    def run_until(self, time):
        while self.tasks and self.tasks[0][0] <= time:
            self.run(self.tasks.pop(0))

    def take_until(self, time):
        taken = []
        while self.tasks and self.tasks[0][0] <= time:
            taken.append(self.tasks.pop(0))
        return taken

    def finish(self):
        self.run_until(10**6)
        for copy in self.sends:
            copy.wait_send()


def scatter_scratch(grads):
    shapes = []
    for g in grads:
        for lead in ((4, 4), (4, 4), (4,), (4,), (4,), (2, 4)):
            shapes.append(pltpu.VMEM(lead + g.shape[1:], g.dtype))
    count = len(grads)
    return shapes + [
        pltpu.SemaphoreType.DMA((20 * count,)),
        pltpu.SemaphoreType.DMA((count, 4)),
        pltpu.SemaphoreType.DMA((count, 4)),
        pltpu.SemaphoreType.DMA((count, 3, 4)),
        pltpu.SemaphoreType.DMA((count, 2, 4)),
    ]


def scatter_view(grad):
    return grad.reshape((4, 4, 2) + grad.shape[1:])


BACK_TIMES = ((0, (0, 4, 6, 12, 22, 27, 32, 38)), (1, (0, 14, 16, 22, 34, 39, 44, 50)))


def norm_rows_back(values, gain, grad):
    average = jnp.mean(values, -1, keepdims=True)
    centred = values - average
    scale = lax.rsqrt(jnp.mean(centred * centred, -1, keepdims=True) + 1e-05)
    normed = centred * scale
    inner = grad * gain
    mean_inner = jnp.mean(inner, -1, keepdims=True)
    mean_both = jnp.mean(inner * normed, -1, keepdims=True)
    result = scale * (inner - mean_inner - normed * mean_both)
    return result, jnp.sum(grad * normed, 0, keepdims=True), jnp.sum(grad, 0, keepdims=True)


def backward_kernel(*refs):
    (group_ref, x_ref, bias_ref, seg_ref, vec_ref, gac_ref, mixed_ref, cross_lse_ref, row_query_ref, after_self_ref,
     attended_ref, self_lse_ref, query_ref, kv_row_ref, cqo_hbm, self_hbm, kv_hbm, up_hbm, down_hbm) = refs[:19]
    (input_grad_ref, cq_ref, self_low_ref, qkv_ref, vec_grad_ref, dkv_hbm, up_out, down_out) = refs[19:27]
    scratch = refs[27:]
    scatter_refs, scratch = scratch[:17], scratch[17:]
    (cross_vm, self_vm, kv_vm, row_grad_ref, row_stat_ref, acc_ref, own_ref, give_ref, take_ref,
     take_query_ref, load_sem, mate_sems) = scratch
    me = Place()
    core = me.core
    toks, width = x_ref.shape
    loads = [
        pltpu.make_async_copy(cqo_hbm.at[:, pl.ds(0, width)], cross_vm.at[0], load_sem.at[0]),
        pltpu.make_async_copy(cqo_hbm.at[:, pl.ds(width, width)], cross_vm.at[1], load_sem.at[1]),
        pltpu.make_async_copy(kv_hbm, kv_vm, load_sem.at[2]),
        pltpu.make_async_copy(self_hbm, self_vm, load_sem.at[3]),
    ]
    for copy in (loads[1], loads[0], loads[2], loads[3]):
        copy.start()
    me.greet()
    scatter = Scatter(me, (up_hbm, down_hbm), (up_out, down_out), (scatter_refs[:6], scatter_refs[6:12]),
                      scatter_refs[12:], BACK_TIMES)
    scatter.run_until(1)

    def to_mate(src, dst, k):
        return pltpu.make_async_remote_copy(
            src_ref=src, dst_ref=dst, send_sem=mate_sems.at[0, k], recv_sem=mate_sems.at[1, k], device_id=me.mate,
            device_id_type=MESH)

    my_rows = pl.ds(pl.multiple_of(core * toks, toks), toks)
    my_cols = columns(core, toks)

    def head_rows(product, store):
        turned = product.T
        for h in range(2):
            store(h, jnp.sum(turned[h * 64:(h + 1) * 64], 0, keepdims=True))

    loads[1].wait()
    grad_mixed = dot(gac_ref[...].astype(jnp.bfloat16), cross_vm[1], NT).astype(jnp.bfloat16)
    row_grad_ref[my_rows] = grad_mixed
    grad_copy = to_mate(row_grad_ref.at[my_rows], row_grad_ref.at[my_rows], 0)
    grad_copy.start()
    for j in range(6):
        cols = slice(j * 128, (j + 1) * 128)
        product = grad_mixed[:, cols].astype(jnp.float32) * mixed_ref[:, cols]
        row_stat_ref[j, 0:2, my_cols] = cross_lse_ref[j]

        def keep(h, row, j=j):
            row_stat_ref[j, 2 + h:3 + h, my_cols] = row

        head_rows(product, keep)
    stat_copy = to_mate(row_stat_ref.at[:, :, my_cols], row_stat_ref.at[:, :, my_cols], 1)
    stat_copy.start()
    loads[2].wait()
    scatter.run_until(5)
    grad_copy.wait()
    stat_copy.wait()

    def cross_pair(j):
        def back(clip, keys_t, query, grad, lse, inner, h):
            weights = jnp.exp(dot(kv_vm[clip, :, columns(j)], query, NT) - lse)
            grad_v = dot(weights.astype(jnp.bfloat16), grad, NN)
            grad_s = (weights * (dot(kv_vm[clip, :, columns(j + 6)], grad, NT) - inner)).astype(jnp.bfloat16)
            return dot(keys_t[h * 64:(h + 1) * 64], grad_s, NN), dot(grad_s, query, NN), grad_v

        for clip in range(3):
            keys_t = kv_vm[clip, :, columns(j)].T
            grads = []
            for h in range(2):
                if clip == 0:
                    query, grad = row_query_ref[:, columns(j)], row_grad_ref[:, columns(j)]
                    mine = seg_ref[...] == 0
                    lse, inner = row_stat_ref[j, h:h + 1], row_stat_ref[j, 2 + h:3 + h]
                else:
                    low = group_ref[clip - 1:clip] == 0

                    def chosen(ref):
                        return jnp.where(low, ref[:128, columns(j)], ref[384:, columns(j)])

                    def chosen_row(row):
                        return jnp.where(low, row_stat_ref[j, row:row + 1, :128], row_stat_ref[j, row:row + 1, 384:])

                    query, grad = chosen(row_query_ref), chosen(row_grad_ref)
                    mine = jnp.where(low, seg_ref[:, :128], seg_ref[:, 384:]) == clip
                    lse, inner = chosen_row(h), chosen_row(2 + h)
                grads.append(back(clip, keys_t, one_head(query, h), one_head(grad, h), jnp.where(mine, lse, 1e30),
                                  inner, h))
            grad_q, grad_k, grad_v = zip(*grads)
            grad_q = jnp.concatenate(grad_q, 0)
            if clip == 0:
                acc_ref[...] = grad_q
            else:
                for spot in (0, 3):
                    cols = slice(spot * 128, (spot + 1) * 128)
                    acc_ref[:, cols] += jnp.where(low == (spot == 0), grad_q, 0.0)
            kv_vm[clip, :, columns(j)] = (grad_k[0] + grad_k[1]).astype(jnp.bfloat16)
            kv_vm[clip, :, columns(j + 6)] = (grad_v[0] + grad_v[1]).astype(jnp.bfloat16)
        own_ref[:, columns(j)] = (acc_ref[:, my_cols] * 0.125).T
        give_ref[:, columns(j)] = (acc_ref[:, columns(1 - core, toks)] * 0.125).T.astype(jnp.bfloat16)

    loop_with(scatter, 6, 6, 4.7, cross_pair)
    query_copy = to_mate(give_ref.at[:, pl.ds(0, width)], take_query_ref, 2)
    query_copy.start()
    dkv_store = pltpu.make_async_copy(kv_vm, dkv_hbm, load_sem.at[2])
    dkv_store.start()
    vec_grad_ref[...] = jnp.zeros_like(vec_grad_ref)
    cv_bias = sum(jnp.sum(kv_vm[clip, :, width:].astype(jnp.float32), 0, keepdims=True) for clip in range(3))
    vec_grad_ref[10:11] = cv_bias
    loads[0].wait()
    loads[3].wait()
    scatter.run_until(35)
    query_copy.wait()
    grad_query = (own_ref[:, :width] + take_query_ref[...].astype(jnp.float32)).astype(jnp.bfloat16)
    cq_ref[...] = grad_query
    vec_grad_ref[9:10] = jnp.sum(grad_query.astype(jnp.float32), 0, keepdims=True)
    grad_part, gain, shift = norm_rows_back(after_self_ref[...], vec_ref[2:3], dot(grad_query, cross_vm[0], NT))
    vec_grad_ref[2:3] = gain
    vec_grad_ref[3:4] = shift
    grad_after_self = gac_ref[...] + grad_part
    input_grad_ref[...] = grad_after_self
    grad_low = grad_after_self.astype(jnp.bfloat16)
    self_low_ref[...] = grad_low
    vec_grad_ref[8:9] = jnp.sum(grad_low.astype(jnp.float32), 0, keepdims=True)
    grad_attended = dot(grad_low, self_vm[:, 3 * width:], NT).astype(jnp.bfloat16)
    row_grad_ref[:toks] = grad_attended
    for j in range(6):
        cols = slice(j * 128, (j + 1) * 128)

        def keep_self(h, row, j=j):
            row_stat_ref[j, h:h + 1, :toks] = row

        head_rows(grad_attended[:, cols].astype(jnp.float32) * attended_ref[:, cols], keep_self)

    def self_pair(j):
        cols, value_cols = columns(j), columns(j + 6)
        keys, values = kv_row_ref[:, cols], kv_row_ref[:, value_cols]
        keys_t = keys.T
        grad_k = grad_v = None
        parts = []
        for h in range(2):
            query, grad = one_head(query_ref[:, cols], h), one_head(row_grad_ref[:toks, cols], h)
            weights = jnp.exp(dot(keys, query, NT) + bias_ref[...] - self_lse_ref[j, h:h + 1])
            part = dot(weights.astype(jnp.bfloat16), grad, NN)
            grad_v = part if grad_v is None else grad_v + part
            inner = row_stat_ref[j, h:h + 1, :toks]
            grad_s = (weights * (dot(values, grad, NT) - inner)).astype(jnp.bfloat16)
            part = dot(grad_s, query, NN)
            grad_k = part if grad_k is None else grad_k + part
            parts.append(dot(keys_t[h * 64:(h + 1) * 64], grad_s, NN))
        qkv_ref[:, cols] = (jnp.concatenate(parts, 0) * 0.125).T.astype(jnp.bfloat16)
        own_ref[:, cols] = grad_k[toks:]
        own_ref[:, value_cols] = grad_v[toks:]
        give_ref[:, cols] = grad_k[:toks].astype(jnp.bfloat16)
        give_ref[:, value_cols] = grad_v[:toks].astype(jnp.bfloat16)

    loop_with(scatter, 6, 42, 1.3, self_pair)
    row_copy = to_mate(give_ref, take_ref, 3)
    row_copy.start()
    scatter.run_until(51)
    row_copy.wait()
    qkv_ref[:, width:] = (own_ref[...] + take_ref[...].astype(jnp.float32)).astype(jnp.bfloat16)
    sums = jnp.sum(qkv_ref[...].astype(jnp.float32), 0, keepdims=True)
    vec_grad_ref[6:7] = sums[:, :width]
    vec_grad_ref[7:8] = sums[:, 2 * width:]
    grad_normed = dot(qkv_ref[...], self_vm[:, :3 * width], NT)
    grad_part, gain, shift = norm_rows_back(x_ref[...].astype(jnp.float32), vec_ref[0:1], grad_normed)
    vec_grad_ref[0:1] = gain
    vec_grad_ref[1:2] = shift
    input_grad_ref[...] += grad_part
    scatter.finish()
    dkv_store.wait()


def fused_backward(group, x, bias, seg, vec, gac, mixed, cross_lse, row_query, after_self, attended, self_lse, query,
                   kv_row, cqo_full, self_full, kv, grad_up, grad_down):
    toks, width = x.shape
    low, full = jnp.bfloat16, jnp.float32
    pairs = width // 128
    vmem, hbm = pl.BlockSpec(memory_space=pltpu.VMEM), pl.BlockSpec(memory_space=pl.ANY)
    shape = jax.ShapeDtypeStruct
    outs = [
        (vmem, shape((toks, width), full)), (vmem, shape((toks, width), low)), (vmem, shape((toks, width), low)),
        (vmem, shape((toks, 3 * width), low)), (vmem, shape((16, width), full)), (hbm, shape(kv.shape, low)),
        (vmem, shape(grad_up.shape[1:], full)), (vmem, shape(grad_down.shape[1:], full)),
    ]
    return pl.pallas_call(
        backward_kernel,
        in_specs=[vmem] * 14 + [hbm] * 5,
        out_specs=tuple(spec for spec, _ in outs),
        out_shape=tuple(s for _, s in outs),
        scratch_shapes=scatter_scratch((grad_up, grad_down)) + [
            pltpu.VMEM((2, width, width), low), pltpu.VMEM((width, 4 * width), low), pltpu.VMEM(kv.shape, low),
            pltpu.VMEM((2 * toks, width), low), pltpu.VMEM((pairs, 4, 2 * toks), full),
            pltpu.VMEM((128, 2 * toks), full), pltpu.VMEM((toks, 2 * width), full), pltpu.VMEM((toks, 2 * width), low),
            pltpu.VMEM((toks, 2 * width), low), pltpu.VMEM((toks, width), low), pltpu.SemaphoreType.DMA((4,)), pltpu.SemaphoreType.DMA((2, 4)),
        ],
        compiler_params=pltpu.CompilerParams(collective_id=2, has_side_effects=True, vmem_limit_bytes=63 * 2**20),
        name="fused_backward",
    )(group, x, bias, seg, vec, gac, mixed, cross_lse, row_query, after_self, attended, self_lse, query, kv_row,
      cqo_full, self_full, kv, scatter_view(grad_up), scatter_view(grad_down))


def ffn_kernel(normed_ref, grad_ref, after_ref, vec_ref, up_ref, bias_ref, down_ref, out_ref, back_ref, grad_up_ref,
               grad_down_ref, grad_bias_ref, rows_ref, turned_ref, sum_ref, back_sum_ref):
    t = pl.program_id(0)

    @pl.when(t == 0)
    def _():
        turned_ref[...] = normed_ref[...].T
        sum_ref[...] = jnp.zeros_like(sum_ref)
        back_sum_ref[...] = jnp.zeros_like(back_sum_ref)

    grad = grad_ref[...]
    pre = dot(normed_ref[...], up_ref[...], NN) + bias_ref[...]
    below = 0.5 * (1.0 + lax.erf(pre * 0.7071067811865476))
    activated = (pre * below).astype(jnp.bfloat16)
    sum_ref[...] += dot(activated, down_ref[...], NN)
    grad_act = dot(grad, down_ref[...], NT).astype(jnp.bfloat16).astype(jnp.float32)
    density = jnp.exp(-0.5 * pre * pre) * 0.3989422804014327
    grad_pre = (grad_act * (below + pre * density)).astype(jnp.bfloat16)
    back_sum_ref[...] += dot(grad_pre, up_ref[...], NT)
    grad_up_ref[...] = dot(turned_ref[...], grad_pre, NN).astype(jnp.bfloat16)
    grad_down_ref[...] = dot(activated.T, grad, NN).astype(jnp.bfloat16)
    grad_bias_ref[...] = jnp.sum(grad_pre.astype(jnp.float32), 0, keepdims=True)

    @pl.when(t == pl.num_programs(0) - 1)
    def _():
        out_ref[...] = (after_ref[...] + sum_ref[...] + vec_ref[12:13]).astype(jnp.bfloat16)
        grad_rows = grad_ref[...].astype(jnp.float32)
        part, gain, shift = norm_rows_back(after_ref[...], vec_ref[4:5], back_sum_ref[...])
        back = grad_rows + part
        back_ref[...] = back
        rows_ref[...] = jnp.zeros_like(rows_ref)
        rows_ref[4:5] = gain
        rows_ref[5:6] = shift
        rows_ref[11:12] = jnp.sum(back.astype(jnp.bfloat16).astype(jnp.float32), 0, keepdims=True)
        rows_ref[12:13] = jnp.sum(grad_rows, 0, keepdims=True)


def ffn(normed, grad, after, vec, up_full, bias, down_full):
    toks, width = normed.shape
    hidden = up_full.shape[1]
    size = 256
    low, full = jnp.bfloat16, jnp.float32
    shape = jax.ShapeDtypeStruct
    rows = pl.BlockSpec((toks, width), lambda t: (0, 0))
    vecs = pl.BlockSpec((16, width), lambda t: (0, 0))
    up_spec = pl.BlockSpec((width, size), lambda t: (0, t))
    down_spec = pl.BlockSpec((size, width), lambda t: (t, 0))
    bias_spec = pl.BlockSpec((1, size), lambda t: (0, t))
    return pl.pallas_call(
        ffn_kernel,
        grid=(hidden // size,),
        in_specs=[rows, rows, rows, vecs, up_spec, bias_spec, down_spec],
        out_specs=[rows, rows, up_spec, down_spec, bias_spec, vecs],
        out_shape=[
            shape((toks, width), low), shape((toks, width), full), shape(up_full.shape, low),
            shape(down_full.shape, low), shape((1, hidden), full), shape((16, width), full),
        ],
        scratch_shapes=[pltpu.VMEM((width, toks), low), pltpu.VMEM((toks, width), full), pltpu.VMEM((toks, width), full)],
        compiler_params=pltpu.CompilerParams(vmem_limit_bytes=48 * 2**20),
        name="ffn",
    )(normed, grad, after, vec, up_full, bias, down_full)


def place_clips_kernel(order, in_ref, out_ref):
    frames, width = in_ref.shape[1:]
    blocks = width // 128
    for k in range(blocks):
        out_ref[pl.ds(k, frames, stride=blocks), 0] = in_ref[0, :, k * 128:(k + 1) * 128]


def place_clips(order, values):
    clips, frames, width = values.shape
    rows = frames * width // 128
    flat = pl.pallas_call(
        place_clips_kernel,
        grid_spec=pltpu.PrefetchScalarGridSpec(
            num_scalar_prefetch=1,
            grid=(clips,),
            in_specs=[pl.BlockSpec((1, frames, width), lambda k, order: (k, 0, 0))],
            out_specs=pl.BlockSpec((rows, 1, 128), lambda k, order: (order[k], 0, 0)),
        ),
        out_shape=jax.ShapeDtypeStruct((clips * rows, 1, 128), values.dtype),
        compiler_params=pltpu.CompilerParams(vmem_limit_bytes=48 * 2**20),
        name="place_clips",
    )(order, values)
    return flat.reshape(1, clips, frames, width)


FINISH_TIMES = ((3, (0, 4, 6, 12, 22, 27, 32, 38)), (12, (0, 6, 8, 14, 26, 31, 36, 42)), (13, (0, 6, 8, 14, 26, 31, 36, 42)))


def finish_kernel(*refs):
    (normed_one_ref, qkv_ref, attended_ref, self_low_ref, normed_two_ref, cq_ref, mixed_ref, cross_low_ref, frames_ref,
     dkv_ref, ckv_hbm, small_hbm) = refs[:12]
    encoder_hbm, self_out, cross_out, small_out = refs[12:16]
    scratch = refs[16:]
    scatter_refs, scratch = scratch[:18], scratch[18:]
    sems, (turned_ref, weight_ref, stage_ref, load_sem, store_sem) = scratch[:5], scratch[5:]
    self_grad, cross_grad = scatter_refs[0], scatter_refs[6]
    width = normed_one_ref.shape[1]
    load = pltpu.make_async_copy(ckv_hbm, weight_ref, load_sem.at[0])
    load.start()
    me = Place()
    me.greet()
    scatter = Scatter(
        me, (self_grad, cross_grad, small_hbm), (self_out, cross_out, small_out),
        ((None,) + tuple(scatter_refs[1:6]), (None,) + tuple(scatter_refs[7:12]), tuple(scatter_refs[12:18])), sems,
        FINISH_TIMES)

    def store(grad, cols, value):
        grad[..., cols] = value.reshape(4, 4, 2, 24, value.shape[1]).astype(jnp.bfloat16)

    def weight_grad(grad, left_ref, right_ref, first_tile):
        left = left_ref[...].T

        def tile(t, carry):
            store(grad, columns(first_tile + t, 256), dot(left, right_ref[:, columns(t, 256)], NN))
            return carry

        lax.fori_loop(0, right_ref.shape[1] // 256, tile, 0)

    weight_grad(self_grad, normed_one_ref, qkv_ref, 0)
    weight_grad(self_grad, attended_ref, self_low_ref, 9)
    scatter.run_until(3)
    weight_grad(cross_grad, normed_two_ref, cq_ref, 0)
    weight_grad(cross_grad, mixed_ref, cross_low_ref, 9)
    clips = frames_ref.shape[0]
    for clip in range(clips):
        turned_ref[clip] = frames_ref[clip].T
    scatter.run_until(5)

    def frames_tile(t):
        cols = columns(t, 256)
        total = dot(turned_ref[0], dkv_ref[0, :, cols], NN)
        for clip in range(1, clips):
            total = total + dot(turned_ref[clip], dkv_ref[clip, :, cols], NN)
        store(cross_grad, columns(t + 3, 256), total)

    loop_with(scatter, 6, 6, 1, frames_tile)
    scatter.run_until(13)
    load.wait()
    stores = []
    for clip in range(clips):
        slot = clip % 2
        if clip >= 2:
            stores[clip - 2].wait()

        def encoder_tile(t, clip=clip, slot=slot):
            rows = columns(t, 256)
            stage_ref[slot, :, rows] = dot(dkv_ref[clip], weight_ref[rows], NT)

        loop_with(scatter, width // 256, 14 + 4 * clip, 1.3, encoder_tile)
        stores.append(pltpu.make_async_copy(stage_ref.at[slot], encoder_hbm.at[clip], store_sem.at[slot]))
        stores[clip].start()
    scatter.finish()
    for clip in range(max(0, clips - 2), clips):
        stores[clip].wait()


def fused_finish(normed_one, qkv, attended, self_low, normed_two, cq, mixed, cross_low, frames, dkv, ckv_full, small):
    width = normed_one.shape[1]
    clips, count = frames.shape[:2]
    low, full = jnp.bfloat16, jnp.float32
    vmem, hbm = pl.BlockSpec(memory_space=pltpu.VMEM), pl.BlockSpec(memory_space=pl.ANY)
    shape = jax.ShapeDtypeStruct
    large = shape((32, width // 32, 4 * width), low)
    scratch = scatter_scratch((large, large, small))
    for m in range(2):
        scratch[6 * m] = pltpu.VMEM((4, 4, 2) + large.shape[1:], low)
    outs = [
        (hbm, shape(frames.shape, full)), (vmem, shape(large.shape[1:], full)), (vmem, shape(large.shape[1:], full)),
        (vmem, shape(small.shape[1:], full)),
    ]
    return pl.pallas_call(
        finish_kernel,
        in_specs=[vmem] * 10 + [hbm] * 2,
        out_specs=tuple(spec for spec, _ in outs),
        out_shape=tuple(s for _, s in outs),
        scratch_shapes=scratch + [
            pltpu.VMEM((clips, width, count), low), pltpu.VMEM((width, 2 * width), low),
            pltpu.VMEM((2, count, width), full), pltpu.SemaphoreType.DMA((1,)), pltpu.SemaphoreType.DMA((2,)),
        ],
        compiler_params=pltpu.CompilerParams(collective_id=1, has_side_effects=True, vmem_limit_bytes=63 * 2**20),
        name="fused_finish",
    )(normed_one, qkv, attended, self_low, normed_two, cq, mixed, cross_low, frames, dkv, ckv_full,
      scatter_view(small))


def from_behind(value, axis, steps):
    count = lax.axis_size(axis)
    leading, last = (max(0, -steps), min(count, count - steps))
    return lax.ppermute(value, axis, [(source, source + steps) for source in range(leading, last)])


def layer_norm(values, gain, shift):
    average = jnp.mean(values, -1, keepdims=True)
    centred = values - average
    spread = jnp.mean(centred * centred, -1, keepdims=True)
    return centred * lax.rsqrt(spread + 1e-05) * gain + shift


def matmul(left, right):
    return jnp.dot(left, right, preferred_element_type=jnp.float32)


def swap_halves(value):
    return lax.ppermute(value, "seq", [(0, 1), (1, 0)])


def seq_halves(value, axis):
    span = value.shape[axis] // 2
    half = lax.axis_index("seq")
    mine = lax.dynamic_slice_in_dim(value, half * span, span, axis)
    other = lax.dynamic_slice_in_dim(value, (1 - half) * span, span, axis)
    return mine, other


def seq_scatter(value):
    mine, other = seq_halves(value, 0)
    return mine + swap_halves(other.astype(jnp.bfloat16)).astype(value.dtype)


def per_head(values):
    rows = values.reshape(-1, values.shape[2]).T
    return jnp.repeat(rows, HEAD_DIM, axis=1)


def head_sums(values):
    sums = jnp.sum(values.reshape(values.shape[0], -1, HEAD_DIM), -1)
    return sums.T.reshape(-1, 2, values.shape[0])


def plain_forward(
    which, layer_input, frames, mask_bias, row_segment, weights
):
    self_full, cross_full, up_full, down_full, bias_full, out_bias_full, vectors = (
        lax.all_gather(part, ("dp", "seq"), axis=0, tiled=True) for part in weights
    )
    vec = jnp.pad(
        jnp.concatenate([vectors.T, out_bias_full[None]]).astype(jnp.float32), ((0, 3), (0, 0))
    )
    model_width = layer_input.shape[1]
    cross_in = [cross_full[:, k * model_width : (k + 1) * model_width] for k in range(4)]
    ckv_full = cross_full[:, model_width : 3 * model_width]
    cqo_full = jnp.concatenate([cross_in[0], cross_in[3]], 1)
    source = layer_input.astype(jnp.float32)
    normed_one = layer_norm(source, vec[0], vec[1]).astype(jnp.bfloat16)
    proj_bias = jnp.concatenate([vec[6], jnp.zeros_like(vec[6]), vec[7]])
    qkv_low = (matmul(normed_one, self_full[:, : 3 * model_width]) + proj_bias).astype(jnp.bfloat16)
    query = qkv_low[:, :model_width] * jnp.bfloat16(0.125)
    kv_own = qkv_low[:, model_width:]
    kv_row = jnp.concatenate([from_behind(kv_own, "seq", 1), kv_own])
    attended, self_lse = self_forward(query, kv_row, mask_bias)
    attended_low = attended.astype(jnp.bfloat16)
    after_self = source + matmul(attended_low, self_full[:, 3 * model_width :]) + vec[8]
    normed_two = layer_norm(after_self, vec[2], vec[3]).astype(jnp.bfloat16)
    cross_query = (matmul(normed_two, cross_in[0]) + vec[9]).astype(jnp.bfloat16)
    cross_key = jnp.einsum(
        "cfd,de->cfe", frames, cross_in[1], preferred_element_type=jnp.float32
    ).astype(jnp.bfloat16)
    cross_value = (
        jnp.einsum("cfd,de->cfe", frames, cross_in[2], preferred_element_type=jnp.float32)
        + vec[10]
    ).astype(jnp.bfloat16)
    row_query = lax.all_gather(cross_query * jnp.bfloat16(0.125), "seq", axis=0, tiled=True)
    cross_kv = jnp.concatenate([cross_key, cross_value], 2)
    part_mixed, part_stats = cross_forward(which, row_query, cross_kv, row_segment)
    mixed_mine, mixed_other = seq_halves(part_mixed, 0)
    stats_mine, stats_other = seq_halves(part_stats, 2)
    mixed_came = swap_halves(mixed_other.astype(jnp.bfloat16))
    stats_came = swap_halves(stats_other)
    peak = jnp.maximum(stats_mine[:, :2], stats_came[:, :2])
    share_mine = stats_mine[:, 2:] * jnp.exp(stats_mine[:, :2] - peak)
    share_came = stats_came[:, 2:] * jnp.exp(stats_came[:, :2] - peak)
    total = share_mine + share_came
    cross_lse = peak + jnp.log(total)
    mixed_full = mixed_mine * per_head(share_mine / total) + mixed_came.astype(
        jnp.float32
    ) * per_head(share_came / total)
    mixed = mixed_full.astype(jnp.bfloat16)
    after_cross = after_self + matmul(mixed, cross_in[3]) + vec[11]
    normed_three = layer_norm(after_cross, vec[4], vec[5]).astype(jnp.bfloat16)
    return (
        bias_full, ckv_full, self_full, cqo_full, up_full, down_full, cross_kv, vec, normed_one, query, kv_row, attended,
        self_lse, after_self, normed_two, row_query, cross_lse, mixed_full, after_cross, normed_three,
    )


def forward(which, layer_input, frames, mask_bias, row_segment, weights):
    if lax.axis_size("dp") != 16:
        return plain_forward(which, layer_input, frames, mask_bias, row_segment, weights)
    self_weights, cross_weights, up_weights, down_weights, up_bias, down_bias, vectors = weights

    def as_row(values):
        return jnp.pad(values, ((0, 0), (0, 128 - values.shape[1])))

    small = jnp.concatenate(
        [as_row(vectors.T), as_row(down_bias[None]), as_row(up_bias[None]), jnp.zeros((2, 128), vectors.dtype)]
    )
    group = jnp.broadcast_to(which[:, None], (2, 128))
    whole = fused_forward(
        group, layer_input, frames, mask_bias, row_segment, small, self_weights, cross_weights, up_weights,
        down_weights,
    )
    return (whole[0][:, 13, : up_bias.shape[0]].reshape(-1),) + tuple(whole[1:])


def plain_backward(
    which, layer_input, mask_bias, row_segment, vec, grad_after_cross, mixed_full, cross_lse, row_query, after_self,
    attended, self_lse, query, kv_row, cqo_full, self_full, cross_kv
):
    tok_span, model_width = layer_input.shape
    source = layer_input.astype(jnp.float32)
    grad_cross_low = grad_after_cross.astype(jnp.bfloat16)
    grad_mixed = matmul(grad_cross_low, cqo_full[:, model_width:].T).astype(jnp.bfloat16)
    row_grad = lax.all_gather(grad_mixed, "seq", axis=0, tiled=True)
    cross_inner = head_sums(grad_mixed.astype(jnp.float32) * mixed_full)
    row_stats = lax.all_gather(jnp.stack([cross_lse, cross_inner]), "seq", axis=3, tiled=True)
    part_query, grad_key, grad_value = cross_backward(
        which, row_query, cross_kv, row_segment, row_stats[0], row_stats[1], row_grad
    )
    grad_query_sum = seq_scatter(part_query).astype(jnp.bfloat16)
    grad_cq_bias = jnp.sum(grad_query_sum, 0, dtype=jnp.float32)
    grad_normed_two = matmul(grad_query_sum, cqo_full[:, :model_width].T)
    grad_cv_bias = jnp.sum(grad_value, (0, 1), dtype=jnp.float32)
    _, norm_pull_two = jax.vjp(layer_norm, after_self, vec[2], vec[3])
    grad_part, grad_gain_two, grad_shift_two = norm_pull_two(grad_normed_two)
    grad_after_self = grad_after_cross + grad_part
    grad_self_low = grad_after_self.astype(jnp.bfloat16)
    grad_self_bias = jnp.sum(grad_self_low, 0, dtype=jnp.float32)
    grad_attended = matmul(grad_self_low, self_full[:, 3 * model_width :].T).astype(jnp.bfloat16)
    self_inner = head_sums(grad_attended.astype(jnp.float32) * attended)
    grad_query, grad_key_row, grad_value_row = self_backward(
        query, kv_row, mask_bias, self_lse, self_inner, grad_attended
    )
    grad_kv = jnp.concatenate([grad_key_row, grad_value_row], 1)
    back_kv = from_behind(grad_kv[:tok_span].astype(jnp.bfloat16), "seq", -1)
    grad_qkv_low = jnp.concatenate(
        [grad_query, grad_kv[tok_span:] + back_kv.astype(jnp.float32)], 1
    ).astype(jnp.bfloat16)
    grad_qkv_bias = jnp.sum(grad_qkv_low, 0, dtype=jnp.float32)
    grad_normed_one = matmul(grad_qkv_low, self_full[:, : 3 * model_width].T)
    _, norm_pull_one = jax.vjp(layer_norm, source, vec[0], vec[1])
    grad_part, grad_gain_one, grad_shift_one = norm_pull_one(grad_normed_one)
    input_grad = grad_after_self + grad_part
    nothing = jnp.zeros_like(grad_cq_bias)
    vec_grads = jnp.stack(
        [
            grad_gain_one,
            grad_shift_one,
            grad_gain_two,
            grad_shift_two,
            nothing,
            nothing,
            grad_qkv_bias[:model_width],
            grad_qkv_bias[2 * model_width :],
            grad_self_bias,
            grad_cq_bias,
            grad_cv_bias,
        ]
        + [nothing] * 5
    )
    return (
        input_grad, grad_query_sum, grad_self_low, grad_qkv_low, vec_grads,
        jnp.concatenate([grad_key, grad_value], 2),
    )


def plain_finish(
    normed_one, grad_qkv_low, attended_low, grad_self_low, normed_two, grad_query_sum, mixed, grad_cross_low, frames,
    cross_kv_grad, ckv_full
):
    width = normed_one.shape[1]
    grads_self = jnp.concatenate([matmul(normed_one.T, grad_qkv_low), matmul(attended_low.T, grad_self_low)], 1)
    grad_ckv = jnp.einsum("cfd,cfe->de", frames, cross_kv_grad, preferred_element_type=jnp.float32)
    grads_cross = jnp.concatenate(
        [matmul(normed_two.T, grad_query_sum), grad_ckv, matmul(mixed.T, grad_cross_low)], 1
    )
    encoder_grad = jnp.einsum(
        "cfe,de->cfd", cross_kv_grad, ckv_full, preferred_element_type=jnp.float32
    )
    return encoder_grad, (grads_self, grads_cross)


def per_device(
    layer_input,
    encoder_states,
    clip_lengths,
    out_grad,
    self_weights,
    cross_weights,
    up_weights,
    down_weights,
    up_bias,
    down_bias,
    vectors,
):
    model_width = layer_input.shape[2]
    tok_span = layer_input.shape[1]
    seq_half = lax.axis_index("seq")
    source = layer_input[0].astype(jnp.float32)
    position = seq_half * tok_span + jnp.arange(tok_span, dtype=jnp.int32)
    clip_ends = jnp.cumsum(clip_lengths[0])
    segment = jnp.sum((position[:, None] >= clip_ends[None, :]).astype(jnp.int32), 1)
    key_position = jnp.concatenate([position - tok_span, position])
    key_segment = jnp.sum((key_position[:, None] >= clip_ends[None, :]).astype(jnp.int32), 1)
    allowed = (
        (key_segment[:, None] == segment[None, :])
        & (key_position[:, None] <= position[None, :])
        & (key_position[:, None] >= 0)
    )
    mask_bias = jnp.where(allowed, 0.0, -1e30).astype(jnp.float32)
    row_position = jnp.arange(2 * tok_span, dtype=jnp.int32)
    row_segment = jnp.sum((row_position[:, None] >= clip_ends[None, :]).astype(jnp.int32), 1)[None]
    big = jnp.argmax(clip_lengths[0]).astype(jnp.int32)
    small_one = jnp.where(big == 0, 1, 0)
    small_two = jnp.where(big == 2, 1, 2)
    last_group = 2 * tok_span // 128 - 1
    order = jnp.stack([big, small_one, small_two]).astype(jnp.int32)
    row_segment = jnp.where(
        row_segment == order[0], 0, jnp.where(row_segment == order[1], 1, jnp.where(row_segment == order[2], 2, 3))
    )
    which = jnp.where(order[1:] < big, 0, last_group).astype(jnp.int32)

    frames = jnp.take(encoder_states[0], order, axis=0, mode="clip")
    (
        bias_full, ckv_full, self_full, cqo_full, up_full, down_full, cross_kv, vec, normed_one, query, kv_row, attended,
        self_lse, after_self, normed_two, row_query, cross_lse, mixed_full, after_cross, normed_three,
    ) = forward(
        which, layer_input[0], frames, mask_bias, row_segment,
        (self_weights, cross_weights, up_weights, down_weights, up_bias, down_bias, vectors),
    )
    bias_full = bias_full.astype(jnp.float32)
    attended_low = attended.astype(jnp.bfloat16)
    mixed = mixed_full.astype(jnp.bfloat16)
    layer_output, grad_after_cross, grad_up, grad_down, grad_up_bias, ffn_rows = ffn(
        normed_three, out_grad[0], after_cross, vec, up_full, bias_full[None], down_full
    )
    grad_cross_low = grad_after_cross.astype(jnp.bfloat16)
    grad_out_bias = ffn_rows[12]
    operands = (
        layer_input[0], mask_bias, row_segment, vec, grad_after_cross, mixed_full, cross_lse, row_query, after_self,
        attended, self_lse, query, kv_row, cqo_full, self_full, cross_kv,
    )
    fused = lax.axis_size("dp") == 16
    if fused:
        group = jnp.broadcast_to(which[:, None], (2, 128))
        large = [g.reshape(32, -1, g.shape[1]) for g in (grad_up, grad_down)]
        *results, up_share, down_share = fused_backward(group, *operands, *large)
    else:
        results = plain_backward(which, *operands)
    input_grad, grad_query_sum, grad_self_low, grad_qkv_low, vec_grads, cross_kv_grad = results
    vector_grads = (vec_grads + ffn_rows)[:12]
    last_operands = (
        normed_one, grad_qkv_low, attended_low, grad_self_low, normed_two, grad_query_sum, mixed, grad_cross_low, frames,
        cross_kv_grad, ckv_full,
    )
    if fused:
        blocks = jnp.pad(vector_grads.reshape(12, 32, -1).transpose(1, 0, 2), ((0, 0), (0, 0), (0, 104)))
        ups = jnp.pad(grad_up_bias.reshape(32, 1, -1), ((0, 0), (0, 0), (0, 32)))
        downs = jnp.pad(grad_out_bias.reshape(32, 1, -1), ((0, 0), (0, 0), (0, 104)))
        small = jnp.concatenate([blocks, ups, downs, jnp.zeros((32, 2, 128), jnp.float32)], 1)
        encoder_grad, self_share, cross_share, row = fused_finish(*last_operands, small)
        shares = (
            self_share, cross_share, up_share, down_share, row[12, : up_bias.shape[0]], row[13, : down_bias.shape[0]],
            row[:12, : vectors.shape[0]].T,
        )
    else:
        encoder_grad, large = plain_finish(*last_operands)
        shares = tuple(
            lax.psum_scatter(part, ("dp", "seq"), scatter_dimension=0, tiled=True)
            for part in large
            + (grad_up.astype(jnp.float32), grad_down.astype(jnp.float32), grad_up_bias[0], grad_out_bias, vector_grads.T)
        )
    return (layer_output[None], input_grad[None], place_clips(order, encoder_grad)) + shares


def solution(mesh):
    return jax.shard_map(
        per_device,
        mesh=mesh,
        in_specs=(
            P("dp", "seq", None),
            P("dp", None, "seq", None),
            P("dp", None),
            P("dp", "seq", None),
            P(("dp", "seq"), None),
            P(("dp", "seq"), None),
            P(("dp", "seq"), None),
            P(("dp", "seq"), None),
            P(("dp", "seq")),
            P(("dp", "seq")),
            P(("dp", "seq"), None),
        ),
        out_specs=(
            P("dp", "seq", None),
            P("dp", "seq", None),
            P("dp", None, "seq", None),
            P(("dp", "seq"), None),
            P(("dp", "seq"), None),
            P(("dp", "seq"), None),
            P(("dp", "seq"), None),
            P(("dp", "seq")),
            P(("dp", "seq")),
            P(("dp", "seq"), None),
        ),
        check_vma=False,
    )
```

```python
import functools

import jax
import jax.numpy as jnp
from jax import lax
from jax.experimental import pallas as pl
from jax.experimental.pallas import tpu as pltpu
from jax.sharding import PartitionSpec as P

HEAD_DIM = 64
CLIPS = 3
MESH = pl.DeviceIdType.MESH
NT = (((1,), (1,)), ((), ()))
NN = (((1,), (0,)), ((), ()))


def dot(left, right, dims):
    return lax.dot_general(left, right, dims, preferred_element_type=jnp.float32)


def one_head(values, h):
    lane = lax.broadcasted_iota(jnp.int32, values.shape, 1)
    return jnp.where((lane >= 64) == (h == 1), values, jnp.zeros_like(values))


def self_forward_kernel(q_ref, k_ref, v_ref, bias_ref, out_ref, lse_ref):
    keys = k_ref[...]
    values_t = v_ref[...].T
    halves = []
    for h in range(2):
        scores = dot(keys, one_head(q_ref[...], h), NT) + bias_ref[...]
        peak = jnp.max(scores, 0, keepdims=True)
        terms = jnp.exp(scores - peak)
        total = jnp.sum(terms, 0, keepdims=True)
        result = dot(values_t[h * 64:(h + 1) * 64], terms.astype(jnp.bfloat16), NN)
        halves.append(result / total)
        lse_ref[0, h:h + 1] = peak + jnp.log(total)
    out_ref[...] = jnp.concatenate(halves, 0).T.astype(out_ref.dtype)


def self_forward(q, kv, bias):
    toks, width = q.shape
    keys, pairs = kv.shape[0], width // 128
    return pl.pallas_call(
        self_forward_kernel,
        grid=(width // 128,),
        in_specs=[
            pl.BlockSpec((toks, 128), lambda j: (0, j)),
            pl.BlockSpec((keys, 128), lambda j: (0, j)),
            pl.BlockSpec((keys, 128), lambda j: (0, j + pairs)),
            pl.BlockSpec((keys, toks), lambda j: (0, 0)),
        ],
        out_specs=[
            pl.BlockSpec((toks, 128), lambda j: (0, j)),
            pl.BlockSpec((1, 2, toks), lambda j: (j, 0, 0)),
        ],
        out_shape=[
            jax.ShapeDtypeStruct((toks, width), jnp.float32),
            jax.ShapeDtypeStruct((width // 128, 2, toks), jnp.float32),
        ],
        compiler_params=pltpu.CompilerParams(vmem_limit_bytes=48 * 2**20),
        name="self_forward",
    )(q, kv, kv, bias)


def self_backward_kernel(q_ref, k_ref, v_ref, bias_ref, lse_ref, inner_ref, g_ref, dq_ref, dk_ref, dv_ref):
    keys, values = k_ref[...], v_ref[...]
    keys_t = keys.T
    grad_k = grad_v = None
    halves = []
    for h in range(2):
        query, grad = one_head(q_ref[...], h), one_head(g_ref[...], h)
        weights = jnp.exp(dot(keys, query, NT) + bias_ref[...] - lse_ref[0, h:h + 1])
        part = dot(weights.astype(jnp.bfloat16), grad, NN)
        grad_v = part if grad_v is None else grad_v + part
        grad_s = (weights * (dot(values, grad, NT) - inner_ref[0, h:h + 1])).astype(jnp.bfloat16)
        part = dot(grad_s, query, NN)
        grad_k = part if grad_k is None else grad_k + part
        halves.append(dot(keys_t[h * 64:(h + 1) * 64], grad_s, NN))
    dq_ref[...] = (jnp.concatenate(halves, 0) * 0.125).T
    dk_ref[...] = grad_k
    dv_ref[...] = grad_v


def self_backward(q, kv, bias, lse, inner, grad):
    toks, width = q.shape
    keys, pairs = kv.shape[0], width // 128
    tok_spec = pl.BlockSpec((toks, 128), lambda j: (0, j))
    key_spec = pl.BlockSpec((keys, 128), lambda j: (0, j))
    row_spec = pl.BlockSpec((1, 2, toks), lambda j: (j, 0, 0))
    return pl.pallas_call(
        self_backward_kernel,
        grid=(width // 128,),
        in_specs=[tok_spec, key_spec, pl.BlockSpec((keys, 128), lambda j: (0, j + pairs)), pl.BlockSpec((keys, toks), lambda j: (0, 0)), row_spec, row_spec, tok_spec],
        out_specs=[tok_spec, key_spec, key_spec],
        out_shape=[
            jax.ShapeDtypeStruct((toks, width), jnp.float32),
            jax.ShapeDtypeStruct((keys, width), jnp.float32),
            jax.ShapeDtypeStruct((keys, width), jnp.float32),
        ],
        compiler_params=pltpu.CompilerParams(vmem_limit_bytes=48 * 2**20),
        name="self_backward",
    )(q, kv, kv, bias, lse, inner, grad)


def cross_forward_kernel(which, q_ref, k_ref, v_ref, seg_ref, out_ref, stat_ref, acc_ref):
    def attend(clip, values_t, query, h):
        scores = dot(k_ref[clip], query, NT)
        peak = jnp.max(scores, 0, keepdims=True)
        terms = jnp.exp(scores - peak)
        total = jnp.sum(terms, 0, keepdims=True)
        result = dot(values_t[h * 64:(h + 1) * 64], terms.astype(jnp.bfloat16), NN)
        return result / total, peak, total

    values_t = v_ref[0].T
    for h in range(2):
        mine = seg_ref[...] == 0
        result, peak, total = attend(0, values_t, one_head(q_ref[...], h), h)
        acc_ref[h * 64:(h + 1) * 64] = jnp.where(mine, result, 0.0)
        stat_ref[0, h:h + 1] = jnp.where(mine, peak, 0.0)
        stat_ref[0, 2 + h:3 + h] = jnp.where(mine, total, 1.0)
    for clip in (1, 2):
        cols = pl.ds(pl.multiple_of(which[clip - 1] * 128, 128), 128)
        values_t = v_ref[clip].T
        mine = seg_ref[:, cols] == clip
        for h in range(2):
            result, peak, total = attend(clip, values_t, one_head(q_ref[cols], h), h)
            rows = slice(h * 64, (h + 1) * 64)
            acc_ref[rows, cols] = jnp.where(mine, result, acc_ref[rows, cols])
            stat_ref[0, h:h + 1, cols] = jnp.where(mine, peak, stat_ref[0, h:h + 1, cols])
            stat_ref[0, 2 + h:3 + h, cols] = jnp.where(mine, total, stat_ref[0, 2 + h:3 + h, cols])
    out_ref[...] = acc_ref[...].T


def cross_forward(which, q, kv, seg):
    toks, width = q.shape
    clips, frames = kv.shape[:2]
    pairs = width // 128
    kv_spec = pl.BlockSpec((clips, frames, 128), lambda j, w: (0, 0, j))
    v_spec = pl.BlockSpec((clips, frames, 128), lambda j, w: (0, 0, j + pairs))
    tok_spec = pl.BlockSpec((toks, 128), lambda j, w: (0, j))
    return pl.pallas_call(
        cross_forward_kernel,
        grid_spec=pltpu.PrefetchScalarGridSpec(
            num_scalar_prefetch=1,
            grid=(width // 128,),
            in_specs=[tok_spec, kv_spec, v_spec, pl.BlockSpec((1, toks), lambda j, w: (0, 0))],
            out_specs=[tok_spec, pl.BlockSpec((1, 4, toks), lambda j, w: (j, 0, 0))],
            scratch_shapes=[pltpu.VMEM((128, toks), jnp.float32)],
        ),
        out_shape=[
            jax.ShapeDtypeStruct((toks, width), jnp.float32),
            jax.ShapeDtypeStruct((width // 128, 4, toks), jnp.float32),
        ],
        compiler_params=pltpu.CompilerParams(vmem_limit_bytes=48 * 2**20),
        name="cross_forward",
    )(which, q, kv, kv, seg)


def cross_backward_kernel(which, q_ref, k_ref, v_ref, seg_ref, lse_ref, inner_ref, g_ref, dq_ref, dk_ref, dv_ref, acc_ref):
    def back(clip, keys_t, cols, h):
        query, grad = one_head(q_ref[cols], h), one_head(g_ref[cols], h)
        lse = jnp.where(seg_ref[:, cols] == clip, lse_ref[0, h:h + 1, cols], 1e30)
        weights = jnp.exp(dot(k_ref[clip], query, NT) - lse)
        grad_v = dot(weights.astype(jnp.bfloat16), grad, NN)
        grad_s = (weights * (dot(v_ref[clip], grad, NT) - inner_ref[0, h:h + 1, cols])).astype(jnp.bfloat16)
        grad_k = dot(grad_s, query, NN)
        return dot(keys_t[h * 64:(h + 1) * 64], grad_s, NN), grad_k, grad_v

    for clip in range(3):
        cols = slice(None) if clip == 0 else pl.ds(pl.multiple_of(which[clip - 1] * 128, 128), 128)
        keys_t = k_ref[clip].T
        grad_q, grad_k, grad_v = zip(*(back(clip, keys_t, cols, h) for h in range(2)))
        grad_q = jnp.concatenate(grad_q, 0)
        if clip == 0:
            acc_ref[...] = grad_q
        else:
            acc_ref[:, cols] += grad_q
        dk_ref[clip] = (grad_k[0] + grad_k[1]).astype(jnp.bfloat16)
        dv_ref[clip] = (grad_v[0] + grad_v[1]).astype(jnp.bfloat16)
    dq_ref[...] = (acc_ref[...] * 0.125).T


def cross_backward(which, q, kv, seg, lse, inner, grad):
    toks, width = q.shape
    clips, frames = kv.shape[:2]
    pairs = width // 128
    kv_spec = pl.BlockSpec((clips, frames, 128), lambda j, w: (0, 0, j))
    v_spec = pl.BlockSpec((clips, frames, 128), lambda j, w: (0, 0, j + pairs))
    tok_spec = pl.BlockSpec((toks, 128), lambda j, w: (0, j))
    row_spec = pl.BlockSpec((1, 2, toks), lambda j, w: (j, 0, 0))
    return pl.pallas_call(
        cross_backward_kernel,
        grid_spec=pltpu.PrefetchScalarGridSpec(
            num_scalar_prefetch=1,
            grid=(width // 128,),
            in_specs=[tok_spec, kv_spec, v_spec, pl.BlockSpec((1, toks), lambda j, w: (0, 0)), row_spec, row_spec, tok_spec],
            out_specs=[tok_spec, kv_spec, kv_spec],
            scratch_shapes=[pltpu.VMEM((128, toks), jnp.float32)],
        ),
        out_shape=[
            jax.ShapeDtypeStruct((toks, width), jnp.float32),
            jax.ShapeDtypeStruct((clips, frames, width), jnp.bfloat16),
            jax.ShapeDtypeStruct((clips, frames, width), jnp.bfloat16),
        ],
        compiler_params=pltpu.CompilerParams(vmem_limit_bytes=48 * 2**20),
        name="cross_backward",
    )(which, q, kv, kv, seg, lse, inner, grad)


Z = 4


class Place:
    def __init__(self):
        self.dp = lax.axis_index("dp")
        self.core = lax.axis_index("seq")
        self.z = self.dp // 4
        self.p = self.dp % 4
        x, y = self.p % 2, self.p // 2
        px, py = self.p + 1 - 2 * x, self.p + 2 - 4 * y
        self.p_first = px * (1 - self.core) + py * self.core
        self.p_second = py * (1 - self.core) + px * self.core
        self.p_diag = 3 - self.p
        base = self.z * 4
        self.first = (base + self.p_first, self.core)
        self.second = (base + self.p_second, self.core)
        self.mate = (self.dp, 1 - self.core)
        half = self.z // 2
        near = self.z + half * (3 - 2 * self.z)
        self.line = [base + half * (3 - 2 * base) for base in (3, 2, 1 - near)]
        self.peers = [self.mate, self.first, self.second] + [self.on_line(z) for z in self.line]

    def on_line(self, z):
        return (z * 4 + self.p, self.core)

    def greet(self):
        barrier = pltpu.get_barrier_semaphore()
        for target in self.peers:
            pl.semaphore_signal(barrier, inc=1, device_id=target, device_id_type=MESH)
        pl.semaphore_wait(barrier, len(self.peers))


HALF_COLS = {1: 768, 2: 1536, 3: 768, 4: 1536}


class Gather:
    def __init__(self, me, srcs, outs, send_sem, recv_sem, own_sem):
        self.me, self.srcs, self.outs = me, srcs, outs
        self.send_sem, self.recv_sem, self.own_sem = send_sem, recv_sem, own_sem
        self.sends = []
        self.tasks = []
        for m, times in enumerate(GATHER_TIMES):
            for time, task in zip(times, self.steps(m)):
                self.tasks.append((time, m, task))
        self.tasks.sort(key=lambda entry: entry[:2])

    def piece(self, m, chip, core):
        if m == 0:
            return self.outs[m].at[chip * 2 + core]
        if m == 5:
            return self.outs[m].at[pl.ds(pl.multiple_of(chip * 192 + core * 96, 96), 96)]
        rows = pl.ds(pl.multiple_of(chip * 48, 48), 48)
        return self.outs[m].at[rows, columns(core, HALF_COLS[m])]

    def sender(self, m, src, chip, target):
        copy = pltpu.make_async_remote_copy(
            src_ref=src, dst_ref=self.piece(m, chip, self.me.core), send_sem=self.send_sem.at[len(self.sends)],
            recv_sem=self.recv_sem.at[m, chip * 2 + self.me.core], device_id=target, device_id_type=MESH)
        self.sends.append(copy)
        return copy.start

    def arrival(self, m, chip, core):
        piece = self.piece(m, chip, core)
        return pltpu.make_async_remote_copy(
            src_ref=piece, dst_ref=piece, send_sem=self.send_sem.at[0],
            recv_sem=self.recv_sem.at[m, chip * 2 + core], device_id=self.me.mate, device_id_type=MESH).wait_recv

    def forward(self, m, z, p, targets):
        chip = z * 4 + p
        return [self.arrival(m, chip, self.me.core)] + [
            self.sender(m, self.piece(m, chip, self.me.core), chip, target) for target in targets
        ]

    def steps(self, m):
        me = self.me
        begin = [
            self.sender(m, self.srcs[m], me.dp, target)
            for target in [me.on_line(z) for z in me.line] + [me.first, me.second, me.mate]
        ]
        begin.append(pltpu.make_async_copy(self.srcs[m], self.piece(m, me.dp, me.core), self.own_sem.at[m]).start)
        line = []
        for z in me.line[::-1]:
            line += self.forward(m, z, me.p, [me.first, me.second, me.mate])
        beside = []
        for z in [me.z] + me.line[::-1]:
            beside += self.forward(m, z, me.p_first, [me.second, me.mate])
        rest = []
        for p in (me.p_second, me.p_diag):
            for z in [me.z] + me.line[::-1]:
                rest += self.forward(m, z, p, [me.mate])
        return [begin, line, beside, rest]

    def run(self, entry):
        for act in entry[2]:
            act()

    def run_until(self, time):
        while self.tasks and self.tasks[0][0] <= time:
            self.run(self.tasks.pop(0))

    def take_until(self, time):
        taken = []
        while self.tasks and self.tasks[0][0] <= time:
            taken.append(self.tasks.pop(0))
        return taken

    def need(self, m):
        for entry in [e for e in self.tasks if e[1] == m]:
            self.run(entry)
        self.tasks = [e for e in self.tasks if e[1] != m]
        pltpu.make_async_copy(self.srcs[m], self.piece(m, self.me.dp, self.me.core), self.own_sem.at[m]).wait()
        for chip in range(16):
            self.arrival(m, chip, 1 - self.me.core)()

    def finish(self):
        for copy in self.sends:
            copy.wait_send()


GATHER_TIMES = (
    (1, 6, 10, 15),
    (0, 5, 9, 14),
    (2, 11, 19, 27),
    (10, 20, 26, 34),
    (18, 31, 42, 54),
    (30, 48, 60, 74),
)


def loop_with(steps, count, begin, length, body, slots=(0,)):
    due = {}
    for i in range(count):
        for part, k in sorted((part, k) for k, part in enumerate(slots)):
            due[i, k] = steps.take_until(begin + length * (i + part))

    def turn(i, carry):
        def tick(k):
            for at in range(count):
                if due[at, k]:

                    def run(entries=due[at, k]):
                        for entry in entries:
                            steps.run(entry)

                    pl.when(i == at)(run)

        body(i, tick)
        return carry

    lax.fori_loop(0, count, turn, 0)


def norm_rows(values, gain, shift):
    average = jnp.mean(values, -1, keepdims=True)
    centred = values - average
    spread = jnp.mean(centred * centred, -1, keepdims=True)
    return centred * lax.rsqrt(spread + 1e-05) * gain + shift


def two_heads(values):
    return jnp.concatenate([one_head(values, 0), one_head(values, 1)], 0)


def columns(j, size=128):
    return pl.ds(pl.multiple_of(j * size, size), size)


def forward_kernel(*refs):
    (group_ref, x_ref, frames_ref, bias_ref, seg_ref, small_in, self_in, cross_in, up_in, down_in) = refs[:10]
    (small_out, ckv_out, self_out, cqo_out, up_out, down_out, kv_out, vec_ref, normed_one_ref, query_ref, kv_row_ref,
     attended_ref, self_lse_ref, after_self_ref, normed_two_ref, row_query_ref, cross_lse_ref, mixed_ref,
     after_cross_ref, normed_three_ref) = refs[10:30]
    (half_wide, half_narrow, pair_wide, pair_narrow, small_vm, ckv_vm, self_vm, cqo_vm, kv_vm, acc_ref, stat_ref, part_ref, part_stat_ref, give_ref,
     give_stat_ref, take_ref, take_stat_ref, send_sem, recv_sem, own_sem, half_sems, mate_sems, load_sem) = refs[30:]
    me = Place()
    core = me.core
    width = x_ref.shape[1]
    toks = x_ref.shape[0]
    me.greet()

    def to_mate(src, dst, k):
        return pltpu.make_async_remote_copy(
            src_ref=src, dst_ref=dst, send_sem=mate_sems.at[0, k], recv_sem=mate_sems.at[1, k], device_id=me.mate,
            device_id_type=MESH)

    def half_of(m, which):
        shard = (None, cross_in, self_in, cross_in, up_in)[m]
        size = HALF_COLS[m]
        begin = (0, width, 0, 0, 0)[m] + which * (0, width, size, 3 * width, size)[m]
        return shard.at[:, pl.ds(pl.multiple_of(begin, size), size)]

    buffers = {1: (half_narrow.at[0], pair_narrow.at[0]), 2: (half_wide.at[0], pair_wide.at[0]),
               3: (half_narrow.at[1], pair_narrow.at[1]), 4: (half_wide.at[1], pair_wide.at[1])}
    halves = {
        m: pltpu.make_async_remote_copy(
            src_ref=half_of(m, 1 - core), dst_ref=buffers[m][0], send_sem=half_sems.at[0, m],
            recv_sem=half_sems.at[1, m], device_id=me.mate, device_id_type=MESH)
        for m in buffers
    }
    for copy in halves.values():
        copy.start()
    sources = (small_in,) + tuple(buffers[m][1] for m in buffers) + (down_in,)
    gather = Gather(me, sources, (small_out, ckv_out, self_out, cqo_out, up_out, down_out), send_sem, recv_sem, own_sem)
    for m, (came_ref, both_ref) in buffers.items():
        halves[m].wait()
        own = half_of(m, core)[...].astype(jnp.float32)
        came = came_ref[...].astype(jnp.float32)
        both_ref[...] = jnp.concatenate(
            [jnp.where(core == 0, own, came), jnp.where(core == 0, came, own)], 0).astype(jnp.bfloat16)
        gather.run_until((0, 1, 2, 2, 2)[m])

    def fetch(src, dst, k):
        copy = pltpu.make_async_copy(src, dst, load_sem.at[k])
        copy.start()
        copy.wait()

    gather.run_until(15)
    gather.need(0)
    fetch(small_out, small_vm, 0)
    row = lax.broadcasted_iota(jnp.int32, (128, width), 0)
    spot = lax.broadcasted_iota(jnp.int32, (128, width), 1) - row

    def place_small(d, total):
        chosen = jnp.where((spot == d * 24) & (row < 24), 1.0, 0.0).astype(jnp.bfloat16)
        return total + dot(small_vm[d], chosen, NN)

    vec_ref[...] = lax.fori_loop(0, 32, place_small, jnp.zeros(vec_ref.shape, jnp.float32))

    def vec(k):
        return vec_ref[k:k + 1]

    source = x_ref[...].astype(jnp.float32)
    normed_one_ref[...] = norm_rows(source, vec(0), vec(1)).astype(jnp.bfloat16)
    gather.need(1)
    fetch(ckv_out, ckv_vm, 0)
    clips = frames_ref.shape[0]
    tiles = 2 * width // 256

    def project(t, tick):
        tick(0)
        clip, tile = t // tiles, t % tiles
        result = dot(frames_ref[clip], ckv_vm[:, columns(tile, 256)], NN)
        is_value = (tile >= 3).astype(jnp.float32)
        shift = vec_ref[10:11, columns(tile % 3, 256)] * is_value
        kv_vm[clip, :frames_ref.shape[1], columns(tile, 256)] = (result + shift).astype(jnp.bfloat16)

    loop_with(gather, clips * tiles, 20, 0.65, project)
    kv_store = pltpu.make_async_copy(kv_vm, kv_out, load_sem.at[1])
    kv_store.start()
    gather.run_until(31)
    gather.need(2)
    fetch(self_out, self_vm, 0)

    normed = normed_one_ref[...]
    own_rows = slice(toks, 2 * toks)
    kv_row_ref[own_rows, :width] = dot(normed, self_vm[:, width:2 * width], NN).astype(jnp.bfloat16)
    kv_row_ref[own_rows, width:] = (dot(normed, self_vm[:, 2 * width:3 * width], NN) + vec(7)).astype(jnp.bfloat16)
    kv_copy = to_mate(kv_row_ref.at[own_rows], kv_row_ref.at[slice(0, toks)], 0)
    kv_copy.start()
    query = (dot(normed, self_vm[:, :width], NN) + vec(6)).astype(jnp.bfloat16)
    query_ref[...] = query * jnp.bfloat16(0.125)
    gather.run_until(35)
    kv_copy.wait()

    def self_pair(j, tick):
        tick(0)
        cols = columns(j)
        keys = kv_row_ref[:, cols]
        values_t = kv_row_ref[:, columns(j + 6)].T
        parts = []
        for h in range(2):
            scores = dot(keys, one_head(query_ref[:, cols], h), NT) + bias_ref[...]
            peak = jnp.max(scores, 0, keepdims=True)
            terms = jnp.exp(scores - peak)
            total = jnp.sum(terms, 0, keepdims=True)
            parts.append(dot(values_t[h * 64:(h + 1) * 64], terms.astype(jnp.bfloat16), NN) / total)
            self_lse_ref[j, h:h + 1] = peak + jnp.log(total)
        attended_ref[:, cols] = jnp.concatenate(parts, 0).T

    loop_with(gather, 6, 35, 1.2, self_pair)
    after_self = source + dot(attended_ref[...].astype(jnp.bfloat16), self_vm[:, 3 * width:], NN) + vec(8)
    after_self_ref[...] = after_self
    normed_two = norm_rows(after_self, vec(2), vec(3)).astype(jnp.bfloat16)
    normed_two_ref[...] = normed_two
    gather.run_until(44)
    gather.need(3)
    fetch(cqo_out, cqo_vm, 0)
    my_rows = pl.ds(pl.multiple_of(core * toks, toks), toks)
    cross_query = (dot(normed_two, cqo_vm[:, :width], NN) + vec(9)).astype(jnp.bfloat16)
    row_query_ref[my_rows] = cross_query * jnp.bfloat16(0.125)
    query_copy = to_mate(row_query_ref.at[my_rows], row_query_ref.at[my_rows], 1)
    query_copy.start()
    gather.run_until(48)
    query_copy.wait()

    frame_count = frames_ref.shape[1]

    def attend(clip, values_t, query, j):
        scores = dot(kv_vm[clip, :frame_count, columns(j)], query, NT)
        peak = jnp.max(scores, 0, keepdims=True)
        terms = jnp.exp(scores - peak)
        total = jnp.sum(terms, 0, keepdims=True)
        return dot(values_t, terms.astype(jnp.bfloat16), NN), peak, total

    def cross_pair(j, tick):
        values_t = kv_vm[0, :frame_count, columns(j + 6)].T
        mine = seg_ref[...] == 0
        for h in range(2):
            tick(h)
            rows = slice(h * 64, (h + 1) * 64)
            result, peak, total = attend(0, values_t[rows], one_head(row_query_ref[:, columns(j)], h), j)
            acc_ref[rows] = jnp.where(mine, result / total, 0.0)
            stat_ref[h:h + 1] = jnp.where(mine, peak, 0.0)
            stat_ref[2 + h:3 + h] = jnp.where(mine, total, 1.0)
        for clip in (1, 2):
            tick(clip + 1)
            values_t = kv_vm[clip, :frame_count, columns(j + 6)].T
            query_rows = jnp.where(
                group_ref[clip - 1:clip] == 0, row_query_ref[:128, columns(j)], row_query_ref[384:, columns(j)])
            result, peak, total = attend(clip, values_t, two_heads(query_rows), j)
            for h in range(2):
                rows, part = slice(h * 64, (h + 1) * 64), slice(h * 128, (h + 1) * 128)
                of_head = result[rows, part] / total[:, part]
                for spot in (0, 3):
                    cols = slice(spot * 128, (spot + 1) * 128)
                    mine = seg_ref[:, cols] == clip
                    acc_ref[rows, cols] = jnp.where(mine, of_head, acc_ref[rows, cols])
                    stat_ref[h:h + 1, cols] = jnp.where(mine, peak[:, part], stat_ref[h:h + 1, cols])
                    stat_ref[2 + h:3 + h, cols] = jnp.where(mine, total[:, part], stat_ref[2 + h:3 + h, cols])
        my_cols, mate_cols = columns(core, toks), columns(1 - core, toks)
        part_ref[j] = acc_ref[:, my_cols]
        part_stat_ref[j] = stat_ref[:, my_cols]
        give_ref[j] = acc_ref[:, mate_cols].astype(jnp.bfloat16)
        give_stat_ref[j] = stat_ref[:, mate_cols]

    loop_with(gather, 6, 48, 3, cross_pair, (0, 0.33, 0.66, 0.83))
    give_copy = to_mate(give_ref, take_ref, 2)
    give_copy.start()
    give_stat_copy = to_mate(give_stat_ref, take_stat_ref, 3)
    give_stat_copy.start()
    gather.run_until(1000)
    give_copy.wait()
    give_stat_copy.wait()

    def combine(j, carry):
        parts = []
        for h in range(2):
            rows = slice(h * 64, (h + 1) * 64)
            peak_a, peak_b = part_stat_ref[j, h:h + 1], take_stat_ref[j, h:h + 1]
            peak = jnp.maximum(peak_a, peak_b)
            share_a = part_stat_ref[j, 2 + h:3 + h] * jnp.exp(peak_a - peak)
            share_b = take_stat_ref[j, 2 + h:3 + h] * jnp.exp(peak_b - peak)
            total = share_a + share_b
            cross_lse_ref[j, h:h + 1] = peak + jnp.log(total)
            parts.append(part_ref[j, rows] * (share_a / total)
                         + take_ref[j, rows].astype(jnp.float32) * (share_b / total))
        mixed_ref[:, columns(j)] = jnp.concatenate(parts, 0).T
        return carry

    lax.fori_loop(0, 6, combine, 0)
    after_cross = after_self_ref[...] + dot(mixed_ref[...].astype(jnp.bfloat16), cqo_vm[:, width:], NN) + vec(11)
    after_cross_ref[...] = after_cross
    normed_three_ref[...] = norm_rows(after_cross, vec(4), vec(5)).astype(jnp.bfloat16)
    gather.run_until(1000)
    gather.need(4)
    gather.need(5)
    kv_store.wait()
    gather.finish()


def fused_forward(group, x, frames, bias, seg, small, self_w, cross_w, up_w, down_w):
    toks, width = x.shape
    clips, count = frames.shape[:2]
    low, full = jnp.bfloat16, jnp.float32
    pairs = width // 128
    vmem, hbm = pl.BlockSpec(memory_space=pltpu.VMEM), pl.BlockSpec(memory_space=pl.ANY)
    shape = jax.ShapeDtypeStruct
    outs = [
        (hbm, shape((32, 16, 128), low)), (hbm, shape((width, 2 * width), low)), (hbm, shape((width, 4 * width), low)),
        (hbm, shape((width, 2 * width), low)), (hbm, shape((width, 4 * width), low)),
        (hbm, shape((4 * width, width), low)),
        (hbm, shape((clips, width, 2 * width), low)),
        (vmem, shape((16, width), full)), (vmem, shape((toks, width), low)), (vmem, shape((toks, width), low)),
        (vmem, shape((2 * toks, 2 * width), low)), (vmem, shape((toks, width), full)),
        (vmem, shape((pairs, 2, toks), full)), (vmem, shape((toks, width), full)), (vmem, shape((toks, width), low)),
        (vmem, shape((2 * toks, width), low)), (vmem, shape((pairs, 2, toks), full)), (vmem, shape((toks, width), full)),
        (vmem, shape((toks, width), full)), (vmem, shape((toks, width), low)),
    ]
    return pl.pallas_call(
        forward_kernel,
        in_specs=[vmem] * 5 + [hbm] + [vmem] * 3 + [hbm],
        out_specs=tuple(spec for spec, _ in outs),
        out_shape=tuple(s for _, s in outs),
        scratch_shapes=[
            pltpu.VMEM((2, 24, 2 * width), low), pltpu.VMEM((2, 24, width), low), pltpu.VMEM((2, 48, 2 * width), low),
            pltpu.VMEM((2, 48, width), low), pltpu.VMEM((32, 16, 128), low),
            pltpu.VMEM((width, 2 * width), low), pltpu.VMEM((width, 4 * width), low), pltpu.VMEM((width, 2 * width), low),
            pltpu.VMEM((clips, width, 2 * width), low), pltpu.VMEM((128, 2 * toks), full), pltpu.VMEM((4, 2 * toks), full),
            pltpu.VMEM((pairs, 128, toks), full), pltpu.VMEM((pairs, 4, toks), full),
            pltpu.VMEM((pairs, 128, toks), low), pltpu.VMEM((pairs, 4, toks), full),
            pltpu.VMEM((pairs, 128, toks), low), pltpu.VMEM((pairs, 4, toks), full),
            pltpu.SemaphoreType.DMA((400,)), pltpu.SemaphoreType.DMA((6, 32)), pltpu.SemaphoreType.DMA((6,)),
            pltpu.SemaphoreType.DMA((2, 5)), pltpu.SemaphoreType.DMA((2, 4)), pltpu.SemaphoreType.DMA((2,)),
        ],
        compiler_params=pltpu.CompilerParams(collective_id=0, has_side_effects=True, vmem_limit_bytes=60 * 2**20),
        name="fused_forward",
    )(group, x, frames, bias, seg, small, self_w, cross_w, up_w, down_w)


class Scatter:
    def __init__(self, me, grads, outs, buffers, sems, times, after):
        self.me, self.grads, self.outs, self.buffers = me, grads, outs, buffers
        self.send_sem, self.own_sem, self.pair_sem, self.plane_sem, self.line_sem, self.free_sem = sems
        self.sends = {m: [] for m in range(len(grads))}
        self.count = 0
        self.order = me.line + [me.z]
        self.tasks = []
        for m, times_of in enumerate(times):
            for time, acts in zip(times_of, self.steps(m)):
                self.tasks.append((time, m, acts))
        for late, early in after.items():
            self.tasks = [
                (time, m, ([self.wait_free] if m == late and time == times[late][0] else []) + acts
                 + ([functools.partial(self.give_free, early)] if m == early and time == times[early][-1] else []))
                for time, m, acts in self.tasks
            ]
        self.tasks.sort(key=lambda entry: entry[:2])

    def give_free(self, m):
        for copy in self.sends.pop(m):
            copy.wait_send()
        for target in self.me.peers:
            pl.semaphore_signal(self.free_sem, inc=1, device_id=target, device_id_type=MESH)

    def wait_free(self):
        pl.semaphore_wait(self.free_sem, len(self.me.peers))

    def sender(self, m, src, dst, sem, target):
        copy = pltpu.make_async_remote_copy(
            src_ref=src, dst_ref=dst, send_sem=self.send_sem.at[self.count], recv_sem=sem, device_id=target,
            device_id_type=MESH)
        self.count += 1
        self.sends[m].append(copy)
        return copy.start

    def arrival(self, dst, sem):
        return pltpu.make_async_remote_copy(
            src_ref=dst, dst_ref=dst, send_sem=self.send_sem.at[0], recv_sem=sem, device_id=self.me.mate,
            device_id_type=MESH).wait_recv

    def steps(self, m):
        me, order = self.me, self.order
        grad, out = self.grads[m], self.outs[m]
        own, pair, plane_a, plane_b, plane_c, line = self.buffers[m]
        own_sem, pair_sem, plane_sem, line_sem = self.own_sem, self.pair_sem, self.plane_sem, self.line_sem

        def adder(dst, *others):
            def act():
                total = dst[...].astype(jnp.float32)
                for other in others:
                    total = total + other[...].astype(jnp.float32)
                dst[...] = total.astype(dst.dtype)
            return act

        loads = [
            pltpu.make_async_copy(grad.at[:, p, me.core], own, own_sem.at[m, k])
            for k, p in enumerate((me.p_diag, me.p_second, me.p_first, me.p))
        ]
        begin = [loads[0].start]
        for p in (me.p_diag, me.p_first, me.p_second, me.p):
            begin.append(self.sender(m, grad.at[:, p, 1 - me.core], pair.at[:, p], pair_sem.at[m, p], me.mate))
        diag, second, first, last = (
            [loads[k].wait, self.arrival(pair.at[:, p], pair_sem.at[m, p])]
            for k, p in enumerate((me.p_diag, me.p_second, me.p_first, me.p))
        )
        for z in order:
            diag += [adder(pair.at[z, me.p_diag], own.at[z]),
                     self.sender(m, pair.at[z, me.p_diag], plane_a.at[z], plane_sem.at[m, 0, z], me.second)]
            second += [adder(pair.at[z, me.p_second], own.at[z]),
                       self.sender(m, pair.at[z, me.p_second], plane_c.at[z], plane_sem.at[m, 2, z], me.second)]
            first += [self.arrival(plane_a.at[z], plane_sem.at[m, 0, z]),
                      adder(pair.at[z, me.p_first], own.at[z], plane_a.at[z]),
                      self.sender(m, pair.at[z, me.p_first], plane_b.at[z], plane_sem.at[m, 1, z], me.first)]
        diag.append(loads[1].start)
        second.append(loads[2].start)
        first.append(loads[3].start)
        for z in me.line:
            last += [self.arrival(plane_b.at[z], plane_sem.at[m, 1, z]),
                     self.arrival(plane_c.at[z], plane_sem.at[m, 2, z]),
                     adder(pair.at[z, me.p], own.at[z], plane_b.at[z], plane_c.at[z]),
                     self.sender(m, pair.at[z, me.p], line.at[me.z], line_sem.at[m, me.z], me.on_line(z))]

        def total():
            part = own[me.z].astype(jnp.float32) + pair[me.z, me.p].astype(jnp.float32)
            out[...] = part + plane_b[me.z].astype(jnp.float32) + plane_c[me.z].astype(jnp.float32)

        def from_line(source):
            def act():
                out[...] += line[source].astype(jnp.float32)
            return act

        final = [self.arrival(plane_b.at[me.z], plane_sem.at[m, 1, me.z]),
                 self.arrival(plane_c.at[me.z], plane_sem.at[m, 2, me.z]), total]
        for source in me.line[::-1]:
            final += [self.arrival(line.at[source], line_sem.at[m, source]), from_line(source)]
        return [begin, diag, second, first, last, final]

    def run(self, entry):
        for act in entry[2]:
            act()

    def run_until(self, time):
        while self.tasks and self.tasks[0][0] <= time:
            self.run(self.tasks.pop(0))

    def take_until(self, time):
        taken = []
        while self.tasks and self.tasks[0][0] <= time:
            taken.append(self.tasks.pop(0))
        return taken

    def finish(self):
        self.run_until(10**6)
        for copies in self.sends.values():
            for copy in copies:
                copy.wait_send()


def scatter_buffers(grad):
    leads = ((4,), (4, 4), (4,), (4,), (4,), (4,))
    return [pltpu.VMEM(lead + grad.shape[1:], grad.dtype) for lead in leads]


def scatter_sems(count):
    dma = pltpu.SemaphoreType.DMA
    return [dma((20 * count,)), dma((count, 4)), dma((count, 4)), dma((count, 3, 4)), dma((count, 4)),
            pltpu.SemaphoreType.REGULAR]


def scatter_view(grad):
    return grad.reshape((4, 4, 2) + grad.shape[1:])


BACK_TIMES = (
    (0, 8, 9, 20, 32, 44),
    (1, 20, 21, 34, 46, 58),
    (44, 54, 55, 68, 78, 88),
    (80, 85, 86, 94, 102, 110),
    (80.5, 86.0, 87.0, 95.0, 103.0, 111.5),
)


def norm_rows_back(values, gain, grad):
    average = jnp.mean(values, -1, keepdims=True)
    centred = values - average
    scale = lax.rsqrt(jnp.mean(centred * centred, -1, keepdims=True) + 1e-05)
    normed = centred * scale
    inner = grad * gain
    mean_inner = jnp.mean(inner, -1, keepdims=True)
    mean_both = jnp.mean(inner * normed, -1, keepdims=True)
    result = scale * (inner - mean_inner - normed * mean_both)
    return result, jnp.sum(grad * normed, 0, keepdims=True), jnp.sum(grad, 0, keepdims=True)


def backward_kernel(*refs):
    (group_ref, x_ref, bias_ref, seg_ref, vec_ref, gac_ref, mixed_ref, cross_lse_ref, row_query_ref, after_self_ref,
     attended_ref, self_lse_ref, query_ref, kv_row_ref, normed_one_ref, normed_two_ref, rows_ref, up_bias_ref, cqo_hbm,
     ckv_hbm, self_hbm, kv_hbm, frames_hbm, up_hbm, down_hbm) = refs[:25]
    (input_grad_ref, encoder_hbm, up_out, down_out, cross_out, self_out, small_out, dkv_hbm, cross_hbm,
     self_grad_hbm) = refs[25:35]
    scratch = refs[35:]
    up_buffers, down_buffers, cross_buffers, small_buffers = (scratch[k * 6:(k + 1) * 6] for k in range(4))
    sems, scratch = scratch[24:30], scratch[30:]
    (cross_vm, kv_vm, frame_ref, turned_ref, tile_ref, stage_ref, small_ref, row_grad_ref, row_stat_ref, acc_ref,
     own_ref, give_ref, take_ref, take_query_ref, cq_ref, qkv_ref, vec_grad_ref, load_sem, mate_sems, tile_sem,
     stage_sem) = scratch
    me = Place()
    core = me.core
    toks, width = x_ref.shape
    frames = frames_hbm.shape[1]
    clips = kv_hbm.shape[0]
    low, full = jnp.bfloat16, jnp.float32
    halves = [pltpu.make_async_copy(cqo_hbm.at[:, pl.ds(k * width, width)], cross_vm.at[k], load_sem.at[k])
              for k in range(2)]
    kv_load = pltpu.make_async_copy(kv_hbm, kv_vm, load_sem.at[2])
    for copy in (halves[1], kv_load, halves[0]):
        copy.start()
    me.greet()
    scatter = Scatter(
        me, (up_hbm, down_hbm, cross_hbm, self_grad_hbm, small_ref), (up_out, down_out, cross_out, self_out, small_out),
        (up_buffers, down_buffers, cross_buffers, up_buffers, small_buffers), sems, BACK_TIMES, {3: 0})
    scatter.run_until(1)

    def to_mate(src, dst, k):
        return pltpu.make_async_remote_copy(
            src_ref=src, dst_ref=dst, send_sem=mate_sems.at[0, k], recv_sem=mate_sems.at[1, k], device_id=me.mate,
            device_id_type=MESH)

    my_rows = pl.ds(pl.multiple_of(core * toks, toks), toks)
    my_cols = columns(core, toks)

    def head_rows(product, store):
        turned = product.T
        for h in range(2):
            store(h, jnp.sum(turned[h * 64:(h + 1) * 64], 0, keepdims=True))

    def tile_store(grad_hbm, slot, t):
        return pltpu.make_async_copy(tile_ref.at[slot], grad_hbm.at[:, :, :, :, columns(t, 256)], tile_sem.at[slot])

    def weight_tiles(grad_hbm, first_tile, count, tile, before=None):
        def turn(t, carry):
            slot = t % 2

            @pl.when(t >= 2)
            def _():
                tile_store(grad_hbm, slot, first_tile + t - 2).wait()

            value = tile(columns(t, 256))
            tile_ref[slot] = value.reshape(4, 4, 2, width // 32, 256).astype(low)
            tile_store(grad_hbm, slot, first_tile + t).start()
            return carry

        lax.fori_loop(0, count, turn, 0)
        for t in range(max(0, count - 2), count):
            tile_store(grad_hbm, t % 2, first_tile + t).wait()

    def product_tiles(grad_hbm, first_tile, left, right_ref):
        turned = left.T
        weight_tiles(grad_hbm, first_tile, right_ref.shape[1] // 256, lambda cols: dot(turned, right_ref[:, cols], NN))

    halves[1].wait()
    grad_cross = gac_ref[...].astype(low)
    grad_mixed = dot(grad_cross, cross_vm[1], NT).astype(low)
    row_grad_ref[my_rows] = grad_mixed
    grad_copy = to_mate(row_grad_ref.at[my_rows], row_grad_ref.at[my_rows], 0)
    grad_copy.start()
    for j in range(6):
        cols = slice(j * 128, (j + 1) * 128)
        product = grad_mixed[:, cols].astype(full) * mixed_ref[:, cols]
        row_stat_ref[j, 0:2, my_cols] = cross_lse_ref[j]

        def keep(h, row, j=j):
            row_stat_ref[j, 2 + h:3 + h, my_cols] = row

        head_rows(product, keep)
    stat_copy = to_mate(row_stat_ref.at[:, :, my_cols], row_stat_ref.at[:, :, my_cols], 1)
    stat_copy.start()
    cq_ref[...] = grad_cross
    product_tiles(cross_hbm, 9, mixed_ref[...].astype(low), cq_ref)
    kv_load.wait()
    scatter.run_until(5)
    grad_copy.wait()
    stat_copy.wait()

    def cross_pair(j, tick):
        def back(clip, keys_t, query, grad, lse, inner):
            weights = jnp.exp(dot(kv_vm[clip, :frames, columns(j)], query, NT) - lse)
            grad_v = dot(weights.astype(low), grad, NN)
            grad_s = (weights * (dot(kv_vm[clip, :frames, columns(j + 6)], grad, NT) - inner)).astype(low)
            return dot(keys_t, grad_s, NN), dot(grad_s, query, NN), grad_v

        keys_t = kv_vm[0, :frames, columns(j)].T
        mine = seg_ref[...] == 0
        grad_k = grad_v = None
        for h in range(2):
            tick(h)
            query, grad = one_head(row_query_ref[:, columns(j)], h), one_head(row_grad_ref[:, columns(j)], h)
            rows = slice(h * 64, (h + 1) * 64)
            acc_ref[rows], part_k, part_v = back(
                0, keys_t[rows], query, grad, jnp.where(mine, row_stat_ref[j, h:h + 1], 1e30),
                row_stat_ref[j, 2 + h:3 + h])
            grad_k = part_k if grad_k is None else grad_k + part_k
            grad_v = part_v if grad_v is None else grad_v + part_v
        kv_vm[0, :frames, columns(j)] = grad_k.astype(low)
        kv_vm[0, :frames, columns(j + 6)] = grad_v.astype(low)
        for clip in (1, 2):
            tick(clip + 1)
            in_first = group_ref[clip - 1:clip] == 0

            def chosen(ref):
                return two_heads(jnp.where(in_first, ref[:128, columns(j)], ref[384:, columns(j)]))

            def chosen_row(row):
                return jnp.where(in_first, row_stat_ref[j, row:row + 1, :128], row_stat_ref[j, row:row + 1, 384:])

            mine = jnp.where(in_first, seg_ref[:, :128], seg_ref[:, 384:]) == clip
            lse = jnp.concatenate([jnp.where(mine, chosen_row(h), 1e30) for h in range(2)], 1)
            inner = jnp.concatenate([chosen_row(2 + h) for h in range(2)], 1)
            grad_q, grad_k, grad_v = back(
                clip, kv_vm[clip, :frames, columns(j)].T, chosen(row_query_ref), chosen(row_grad_ref), lse, inner)
            for h in range(2):
                rows, part = slice(h * 64, (h + 1) * 64), slice(h * 128, (h + 1) * 128)
                for spot in (0, 3):
                    cols = slice(spot * 128, (spot + 1) * 128)
                    acc_ref[rows, cols] += jnp.where(in_first == (spot == 0), grad_q[rows, part], 0.0)
            kv_vm[clip, :frames, columns(j)] = grad_k.astype(low)
            kv_vm[clip, :frames, columns(j + 6)] = grad_v.astype(low)
        own_ref[:, columns(j)] = (acc_ref[:, my_cols] * 0.125).T
        give_ref[:, columns(j)] = (acc_ref[:, columns(1 - core, toks)] * 0.125).T.astype(low)

    loop_with(scatter, 6, 6, 4, cross_pair, (0, 0.33, 0.66, 0.83))
    query_copy = to_mate(give_ref.at[:, pl.ds(0, width)], take_query_ref, 2)
    query_copy.start()
    dkv_store = pltpu.make_async_copy(kv_vm, dkv_hbm, load_sem.at[2])
    dkv_store.start()
    vec_grad_ref[...] = rows_ref[...]
    vec_grad_ref[10:11] = sum(
        jnp.sum(kv_vm[clip, :frames, width:].astype(full), 0, keepdims=True) for clip in range(clips))
    for clip in range(clips):
        copy = pltpu.make_async_copy(frames_hbm.at[clip], frame_ref, load_sem.at[3])
        copy.start()
        copy.wait()
        turned_ref[clip] = frame_ref[...].T
    scatter.run_until(37)

    def frames_tile(cols):
        total = dot(turned_ref[0], kv_vm[0, :frames, cols], NN)
        for clip in range(1, clips):
            total = total + dot(turned_ref[clip], kv_vm[clip, :frames, cols], NN)
        return total

    weight_tiles(cross_hbm, 3, 6, frames_tile)
    halves[0].wait()
    query_copy.wait()
    grad_query = (own_ref[:, :width] + take_query_ref[...].astype(full)).astype(low)
    cq_ref[...] = grad_query
    product_tiles(cross_hbm, 0, normed_two_ref[...], cq_ref)
    dkv_store.wait()
    self_loads = [
        pltpu.make_async_copy(
            self_hbm.at[:, pl.ds(k * 2 * width, 2 * width)], kv_vm.at[k], load_sem.at[2 + k]) for k in range(2)
    ]
    for copy in self_loads:
        copy.start()
    scatter.run_until(46)
    vec_grad_ref[9:10] = jnp.sum(grad_query.astype(full), 0, keepdims=True)
    grad_part, gain, shift = norm_rows_back(after_self_ref[...], vec_ref[2:3], dot(grad_query, cross_vm[0], NT))
    vec_grad_ref[2:3] = gain
    vec_grad_ref[3:4] = shift
    grad_after_self = gac_ref[...] + grad_part
    input_grad_ref[...] = grad_after_self
    grad_low = grad_after_self.astype(low)
    vec_grad_ref[8:9] = jnp.sum(grad_low.astype(full), 0, keepdims=True)
    for copy in self_loads:
        copy.wait()
    grad_attended = dot(grad_low, kv_vm[1, :width, width:], NT).astype(low)
    row_grad_ref[:toks] = grad_attended
    for j in range(6):
        cols = slice(j * 128, (j + 1) * 128)

        def keep_self(h, row, j=j):
            row_stat_ref[j, h:h + 1, :toks] = row

        head_rows(grad_attended[:, cols].astype(full) * attended_ref[:, cols], keep_self)

    def self_pair(j, tick):
        tick(0)
        cols, value_cols = columns(j), columns(j + 6)
        keys, values = kv_row_ref[:, cols], kv_row_ref[:, value_cols]
        keys_t = keys.T
        grad_k = grad_v = None
        parts = []
        for h in range(2):
            query, grad = one_head(query_ref[:, cols], h), one_head(row_grad_ref[:toks, cols], h)
            weights = jnp.exp(dot(keys, query, NT) + bias_ref[...] - self_lse_ref[j, h:h + 1])
            part = dot(weights.astype(low), grad, NN)
            grad_v = part if grad_v is None else grad_v + part
            inner = row_stat_ref[j, h:h + 1, :toks]
            grad_s = (weights * (dot(values, grad, NT) - inner)).astype(low)
            part = dot(grad_s, query, NN)
            grad_k = part if grad_k is None else grad_k + part
            parts.append(dot(keys_t[h * 64:(h + 1) * 64], grad_s, NN))
        qkv_ref[:, cols] = (jnp.concatenate(parts, 0) * 0.125).T.astype(low)
        own_ref[:, cols] = grad_k[toks:]
        own_ref[:, value_cols] = grad_v[toks:]
        give_ref[:, cols] = grad_k[:toks].astype(low)
        give_ref[:, value_cols] = grad_v[:toks].astype(low)

    loop_with(scatter, 6, 52, 1.4, self_pair)
    row_copy = to_mate(give_ref, take_ref, 3)
    row_copy.start()
    cq_ref[...] = grad_low
    product_tiles(self_grad_hbm, 9, attended_ref[...].astype(low), cq_ref)
    scatter.run_until(62)
    row_copy.wait()
    qkv_ref[:, width:] = (own_ref[...] + take_ref[...].astype(full)).astype(low)
    product_tiles(self_grad_hbm, 0, normed_one_ref[...], qkv_ref)
    sums = jnp.sum(qkv_ref[...].astype(full), 0, keepdims=True)
    vec_grad_ref[6:7] = sums[:, :width]
    vec_grad_ref[7:8] = sums[:, 2 * width:]
    grad_normed = dot(qkv_ref[:, :2 * width], kv_vm[0, :width], NT) + dot(
        qkv_ref[:, 2 * width:], kv_vm[1, :width, :width], NT)
    grad_part, gain, shift = norm_rows_back(x_ref[...].astype(full), vec_ref[0:1], grad_normed)
    vec_grad_ref[0:1] = gain
    vec_grad_ref[1:2] = shift
    input_grad_ref[...] += grad_part
    kv_load = pltpu.make_async_copy(dkv_hbm, kv_vm, load_sem.at[2])
    kv_load.start()
    for k in range(2):
        pltpu.make_async_copy(ckv_hbm.at[:, pl.ds(k * width, width)], cross_vm.at[k], load_sem.at[k]).start()
    small_ref[...] = jnp.zeros_like(small_ref)
    rows = vec_grad_ref[...]
    for d in range(32):
        place = (d // 8, d // 2 % 4, d % 2)
        turned_rows = rows if d == 0 else pltpu.roll(rows, width - d * 24, 1)
        small_ref[place] = turned_rows[:, :128]
        small_ref[place + (slice(13, 14),)] = up_bias_ref[d:d + 1]
    scatter.run_until(70)
    for k in range(2):
        pltpu.make_async_copy(ckv_hbm.at[:, pl.ds(k * width, width)], cross_vm.at[k], load_sem.at[k]).wait()
    kv_load.wait()
    tiles = width // 256

    def encoder_store(slot, t):
        return pltpu.make_async_copy(
            stage_ref.at[slot], encoder_hbm.at[t // tiles, :, columns(t % tiles, 256)], stage_sem.at[slot])

    def encoder_tile(t, tick):
        tick(0)
        clip, tile, slot = t // tiles, t % tiles, t % 2

        @pl.when(t >= 2)
        def _():
            encoder_store(slot, t - 2).wait()

        cols = columns(tile, 256)
        stage_ref[slot] = dot(kv_vm[clip, :frames, :width], cross_vm[0, cols], NT) + dot(
            kv_vm[clip, :frames, width:], cross_vm[1, cols], NT)
        encoder_store(slot, t).start()

    loop_with(scatter, clips * tiles, 71, 0.8, encoder_tile)
    for t in range(clips * tiles - 2, clips * tiles):
        encoder_store(t % 2, t).wait()
    scatter.finish()


def fused_backward(group, x, bias, seg, vec, gac, mixed, cross_lse, row_query, after_self, attended, self_lse, query,
                   kv_row, normed_one, normed_two, rows, up_bias, cqo_full, ckv_full, self_full, kv, frames, grad_up,
                   grad_down):
    toks, width = x.shape
    clips, count = frames.shape[:2]
    low, full = jnp.bfloat16, jnp.float32
    pairs = width // 128
    vmem, hbm = pl.BlockSpec(memory_space=pltpu.VMEM), pl.BlockSpec(memory_space=pl.ANY)
    shape = jax.ShapeDtypeStruct
    small = shape((32, 16, 128), full)
    wide = (4, 4, 2, width // 32, 4 * width)
    outs = [
        (vmem, shape((toks, width), full)), (hbm, shape(frames.shape, full)), (vmem, shape(grad_up.shape[1:], full)),
        (vmem, shape(grad_down.shape[1:], full)), (vmem, shape(grad_up.shape[1:], full)),
        (vmem, shape(grad_up.shape[1:], full)), (vmem, shape(small.shape[1:], full)), (hbm, shape(kv.shape, low)),
        (hbm, shape(wide, low)), (hbm, shape(wide, low)),
    ]
    return pl.pallas_call(
        backward_kernel,
        in_specs=[vmem] * 18 + [hbm] * 7,
        out_specs=tuple(spec for spec, _ in outs),
        out_shape=tuple(s for _, s in outs),
        scratch_shapes=scatter_buffers(grad_up) + scatter_buffers(grad_down) + scatter_buffers(grad_up)
        + scatter_buffers(small) + scatter_sems(5) + [
            pltpu.VMEM((2, width, width), low), pltpu.VMEM((clips, width, 2 * width), low),
            pltpu.VMEM((count, width), low), pltpu.VMEM((clips, width, count), low),
            pltpu.VMEM((2,) + wide[:4] + (256,), low), pltpu.VMEM((2, count, 256), full),
            pltpu.VMEM((4, 4, 2, 16, 128), full), pltpu.VMEM((2 * toks, width), low),
            pltpu.VMEM((pairs, 4, 2 * toks), full), pltpu.VMEM((128, 2 * toks), full),
            pltpu.VMEM((toks, 2 * width), full), pltpu.VMEM((toks, 2 * width), low),
            pltpu.VMEM((toks, 2 * width), low), pltpu.VMEM((toks, width), low), pltpu.VMEM((toks, width), low),
            pltpu.VMEM((toks, 3 * width), low), pltpu.VMEM((16, width), full), pltpu.SemaphoreType.DMA((4,)),
            pltpu.SemaphoreType.DMA((2, 4)), pltpu.SemaphoreType.DMA((2,)), pltpu.SemaphoreType.DMA((2,)),
        ],
        compiler_params=pltpu.CompilerParams(collective_id=2, has_side_effects=True, vmem_limit_bytes=63 * 2**20),
        name="fused_backward",
    )(group, x, bias, seg, vec, gac, mixed, cross_lse, row_query, after_self, attended, self_lse, query, kv_row,
      normed_one, normed_two, rows, up_bias, cqo_full, ckv_full, self_full, kv, frames, scatter_view(grad_up),
      scatter_view(grad_down))


def ffn_kernel(normed_ref, grad_ref, after_ref, vec_ref, up_ref, bias_ref, down_ref, out_ref, back_ref, grad_up_ref,
               grad_down_ref, grad_bias_ref, rows_ref, turned_ref, sum_ref, back_sum_ref):
    t = pl.program_id(0)

    @pl.when(t == 0)
    def _():
        turned_ref[...] = normed_ref[...].T
        sum_ref[...] = jnp.zeros_like(sum_ref)
        back_sum_ref[...] = jnp.zeros_like(back_sum_ref)

    grad = grad_ref[...]
    pre = dot(normed_ref[...], up_ref[...], NN) + bias_ref[...]
    below = 0.5 * (1.0 + lax.erf(pre * 0.7071067811865476))
    activated = (pre * below).astype(jnp.bfloat16)
    sum_ref[...] += dot(activated, down_ref[...], NN)
    grad_act = dot(grad, down_ref[...], NT).astype(jnp.bfloat16).astype(jnp.float32)
    density = jnp.exp(-0.5 * pre * pre) * 0.3989422804014327
    grad_pre = (grad_act * (below + pre * density)).astype(jnp.bfloat16)
    back_sum_ref[...] += dot(grad_pre, up_ref[...], NT)
    grad_up_ref[...] = dot(turned_ref[...], grad_pre, NN).astype(jnp.bfloat16)
    grad_down_ref[...] = dot(activated.T, grad, NN).astype(jnp.bfloat16)
    grad_bias_ref[...] = jnp.sum(grad_pre.astype(jnp.float32), 0, keepdims=True)

    @pl.when(t == pl.num_programs(0) - 1)
    def _():
        out_ref[...] = (after_ref[...] + sum_ref[...] + vec_ref[12:13]).astype(jnp.bfloat16)
        grad_rows = grad_ref[...].astype(jnp.float32)
        part, gain, shift = norm_rows_back(after_ref[...], vec_ref[4:5], back_sum_ref[...])
        back = grad_rows + part
        back_ref[...] = back
        rows_ref[...] = jnp.zeros_like(rows_ref)
        rows_ref[4:5] = gain
        rows_ref[5:6] = shift
        rows_ref[11:12] = jnp.sum(back.astype(jnp.bfloat16).astype(jnp.float32), 0, keepdims=True)
        rows_ref[12:13] = jnp.sum(grad_rows, 0, keepdims=True)


def ffn(normed, grad, after, vec, up_full, bias, down_full):
    toks, width = normed.shape
    hidden = up_full.shape[1]
    size = 256
    low, full = jnp.bfloat16, jnp.float32
    shape = jax.ShapeDtypeStruct
    rows = pl.BlockSpec((toks, width), lambda t: (0, 0))
    vecs = pl.BlockSpec((16, width), lambda t: (0, 0))
    up_spec = pl.BlockSpec((width, size), lambda t: (0, t))
    down_spec = pl.BlockSpec((size, width), lambda t: (t, 0))
    bias_spec = pl.BlockSpec((1, size), lambda t: (0, t))
    return pl.pallas_call(
        ffn_kernel,
        grid=(hidden // size,),
        in_specs=[rows, rows, rows, vecs, up_spec, bias_spec, down_spec],
        out_specs=[rows, rows, up_spec, down_spec, bias_spec, vecs],
        out_shape=[
            shape((toks, width), low), shape((toks, width), full), shape(up_full.shape, low),
            shape(down_full.shape, low), shape((1, hidden), full), shape((16, width), full),
        ],
        scratch_shapes=[pltpu.VMEM((width, toks), low), pltpu.VMEM((toks, width), full), pltpu.VMEM((toks, width), full)],
        compiler_params=pltpu.CompilerParams(vmem_limit_bytes=48 * 2**20),
        name="ffn",
    )(normed, grad, after, vec, up_full, bias, down_full)


def place_clips_kernel(order, in_ref, out_ref):
    frames, width = in_ref.shape[1:]
    blocks = width // 128
    for k in range(blocks):
        out_ref[pl.ds(k, frames, stride=blocks), 0] = in_ref[0, :, k * 128:(k + 1) * 128]


def place_clips(order, values):
    clips, frames, width = values.shape
    rows = frames * width // 128
    flat = pl.pallas_call(
        place_clips_kernel,
        grid_spec=pltpu.PrefetchScalarGridSpec(
            num_scalar_prefetch=1,
            grid=(clips,),
            in_specs=[pl.BlockSpec((1, frames, width), lambda k, order: (k, 0, 0))],
            out_specs=pl.BlockSpec((rows, 1, 128), lambda k, order: (order[k], 0, 0)),
        ),
        out_shape=jax.ShapeDtypeStruct((clips * rows, 1, 128), values.dtype),
        compiler_params=pltpu.CompilerParams(vmem_limit_bytes=48 * 2**20),
        name="place_clips",
    )(order, values)
    return flat.reshape(1, clips, frames, width)


def from_behind(value, axis, steps):
    count = lax.axis_size(axis)
    leading, last = (max(0, -steps), min(count, count - steps))
    return lax.ppermute(value, axis, [(source, source + steps) for source in range(leading, last)])


def layer_norm(values, gain, shift):
    average = jnp.mean(values, -1, keepdims=True)
    centred = values - average
    spread = jnp.mean(centred * centred, -1, keepdims=True)
    return centred * lax.rsqrt(spread + 1e-05) * gain + shift


def matmul(left, right):
    return jnp.dot(left, right, preferred_element_type=jnp.float32)


def swap_halves(value):
    return lax.ppermute(value, "seq", [(0, 1), (1, 0)])


def seq_halves(value, axis):
    span = value.shape[axis] // 2
    half = lax.axis_index("seq")
    mine = lax.dynamic_slice_in_dim(value, half * span, span, axis)
    other = lax.dynamic_slice_in_dim(value, (1 - half) * span, span, axis)
    return mine, other


def seq_scatter(value):
    mine, other = seq_halves(value, 0)
    return mine + swap_halves(other.astype(jnp.bfloat16)).astype(value.dtype)


def per_head(values):
    rows = values.reshape(-1, values.shape[2]).T
    return jnp.repeat(rows, HEAD_DIM, axis=1)


def head_sums(values):
    sums = jnp.sum(values.reshape(values.shape[0], -1, HEAD_DIM), -1)
    return sums.T.reshape(-1, 2, values.shape[0])


def plain_forward(
    which, layer_input, frames, mask_bias, row_segment, weights
):
    self_full, cross_full, up_full, down_full, bias_full, out_bias_full, vectors = (
        lax.all_gather(part, ("dp", "seq"), axis=0, tiled=True) for part in weights
    )
    vec = jnp.pad(
        jnp.concatenate([vectors.T, out_bias_full[None]]).astype(jnp.float32), ((0, 3), (0, 0))
    )
    model_width = layer_input.shape[1]
    cross_in = [cross_full[:, k * model_width : (k + 1) * model_width] for k in range(4)]
    ckv_full = cross_full[:, model_width : 3 * model_width]
    cqo_full = jnp.concatenate([cross_in[0], cross_in[3]], 1)
    source = layer_input.astype(jnp.float32)
    normed_one = layer_norm(source, vec[0], vec[1]).astype(jnp.bfloat16)
    proj_bias = jnp.concatenate([vec[6], jnp.zeros_like(vec[6]), vec[7]])
    qkv_low = (matmul(normed_one, self_full[:, : 3 * model_width]) + proj_bias).astype(jnp.bfloat16)
    query = qkv_low[:, :model_width] * jnp.bfloat16(0.125)
    kv_own = qkv_low[:, model_width:]
    kv_row = jnp.concatenate([from_behind(kv_own, "seq", 1), kv_own])
    attended, self_lse = self_forward(query, kv_row, mask_bias)
    attended_low = attended.astype(jnp.bfloat16)
    after_self = source + matmul(attended_low, self_full[:, 3 * model_width :]) + vec[8]
    normed_two = layer_norm(after_self, vec[2], vec[3]).astype(jnp.bfloat16)
    cross_query = (matmul(normed_two, cross_in[0]) + vec[9]).astype(jnp.bfloat16)
    cross_key = jnp.einsum(
        "cfd,de->cfe", frames, cross_in[1], preferred_element_type=jnp.float32
    ).astype(jnp.bfloat16)
    cross_value = (
        jnp.einsum("cfd,de->cfe", frames, cross_in[2], preferred_element_type=jnp.float32)
        + vec[10]
    ).astype(jnp.bfloat16)
    row_query = lax.all_gather(cross_query * jnp.bfloat16(0.125), "seq", axis=0, tiled=True)
    cross_kv = jnp.concatenate([cross_key, cross_value], 2)
    part_mixed, part_stats = cross_forward(which, row_query, cross_kv, row_segment)
    mixed_mine, mixed_other = seq_halves(part_mixed, 0)
    stats_mine, stats_other = seq_halves(part_stats, 2)
    mixed_came = swap_halves(mixed_other.astype(jnp.bfloat16))
    stats_came = swap_halves(stats_other)
    peak = jnp.maximum(stats_mine[:, :2], stats_came[:, :2])
    share_mine = stats_mine[:, 2:] * jnp.exp(stats_mine[:, :2] - peak)
    share_came = stats_came[:, 2:] * jnp.exp(stats_came[:, :2] - peak)
    total = share_mine + share_came
    cross_lse = peak + jnp.log(total)
    mixed_full = mixed_mine * per_head(share_mine / total) + mixed_came.astype(
        jnp.float32
    ) * per_head(share_came / total)
    mixed = mixed_full.astype(jnp.bfloat16)
    after_cross = after_self + matmul(mixed, cross_in[3]) + vec[11]
    normed_three = layer_norm(after_cross, vec[4], vec[5]).astype(jnp.bfloat16)
    return (
        bias_full, ckv_full, self_full, cqo_full, up_full, down_full, cross_kv, vec, normed_one, query, kv_row, attended,
        self_lse, after_self, normed_two, row_query, cross_lse, mixed_full, after_cross, normed_three,
    )


def forward(which, layer_input, frames, mask_bias, row_segment, weights):
    if lax.axis_size("dp") != 16:
        return plain_forward(which, layer_input, frames, mask_bias, row_segment, weights)
    self_weights, cross_weights, up_weights, down_weights, up_bias, down_bias, vectors = weights

    def as_row(values):
        return jnp.pad(values, ((0, 0), (0, 128 - values.shape[1])))

    small = jnp.concatenate(
        [as_row(vectors.T), as_row(down_bias[None]), as_row(up_bias[None]), jnp.zeros((2, 128), vectors.dtype)]
    )
    group = jnp.broadcast_to(which[:, None], (2, 128))
    whole = fused_forward(
        group, layer_input, frames, mask_bias, row_segment, small, self_weights, cross_weights, up_weights,
        down_weights,
    )
    return (whole[0][:, 13, : up_bias.shape[0]].reshape(-1),) + tuple(whole[1:])


def plain_backward(
    which, layer_input, mask_bias, row_segment, vec, grad_after_cross, mixed_full, cross_lse, row_query, after_self,
    attended, self_lse, query, kv_row, cqo_full, self_full, cross_kv
):
    tok_span, model_width = layer_input.shape
    source = layer_input.astype(jnp.float32)
    grad_cross_low = grad_after_cross.astype(jnp.bfloat16)
    grad_mixed = matmul(grad_cross_low, cqo_full[:, model_width:].T).astype(jnp.bfloat16)
    row_grad = lax.all_gather(grad_mixed, "seq", axis=0, tiled=True)
    cross_inner = head_sums(grad_mixed.astype(jnp.float32) * mixed_full)
    row_stats = lax.all_gather(jnp.stack([cross_lse, cross_inner]), "seq", axis=3, tiled=True)
    part_query, grad_key, grad_value = cross_backward(
        which, row_query, cross_kv, row_segment, row_stats[0], row_stats[1], row_grad
    )
    grad_query_sum = seq_scatter(part_query).astype(jnp.bfloat16)
    grad_cq_bias = jnp.sum(grad_query_sum, 0, dtype=jnp.float32)
    grad_normed_two = matmul(grad_query_sum, cqo_full[:, :model_width].T)
    grad_cv_bias = jnp.sum(grad_value, (0, 1), dtype=jnp.float32)
    _, norm_pull_two = jax.vjp(layer_norm, after_self, vec[2], vec[3])
    grad_part, grad_gain_two, grad_shift_two = norm_pull_two(grad_normed_two)
    grad_after_self = grad_after_cross + grad_part
    grad_self_low = grad_after_self.astype(jnp.bfloat16)
    grad_self_bias = jnp.sum(grad_self_low, 0, dtype=jnp.float32)
    grad_attended = matmul(grad_self_low, self_full[:, 3 * model_width :].T).astype(jnp.bfloat16)
    self_inner = head_sums(grad_attended.astype(jnp.float32) * attended)
    grad_query, grad_key_row, grad_value_row = self_backward(
        query, kv_row, mask_bias, self_lse, self_inner, grad_attended
    )
    grad_kv = jnp.concatenate([grad_key_row, grad_value_row], 1)
    back_kv = from_behind(grad_kv[:tok_span].astype(jnp.bfloat16), "seq", -1)
    grad_qkv_low = jnp.concatenate(
        [grad_query, grad_kv[tok_span:] + back_kv.astype(jnp.float32)], 1
    ).astype(jnp.bfloat16)
    grad_qkv_bias = jnp.sum(grad_qkv_low, 0, dtype=jnp.float32)
    grad_normed_one = matmul(grad_qkv_low, self_full[:, : 3 * model_width].T)
    _, norm_pull_one = jax.vjp(layer_norm, source, vec[0], vec[1])
    grad_part, grad_gain_one, grad_shift_one = norm_pull_one(grad_normed_one)
    input_grad = grad_after_self + grad_part
    nothing = jnp.zeros_like(grad_cq_bias)
    vec_grads = jnp.stack(
        [
            grad_gain_one,
            grad_shift_one,
            grad_gain_two,
            grad_shift_two,
            nothing,
            nothing,
            grad_qkv_bias[:model_width],
            grad_qkv_bias[2 * model_width :],
            grad_self_bias,
            grad_cq_bias,
            grad_cv_bias,
        ]
        + [nothing] * 5
    )
    return (
        input_grad, grad_query_sum, grad_self_low, grad_qkv_low, vec_grads,
        jnp.concatenate([grad_key, grad_value], 2),
    )


def plain_finish(
    normed_one, grad_qkv_low, attended_low, grad_self_low, normed_two, grad_query_sum, mixed, grad_cross_low, frames,
    cross_kv_grad, ckv_full
):
    width = normed_one.shape[1]
    grads_self = jnp.concatenate([matmul(normed_one.T, grad_qkv_low), matmul(attended_low.T, grad_self_low)], 1)
    grad_ckv = jnp.einsum("cfd,cfe->de", frames, cross_kv_grad, preferred_element_type=jnp.float32)
    grads_cross = jnp.concatenate(
        [matmul(normed_two.T, grad_query_sum), grad_ckv, matmul(mixed.T, grad_cross_low)], 1
    )
    encoder_grad = jnp.einsum(
        "cfe,de->cfd", cross_kv_grad, ckv_full, preferred_element_type=jnp.float32
    )
    return encoder_grad, (grads_self, grads_cross)


def per_device(
    layer_input,
    encoder_states,
    clip_lengths,
    out_grad,
    self_weights,
    cross_weights,
    up_weights,
    down_weights,
    up_bias,
    down_bias,
    vectors,
):
    model_width = layer_input.shape[2]
    tok_span = layer_input.shape[1]
    seq_half = lax.axis_index("seq")
    source = layer_input[0].astype(jnp.float32)
    position = seq_half * tok_span + jnp.arange(tok_span, dtype=jnp.int32)
    clip_ends = jnp.cumsum(clip_lengths[0])
    segment = jnp.sum((position[:, None] >= clip_ends[None, :]).astype(jnp.int32), 1)
    key_position = jnp.concatenate([position - tok_span, position])
    key_segment = jnp.sum((key_position[:, None] >= clip_ends[None, :]).astype(jnp.int32), 1)
    allowed = (
        (key_segment[:, None] == segment[None, :])
        & (key_position[:, None] <= position[None, :])
        & (key_position[:, None] >= 0)
    )
    mask_bias = jnp.where(allowed, 0.0, -1e30).astype(jnp.float32)
    row_position = jnp.arange(2 * tok_span, dtype=jnp.int32)
    row_segment = jnp.sum((row_position[:, None] >= clip_ends[None, :]).astype(jnp.int32), 1)[None]
    big = jnp.argmax(clip_lengths[0]).astype(jnp.int32)
    small_one = jnp.where(big == 0, 1, 0)
    small_two = jnp.where(big == 2, 1, 2)
    last_group = 2 * tok_span // 128 - 1
    order = jnp.stack([big, small_one, small_two]).astype(jnp.int32)
    row_segment = jnp.where(
        row_segment == order[0], 0, jnp.where(row_segment == order[1], 1, jnp.where(row_segment == order[2], 2, 3))
    )
    which = jnp.where(order[1:] < big, 0, last_group).astype(jnp.int32)

    frames = jnp.take(encoder_states[0], order, axis=0, mode="clip")
    (
        bias_full, ckv_full, self_full, cqo_full, up_full, down_full, cross_kv, vec, normed_one, query, kv_row, attended,
        self_lse, after_self, normed_two, row_query, cross_lse, mixed_full, after_cross, normed_three,
    ) = forward(
        which, layer_input[0], frames, mask_bias, row_segment,
        (self_weights, cross_weights, up_weights, down_weights, up_bias, down_bias, vectors),
    )
    bias_full = bias_full.astype(jnp.float32)
    layer_output, grad_after_cross, grad_up, grad_down, grad_up_bias, ffn_rows = ffn(
        normed_three, out_grad[0], after_cross, vec, up_full, bias_full[None], down_full
    )
    operands = (
        layer_input[0], mask_bias, row_segment, vec, grad_after_cross, mixed_full, cross_lse, row_query, after_self,
        attended, self_lse, query, kv_row,
    )
    if lax.axis_size("dp") == 16:
        group = jnp.broadcast_to(which[:, None], (2, 128))
        large = [g.reshape(32, -1, g.shape[1]) for g in (grad_up, grad_down)]
        bias_rows = jnp.pad(grad_up_bias.reshape(32, -1), ((0, 0), (0, 128 - up_bias.shape[0])))
        input_grad, encoder_grad, up_share, down_share, cross_share, self_share, row, *_ = fused_backward(
            group, *operands, normed_one, normed_two, ffn_rows, bias_rows, cqo_full, ckv_full, self_full, cross_kv, frames,
            *large
        )
        shares = (
            self_share, cross_share, up_share, down_share, row[13, : up_bias.shape[0]], row[12, : down_bias.shape[0]],
            row[:12, : vectors.shape[0]].T,
        )
    else:
        input_grad, grad_query_sum, grad_self_low, grad_qkv_low, vec_grads, cross_kv_grad = plain_backward(
            which, *operands, cqo_full, self_full, cross_kv
        )
        encoder_grad, large = plain_finish(
            normed_one, grad_qkv_low, attended.astype(jnp.bfloat16), grad_self_low, normed_two, grad_query_sum,
            mixed_full.astype(jnp.bfloat16), grad_after_cross.astype(jnp.bfloat16), frames, cross_kv_grad, ckv_full,
        )
        vector_grads = vec_grads + ffn_rows
        shares = tuple(
            lax.psum_scatter(part, ("dp", "seq"), scatter_dimension=0, tiled=True)
            for part in large
            + (grad_up.astype(jnp.float32), grad_down.astype(jnp.float32), grad_up_bias[0], vector_grads[12],
               vector_grads[:12].T)
        )
    return (layer_output[None], input_grad[None], place_clips(order, encoder_grad)) + shares


def solution(mesh):
    return jax.shard_map(
        per_device,
        mesh=mesh,
        in_specs=(
            P("dp", "seq", None),
            P("dp", None, "seq", None),
            P("dp", None),
            P("dp", "seq", None),
            P(("dp", "seq"), None),
            P(("dp", "seq"), None),
            P(("dp", "seq"), None),
            P(("dp", "seq"), None),
            P(("dp", "seq")),
            P(("dp", "seq")),
            P(("dp", "seq"), None),
        ),
        out_specs=(
            P("dp", "seq", None),
            P("dp", "seq", None),
            P("dp", None, "seq", None),
            P(("dp", "seq"), None),
            P(("dp", "seq"), None),
            P(("dp", "seq"), None),
            P(("dp", "seq"), None),
            P(("dp", "seq")),
            P(("dp", "seq")),
            P(("dp", "seq"), None),
        ),
        check_vma=False,
    )
```

```python
import functools

import jax
import jax.numpy as jnp
from jax import lax
from jax.experimental import pallas as pl
from jax.experimental.pallas import tpu as pltpu
from jax.sharding import PartitionSpec as P

HEAD_DIM = 64
CLIPS = 3
MESH = pl.DeviceIdType.MESH
NT = (((1,), (1,)), ((), ()))
NN = (((1,), (0,)), ((), ()))


def dot(left, right, dims):
    return lax.dot_general(left, right, dims, preferred_element_type=jnp.float32)


def one_head(values, h):
    lane = lax.broadcasted_iota(jnp.int32, values.shape, 1)
    return jnp.where((lane >= 64) == (h == 1), values, jnp.zeros_like(values))


def self_forward_kernel(q_ref, k_ref, v_ref, bias_ref, out_ref, lse_ref):
    keys = k_ref[...]
    values_t = v_ref[...].T
    halves = []
    for h in range(2):
        scores = dot(keys, one_head(q_ref[...], h), NT) + bias_ref[...]
        peak = jnp.max(scores, 0, keepdims=True)
        terms = jnp.exp(scores - peak)
        total = jnp.sum(terms, 0, keepdims=True)
        result = dot(values_t[h * 64:(h + 1) * 64], terms.astype(jnp.bfloat16), NN)
        halves.append(result / total)
        lse_ref[0, h:h + 1] = peak + jnp.log(total)
    out_ref[...] = jnp.concatenate(halves, 0).T.astype(out_ref.dtype)


def self_forward(q, kv, bias):
    toks, width = q.shape
    keys, pairs = kv.shape[0], width // 128
    return pl.pallas_call(
        self_forward_kernel,
        grid=(width // 128,),
        in_specs=[
            pl.BlockSpec((toks, 128), lambda j: (0, j)),
            pl.BlockSpec((keys, 128), lambda j: (0, j)),
            pl.BlockSpec((keys, 128), lambda j: (0, j + pairs)),
            pl.BlockSpec((keys, toks), lambda j: (0, 0)),
        ],
        out_specs=[
            pl.BlockSpec((toks, 128), lambda j: (0, j)),
            pl.BlockSpec((1, 2, toks), lambda j: (j, 0, 0)),
        ],
        out_shape=[
            jax.ShapeDtypeStruct((toks, width), jnp.float32),
            jax.ShapeDtypeStruct((width // 128, 2, toks), jnp.float32),
        ],
        compiler_params=pltpu.CompilerParams(vmem_limit_bytes=48 * 2**20),
        name="self_forward",
    )(q, kv, kv, bias)


def self_backward_kernel(q_ref, k_ref, v_ref, bias_ref, lse_ref, inner_ref, g_ref, dq_ref, dk_ref, dv_ref):
    keys, values = k_ref[...], v_ref[...]
    keys_t = keys.T
    grad_k = grad_v = None
    halves = []
    for h in range(2):
        query, grad = one_head(q_ref[...], h), one_head(g_ref[...], h)
        weights = jnp.exp(dot(keys, query, NT) + bias_ref[...] - lse_ref[0, h:h + 1])
        part = dot(weights.astype(jnp.bfloat16), grad, NN)
        grad_v = part if grad_v is None else grad_v + part
        grad_s = (weights * (dot(values, grad, NT) - inner_ref[0, h:h + 1])).astype(jnp.bfloat16)
        part = dot(grad_s, query, NN)
        grad_k = part if grad_k is None else grad_k + part
        halves.append(dot(keys_t[h * 64:(h + 1) * 64], grad_s, NN))
    dq_ref[...] = (jnp.concatenate(halves, 0) * 0.125).T
    dk_ref[...] = grad_k
    dv_ref[...] = grad_v


def self_backward(q, kv, bias, lse, inner, grad):
    toks, width = q.shape
    keys, pairs = kv.shape[0], width // 128
    tok_spec = pl.BlockSpec((toks, 128), lambda j: (0, j))
    key_spec = pl.BlockSpec((keys, 128), lambda j: (0, j))
    row_spec = pl.BlockSpec((1, 2, toks), lambda j: (j, 0, 0))
    return pl.pallas_call(
        self_backward_kernel,
        grid=(width // 128,),
        in_specs=[tok_spec, key_spec, pl.BlockSpec((keys, 128), lambda j: (0, j + pairs)), pl.BlockSpec((keys, toks), lambda j: (0, 0)), row_spec, row_spec, tok_spec],
        out_specs=[tok_spec, key_spec, key_spec],
        out_shape=[
            jax.ShapeDtypeStruct((toks, width), jnp.float32),
            jax.ShapeDtypeStruct((keys, width), jnp.float32),
            jax.ShapeDtypeStruct((keys, width), jnp.float32),
        ],
        compiler_params=pltpu.CompilerParams(vmem_limit_bytes=48 * 2**20),
        name="self_backward",
    )(q, kv, kv, bias, lse, inner, grad)


def cross_forward_kernel(which, q_ref, k_ref, v_ref, seg_ref, out_ref, stat_ref, acc_ref):
    def attend(clip, values_t, query, h):
        scores = dot(k_ref[clip], query, NT)
        peak = jnp.max(scores, 0, keepdims=True)
        terms = jnp.exp(scores - peak)
        total = jnp.sum(terms, 0, keepdims=True)
        result = dot(values_t[h * 64:(h + 1) * 64], terms.astype(jnp.bfloat16), NN)
        return result / total, peak, total

    values_t = v_ref[0].T
    for h in range(2):
        mine = seg_ref[...] == 0
        result, peak, total = attend(0, values_t, one_head(q_ref[...], h), h)
        acc_ref[h * 64:(h + 1) * 64] = jnp.where(mine, result, 0.0)
        stat_ref[0, h:h + 1] = jnp.where(mine, peak, 0.0)
        stat_ref[0, 2 + h:3 + h] = jnp.where(mine, total, 1.0)
    for clip in (1, 2):
        cols = pl.ds(pl.multiple_of(which[clip - 1] * 128, 128), 128)
        values_t = v_ref[clip].T
        mine = seg_ref[:, cols] == clip
        for h in range(2):
            result, peak, total = attend(clip, values_t, one_head(q_ref[cols], h), h)
            rows = slice(h * 64, (h + 1) * 64)
            acc_ref[rows, cols] = jnp.where(mine, result, acc_ref[rows, cols])
            stat_ref[0, h:h + 1, cols] = jnp.where(mine, peak, stat_ref[0, h:h + 1, cols])
            stat_ref[0, 2 + h:3 + h, cols] = jnp.where(mine, total, stat_ref[0, 2 + h:3 + h, cols])
    out_ref[...] = acc_ref[...].T


def cross_forward(which, q, kv, seg):
    toks, width = q.shape
    clips, frames = kv.shape[:2]
    pairs = width // 128
    kv_spec = pl.BlockSpec((clips, frames, 128), lambda j, w: (0, 0, j))
    v_spec = pl.BlockSpec((clips, frames, 128), lambda j, w: (0, 0, j + pairs))
    tok_spec = pl.BlockSpec((toks, 128), lambda j, w: (0, j))
    return pl.pallas_call(
        cross_forward_kernel,
        grid_spec=pltpu.PrefetchScalarGridSpec(
            num_scalar_prefetch=1,
            grid=(width // 128,),
            in_specs=[tok_spec, kv_spec, v_spec, pl.BlockSpec((1, toks), lambda j, w: (0, 0))],
            out_specs=[tok_spec, pl.BlockSpec((1, 4, toks), lambda j, w: (j, 0, 0))],
            scratch_shapes=[pltpu.VMEM((128, toks), jnp.float32)],
        ),
        out_shape=[
            jax.ShapeDtypeStruct((toks, width), jnp.float32),
            jax.ShapeDtypeStruct((width // 128, 4, toks), jnp.float32),
        ],
        compiler_params=pltpu.CompilerParams(vmem_limit_bytes=48 * 2**20),
        name="cross_forward",
    )(which, q, kv, kv, seg)


def cross_backward_kernel(which, q_ref, k_ref, v_ref, seg_ref, lse_ref, inner_ref, g_ref, dq_ref, dk_ref, dv_ref, acc_ref):
    def back(clip, keys_t, cols, h):
        query, grad = one_head(q_ref[cols], h), one_head(g_ref[cols], h)
        lse = jnp.where(seg_ref[:, cols] == clip, lse_ref[0, h:h + 1, cols], 1e30)
        weights = jnp.exp(dot(k_ref[clip], query, NT) - lse)
        grad_v = dot(weights.astype(jnp.bfloat16), grad, NN)
        grad_s = (weights * (dot(v_ref[clip], grad, NT) - inner_ref[0, h:h + 1, cols])).astype(jnp.bfloat16)
        grad_k = dot(grad_s, query, NN)
        return dot(keys_t[h * 64:(h + 1) * 64], grad_s, NN), grad_k, grad_v

    for clip in range(3):
        cols = slice(None) if clip == 0 else pl.ds(pl.multiple_of(which[clip - 1] * 128, 128), 128)
        keys_t = k_ref[clip].T
        grad_q, grad_k, grad_v = zip(*(back(clip, keys_t, cols, h) for h in range(2)))
        grad_q = jnp.concatenate(grad_q, 0)
        if clip == 0:
            acc_ref[...] = grad_q
        else:
            acc_ref[:, cols] += grad_q
        dk_ref[clip] = (grad_k[0] + grad_k[1]).astype(jnp.bfloat16)
        dv_ref[clip] = (grad_v[0] + grad_v[1]).astype(jnp.bfloat16)
    dq_ref[...] = (acc_ref[...] * 0.125).T


def cross_backward(which, q, kv, seg, lse, inner, grad):
    toks, width = q.shape
    clips, frames = kv.shape[:2]
    pairs = width // 128
    kv_spec = pl.BlockSpec((clips, frames, 128), lambda j, w: (0, 0, j))
    v_spec = pl.BlockSpec((clips, frames, 128), lambda j, w: (0, 0, j + pairs))
    tok_spec = pl.BlockSpec((toks, 128), lambda j, w: (0, j))
    row_spec = pl.BlockSpec((1, 2, toks), lambda j, w: (j, 0, 0))
    return pl.pallas_call(
        cross_backward_kernel,
        grid_spec=pltpu.PrefetchScalarGridSpec(
            num_scalar_prefetch=1,
            grid=(width // 128,),
            in_specs=[tok_spec, kv_spec, v_spec, pl.BlockSpec((1, toks), lambda j, w: (0, 0)), row_spec, row_spec, tok_spec],
            out_specs=[tok_spec, kv_spec, kv_spec],
            scratch_shapes=[pltpu.VMEM((128, toks), jnp.float32)],
        ),
        out_shape=[
            jax.ShapeDtypeStruct((toks, width), jnp.float32),
            jax.ShapeDtypeStruct((clips, frames, width), jnp.bfloat16),
            jax.ShapeDtypeStruct((clips, frames, width), jnp.bfloat16),
        ],
        compiler_params=pltpu.CompilerParams(vmem_limit_bytes=48 * 2**20),
        name="cross_backward",
    )(which, q, kv, kv, seg, lse, inner, grad)


Z = 4


class Place:
    def __init__(self):
        self.dp = lax.axis_index("dp")
        self.core = lax.axis_index("seq")
        self.z = self.dp // 4
        self.p = self.dp % 4
        x, y = self.p % 2, self.p // 2
        px, py = self.p + 1 - 2 * x, self.p + 2 - 4 * y
        self.p_first = px * (1 - self.core) + py * self.core
        self.p_second = py * (1 - self.core) + px * self.core
        self.p_diag = 3 - self.p
        base = self.z * 4
        self.first = (base + self.p_first, self.core)
        self.second = (base + self.p_second, self.core)
        self.mate = (self.dp, 1 - self.core)
        half = self.z // 2
        near = self.z + half * (3 - 2 * self.z)
        self.line = [base + half * (3 - 2 * base) for base in (3, 2, 1 - near)]
        self.peers = [self.mate, self.first, self.second] + [self.on_line(z) for z in self.line]

    def on_line(self, z):
        return (z * 4 + self.p, self.core)

    def greet(self):
        barrier = pltpu.get_barrier_semaphore()
        for target in self.peers:
            pl.semaphore_signal(barrier, inc=1, device_id=target, device_id_type=MESH)
        pl.semaphore_wait(barrier, len(self.peers))


HALF_COLS = {1: 768, 2: 1536, 3: 768, 4: 1536}


class Gather:
    def __init__(self, me, srcs, outs, send_sem, recv_sem, own_sem):
        self.me, self.srcs, self.outs = me, srcs, outs
        self.send_sem, self.recv_sem, self.own_sem = send_sem, recv_sem, own_sem
        self.sends = []
        self.tasks = []
        for m, times in enumerate(GATHER_TIMES):
            for time, task in zip(times, self.steps(m)):
                self.tasks.append((time, m, task))
        self.tasks.sort(key=lambda entry: entry[:2])

    def piece(self, m, chip, core):
        if m == 0:
            return self.outs[m].at[chip * 2 + core]
        if m == 5:
            return self.outs[m].at[pl.ds(pl.multiple_of(chip * 192 + core * 96, 96), 96)]
        rows = pl.ds(pl.multiple_of(chip * 48, 48), 48)
        return self.outs[m].at[rows, columns(core, HALF_COLS[m])]

    def sender(self, m, src, chip, target):
        copy = pltpu.make_async_remote_copy(
            src_ref=src, dst_ref=self.piece(m, chip, self.me.core), send_sem=self.send_sem.at[len(self.sends)],
            recv_sem=self.recv_sem.at[m, chip * 2 + self.me.core], device_id=target, device_id_type=MESH)
        self.sends.append(copy)
        return copy.start

    def arrival(self, m, chip, core):
        piece = self.piece(m, chip, core)
        return pltpu.make_async_remote_copy(
            src_ref=piece, dst_ref=piece, send_sem=self.send_sem.at[0],
            recv_sem=self.recv_sem.at[m, chip * 2 + core], device_id=self.me.mate, device_id_type=MESH).wait_recv

    def forward(self, m, z, p, targets):
        chip = z * 4 + p
        return [self.arrival(m, chip, self.me.core)] + [
            self.sender(m, self.piece(m, chip, self.me.core), chip, target) for target in targets
        ]

    def steps(self, m):
        me = self.me
        begin = [
            self.sender(m, self.srcs[m], me.dp, target)
            for target in [me.on_line(z) for z in me.line] + [me.first, me.second, me.mate]
        ]
        begin.append(pltpu.make_async_copy(self.srcs[m], self.piece(m, me.dp, me.core), self.own_sem.at[m]).start)
        line = []
        for z in me.line[::-1]:
            line += self.forward(m, z, me.p, [me.first, me.second, me.mate])
        beside = []
        for z in [me.z] + me.line[::-1]:
            beside += self.forward(m, z, me.p_first, [me.second, me.mate])
        rest = []
        for p in (me.p_second, me.p_diag):
            for z in [me.z] + me.line[::-1]:
                rest += self.forward(m, z, p, [me.mate])
        return [begin, line, beside, rest]

    def run(self, entry):
        for act in entry[2]:
            act()

    def run_until(self, time):
        while self.tasks and self.tasks[0][0] <= time:
            self.run(self.tasks.pop(0))

    def take_until(self, time):
        taken = []
        while self.tasks and self.tasks[0][0] <= time:
            taken.append(self.tasks.pop(0))
        return taken

    def need(self, m):
        for entry in [e for e in self.tasks if e[1] == m]:
            self.run(entry)
        self.tasks = [e for e in self.tasks if e[1] != m]
        pltpu.make_async_copy(self.srcs[m], self.piece(m, self.me.dp, self.me.core), self.own_sem.at[m]).wait()
        for chip in range(16):
            self.arrival(m, chip, 1 - self.me.core)()

    def finish(self):
        for copy in self.sends:
            copy.wait_send()


GATHER_TIMES = (
    (1, 6, 10, 15),
    (0, 5, 9, 14),
    (2, 11, 19, 27),
    (10, 20, 26, 34),
    (18, 31, 42, 54),
    (30, 48, 60, 74),
)


def loop_with(steps, count, begin, length, body, slots=(0,)):
    due = {}
    for i in range(count):
        for part, k in sorted((part, k) for k, part in enumerate(slots)):
            due[i, k] = steps.take_until(begin + length * (i + part))

    def turn(i, carry):
        def tick(k):
            for at in range(count):
                if due[at, k]:

                    def run(entries=due[at, k]):
                        for entry in entries:
                            steps.run(entry)

                    pl.when(i == at)(run)

        body(i, tick)
        return carry

    lax.fori_loop(0, count, turn, 0)


def norm_rows(values, gain, shift):
    average = jnp.mean(values, -1, keepdims=True)
    centred = values - average
    spread = jnp.mean(centred * centred, -1, keepdims=True)
    return centred * lax.rsqrt(spread + 1e-05) * gain + shift


def two_heads(values):
    return jnp.concatenate([one_head(values, 0), one_head(values, 1)], 0)


def columns(j, size=128):
    return pl.ds(pl.multiple_of(j * size, size), size)


def forward_kernel(*refs):
    (length_ref, x_ref, vectors_in, up_bias_in, down_bias_in, self_in, cross_in, up_in, frames_hbm, down_in) = refs[:10]
    (small_out, ckv_out, self_out, cqo_out, up_out, down_out, kv_out, vec_ref, normed_one_ref, query_ref, kv_row_ref,
     attended_ref, self_lse_ref, after_self_ref, normed_two_ref, row_query_ref, cross_lse_ref, mixed_ref,
     after_cross_ref, normed_three_ref, bias_ref, seg_ref, info_ref, ranked_hbm) = refs[10:34]
    (frames_in, frames_ref, small_f32, small_in, half_wide, half_narrow, pair_wide, pair_narrow, small_vm, ckv_vm, self_vm, cqo_vm, kv_vm, acc_ref, stat_ref, part_ref, part_stat_ref, give_ref,
     give_stat_ref, take_ref, take_stat_ref, send_sem, recv_sem, own_sem, half_sems, mate_sems, load_sem,
     frame_sem) = refs[34:]
    me = Place()
    core = me.core
    width = x_ref.shape[1]
    toks = x_ref.shape[0]
    frames_load = pltpu.make_async_copy(frames_hbm, frames_in, frame_sem.at[0])
    frames_load.start()
    small_f32[...] = jnp.zeros_like(small_f32)
    small_f32[:12, :vectors_in.shape[1]] = vectors_in[...].astype(jnp.float32)
    small_f32[12:13, :down_bias_in.shape[1]] = down_bias_in[...].astype(jnp.float32)
    small_f32[13:14, :up_bias_in.shape[1]] = up_bias_in[...].astype(jnp.float32)
    small_in[...] = small_f32[...].astype(jnp.bfloat16)
    me.greet()

    def to_mate(src, dst, k):
        return pltpu.make_async_remote_copy(
            src_ref=src, dst_ref=dst, send_sem=mate_sems.at[0, k], recv_sem=mate_sems.at[1, k], device_id=me.mate,
            device_id_type=MESH)

    def half_of(m, which):
        shard = (None, cross_in, self_in, cross_in, up_in)[m]
        size = HALF_COLS[m]
        begin = (0, width, 0, 0, 0)[m] + which * (0, width, size, 3 * width, size)[m]
        return shard.at[:, pl.ds(pl.multiple_of(begin, size), size)]

    buffers = {1: (half_narrow.at[0], pair_narrow.at[0]), 2: (half_wide.at[0], pair_wide.at[0]),
               3: (half_narrow.at[1], pair_narrow.at[1]), 4: (half_wide.at[1], pair_wide.at[1])}
    halves = {
        m: pltpu.make_async_remote_copy(
            src_ref=half_of(m, 1 - core), dst_ref=buffers[m][0], send_sem=half_sems.at[0, m],
            recv_sem=half_sems.at[1, m], device_id=me.mate, device_id_type=MESH)
        for m in buffers
    }
    for copy in halves.values():
        copy.start()
    sources = (small_in,) + tuple(buffers[m][1] for m in buffers) + (down_in,)
    gather = Gather(me, sources, (small_out, ckv_out, self_out, cqo_out, up_out, down_out), send_sem, recv_sem, own_sem)
    for m, (came_ref, both_ref) in buffers.items():
        halves[m].wait()
        own = half_of(m, core)[...].astype(jnp.float32)
        came = came_ref[...].astype(jnp.float32)
        both_ref[...] = jnp.concatenate(
            [jnp.where(core == 0, own, came), jnp.where(core == 0, came, own)], 0).astype(jnp.bfloat16)
        gather.run_until((0, 1, 2, 2, 2)[m])

    def fetch(src, dst, k):
        copy = pltpu.make_async_copy(src, dst, load_sem.at[k])
        copy.start()
        copy.wait()

    lengths = [length_ref[0, clip] for clip in range(3)]
    ends = [lengths[0], lengths[0] + lengths[1], lengths[0] + lengths[1] + lengths[2]]

    def clip_at(position):
        return sum((position >= end).astype(jnp.int32) for end in ends)

    def number_row(value):
        return jnp.zeros((1, width), jnp.int32) + value

    length_rows = [number_row(length) for length in lengths]
    big = jnp.where(length_rows[1] > length_rows[0], 1, 0)
    big = jnp.where(length_rows[2] > jnp.maximum(length_rows[0], length_rows[1]), 2, big)
    order = [big, jnp.where(big == 0, 1, 0), jnp.where(big == 2, 1, 2)]
    info_ref[...] = jnp.zeros_like(info_ref)
    for k in (1, 2):
        info_ref[k - 1:k] = jnp.where(order[k] < big, 0, 3)
    for clip in range(3):
        info_ref[2 + clip:3 + clip] = jnp.where(order[0] == clip, 0, jnp.where(order[1] == clip, 1, 2))
    group_ref = info_ref.at[:, pl.ds(0, 128)]
    places = clip_at(lax.broadcasted_iota(jnp.int32, (1, 2 * toks), 1))
    seg_ref[...] = jnp.where(
        places == order[0][:, :2 * toks], 0,
        jnp.where(places == order[1][:, :2 * toks], 1, jnp.where(places == order[2][:, :2 * toks], 2, 3)))
    key_at = core * toks - toks + lax.broadcasted_iota(jnp.int32, bias_ref.shape, 0)
    query_at = core * toks + lax.broadcasted_iota(jnp.int32, bias_ref.shape, 1)
    allowed = (clip_at(key_at) == clip_at(query_at)) & (key_at <= query_at) & (key_at >= 0)
    bias_ref[...] = jnp.where(allowed, 0.0, -1e30)
    frames_load.wait()
    for k in range(3):
        frames_ref[k] = jnp.where(
            order[k] == 0, frames_in[0], jnp.where(order[k] == 1, frames_in[1], frames_in[2]))
    ranked_store = pltpu.make_async_copy(frames_ref, ranked_hbm, frame_sem.at[0])
    ranked_store.start()
    gather.run_until(15)
    gather.need(0)
    fetch(small_out, small_vm, 0)
    row = lax.broadcasted_iota(jnp.int32, (128, width), 0)
    spot = lax.broadcasted_iota(jnp.int32, (128, width), 1) - row

    def place_small(d, total):
        chosen = jnp.where((spot == d * 24) & (row < 24), 1.0, 0.0).astype(jnp.bfloat16)
        return total + dot(small_vm[d], chosen, NN)

    vec_ref[...] = lax.fori_loop(0, 32, place_small, jnp.zeros(vec_ref.shape, jnp.float32))

    def vec(k):
        return vec_ref[k:k + 1]

    source = x_ref[...].astype(jnp.float32)
    normed_one_ref[...] = norm_rows(source, vec(0), vec(1)).astype(jnp.bfloat16)
    gather.need(1)
    fetch(ckv_out, ckv_vm, 0)
    clips = frames_ref.shape[0]
    tiles = 2 * width // 256

    def project(t, tick):
        tick(0)
        clip, tile = t // tiles, t % tiles
        result = dot(frames_ref[clip], ckv_vm[:, columns(tile, 256)], NN)
        is_value = (tile >= 3).astype(jnp.float32)
        shift = vec_ref[10:11, columns(tile % 3, 256)] * is_value
        kv_vm[clip, :frames_ref.shape[1], columns(tile, 256)] = (result + shift).astype(jnp.bfloat16)

    loop_with(gather, clips * tiles, 20, 0.65, project)
    kv_store = pltpu.make_async_copy(kv_vm, kv_out, load_sem.at[1])
    kv_store.start()
    gather.run_until(31)
    gather.need(2)
    fetch(self_out, self_vm, 0)

    normed = normed_one_ref[...]
    own_rows = slice(toks, 2 * toks)
    kv_row_ref[own_rows, :width] = dot(normed, self_vm[:, width:2 * width], NN).astype(jnp.bfloat16)
    kv_row_ref[own_rows, width:] = (dot(normed, self_vm[:, 2 * width:3 * width], NN) + vec(7)).astype(jnp.bfloat16)
    kv_copy = to_mate(kv_row_ref.at[own_rows], kv_row_ref.at[slice(0, toks)], 0)
    kv_copy.start()
    query = (dot(normed, self_vm[:, :width], NN) + vec(6)).astype(jnp.bfloat16)
    query_ref[...] = query * jnp.bfloat16(0.125)
    gather.run_until(35)
    kv_copy.wait()

    def self_pair(j, tick):
        tick(0)
        cols = columns(j)
        keys = kv_row_ref[:, cols]
        values_t = kv_row_ref[:, columns(j + 6)].T
        parts = []
        for h in range(2):
            scores = dot(keys, one_head(query_ref[:, cols], h), NT) + bias_ref[...]
            peak = jnp.max(scores, 0, keepdims=True)
            terms = jnp.exp(scores - peak)
            total = jnp.sum(terms, 0, keepdims=True)
            parts.append(dot(values_t[h * 64:(h + 1) * 64], terms.astype(jnp.bfloat16), NN) / total)
            self_lse_ref[j, h:h + 1] = peak + jnp.log(total)
        attended_ref[:, cols] = jnp.concatenate(parts, 0).T

    loop_with(gather, 6, 35, 1.2, self_pair)
    after_self = source + dot(attended_ref[...].astype(jnp.bfloat16), self_vm[:, 3 * width:], NN) + vec(8)
    after_self_ref[...] = after_self
    normed_two = norm_rows(after_self, vec(2), vec(3)).astype(jnp.bfloat16)
    normed_two_ref[...] = normed_two
    gather.run_until(44)
    gather.need(3)
    fetch(cqo_out, cqo_vm, 0)
    my_rows = pl.ds(pl.multiple_of(core * toks, toks), toks)
    cross_query = (dot(normed_two, cqo_vm[:, :width], NN) + vec(9)).astype(jnp.bfloat16)
    row_query_ref[my_rows] = cross_query * jnp.bfloat16(0.125)
    query_copy = to_mate(row_query_ref.at[my_rows], row_query_ref.at[my_rows], 1)
    query_copy.start()
    gather.run_until(48)
    query_copy.wait()

    frame_count = frames_ref.shape[1]

    def attend(clip, values_t, query, j):
        scores = dot(kv_vm[clip, :frame_count, columns(j)], query, NT)
        peak = jnp.max(scores, 0, keepdims=True)
        terms = jnp.exp(scores - peak)
        total = jnp.sum(terms, 0, keepdims=True)
        return dot(values_t, terms.astype(jnp.bfloat16), NN), peak, total

    def cross_pair(j, tick):
        values_t = kv_vm[0, :frame_count, columns(j + 6)].T
        mine = seg_ref[...] == 0
        for h in range(2):
            tick(h)
            rows = slice(h * 64, (h + 1) * 64)
            result, peak, total = attend(0, values_t[rows], one_head(row_query_ref[:, columns(j)], h), j)
            acc_ref[rows] = jnp.where(mine, result / total, 0.0)
            stat_ref[h:h + 1] = jnp.where(mine, peak, 0.0)
            stat_ref[2 + h:3 + h] = jnp.where(mine, total, 1.0)
        for clip in (1, 2):
            tick(clip + 1)
            values_t = kv_vm[clip, :frame_count, columns(j + 6)].T
            query_rows = jnp.where(
                group_ref[clip - 1:clip] == 0, row_query_ref[:128, columns(j)], row_query_ref[384:, columns(j)])
            result, peak, total = attend(clip, values_t, two_heads(query_rows), j)
            for h in range(2):
                rows, part = slice(h * 64, (h + 1) * 64), slice(h * 128, (h + 1) * 128)
                of_head = result[rows, part] / total[:, part]
                for spot in (0, 3):
                    cols = slice(spot * 128, (spot + 1) * 128)
                    mine = seg_ref[:, cols] == clip
                    acc_ref[rows, cols] = jnp.where(mine, of_head, acc_ref[rows, cols])
                    stat_ref[h:h + 1, cols] = jnp.where(mine, peak[:, part], stat_ref[h:h + 1, cols])
                    stat_ref[2 + h:3 + h, cols] = jnp.where(mine, total[:, part], stat_ref[2 + h:3 + h, cols])
        my_cols, mate_cols = columns(core, toks), columns(1 - core, toks)
        part_ref[j] = acc_ref[:, my_cols]
        part_stat_ref[j] = stat_ref[:, my_cols]
        give_ref[j] = acc_ref[:, mate_cols].astype(jnp.bfloat16)
        give_stat_ref[j] = stat_ref[:, mate_cols]

    loop_with(gather, 6, 48, 3, cross_pair, (0, 0.33, 0.66, 0.83))
    give_copy = to_mate(give_ref, take_ref, 2)
    give_copy.start()
    give_stat_copy = to_mate(give_stat_ref, take_stat_ref, 3)
    give_stat_copy.start()
    gather.run_until(1000)
    give_copy.wait()
    give_stat_copy.wait()

    def combine(j, carry):
        parts = []
        for h in range(2):
            rows = slice(h * 64, (h + 1) * 64)
            peak_a, peak_b = part_stat_ref[j, h:h + 1], take_stat_ref[j, h:h + 1]
            peak = jnp.maximum(peak_a, peak_b)
            share_a = part_stat_ref[j, 2 + h:3 + h] * jnp.exp(peak_a - peak)
            share_b = take_stat_ref[j, 2 + h:3 + h] * jnp.exp(peak_b - peak)
            total = share_a + share_b
            cross_lse_ref[j, h:h + 1] = peak + jnp.log(total)
            parts.append(part_ref[j, rows] * (share_a / total)
                         + take_ref[j, rows].astype(jnp.float32) * (share_b / total))
        mixed_ref[:, columns(j)] = jnp.concatenate(parts, 0).T
        return carry

    lax.fori_loop(0, 6, combine, 0)
    after_cross = after_self_ref[...] + dot(mixed_ref[...].astype(jnp.bfloat16), cqo_vm[:, width:], NN) + vec(11)
    after_cross_ref[...] = after_cross
    normed_three_ref[...] = norm_rows(after_cross, vec(4), vec(5)).astype(jnp.bfloat16)
    gather.run_until(1000)
    gather.need(4)
    gather.need(5)
    kv_store.wait()
    ranked_store.wait()
    gather.finish()


def fused_forward(lengths, x, vectors, up_bias, down_bias, self_w, cross_w, up_w, frames, down_w):
    toks, width = x.shape
    clips, count = frames.shape[:2]
    low, full = jnp.bfloat16, jnp.float32
    pairs = width // 128
    vmem, hbm = pl.BlockSpec(memory_space=pltpu.VMEM), pl.BlockSpec(memory_space=pl.ANY)
    shape = jax.ShapeDtypeStruct
    outs = [
        (hbm, shape((32, 16, 128), low)), (hbm, shape((width, 2 * width), low)), (hbm, shape((width, 4 * width), low)),
        (hbm, shape((width, 2 * width), low)), (hbm, shape((width, 4 * width), low)),
        (hbm, shape((4 * width, width), low)),
        (hbm, shape((clips, width, 2 * width), low)),
        (vmem, shape((16, width), full)), (vmem, shape((toks, width), low)), (vmem, shape((toks, width), low)),
        (vmem, shape((2 * toks, 2 * width), low)), (vmem, shape((toks, width), full)),
        (vmem, shape((pairs, 2, toks), full)), (vmem, shape((toks, width), full)), (vmem, shape((toks, width), low)),
        (vmem, shape((2 * toks, width), low)), (vmem, shape((pairs, 2, toks), full)), (vmem, shape((toks, width), full)),
        (vmem, shape((toks, width), full)), (vmem, shape((toks, width), low)),
        (vmem, shape((2 * toks, toks), full)), (vmem, shape((1, 2 * toks), jnp.int32)), (vmem, shape((8, width), jnp.int32)),
        (hbm, shape(frames.shape, low)),
    ]
    return pl.pallas_call(
        forward_kernel,
        in_specs=[pl.BlockSpec(memory_space=pltpu.SMEM)] + [vmem] * 7 + [hbm] * 2,
        out_specs=tuple(spec for spec, _ in outs),
        out_shape=tuple(s for _, s in outs),
        scratch_shapes=[
            pltpu.VMEM(frames.shape, low), pltpu.VMEM(frames.shape, low), pltpu.VMEM((16, 128), full),
            pltpu.VMEM((16, 128), low), pltpu.VMEM((2, 24, 2 * width), low), pltpu.VMEM((2, 24, width), low), pltpu.VMEM((2, 48, 2 * width), low),
            pltpu.VMEM((2, 48, width), low), pltpu.VMEM((32, 16, 128), low),
            pltpu.VMEM((width, 2 * width), low), pltpu.VMEM((width, 4 * width), low), pltpu.VMEM((width, 2 * width), low),
            pltpu.VMEM((clips, width, 2 * width), low), pltpu.VMEM((128, 2 * toks), full), pltpu.VMEM((4, 2 * toks), full),
            pltpu.VMEM((pairs, 128, toks), full), pltpu.VMEM((pairs, 4, toks), full),
            pltpu.VMEM((pairs, 128, toks), low), pltpu.VMEM((pairs, 4, toks), full),
            pltpu.VMEM((pairs, 128, toks), low), pltpu.VMEM((pairs, 4, toks), full),
            pltpu.SemaphoreType.DMA((400,)), pltpu.SemaphoreType.DMA((6, 32)), pltpu.SemaphoreType.DMA((6,)),
            pltpu.SemaphoreType.DMA((2, 5)), pltpu.SemaphoreType.DMA((2, 4)), pltpu.SemaphoreType.DMA((2,)),
            pltpu.SemaphoreType.DMA((1,)),
        ],
        compiler_params=pltpu.CompilerParams(collective_id=0, has_side_effects=True, vmem_limit_bytes=60 * 2**20),
        name="fused_forward",
    )(lengths, x, vectors, up_bias, down_bias, self_w, cross_w, up_w, frames, down_w)


class Scatter:
    def __init__(self, me, grads, outs, buffers, sems, times, after):
        self.me, self.grads, self.outs, self.buffers = me, grads, outs, buffers
        self.send_sem, self.own_sem, self.pair_sem, self.plane_sem, self.line_sem, self.free_sem = sems
        self.sends = {m: [] for m in range(len(grads))}
        self.count = 0
        self.order = me.line + [me.z]
        self.tasks = []
        for m, times_of in enumerate(times):
            for time, acts in zip(times_of, self.steps(m)):
                self.tasks.append((time, m, acts))
        for late, early in after.items():
            self.tasks = [
                (time, m, ([self.wait_free] if m == late and time == times[late][0] else []) + acts
                 + ([functools.partial(self.give_free, early)] if m == early and time == times[early][-1] else []))
                for time, m, acts in self.tasks
            ]
        self.tasks.sort(key=lambda entry: entry[:2])

    def give_free(self, m):
        for copy in self.sends.pop(m):
            copy.wait_send()
        for target in self.me.peers:
            pl.semaphore_signal(self.free_sem, inc=1, device_id=target, device_id_type=MESH)

    def wait_free(self):
        pl.semaphore_wait(self.free_sem, len(self.me.peers))

    def sender(self, m, src, dst, sem, target):
        copy = pltpu.make_async_remote_copy(
            src_ref=src, dst_ref=dst, send_sem=self.send_sem.at[self.count], recv_sem=sem, device_id=target,
            device_id_type=MESH)
        self.count += 1
        self.sends[m].append(copy)
        return copy.start

    def arrival(self, dst, sem):
        return pltpu.make_async_remote_copy(
            src_ref=dst, dst_ref=dst, send_sem=self.send_sem.at[0], recv_sem=sem, device_id=self.me.mate,
            device_id_type=MESH).wait_recv

    def steps(self, m):
        me, order = self.me, self.order
        grad, out = self.grads[m], self.outs[m]
        own, pair, plane_a, plane_b, plane_c, line = self.buffers[m]
        own_sem, pair_sem, plane_sem, line_sem = self.own_sem, self.pair_sem, self.plane_sem, self.line_sem

        def adder(dst, *others):
            def act():
                total = dst[...].astype(jnp.float32)
                for other in others:
                    total = total + other[...].astype(jnp.float32)
                dst[...] = total.astype(dst.dtype)
            return act

        loads = [
            pltpu.make_async_copy(grad.at[:, p, me.core], own, own_sem.at[m, k])
            for k, p in enumerate((me.p_diag, me.p_second, me.p_first, me.p))
        ]
        begin = [loads[0].start]
        for p in (me.p_diag, me.p_first, me.p_second, me.p):
            begin.append(self.sender(m, grad.at[:, p, 1 - me.core], pair.at[:, p], pair_sem.at[m, p], me.mate))
        diag, second, first, last = (
            [loads[k].wait, self.arrival(pair.at[:, p], pair_sem.at[m, p])]
            for k, p in enumerate((me.p_diag, me.p_second, me.p_first, me.p))
        )
        for z in order:
            diag += [adder(pair.at[z, me.p_diag], own.at[z]),
                     self.sender(m, pair.at[z, me.p_diag], plane_a.at[z], plane_sem.at[m, 0, z], me.second)]
            second += [adder(pair.at[z, me.p_second], own.at[z]),
                       self.sender(m, pair.at[z, me.p_second], plane_c.at[z], plane_sem.at[m, 2, z], me.second)]
            first += [self.arrival(plane_a.at[z], plane_sem.at[m, 0, z]),
                      adder(pair.at[z, me.p_first], own.at[z], plane_a.at[z]),
                      self.sender(m, pair.at[z, me.p_first], plane_b.at[z], plane_sem.at[m, 1, z], me.first)]
        diag.append(loads[1].start)
        second.append(loads[2].start)
        first.append(loads[3].start)
        for z in me.line:
            last += [self.arrival(plane_b.at[z], plane_sem.at[m, 1, z]),
                     self.arrival(plane_c.at[z], plane_sem.at[m, 2, z]),
                     adder(pair.at[z, me.p], own.at[z], plane_b.at[z], plane_c.at[z]),
                     self.sender(m, pair.at[z, me.p], line.at[me.z], line_sem.at[m, me.z], me.on_line(z))]

        def total():
            part = own[me.z].astype(jnp.float32) + pair[me.z, me.p].astype(jnp.float32)
            out[...] = part + plane_b[me.z].astype(jnp.float32) + plane_c[me.z].astype(jnp.float32)

        def from_line(source):
            def act():
                out[...] += line[source].astype(jnp.float32)
            return act

        final = [self.arrival(plane_b.at[me.z], plane_sem.at[m, 1, me.z]),
                 self.arrival(plane_c.at[me.z], plane_sem.at[m, 2, me.z]), total]
        for source in me.line[::-1]:
            final += [self.arrival(line.at[source], line_sem.at[m, source]), from_line(source)]
        return [begin, diag, second, first, last, final]

    def run(self, entry):
        for act in entry[2]:
            act()

    def run_until(self, time):
        while self.tasks and self.tasks[0][0] <= time:
            self.run(self.tasks.pop(0))

    def take_until(self, time):
        taken = []
        while self.tasks and self.tasks[0][0] <= time:
            taken.append(self.tasks.pop(0))
        return taken

    def finish(self):
        self.run_until(10**6)
        for copies in self.sends.values():
            for copy in copies:
                copy.wait_send()


def scatter_buffers(grad):
    leads = ((4,), (4, 4), (4,), (4,), (4,), (4,))
    return [pltpu.VMEM(lead + grad.shape[1:], grad.dtype) for lead in leads]


def scatter_sems(count):
    dma = pltpu.SemaphoreType.DMA
    return [dma((20 * count,)), dma((count, 4)), dma((count, 4)), dma((count, 3, 4)), dma((count, 4)),
            pltpu.SemaphoreType.REGULAR]


def scatter_view(grad):
    return grad.reshape((4, 4, 2) + grad.shape[1:])


BACK_TIMES = (
    (0, 8, 9, 20, 32, 44),
    (1, 20, 21, 34, 46, 58),
    (44, 52, 53, 62, 68, 78),
    (66, 71, 72, 80, 88, 97),
    (70, 73, 74, 82, 89, 98),
)


def norm_rows_back(values, gain, grad):
    average = jnp.mean(values, -1, keepdims=True)
    centred = values - average
    scale = lax.rsqrt(jnp.mean(centred * centred, -1, keepdims=True) + 1e-05)
    normed = centred * scale
    inner = grad * gain
    mean_inner = jnp.mean(inner, -1, keepdims=True)
    mean_both = jnp.mean(inner * normed, -1, keepdims=True)
    result = scale * (inner - mean_inner - normed * mean_both)
    return result, jnp.sum(grad * normed, 0, keepdims=True), jnp.sum(grad, 0, keepdims=True)


def backward_kernel(*refs):
    (info_ref, x_ref, bias_ref, seg_ref, vec_ref, gac_ref, mixed_ref, cross_lse_ref, row_query_ref, after_self_ref,
     attended_ref, self_lse_ref, query_ref, kv_row_ref, normed_one_ref, normed_two_ref, rows_ref, up_bias_ref, cqo_hbm,
     ckv_hbm, self_hbm, kv_hbm, frames_hbm, up_hbm, down_hbm) = refs[:25]
    (input_grad_ref, encoder_hbm, up_out, down_out, cross_out, self_out, small_out, dkv_hbm, cross_hbm,
     self_grad_hbm) = refs[25:35]
    scratch = refs[35:]
    up_buffers, down_buffers, cross_buffers, small_buffers = (scratch[k * 6:(k + 1) * 6] for k in range(4))
    sems, scratch = scratch[24:30], scratch[30:]
    (cross_vm, kv_vm, frame_ref, turned_ref, tile_ref, stage_ref, small_ref, row_grad_ref, row_stat_ref, acc_ref,
     own_ref, give_ref, take_ref, take_query_ref, cq_ref, qkv_ref, vec_grad_ref, load_sem, mate_sems, tile_sem,
     stage_sem) = scratch
    group_ref = info_ref.at[:, pl.ds(0, 128)]
    me = Place()
    core = me.core
    toks, width = x_ref.shape
    frames = frames_hbm.shape[1]
    clips = kv_hbm.shape[0]
    low, full = jnp.bfloat16, jnp.float32
    halves = [pltpu.make_async_copy(cqo_hbm.at[:, pl.ds(k * width, width)], cross_vm.at[k], load_sem.at[k])
              for k in range(2)]
    kv_load = pltpu.make_async_copy(kv_hbm, kv_vm, load_sem.at[2])
    for copy in (halves[1], kv_load, halves[0]):
        copy.start()
    me.greet()
    scatter = Scatter(
        me, (up_hbm, down_hbm, cross_hbm, self_grad_hbm, small_ref), (up_out, down_out, cross_out, self_out, small_out),
        (up_buffers, down_buffers, cross_buffers, up_buffers, small_buffers), sems, BACK_TIMES, {3: 0})
    scatter.run_until(1)

    def to_mate(src, dst, k):
        return pltpu.make_async_remote_copy(
            src_ref=src, dst_ref=dst, send_sem=mate_sems.at[0, k], recv_sem=mate_sems.at[1, k], device_id=me.mate,
            device_id_type=MESH)

    my_rows = pl.ds(pl.multiple_of(core * toks, toks), toks)
    my_cols = columns(core, toks)

    def head_rows(product, store):
        turned = product.T
        for h in range(2):
            store(h, jnp.sum(turned[h * 64:(h + 1) * 64], 0, keepdims=True))

    def tile_store(grad_hbm, slot, t):
        return pltpu.make_async_copy(tile_ref.at[slot], grad_hbm.at[:, :, :, :, columns(t, 256)], tile_sem.at[slot])

    def weight_tiles(grad_hbm, first_tile, count, tile, before=None):
        def turn(t, carry):
            slot = t % 2

            @pl.when(t >= 2)
            def _():
                tile_store(grad_hbm, slot, first_tile + t - 2).wait()

            value = tile(columns(t, 256))
            tile_ref[slot] = value.reshape(4, 4, 2, width // 32, 256).astype(low)
            tile_store(grad_hbm, slot, first_tile + t).start()
            return carry

        lax.fori_loop(0, count, turn, 0)
        for t in range(max(0, count - 2), count):
            tile_store(grad_hbm, t % 2, first_tile + t).wait()

    def product_tiles(grad_hbm, first_tile, left, right_ref):
        turned = left.T
        weight_tiles(grad_hbm, first_tile, right_ref.shape[1] // 256, lambda cols: dot(turned, right_ref[:, cols], NN))

    halves[1].wait()
    grad_cross = gac_ref[...].astype(low)
    grad_mixed = dot(grad_cross, cross_vm[1], NT).astype(low)
    row_grad_ref[my_rows] = grad_mixed
    grad_copy = to_mate(row_grad_ref.at[my_rows], row_grad_ref.at[my_rows], 0)
    grad_copy.start()
    for j in range(6):
        cols = slice(j * 128, (j + 1) * 128)
        product = grad_mixed[:, cols].astype(full) * mixed_ref[:, cols]
        row_stat_ref[j, 0:2, my_cols] = cross_lse_ref[j]

        def keep(h, row, j=j):
            row_stat_ref[j, 2 + h:3 + h, my_cols] = row

        head_rows(product, keep)
    stat_copy = to_mate(row_stat_ref.at[:, :, my_cols], row_stat_ref.at[:, :, my_cols], 1)
    stat_copy.start()
    cq_ref[...] = grad_cross
    product_tiles(cross_hbm, 9, mixed_ref[...].astype(low), cq_ref)
    kv_load.wait()
    scatter.run_until(5)
    grad_copy.wait()
    stat_copy.wait()

    def cross_pair(j, tick):
        def back(clip, keys_t, query, grad, lse, inner):
            weights = jnp.exp(dot(kv_vm[clip, :frames, columns(j)], query, NT) - lse)
            grad_v = dot(weights.astype(low), grad, NN)
            grad_s = (weights * (dot(kv_vm[clip, :frames, columns(j + 6)], grad, NT) - inner)).astype(low)
            return dot(keys_t, grad_s, NN), dot(grad_s, query, NN), grad_v

        keys_t = kv_vm[0, :frames, columns(j)].T
        mine = seg_ref[...] == 0
        grad_k = grad_v = None
        for h in range(2):
            tick(h)
            query, grad = one_head(row_query_ref[:, columns(j)], h), one_head(row_grad_ref[:, columns(j)], h)
            rows = slice(h * 64, (h + 1) * 64)
            acc_ref[rows], part_k, part_v = back(
                0, keys_t[rows], query, grad, jnp.where(mine, row_stat_ref[j, h:h + 1], 1e30),
                row_stat_ref[j, 2 + h:3 + h])
            grad_k = part_k if grad_k is None else grad_k + part_k
            grad_v = part_v if grad_v is None else grad_v + part_v
        kv_vm[0, :frames, columns(j)] = grad_k.astype(low)
        kv_vm[0, :frames, columns(j + 6)] = grad_v.astype(low)
        for clip in (1, 2):
            tick(clip + 1)
            in_first = group_ref[clip - 1:clip] == 0

            def chosen(ref):
                return two_heads(jnp.where(in_first, ref[:128, columns(j)], ref[384:, columns(j)]))

            def chosen_row(row):
                return jnp.where(in_first, row_stat_ref[j, row:row + 1, :128], row_stat_ref[j, row:row + 1, 384:])

            mine = jnp.where(in_first, seg_ref[:, :128], seg_ref[:, 384:]) == clip
            lse = jnp.concatenate([jnp.where(mine, chosen_row(h), 1e30) for h in range(2)], 1)
            inner = jnp.concatenate([chosen_row(2 + h) for h in range(2)], 1)
            grad_q, grad_k, grad_v = back(
                clip, kv_vm[clip, :frames, columns(j)].T, chosen(row_query_ref), chosen(row_grad_ref), lse, inner)
            for h in range(2):
                rows, part = slice(h * 64, (h + 1) * 64), slice(h * 128, (h + 1) * 128)
                for spot in (0, 3):
                    cols = slice(spot * 128, (spot + 1) * 128)
                    acc_ref[rows, cols] += jnp.where(in_first == (spot == 0), grad_q[rows, part], 0.0)
            kv_vm[clip, :frames, columns(j)] = grad_k.astype(low)
            kv_vm[clip, :frames, columns(j + 6)] = grad_v.astype(low)
        own_ref[:, columns(j)] = (acc_ref[:, my_cols] * 0.125).T
        give_ref[:, columns(j)] = (acc_ref[:, columns(1 - core, toks)] * 0.125).T.astype(low)

    loop_with(scatter, 6, 6, 4, cross_pair, (0, 0.33, 0.66, 0.83))
    query_copy = to_mate(give_ref.at[:, pl.ds(0, width)], take_query_ref, 2)
    query_copy.start()
    dkv_store = pltpu.make_async_copy(kv_vm, dkv_hbm, load_sem.at[2])
    dkv_store.start()
    vec_grad_ref[...] = rows_ref[...]
    vec_grad_ref[10:11] = sum(
        jnp.sum(kv_vm[clip, :frames, width:].astype(full), 0, keepdims=True) for clip in range(clips))
    for clip in range(clips):
        copy = pltpu.make_async_copy(frames_hbm.at[clip], frame_ref.at[:, pl.ds(0, width)], load_sem.at[3])
        copy.start()
        copy.wait()
        turned_ref[clip] = frame_ref[:, :width].T
    scatter.run_until(37)

    def frames_tile(cols):
        total = dot(turned_ref[0], kv_vm[0, :frames, cols], NN)
        for clip in range(1, clips):
            total = total + dot(turned_ref[clip], kv_vm[clip, :frames, cols], NN)
        return total

    weight_tiles(cross_hbm, 3, 6, frames_tile)
    halves[0].wait()
    query_copy.wait()
    grad_query = (own_ref[:, :width] + take_query_ref[...].astype(full)).astype(low)
    cq_ref[...] = grad_query
    product_tiles(cross_hbm, 0, normed_two_ref[...], cq_ref)
    dkv_store.wait()
    self_loads = [
        pltpu.make_async_copy(
            self_hbm.at[:, pl.ds(k * 2 * width, 2 * width)], kv_vm.at[k], load_sem.at[2 + k]) for k in range(2)
    ]
    for copy in self_loads:
        copy.start()
    scatter.run_until(46)
    vec_grad_ref[9:10] = jnp.sum(grad_query.astype(full), 0, keepdims=True)
    grad_part, gain, shift = norm_rows_back(after_self_ref[...], vec_ref[2:3], dot(grad_query, cross_vm[0], NT))
    vec_grad_ref[2:3] = gain
    vec_grad_ref[3:4] = shift
    grad_after_self = gac_ref[...] + grad_part
    input_grad_ref[...] = grad_after_self
    grad_low = grad_after_self.astype(low)
    vec_grad_ref[8:9] = jnp.sum(grad_low.astype(full), 0, keepdims=True)
    for copy in self_loads:
        copy.wait()
    grad_attended = dot(grad_low, kv_vm[1, :width, width:], NT).astype(low)
    row_grad_ref[:toks] = grad_attended
    for j in range(6):
        cols = slice(j * 128, (j + 1) * 128)

        def keep_self(h, row, j=j):
            row_stat_ref[j, h:h + 1, :toks] = row

        head_rows(grad_attended[:, cols].astype(full) * attended_ref[:, cols], keep_self)

    def self_pair(j, tick):
        tick(0)
        cols, value_cols = columns(j), columns(j + 6)
        keys, values = kv_row_ref[:, cols], kv_row_ref[:, value_cols]
        keys_t = keys.T
        grad_k = grad_v = None
        parts = []
        for h in range(2):
            query, grad = one_head(query_ref[:, cols], h), one_head(row_grad_ref[:toks, cols], h)
            weights = jnp.exp(dot(keys, query, NT) + bias_ref[...] - self_lse_ref[j, h:h + 1])
            part = dot(weights.astype(low), grad, NN)
            grad_v = part if grad_v is None else grad_v + part
            inner = row_stat_ref[j, h:h + 1, :toks]
            grad_s = (weights * (dot(values, grad, NT) - inner)).astype(low)
            part = dot(grad_s, query, NN)
            grad_k = part if grad_k is None else grad_k + part
            parts.append(dot(keys_t[h * 64:(h + 1) * 64], grad_s, NN))
        qkv_ref[:, cols] = (jnp.concatenate(parts, 0) * 0.125).T.astype(low)
        own_ref[:, cols] = grad_k[toks:]
        own_ref[:, value_cols] = grad_v[toks:]
        give_ref[:, cols] = grad_k[:toks].astype(low)
        give_ref[:, value_cols] = grad_v[:toks].astype(low)

    loop_with(scatter, 6, 52, 1.4, self_pair)
    row_copy = to_mate(give_ref, take_ref, 3)
    row_copy.start()
    cq_ref[...] = grad_low
    product_tiles(self_grad_hbm, 9, attended_ref[...].astype(low), cq_ref)
    scatter.run_until(62)
    row_copy.wait()
    qkv_ref[:, width:] = (own_ref[...] + take_ref[...].astype(full)).astype(low)
    product_tiles(self_grad_hbm, 0, normed_one_ref[...], qkv_ref)
    scatter.run_until(66)
    sums = jnp.sum(qkv_ref[...].astype(full), 0, keepdims=True)
    vec_grad_ref[6:7] = sums[:, :width]
    vec_grad_ref[7:8] = sums[:, 2 * width:]
    grad_normed = dot(qkv_ref[:, :2 * width], kv_vm[0, :width], NT) + dot(
        qkv_ref[:, 2 * width:], kv_vm[1, :width, :width], NT)
    grad_part, gain, shift = norm_rows_back(x_ref[...].astype(full), vec_ref[0:1], grad_normed)
    vec_grad_ref[0:1] = gain
    vec_grad_ref[1:2] = shift
    input_grad_ref[...] += grad_part
    kv_load = pltpu.make_async_copy(dkv_hbm, kv_vm, load_sem.at[2])
    kv_load.start()
    for k in range(2):
        pltpu.make_async_copy(ckv_hbm.at[:, pl.ds(k * width, width)], cross_vm.at[k], load_sem.at[k]).start()
    small_ref[...] = jnp.zeros_like(small_ref)
    rows = vec_grad_ref[...]
    for d in range(32):
        place = (d // 8, d // 2 % 4, d % 2)
        turned_rows = rows if d == 0 else pltpu.roll(rows, width - d * 24, 1)
        small_ref[place] = turned_rows[:, :128]
        small_ref[place + (slice(13, 14),)] = up_bias_ref[d:d + 1]
    scatter.run_until(70)
    for k in range(2):
        pltpu.make_async_copy(ckv_hbm.at[:, pl.ds(k * width, width)], cross_vm.at[k], load_sem.at[k]).wait()
    kv_load.wait()
    blocks = width // 128

    def encoder_store(clip):
        rows = pl.ds(clip * frames * blocks, frames * blocks)
        return pltpu.make_async_copy(stage_ref, encoder_hbm.at[rows], stage_sem.at[0])

    for clip in range(clips):
        place = info_ref[2 + clip:3 + clip]
        for part in (slice(0, width), slice(width, 2 * width)):
            frame_ref[:, part] = jnp.where(
                place == 0, kv_vm[0, :frames, part],
                jnp.where(place == 1, kv_vm[1, :frames, part], kv_vm[2, :frames, part]))

        def encoder_tile(t, tick, clip=clip):
            tick(0)
            rows = columns(t, 256)
            value = dot(frame_ref[:, :width], cross_vm[0, rows], NT) + dot(frame_ref[:, width:], cross_vm[1, rows], NT)
            if clip > 0:
                pl.when(t == 0)(encoder_store(clip - 1).wait)
            for k in range(2):
                stage_ref[pl.ds(2 * t + k, frames, stride=blocks), 0] = value[:, k * 128:(k + 1) * 128]

        loop_with(scatter, width // 256, 71 + 3 * clip, 1, encoder_tile)
        encoder_store(clip).start()
    encoder_store(clips - 1).wait()
    scatter.finish()


def fused_backward(info, x, bias, seg, vec, gac, mixed, cross_lse, row_query, after_self, attended, self_lse, query,
                   kv_row, normed_one, normed_two, rows, up_bias, cqo_full, ckv_full, self_full, kv, frames, grad_up,
                   grad_down):
    toks, width = x.shape
    clips, count = frames.shape[:2]
    low, full = jnp.bfloat16, jnp.float32
    pairs = width // 128
    vmem, hbm = pl.BlockSpec(memory_space=pltpu.VMEM), pl.BlockSpec(memory_space=pl.ANY)
    shape = jax.ShapeDtypeStruct
    small = shape((32, 16, 128), full)
    wide = (4, 4, 2, width // 32, 4 * width)
    outs = [
        (vmem, shape((toks, width), full)), (hbm, shape((clips * count * width // 128, 1, 128), full)), (vmem, shape(grad_up.shape[1:], full)),
        (vmem, shape(grad_down.shape[1:], full)), (vmem, shape(grad_up.shape[1:], full)),
        (vmem, shape(grad_up.shape[1:], full)), (vmem, shape(small.shape[1:], full)), (hbm, shape(kv.shape, low)),
        (hbm, shape(wide, low)), (hbm, shape(wide, low)),
    ]
    return pl.pallas_call(
        backward_kernel,
        in_specs=[vmem] * 18 + [hbm] * 7,
        out_specs=tuple(spec for spec, _ in outs),
        out_shape=tuple(s for _, s in outs),
        scratch_shapes=scatter_buffers(grad_up) + scatter_buffers(grad_down) + scatter_buffers(grad_up)
        + scatter_buffers(small) + scatter_sems(5) + [
            pltpu.VMEM((2, width, width), low), pltpu.VMEM((clips, width, 2 * width), low),
            pltpu.VMEM((count, 2 * width), low), pltpu.VMEM((clips, width, count), low),
            pltpu.VMEM((2,) + wide[:4] + (256,), low), pltpu.VMEM((count * width // 128, 1, 128), full),
            pltpu.VMEM((4, 4, 2, 16, 128), full), pltpu.VMEM((2 * toks, width), low),
            pltpu.VMEM((pairs, 4, 2 * toks), full), pltpu.VMEM((128, 2 * toks), full),
            pltpu.VMEM((toks, 2 * width), full), pltpu.VMEM((toks, 2 * width), low),
            pltpu.VMEM((toks, 2 * width), low), pltpu.VMEM((toks, width), low), pltpu.VMEM((toks, width), low),
            pltpu.VMEM((toks, 3 * width), low), pltpu.VMEM((16, width), full), pltpu.SemaphoreType.DMA((4,)),
            pltpu.SemaphoreType.DMA((2, 4)), pltpu.SemaphoreType.DMA((2,)), pltpu.SemaphoreType.DMA((1,)),
        ],
        compiler_params=pltpu.CompilerParams(collective_id=2, has_side_effects=True, vmem_limit_bytes=63 * 2**20),
        name="fused_backward",
    )(info, x, bias, seg, vec, gac, mixed, cross_lse, row_query, after_self, attended, self_lse, query, kv_row,
      normed_one, normed_two, rows, up_bias, cqo_full, ckv_full, self_full, kv, frames, scatter_view(grad_up),
      scatter_view(grad_down))


def ffn_kernel(normed_ref, grad_ref, after_ref, vec_ref, up_ref, bias_ref, down_ref, out_ref, back_ref, grad_up_ref,
               grad_down_ref, grad_bias_ref, rows_ref, turned_ref, sum_ref, back_sum_ref):
    t = pl.program_id(0)

    @pl.when(t == 0)
    def _():
        turned_ref[...] = normed_ref[...].T
        sum_ref[...] = jnp.zeros_like(sum_ref)
        back_sum_ref[...] = jnp.zeros_like(back_sum_ref)

    grad = grad_ref[...]
    pre = dot(normed_ref[...], up_ref[...], NN) + bias_ref[...]
    below = 0.5 * (1.0 + lax.erf(pre * 0.7071067811865476))
    activated = (pre * below).astype(jnp.bfloat16)
    sum_ref[...] += dot(activated, down_ref[...], NN)
    grad_act = dot(grad, down_ref[...], NT).astype(jnp.bfloat16).astype(jnp.float32)
    density = jnp.exp(-0.5 * pre * pre) * 0.3989422804014327
    grad_pre = (grad_act * (below + pre * density)).astype(jnp.bfloat16)
    back_sum_ref[...] += dot(grad_pre, up_ref[...], NT)
    grad_up_ref[...] = dot(turned_ref[...], grad_pre, NN).astype(jnp.bfloat16)
    grad_down_ref[...] = dot(activated.T, grad, NN).astype(jnp.bfloat16)
    grad_bias_ref[...] = jnp.sum(grad_pre.astype(jnp.float32), 0, keepdims=True)

    @pl.when(t == pl.num_programs(0) - 1)
    def _():
        out_ref[...] = (after_ref[...] + sum_ref[...] + vec_ref[12:13]).astype(jnp.bfloat16)
        grad_rows = grad_ref[...].astype(jnp.float32)
        part, gain, shift = norm_rows_back(after_ref[...], vec_ref[4:5], back_sum_ref[...])
        back = grad_rows + part
        back_ref[...] = back
        rows_ref[...] = jnp.zeros_like(rows_ref)
        rows_ref[4:5] = gain
        rows_ref[5:6] = shift
        rows_ref[11:12] = jnp.sum(back.astype(jnp.bfloat16).astype(jnp.float32), 0, keepdims=True)
        rows_ref[12:13] = jnp.sum(grad_rows, 0, keepdims=True)


def ffn(normed, grad, after, vec, up_full, bias, down_full):
    toks, width = normed.shape
    hidden = up_full.shape[1]
    size = 256
    low, full = jnp.bfloat16, jnp.float32
    shape = jax.ShapeDtypeStruct
    rows = pl.BlockSpec((toks, width), lambda t: (0, 0))
    vecs = pl.BlockSpec((16, width), lambda t: (0, 0))
    up_spec = pl.BlockSpec((width, size), lambda t: (0, t))
    down_spec = pl.BlockSpec((size, width), lambda t: (t, 0))
    bias_spec = pl.BlockSpec((1, size), lambda t: (0, t))
    return pl.pallas_call(
        ffn_kernel,
        grid=(hidden // size,),
        in_specs=[rows, rows, rows, vecs, up_spec, bias_spec, down_spec],
        out_specs=[rows, rows, up_spec, down_spec, bias_spec, vecs],
        out_shape=[
            shape((toks, width), low), shape((toks, width), full), shape(up_full.shape, low),
            shape(down_full.shape, low), shape((1, hidden), full), shape((16, width), full),
        ],
        scratch_shapes=[pltpu.VMEM((width, toks), low), pltpu.VMEM((toks, width), full), pltpu.VMEM((toks, width), full)],
        compiler_params=pltpu.CompilerParams(vmem_limit_bytes=48 * 2**20),
        name="ffn",
    )(normed, grad, after, vec, up_full, bias, down_full)


def place_clips_kernel(order, in_ref, out_ref):
    frames, width = in_ref.shape[1:]
    blocks = width // 128
    for k in range(blocks):
        out_ref[pl.ds(k, frames, stride=blocks), 0] = in_ref[0, :, k * 128:(k + 1) * 128]


def place_clips(order, values):
    clips, frames, width = values.shape
    rows = frames * width // 128
    flat = pl.pallas_call(
        place_clips_kernel,
        grid_spec=pltpu.PrefetchScalarGridSpec(
            num_scalar_prefetch=1,
            grid=(clips,),
            in_specs=[pl.BlockSpec((1, frames, width), lambda k, order: (k, 0, 0))],
            out_specs=pl.BlockSpec((rows, 1, 128), lambda k, order: (order[k], 0, 0)),
        ),
        out_shape=jax.ShapeDtypeStruct((clips * rows, 1, 128), values.dtype),
        compiler_params=pltpu.CompilerParams(vmem_limit_bytes=48 * 2**20),
        name="place_clips",
    )(order, values)
    return flat.reshape(1, clips, frames, width)


def from_behind(value, axis, steps):
    count = lax.axis_size(axis)
    leading, last = (max(0, -steps), min(count, count - steps))
    return lax.ppermute(value, axis, [(source, source + steps) for source in range(leading, last)])


def layer_norm(values, gain, shift):
    average = jnp.mean(values, -1, keepdims=True)
    centred = values - average
    spread = jnp.mean(centred * centred, -1, keepdims=True)
    return centred * lax.rsqrt(spread + 1e-05) * gain + shift


def matmul(left, right):
    return jnp.dot(left, right, preferred_element_type=jnp.float32)


def swap_halves(value):
    return lax.ppermute(value, "seq", [(0, 1), (1, 0)])


def seq_halves(value, axis):
    span = value.shape[axis] // 2
    half = lax.axis_index("seq")
    mine = lax.dynamic_slice_in_dim(value, half * span, span, axis)
    other = lax.dynamic_slice_in_dim(value, (1 - half) * span, span, axis)
    return mine, other


def seq_scatter(value):
    mine, other = seq_halves(value, 0)
    return mine + swap_halves(other.astype(jnp.bfloat16)).astype(value.dtype)


def per_head(values):
    rows = values.reshape(-1, values.shape[2]).T
    return jnp.repeat(rows, HEAD_DIM, axis=1)


def head_sums(values):
    sums = jnp.sum(values.reshape(values.shape[0], -1, HEAD_DIM), -1)
    return sums.T.reshape(-1, 2, values.shape[0])


def plain_forward(
    which, layer_input, frames, mask_bias, row_segment, weights
):
    self_full, cross_full, up_full, down_full, bias_full, out_bias_full, vectors = (
        lax.all_gather(part, ("dp", "seq"), axis=0, tiled=True) for part in weights
    )
    vec = jnp.pad(
        jnp.concatenate([vectors.T, out_bias_full[None]]).astype(jnp.float32), ((0, 3), (0, 0))
    )
    model_width = layer_input.shape[1]
    cross_in = [cross_full[:, k * model_width : (k + 1) * model_width] for k in range(4)]
    ckv_full = cross_full[:, model_width : 3 * model_width]
    cqo_full = jnp.concatenate([cross_in[0], cross_in[3]], 1)
    source = layer_input.astype(jnp.float32)
    normed_one = layer_norm(source, vec[0], vec[1]).astype(jnp.bfloat16)
    proj_bias = jnp.concatenate([vec[6], jnp.zeros_like(vec[6]), vec[7]])
    qkv_low = (matmul(normed_one, self_full[:, : 3 * model_width]) + proj_bias).astype(jnp.bfloat16)
    query = qkv_low[:, :model_width] * jnp.bfloat16(0.125)
    kv_own = qkv_low[:, model_width:]
    kv_row = jnp.concatenate([from_behind(kv_own, "seq", 1), kv_own])
    attended, self_lse = self_forward(query, kv_row, mask_bias)
    attended_low = attended.astype(jnp.bfloat16)
    after_self = source + matmul(attended_low, self_full[:, 3 * model_width :]) + vec[8]
    normed_two = layer_norm(after_self, vec[2], vec[3]).astype(jnp.bfloat16)
    cross_query = (matmul(normed_two, cross_in[0]) + vec[9]).astype(jnp.bfloat16)
    cross_key = jnp.einsum(
        "cfd,de->cfe", frames, cross_in[1], preferred_element_type=jnp.float32
    ).astype(jnp.bfloat16)
    cross_value = (
        jnp.einsum("cfd,de->cfe", frames, cross_in[2], preferred_element_type=jnp.float32)
        + vec[10]
    ).astype(jnp.bfloat16)
    row_query = lax.all_gather(cross_query * jnp.bfloat16(0.125), "seq", axis=0, tiled=True)
    cross_kv = jnp.concatenate([cross_key, cross_value], 2)
    part_mixed, part_stats = cross_forward(which, row_query, cross_kv, row_segment)
    mixed_mine, mixed_other = seq_halves(part_mixed, 0)
    stats_mine, stats_other = seq_halves(part_stats, 2)
    mixed_came = swap_halves(mixed_other.astype(jnp.bfloat16))
    stats_came = swap_halves(stats_other)
    peak = jnp.maximum(stats_mine[:, :2], stats_came[:, :2])
    share_mine = stats_mine[:, 2:] * jnp.exp(stats_mine[:, :2] - peak)
    share_came = stats_came[:, 2:] * jnp.exp(stats_came[:, :2] - peak)
    total = share_mine + share_came
    cross_lse = peak + jnp.log(total)
    mixed_full = mixed_mine * per_head(share_mine / total) + mixed_came.astype(
        jnp.float32
    ) * per_head(share_came / total)
    mixed = mixed_full.astype(jnp.bfloat16)
    after_cross = after_self + matmul(mixed, cross_in[3]) + vec[11]
    normed_three = layer_norm(after_cross, vec[4], vec[5]).astype(jnp.bfloat16)
    return (
        bias_full, ckv_full, self_full, cqo_full, up_full, down_full, cross_kv, vec, normed_one, query, kv_row, attended,
        self_lse, after_self, normed_two, row_query, cross_lse, mixed_full, after_cross, normed_three,
    )


def plain_backward(
    which, layer_input, mask_bias, row_segment, vec, grad_after_cross, mixed_full, cross_lse, row_query, after_self,
    attended, self_lse, query, kv_row, cqo_full, self_full, cross_kv
):
    tok_span, model_width = layer_input.shape
    source = layer_input.astype(jnp.float32)
    grad_cross_low = grad_after_cross.astype(jnp.bfloat16)
    grad_mixed = matmul(grad_cross_low, cqo_full[:, model_width:].T).astype(jnp.bfloat16)
    row_grad = lax.all_gather(grad_mixed, "seq", axis=0, tiled=True)
    cross_inner = head_sums(grad_mixed.astype(jnp.float32) * mixed_full)
    row_stats = lax.all_gather(jnp.stack([cross_lse, cross_inner]), "seq", axis=3, tiled=True)
    part_query, grad_key, grad_value = cross_backward(
        which, row_query, cross_kv, row_segment, row_stats[0], row_stats[1], row_grad
    )
    grad_query_sum = seq_scatter(part_query).astype(jnp.bfloat16)
    grad_cq_bias = jnp.sum(grad_query_sum, 0, dtype=jnp.float32)
    grad_normed_two = matmul(grad_query_sum, cqo_full[:, :model_width].T)
    grad_cv_bias = jnp.sum(grad_value, (0, 1), dtype=jnp.float32)
    _, norm_pull_two = jax.vjp(layer_norm, after_self, vec[2], vec[3])
    grad_part, grad_gain_two, grad_shift_two = norm_pull_two(grad_normed_two)
    grad_after_self = grad_after_cross + grad_part
    grad_self_low = grad_after_self.astype(jnp.bfloat16)
    grad_self_bias = jnp.sum(grad_self_low, 0, dtype=jnp.float32)
    grad_attended = matmul(grad_self_low, self_full[:, 3 * model_width :].T).astype(jnp.bfloat16)
    self_inner = head_sums(grad_attended.astype(jnp.float32) * attended)
    grad_query, grad_key_row, grad_value_row = self_backward(
        query, kv_row, mask_bias, self_lse, self_inner, grad_attended
    )
    grad_kv = jnp.concatenate([grad_key_row, grad_value_row], 1)
    back_kv = from_behind(grad_kv[:tok_span].astype(jnp.bfloat16), "seq", -1)
    grad_qkv_low = jnp.concatenate(
        [grad_query, grad_kv[tok_span:] + back_kv.astype(jnp.float32)], 1
    ).astype(jnp.bfloat16)
    grad_qkv_bias = jnp.sum(grad_qkv_low, 0, dtype=jnp.float32)
    grad_normed_one = matmul(grad_qkv_low, self_full[:, : 3 * model_width].T)
    _, norm_pull_one = jax.vjp(layer_norm, source, vec[0], vec[1])
    grad_part, grad_gain_one, grad_shift_one = norm_pull_one(grad_normed_one)
    input_grad = grad_after_self + grad_part
    nothing = jnp.zeros_like(grad_cq_bias)
    vec_grads = jnp.stack(
        [
            grad_gain_one,
            grad_shift_one,
            grad_gain_two,
            grad_shift_two,
            nothing,
            nothing,
            grad_qkv_bias[:model_width],
            grad_qkv_bias[2 * model_width :],
            grad_self_bias,
            grad_cq_bias,
            grad_cv_bias,
        ]
        + [nothing] * 5
    )
    return (
        input_grad, grad_query_sum, grad_self_low, grad_qkv_low, vec_grads,
        jnp.concatenate([grad_key, grad_value], 2),
    )


def plain_finish(
    normed_one, grad_qkv_low, attended_low, grad_self_low, normed_two, grad_query_sum, mixed, grad_cross_low, frames,
    cross_kv_grad, ckv_full
):
    width = normed_one.shape[1]
    grads_self = jnp.concatenate([matmul(normed_one.T, grad_qkv_low), matmul(attended_low.T, grad_self_low)], 1)
    grad_ckv = jnp.einsum("cfd,cfe->de", frames, cross_kv_grad, preferred_element_type=jnp.float32)
    grads_cross = jnp.concatenate(
        [matmul(normed_two.T, grad_query_sum), grad_ckv, matmul(mixed.T, grad_cross_low)], 1
    )
    encoder_grad = jnp.einsum(
        "cfe,de->cfd", cross_kv_grad, ckv_full, preferred_element_type=jnp.float32
    )
    return encoder_grad, (grads_self, grads_cross)


def fused_device(
    layer_input,
    encoder_states,
    clip_lengths,
    out_grad,
    self_weights,
    cross_weights,
    up_weights,
    down_weights,
    up_bias,
    down_bias,
    vectors,
):
    small_blocks, ckv_full, self_full, cqo_full, up_full, down_full, cross_kv, vec, normed_one, query, kv_row, attended, \
        self_lse, after_self, normed_two, row_query, cross_lse, mixed_full, after_cross, normed_three, mask_bias, \
        row_segment, info, frames = fused_forward(
            clip_lengths, layer_input[0], vectors.T, up_bias[None], down_bias[None], self_weights, cross_weights, up_weights,
            encoder_states[0], down_weights,
        )
    bias_full = small_blocks[:, 13, : up_bias.shape[0]].reshape(-1).astype(jnp.float32)
    layer_output, grad_after_cross, grad_up, grad_down, grad_up_bias, ffn_rows = ffn(
        normed_three, out_grad[0], after_cross, vec, up_full, bias_full[None], down_full
    )
    large = [g.reshape(32, -1, g.shape[1]) for g in (grad_up, grad_down)]
    bias_rows = jnp.pad(grad_up_bias.reshape(32, -1), ((0, 0), (0, 128 - up_bias.shape[0])))
    input_grad, encoder_grad, up_share, down_share, cross_share, self_share, row, *_ = fused_backward(
        info, layer_input[0], mask_bias, row_segment, vec, grad_after_cross, mixed_full, cross_lse, row_query, after_self,
        attended, self_lse, query, kv_row, normed_one, normed_two, ffn_rows, bias_rows, cqo_full, ckv_full, self_full,
        cross_kv, frames, *large
    )
    return (
        layer_output[None], input_grad[None], encoder_grad.reshape((1,) + encoder_states.shape[1:]), self_share, cross_share,
        up_share, down_share, row[13, : up_bias.shape[0]], row[12, : down_bias.shape[0]], row[:12, : vectors.shape[0]].T,
    )


def plain_device(
    layer_input,
    encoder_states,
    clip_lengths,
    out_grad,
    self_weights,
    cross_weights,
    up_weights,
    down_weights,
    up_bias,
    down_bias,
    vectors,
):
    model_width = layer_input.shape[2]
    tok_span = layer_input.shape[1]
    seq_half = lax.axis_index("seq")
    position = seq_half * tok_span + jnp.arange(tok_span, dtype=jnp.int32)
    clip_ends = jnp.cumsum(clip_lengths[0])
    segment = jnp.sum((position[:, None] >= clip_ends[None, :]).astype(jnp.int32), 1)
    key_position = jnp.concatenate([position - tok_span, position])
    key_segment = jnp.sum((key_position[:, None] >= clip_ends[None, :]).astype(jnp.int32), 1)
    allowed = (
        (key_segment[:, None] == segment[None, :])
        & (key_position[:, None] <= position[None, :])
        & (key_position[:, None] >= 0)
    )
    mask_bias = jnp.where(allowed, 0.0, -1e30).astype(jnp.float32)
    row_position = jnp.arange(2 * tok_span, dtype=jnp.int32)
    row_segment = jnp.sum((row_position[:, None] >= clip_ends[None, :]).astype(jnp.int32), 1)[None]
    big = jnp.argmax(clip_lengths[0]).astype(jnp.int32)
    small_one = jnp.where(big == 0, 1, 0)
    small_two = jnp.where(big == 2, 1, 2)
    last_group = 2 * tok_span // 128 - 1
    order = jnp.stack([big, small_one, small_two]).astype(jnp.int32)
    row_segment = jnp.where(
        row_segment == order[0], 0, jnp.where(row_segment == order[1], 1, jnp.where(row_segment == order[2], 2, 3))
    )
    which = jnp.where(order[1:] < big, 0, last_group).astype(jnp.int32)

    frames = jnp.take(encoder_states[0], order, axis=0, mode="clip")
    (
        bias_full, ckv_full, self_full, cqo_full, up_full, down_full, cross_kv, vec, normed_one, query, kv_row, attended,
        self_lse, after_self, normed_two, row_query, cross_lse, mixed_full, after_cross, normed_three,
    ) = plain_forward(
        which, layer_input[0], frames, mask_bias, row_segment,
        (self_weights, cross_weights, up_weights, down_weights, up_bias, down_bias, vectors),
    )
    bias_full = bias_full.astype(jnp.float32)
    layer_output, grad_after_cross, grad_up, grad_down, grad_up_bias, ffn_rows = ffn(
        normed_three, out_grad[0], after_cross, vec, up_full, bias_full[None], down_full
    )
    operands = (
        layer_input[0], mask_bias, row_segment, vec, grad_after_cross, mixed_full, cross_lse, row_query, after_self,
        attended, self_lse, query, kv_row,
    )
    input_grad, grad_query_sum, grad_self_low, grad_qkv_low, vec_grads, cross_kv_grad = plain_backward(
        which, *operands, cqo_full, self_full, cross_kv
    )
    encoder_grad, large = plain_finish(
        normed_one, grad_qkv_low, attended.astype(jnp.bfloat16), grad_self_low, normed_two, grad_query_sum,
        mixed_full.astype(jnp.bfloat16), grad_after_cross.astype(jnp.bfloat16), frames, cross_kv_grad, ckv_full,
    )
    vector_grads = vec_grads + ffn_rows
    shares = tuple(
        lax.psum_scatter(part, ("dp", "seq"), scatter_dimension=0, tiled=True)
        for part in large
        + (grad_up.astype(jnp.float32), grad_down.astype(jnp.float32), grad_up_bias[0], vector_grads[12],
           vector_grads[:12].T)
    )
    return (layer_output[None], input_grad[None], place_clips(order, encoder_grad)) + shares


def solution(mesh):
    return jax.shard_map(
        fused_device if mesh.shape["dp"] == 16 else plain_device,
        mesh=mesh,
        in_specs=(
            P("dp", "seq", None),
            P("dp", None, "seq", None),
            P("dp", None),
            P("dp", "seq", None),
            P(("dp", "seq"), None),
            P(("dp", "seq"), None),
            P(("dp", "seq"), None),
            P(("dp", "seq"), None),
            P(("dp", "seq")),
            P(("dp", "seq")),
            P(("dp", "seq"), None),
        ),
        out_specs=(
            P("dp", "seq", None),
            P("dp", "seq", None),
            P("dp", None, "seq", None),
            P(("dp", "seq"), None),
            P(("dp", "seq"), None),
            P(("dp", "seq"), None),
            P(("dp", "seq"), None),
            P(("dp", "seq")),
            P(("dp", "seq")),
            P(("dp", "seq"), None),
        ),
        check_vma=False,
    )
```

```python
import functools

import jax
import jax.numpy as jnp
from jax import lax
from jax.experimental import pallas as pl
from jax.experimental.pallas import tpu as pltpu
from jax.sharding import PartitionSpec as P

HEAD_DIM = 64
CLIPS = 3
MESH = pl.DeviceIdType.MESH
NT = (((1,), (1,)), ((), ()))
NN = (((1,), (0,)), ((), ()))


def dot(left, right, dims):
    return lax.dot_general(left, right, dims, preferred_element_type=jnp.float32)


def one_head(values, h):
    lane = lax.broadcasted_iota(jnp.int32, values.shape, 1)
    return jnp.where((lane >= 64) == (h == 1), values, jnp.zeros_like(values))


def self_forward_kernel(q_ref, k_ref, v_ref, bias_ref, out_ref, lse_ref):
    keys = k_ref[...]
    values_t = v_ref[...].T
    halves = []
    for h in range(2):
        scores = dot(keys, one_head(q_ref[...], h), NT) + bias_ref[...]
        peak = jnp.max(scores, 0, keepdims=True)
        terms = jnp.exp(scores - peak)
        total = jnp.sum(terms, 0, keepdims=True)
        result = dot(values_t[h * 64:(h + 1) * 64], terms.astype(jnp.bfloat16), NN)
        halves.append(result / total)
        lse_ref[0, h:h + 1] = peak + jnp.log(total)
    out_ref[...] = jnp.concatenate(halves, 0).T.astype(out_ref.dtype)


def self_forward(q, kv, bias):
    toks, width = q.shape
    keys, pairs = kv.shape[0], width // 128
    return pl.pallas_call(
        self_forward_kernel,
        grid=(width // 128,),
        in_specs=[
            pl.BlockSpec((toks, 128), lambda j: (0, j)),
            pl.BlockSpec((keys, 128), lambda j: (0, j)),
            pl.BlockSpec((keys, 128), lambda j: (0, j + pairs)),
            pl.BlockSpec((keys, toks), lambda j: (0, 0)),
        ],
        out_specs=[
            pl.BlockSpec((toks, 128), lambda j: (0, j)),
            pl.BlockSpec((1, 2, toks), lambda j: (j, 0, 0)),
        ],
        out_shape=[
            jax.ShapeDtypeStruct((toks, width), jnp.float32),
            jax.ShapeDtypeStruct((width // 128, 2, toks), jnp.float32),
        ],
        compiler_params=pltpu.CompilerParams(vmem_limit_bytes=48 * 2**20),
        name="self_forward",
    )(q, kv, kv, bias)


def self_backward_kernel(q_ref, k_ref, v_ref, bias_ref, lse_ref, inner_ref, g_ref, dq_ref, dk_ref, dv_ref):
    keys, values = k_ref[...], v_ref[...]
    keys_t = keys.T
    grad_k = grad_v = None
    halves = []
    for h in range(2):
        query, grad = one_head(q_ref[...], h), one_head(g_ref[...], h)
        weights = jnp.exp(dot(keys, query, NT) + bias_ref[...] - lse_ref[0, h:h + 1])
        part = dot(weights.astype(jnp.bfloat16), grad, NN)
        grad_v = part if grad_v is None else grad_v + part
        grad_s = (weights * (dot(values, grad, NT) - inner_ref[0, h:h + 1])).astype(jnp.bfloat16)
        part = dot(grad_s, query, NN)
        grad_k = part if grad_k is None else grad_k + part
        halves.append(dot(keys_t[h * 64:(h + 1) * 64], grad_s, NN))
    dq_ref[...] = (jnp.concatenate(halves, 0) * 0.125).T
    dk_ref[...] = grad_k
    dv_ref[...] = grad_v


def self_backward(q, kv, bias, lse, inner, grad):
    toks, width = q.shape
    keys, pairs = kv.shape[0], width // 128
    tok_spec = pl.BlockSpec((toks, 128), lambda j: (0, j))
    key_spec = pl.BlockSpec((keys, 128), lambda j: (0, j))
    row_spec = pl.BlockSpec((1, 2, toks), lambda j: (j, 0, 0))
    return pl.pallas_call(
        self_backward_kernel,
        grid=(width // 128,),
        in_specs=[tok_spec, key_spec, pl.BlockSpec((keys, 128), lambda j: (0, j + pairs)), pl.BlockSpec((keys, toks), lambda j: (0, 0)), row_spec, row_spec, tok_spec],
        out_specs=[tok_spec, key_spec, key_spec],
        out_shape=[
            jax.ShapeDtypeStruct((toks, width), jnp.float32),
            jax.ShapeDtypeStruct((keys, width), jnp.float32),
            jax.ShapeDtypeStruct((keys, width), jnp.float32),
        ],
        compiler_params=pltpu.CompilerParams(vmem_limit_bytes=48 * 2**20),
        name="self_backward",
    )(q, kv, kv, bias, lse, inner, grad)


def cross_forward_kernel(which, q_ref, k_ref, v_ref, seg_ref, out_ref, stat_ref, acc_ref):
    def attend(clip, values_t, query, h):
        scores = dot(k_ref[clip], query, NT)
        peak = jnp.max(scores, 0, keepdims=True)
        terms = jnp.exp(scores - peak)
        total = jnp.sum(terms, 0, keepdims=True)
        result = dot(values_t[h * 64:(h + 1) * 64], terms.astype(jnp.bfloat16), NN)
        return result / total, peak, total

    values_t = v_ref[0].T
    for h in range(2):
        mine = seg_ref[...] == 0
        result, peak, total = attend(0, values_t, one_head(q_ref[...], h), h)
        acc_ref[h * 64:(h + 1) * 64] = jnp.where(mine, result, 0.0)
        stat_ref[0, h:h + 1] = jnp.where(mine, peak, 0.0)
        stat_ref[0, 2 + h:3 + h] = jnp.where(mine, total, 1.0)
    for clip in (1, 2):
        cols = pl.ds(pl.multiple_of(which[clip - 1] * 128, 128), 128)
        values_t = v_ref[clip].T
        mine = seg_ref[:, cols] == clip
        for h in range(2):
            result, peak, total = attend(clip, values_t, one_head(q_ref[cols], h), h)
            rows = slice(h * 64, (h + 1) * 64)
            acc_ref[rows, cols] = jnp.where(mine, result, acc_ref[rows, cols])
            stat_ref[0, h:h + 1, cols] = jnp.where(mine, peak, stat_ref[0, h:h + 1, cols])
            stat_ref[0, 2 + h:3 + h, cols] = jnp.where(mine, total, stat_ref[0, 2 + h:3 + h, cols])
    out_ref[...] = acc_ref[...].T


def cross_forward(which, q, kv, seg):
    toks, width = q.shape
    clips, frames = kv.shape[:2]
    pairs = width // 128
    kv_spec = pl.BlockSpec((clips, frames, 128), lambda j, w: (0, 0, j))
    v_spec = pl.BlockSpec((clips, frames, 128), lambda j, w: (0, 0, j + pairs))
    tok_spec = pl.BlockSpec((toks, 128), lambda j, w: (0, j))
    return pl.pallas_call(
        cross_forward_kernel,
        grid_spec=pltpu.PrefetchScalarGridSpec(
            num_scalar_prefetch=1,
            grid=(width // 128,),
            in_specs=[tok_spec, kv_spec, v_spec, pl.BlockSpec((1, toks), lambda j, w: (0, 0))],
            out_specs=[tok_spec, pl.BlockSpec((1, 4, toks), lambda j, w: (j, 0, 0))],
            scratch_shapes=[pltpu.VMEM((128, toks), jnp.float32)],
        ),
        out_shape=[
            jax.ShapeDtypeStruct((toks, width), jnp.float32),
            jax.ShapeDtypeStruct((width // 128, 4, toks), jnp.float32),
        ],
        compiler_params=pltpu.CompilerParams(vmem_limit_bytes=48 * 2**20),
        name="cross_forward",
    )(which, q, kv, kv, seg)


def cross_backward_kernel(which, q_ref, k_ref, v_ref, seg_ref, lse_ref, inner_ref, g_ref, dq_ref, dk_ref, dv_ref, acc_ref):
    def back(clip, keys_t, cols, h):
        query, grad = one_head(q_ref[cols], h), one_head(g_ref[cols], h)
        lse = jnp.where(seg_ref[:, cols] == clip, lse_ref[0, h:h + 1, cols], 1e30)
        weights = jnp.exp(dot(k_ref[clip], query, NT) - lse)
        grad_v = dot(weights.astype(jnp.bfloat16), grad, NN)
        grad_s = (weights * (dot(v_ref[clip], grad, NT) - inner_ref[0, h:h + 1, cols])).astype(jnp.bfloat16)
        grad_k = dot(grad_s, query, NN)
        return dot(keys_t[h * 64:(h + 1) * 64], grad_s, NN), grad_k, grad_v

    for clip in range(3):
        cols = slice(None) if clip == 0 else pl.ds(pl.multiple_of(which[clip - 1] * 128, 128), 128)
        keys_t = k_ref[clip].T
        grad_q, grad_k, grad_v = zip(*(back(clip, keys_t, cols, h) for h in range(2)))
        grad_q = jnp.concatenate(grad_q, 0)
        if clip == 0:
            acc_ref[...] = grad_q
        else:
            acc_ref[:, cols] += grad_q
        dk_ref[clip] = (grad_k[0] + grad_k[1]).astype(jnp.bfloat16)
        dv_ref[clip] = (grad_v[0] + grad_v[1]).astype(jnp.bfloat16)
    dq_ref[...] = (acc_ref[...] * 0.125).T


def cross_backward(which, q, kv, seg, lse, inner, grad):
    toks, width = q.shape
    clips, frames = kv.shape[:2]
    pairs = width // 128
    kv_spec = pl.BlockSpec((clips, frames, 128), lambda j, w: (0, 0, j))
    v_spec = pl.BlockSpec((clips, frames, 128), lambda j, w: (0, 0, j + pairs))
    tok_spec = pl.BlockSpec((toks, 128), lambda j, w: (0, j))
    row_spec = pl.BlockSpec((1, 2, toks), lambda j, w: (j, 0, 0))
    return pl.pallas_call(
        cross_backward_kernel,
        grid_spec=pltpu.PrefetchScalarGridSpec(
            num_scalar_prefetch=1,
            grid=(width // 128,),
            in_specs=[tok_spec, kv_spec, v_spec, pl.BlockSpec((1, toks), lambda j, w: (0, 0)), row_spec, row_spec, tok_spec],
            out_specs=[tok_spec, kv_spec, kv_spec],
            scratch_shapes=[pltpu.VMEM((128, toks), jnp.float32)],
        ),
        out_shape=[
            jax.ShapeDtypeStruct((toks, width), jnp.float32),
            jax.ShapeDtypeStruct((clips, frames, width), jnp.bfloat16),
            jax.ShapeDtypeStruct((clips, frames, width), jnp.bfloat16),
        ],
        compiler_params=pltpu.CompilerParams(vmem_limit_bytes=48 * 2**20),
        name="cross_backward",
    )(which, q, kv, kv, seg, lse, inner, grad)


Z = 4


class Place:
    def __init__(self):
        self.dp = lax.axis_index("dp")
        self.core = lax.axis_index("seq")
        self.z = self.dp // 4
        self.p = self.dp % 4
        x, y = self.p % 2, self.p // 2
        px, py = self.p + 1 - 2 * x, self.p + 2 - 4 * y
        self.p_first = px * (1 - self.core) + py * self.core
        self.p_second = py * (1 - self.core) + px * self.core
        self.p_diag = 3 - self.p
        base = self.z * 4
        self.first = (base + self.p_first, self.core)
        self.second = (base + self.p_second, self.core)
        self.mate = (self.dp, 1 - self.core)
        half = self.z // 2
        near = self.z + half * (3 - 2 * self.z)
        self.line = [base + half * (3 - 2 * base) for base in (3, 2, 1 - near)]
        self.peers = [self.mate, self.first, self.second] + [self.on_line(z) for z in self.line]

    def on_line(self, z):
        return (z * 4 + self.p, self.core)

    def greet(self):
        barrier = pltpu.get_barrier_semaphore()
        for target in self.peers:
            pl.semaphore_signal(barrier, inc=1, device_id=target, device_id_type=MESH)
        pl.semaphore_wait(barrier, len(self.peers))


HALF_COLS = {1: 768, 2: 1536, 3: 768, 4: 1536}


class Gather:
    def __init__(self, me, srcs, outs, send_sem, recv_sem, own_sem):
        self.me, self.srcs, self.outs = me, srcs, outs
        self.send_sem, self.recv_sem, self.own_sem = send_sem, recv_sem, own_sem
        self.sends = []
        self.tasks = []
        for m, times in enumerate(GATHER_TIMES):
            for time, task in zip(times, self.steps(m)):
                self.tasks.append((time, m, task))
        self.tasks.sort(key=lambda entry: entry[:2])

    def piece(self, m, chip, core):
        if m == 0:
            return self.outs[m].at[chip * 2 + core]
        if m == 5:
            return self.outs[m].at[pl.ds(pl.multiple_of(chip * 192 + core * 96, 96), 96)]
        rows = pl.ds(pl.multiple_of(chip * 48, 48), 48)
        return self.outs[m].at[rows, columns(core, HALF_COLS[m])]

    def sender(self, m, src, chip, target):
        copy = pltpu.make_async_remote_copy(
            src_ref=src, dst_ref=self.piece(m, chip, self.me.core), send_sem=self.send_sem.at[len(self.sends)],
            recv_sem=self.recv_sem.at[m, chip * 2 + self.me.core], device_id=target, device_id_type=MESH)
        self.sends.append(copy)
        return copy.start

    def arrival(self, m, chip, core):
        piece = self.piece(m, chip, core)
        return pltpu.make_async_remote_copy(
            src_ref=piece, dst_ref=piece, send_sem=self.send_sem.at[0],
            recv_sem=self.recv_sem.at[m, chip * 2 + core], device_id=self.me.mate, device_id_type=MESH).wait_recv

    def forward(self, m, z, p, targets):
        chip = z * 4 + p
        return [self.arrival(m, chip, self.me.core)] + [
            self.sender(m, self.piece(m, chip, self.me.core), chip, target) for target in targets
        ]

    def steps(self, m):
        me = self.me
        begin = [
            self.sender(m, self.srcs[m], me.dp, target)
            for target in [me.on_line(z) for z in me.line] + [me.first, me.second, me.mate]
        ]
        begin.append(pltpu.make_async_copy(self.srcs[m], self.piece(m, me.dp, me.core), self.own_sem.at[m]).start)
        line = []
        for z in me.line[::-1]:
            line += self.forward(m, z, me.p, [me.first, me.second, me.mate])
        beside = []
        for z in [me.z] + me.line[::-1]:
            beside += self.forward(m, z, me.p_first, [me.second, me.mate])
        rest = []
        for p in (me.p_second, me.p_diag):
            for z in [me.z] + me.line[::-1]:
                rest += self.forward(m, z, p, [me.mate])
        return [begin, line, beside, rest]

    def run(self, entry):
        for act in entry[2]:
            act()

    def run_until(self, time):
        while self.tasks and self.tasks[0][0] <= time:
            self.run(self.tasks.pop(0))

    def take_until(self, time):
        taken = []
        while self.tasks and self.tasks[0][0] <= time:
            taken.append(self.tasks.pop(0))
        return taken

    def need(self, m):
        for entry in [e for e in self.tasks if e[1] == m]:
            self.run(entry)
        self.tasks = [e for e in self.tasks if e[1] != m]
        pltpu.make_async_copy(self.srcs[m], self.piece(m, self.me.dp, self.me.core), self.own_sem.at[m]).wait()
        for chip in range(16):
            self.arrival(m, chip, 1 - self.me.core)()

    def finish(self):
        for copy in self.sends:
            copy.wait_send()


GATHER_TIMES = (
    (1, 6, 10, 15),
    (0, 5, 9, 14),
    (2, 11, 19, 27),
    (10, 20, 26, 34),
    (18, 31, 42, 54),
    (30, 48, 60, 74),
)


def loop_with(steps, count, begin, length, body, slots=(0,)):
    due = {}
    for i in range(count):
        for part, k in sorted((part, k) for k, part in enumerate(slots)):
            due[i, k] = steps.take_until(begin + length * (i + part))

    def turn(i, carry):
        def tick(k):
            for at in range(count):
                if due[at, k]:

                    def run(entries=due[at, k]):
                        for entry in entries:
                            steps.run(entry)

                    pl.when(i == at)(run)

        body(i, tick)
        return carry

    lax.fori_loop(0, count, turn, 0)


def norm_rows(values, gain, shift):
    average = jnp.mean(values, -1, keepdims=True)
    centred = values - average
    spread = jnp.mean(centred * centred, -1, keepdims=True)
    return centred * lax.rsqrt(spread + 1e-05) * gain + shift


def two_heads(values):
    return jnp.concatenate([one_head(values, 0), one_head(values, 1)], 0)


def columns(j, size=128):
    return pl.ds(pl.multiple_of(j * size, size), size)


def forward_kernel(*refs):
    (length_ref, x_ref, vectors_in, up_bias_in, down_bias_in, self_in, cross_in, up_in, frames_hbm, down_in) = refs[:10]
    (small_out, ckv_out, self_out, cqo_out, up_out, down_out, kv_out, vec_ref, normed_one_ref, query_ref, kv_row_ref,
     attended_ref, self_lse_ref, after_self_ref, normed_two_ref, row_query_ref, cross_lse_ref, mixed_ref,
     after_cross_ref, normed_three_ref, bias_ref, seg_ref, info_ref, ranked_hbm) = refs[10:34]
    (frames_in, frames_ref, small_f32, small_in, half_wide, half_narrow, pair_wide, pair_narrow, small_vm, ckv_vm, self_vm, cqo_vm, kv_vm, acc_ref, stat_ref, part_ref, part_stat_ref, give_ref,
     give_stat_ref, take_ref, take_stat_ref, send_sem, recv_sem, own_sem, half_sems, mate_sems, load_sem,
     frame_sem) = refs[34:]
    me = Place()
    core = me.core
    width = x_ref.shape[1]
    toks = x_ref.shape[0]
    frames_load = pltpu.make_async_copy(frames_hbm, frames_in, frame_sem.at[0])
    frames_load.start()
    small_f32[...] = jnp.zeros_like(small_f32)
    small_f32[:12, :vectors_in.shape[1]] = vectors_in[...].astype(jnp.float32)
    small_f32[12:13, :down_bias_in.shape[1]] = down_bias_in[...].astype(jnp.float32)
    small_f32[13:14, :up_bias_in.shape[1]] = up_bias_in[...].astype(jnp.float32)
    small_in[...] = small_f32[...].astype(jnp.bfloat16)
    me.greet()

    def to_mate(src, dst, k):
        return pltpu.make_async_remote_copy(
            src_ref=src, dst_ref=dst, send_sem=mate_sems.at[0, k], recv_sem=mate_sems.at[1, k], device_id=me.mate,
            device_id_type=MESH)

    def half_of(m, which):
        shard = (None, cross_in, self_in, cross_in, up_in)[m]
        size = HALF_COLS[m]
        begin = (0, width, 0, 0, 0)[m] + which * (0, width, size, 3 * width, size)[m]
        return shard.at[:, pl.ds(pl.multiple_of(begin, size), size)]

    buffers = {1: (half_narrow.at[0], pair_narrow.at[0]), 2: (half_wide.at[0], pair_wide.at[0]),
               3: (half_narrow.at[1], pair_narrow.at[1]), 4: (half_wide.at[1], pair_wide.at[1])}
    halves = {
        m: pltpu.make_async_remote_copy(
            src_ref=half_of(m, 1 - core), dst_ref=buffers[m][0], send_sem=half_sems.at[0, m],
            recv_sem=half_sems.at[1, m], device_id=me.mate, device_id_type=MESH)
        for m in buffers
    }
    for copy in halves.values():
        copy.start()
    sources = (small_in,) + tuple(buffers[m][1] for m in buffers) + (down_in,)
    gather = Gather(me, sources, (small_out, ckv_out, self_out, cqo_out, up_out, down_out), send_sem, recv_sem, own_sem)
    for m, (came_ref, both_ref) in buffers.items():
        halves[m].wait()
        own = half_of(m, core)[...].astype(jnp.float32)
        came = came_ref[...].astype(jnp.float32)
        both_ref[...] = jnp.concatenate(
            [jnp.where(core == 0, own, came), jnp.where(core == 0, came, own)], 0).astype(jnp.bfloat16)
        gather.run_until((0, 1, 2, 2, 2)[m])

    def fetch(src, dst, k):
        copy = pltpu.make_async_copy(src, dst, load_sem.at[k])
        copy.start()
        copy.wait()

    lengths = [length_ref[0, clip] for clip in range(3)]
    ends = [lengths[0], lengths[0] + lengths[1], lengths[0] + lengths[1] + lengths[2]]

    def clip_at(position):
        return sum((position >= end).astype(jnp.int32) for end in ends)

    def number_row(value):
        return jnp.zeros((1, width), jnp.int32) + value

    length_rows = [number_row(length) for length in lengths]
    big = jnp.where(length_rows[1] > length_rows[0], 1, 0)
    big = jnp.where(length_rows[2] > jnp.maximum(length_rows[0], length_rows[1]), 2, big)
    order = [big, jnp.where(big == 0, 1, 0), jnp.where(big == 2, 1, 2)]
    info_ref[...] = jnp.zeros_like(info_ref)
    for k in (1, 2):
        info_ref[k - 1:k] = jnp.where(order[k] < big, 0, 3)
    for clip in range(3):
        info_ref[2 + clip:3 + clip] = jnp.where(order[0] == clip, 0, jnp.where(order[1] == clip, 1, 2))
    group_ref = info_ref.at[:, pl.ds(0, 128)]
    places = clip_at(lax.broadcasted_iota(jnp.int32, (1, 2 * toks), 1))
    seg_ref[...] = jnp.where(
        places == order[0][:, :2 * toks], 0,
        jnp.where(places == order[1][:, :2 * toks], 1, jnp.where(places == order[2][:, :2 * toks], 2, 3)))
    key_at = core * toks - toks + lax.broadcasted_iota(jnp.int32, bias_ref.shape, 0)
    query_at = core * toks + lax.broadcasted_iota(jnp.int32, bias_ref.shape, 1)
    allowed = (clip_at(key_at) == clip_at(query_at)) & (key_at <= query_at) & (key_at >= 0)
    bias_ref[...] = jnp.where(allowed, 0.0, -1e30)
    frames_load.wait()
    for k in range(3):
        frames_ref[k] = jnp.where(
            order[k] == 0, frames_in[0], jnp.where(order[k] == 1, frames_in[1], frames_in[2]))
    ranked_store = pltpu.make_async_copy(frames_ref, ranked_hbm, frame_sem.at[0])
    ranked_store.start()
    gather.run_until(15)
    gather.need(0)
    fetch(small_out, small_vm, 0)
    total = jnp.zeros(vec_ref.shape, jnp.float32)
    for d in range(32):
        block = jnp.concatenate(
            [small_vm[d].astype(jnp.float32), jnp.zeros((16, width - 128), jnp.float32)], 1)
        total = total + (block if d == 0 else pltpu.roll(block, d * 24, 1))
    vec_ref[...] = total

    def vec(k):
        return vec_ref[k:k + 1]

    source = x_ref[...].astype(jnp.float32)
    normed_one_ref[...] = norm_rows(source, vec(0), vec(1)).astype(jnp.bfloat16)
    gather.need(1)
    fetch(ckv_out, ckv_vm, 0)
    clips = frames_ref.shape[0]
    tiles = 2 * width // 256

    def project(t, tick):
        tick(0)
        clip, tile = t // tiles, t % tiles
        result = dot(frames_ref[clip], ckv_vm[:, columns(tile, 256)], NN)
        is_value = (tile >= 3).astype(jnp.float32)
        shift = vec_ref[10:11, columns(tile % 3, 256)] * is_value
        kv_vm[clip, :frames_ref.shape[1], columns(tile, 256)] = (result + shift).astype(jnp.bfloat16)

    early, middle = 9, 13
    loop_with(gather, early, 20, 0.65, project)
    gather.run_until(31)
    gather.need(2)
    fetch(self_out, self_vm, 0)

    normed = normed_one_ref[...]
    own_rows = slice(toks, 2 * toks)
    kv_row_ref[own_rows, :width] = dot(normed, self_vm[:, width:2 * width], NN).astype(jnp.bfloat16)
    kv_row_ref[own_rows, width:] = (dot(normed, self_vm[:, 2 * width:3 * width], NN) + vec(7)).astype(jnp.bfloat16)
    kv_copy = to_mate(kv_row_ref.at[own_rows], kv_row_ref.at[slice(0, toks)], 0)
    kv_copy.start()
    query = (dot(normed, self_vm[:, :width], NN) + vec(6)).astype(jnp.bfloat16)
    query_ref[...] = query * jnp.bfloat16(0.125)
    lax.fori_loop(early, middle, lambda t, carry: (project(t, lambda k: None), carry)[1], 0)
    gather.run_until(35)
    kv_copy.wait()

    def self_pair(j, tick):
        tick(0)
        cols = columns(j)
        keys = kv_row_ref[:, cols]
        values_t = kv_row_ref[:, columns(j + 6)].T
        parts = []
        for h in range(2):
            scores = dot(keys, one_head(query_ref[:, cols], h), NT) + bias_ref[...]
            peak = jnp.max(scores, 0, keepdims=True)
            terms = jnp.exp(scores - peak)
            total = jnp.sum(terms, 0, keepdims=True)
            parts.append(dot(values_t[h * 64:(h + 1) * 64], terms.astype(jnp.bfloat16), NN) / total)
            self_lse_ref[j, h:h + 1] = peak + jnp.log(total)
        attended_ref[:, cols] = jnp.concatenate(parts, 0).T

    loop_with(gather, 6, 35, 1.2, self_pair)
    after_self = source + dot(attended_ref[...].astype(jnp.bfloat16), self_vm[:, 3 * width:], NN) + vec(8)
    after_self_ref[...] = after_self
    normed_two = norm_rows(after_self, vec(2), vec(3)).astype(jnp.bfloat16)
    normed_two_ref[...] = normed_two
    gather.run_until(44)
    gather.need(3)
    fetch(cqo_out, cqo_vm, 0)
    my_rows = pl.ds(pl.multiple_of(core * toks, toks), toks)
    cross_query = (dot(normed_two, cqo_vm[:, :width], NN) + vec(9)).astype(jnp.bfloat16)
    row_query_ref[my_rows] = cross_query * jnp.bfloat16(0.125)
    query_copy = to_mate(row_query_ref.at[my_rows], row_query_ref.at[my_rows], 1)
    query_copy.start()
    lax.fori_loop(middle, clips * tiles, lambda t, carry: (project(t, lambda k: None), carry)[1], 0)
    kv_store = pltpu.make_async_copy(kv_vm, kv_out, load_sem.at[1])
    kv_store.start()
    gather.run_until(48)
    query_copy.wait()

    frame_count = frames_ref.shape[1]

    def attend(clip, values_t, query, j):
        scores = dot(kv_vm[clip, :frame_count, columns(j)], query, NT)
        peak = jnp.max(scores, 0, keepdims=True)
        terms = jnp.exp(scores - peak)
        total = jnp.sum(terms, 0, keepdims=True)
        return dot(values_t, terms.astype(jnp.bfloat16), NN), peak, total

    def cross_pair(j, tick):
        values_t = kv_vm[0, :frame_count, columns(j + 6)].T
        mine = seg_ref[...] == 0
        for h in range(2):
            tick(h)
            rows = slice(h * 64, (h + 1) * 64)
            result, peak, total = attend(0, values_t[rows], one_head(row_query_ref[:, columns(j)], h), j)
            acc_ref[rows] = jnp.where(mine, result / total, 0.0)
            stat_ref[h:h + 1] = jnp.where(mine, peak, 0.0)
            stat_ref[2 + h:3 + h] = jnp.where(mine, total, 1.0)
        for clip in (1, 2):
            tick(clip + 1)
            values_t = kv_vm[clip, :frame_count, columns(j + 6)].T
            query_rows = jnp.where(
                group_ref[clip - 1:clip] == 0, row_query_ref[:128, columns(j)], row_query_ref[384:, columns(j)])
            result, peak, total = attend(clip, values_t, two_heads(query_rows), j)
            for h in range(2):
                rows, part = slice(h * 64, (h + 1) * 64), slice(h * 128, (h + 1) * 128)
                of_head = result[rows, part] / total[:, part]
                for spot in (0, 3):
                    cols = slice(spot * 128, (spot + 1) * 128)
                    mine = seg_ref[:, cols] == clip
                    acc_ref[rows, cols] = jnp.where(mine, of_head, acc_ref[rows, cols])
                    stat_ref[h:h + 1, cols] = jnp.where(mine, peak[:, part], stat_ref[h:h + 1, cols])
                    stat_ref[2 + h:3 + h, cols] = jnp.where(mine, total[:, part], stat_ref[2 + h:3 + h, cols])
        my_cols, mate_cols = columns(core, toks), columns(1 - core, toks)
        part_ref[j] = acc_ref[:, my_cols]
        part_stat_ref[j] = stat_ref[:, my_cols]
        give_ref[j] = acc_ref[:, mate_cols].astype(jnp.bfloat16)
        give_stat_ref[j] = stat_ref[:, mate_cols]

    loop_with(gather, 6, 48, 3, cross_pair, (0, 0.33, 0.66, 0.83))
    give_copy = to_mate(give_ref, take_ref, 2)
    give_copy.start()
    give_stat_copy = to_mate(give_stat_ref, take_stat_ref, 3)
    give_stat_copy.start()
    gather.run_until(1000)
    give_copy.wait()
    give_stat_copy.wait()

    def combine(j, carry):
        parts = []
        for h in range(2):
            rows = slice(h * 64, (h + 1) * 64)
            peak_a, peak_b = part_stat_ref[j, h:h + 1], take_stat_ref[j, h:h + 1]
            peak = jnp.maximum(peak_a, peak_b)
            share_a = part_stat_ref[j, 2 + h:3 + h] * jnp.exp(peak_a - peak)
            share_b = take_stat_ref[j, 2 + h:3 + h] * jnp.exp(peak_b - peak)
            total = share_a + share_b
            cross_lse_ref[j, h:h + 1] = peak + jnp.log(total)
            parts.append(part_ref[j, rows] * (share_a / total)
                         + take_ref[j, rows].astype(jnp.float32) * (share_b / total))
        mixed_ref[:, columns(j)] = jnp.concatenate(parts, 0).T
        return carry

    lax.fori_loop(0, 6, combine, 0)
    after_cross = after_self_ref[...] + dot(mixed_ref[...].astype(jnp.bfloat16), cqo_vm[:, width:], NN) + vec(11)
    after_cross_ref[...] = after_cross
    normed_three_ref[...] = norm_rows(after_cross, vec(4), vec(5)).astype(jnp.bfloat16)
    gather.run_until(1000)
    gather.need(4)
    gather.need(5)
    kv_store.wait()
    ranked_store.wait()
    gather.finish()


def fused_forward(lengths, x, vectors, up_bias, down_bias, self_w, cross_w, up_w, frames, down_w):
    toks, width = x.shape
    clips, count = frames.shape[:2]
    low, full = jnp.bfloat16, jnp.float32
    pairs = width // 128
    vmem, hbm = pl.BlockSpec(memory_space=pltpu.VMEM), pl.BlockSpec(memory_space=pl.ANY)
    shape = jax.ShapeDtypeStruct
    outs = [
        (hbm, shape((32, 16, 128), low)), (hbm, shape((width, 2 * width), low)), (hbm, shape((width, 4 * width), low)),
        (hbm, shape((width, 2 * width), low)), (hbm, shape((width, 4 * width), low)),
        (hbm, shape((4 * width, width), low)),
        (hbm, shape((clips, width, 2 * width), low)),
        (vmem, shape((16, width), full)), (vmem, shape((toks, width), low)), (vmem, shape((toks, width), low)),
        (vmem, shape((2 * toks, 2 * width), low)), (vmem, shape((toks, width), full)),
        (vmem, shape((pairs, 2, toks), full)), (vmem, shape((toks, width), full)), (vmem, shape((toks, width), low)),
        (vmem, shape((2 * toks, width), low)), (vmem, shape((pairs, 2, toks), full)), (vmem, shape((toks, width), full)),
        (vmem, shape((toks, width), full)), (vmem, shape((toks, width), low)),
        (vmem, shape((2 * toks, toks), full)), (vmem, shape((1, 2 * toks), jnp.int32)), (vmem, shape((8, width), jnp.int32)),
        (hbm, shape(frames.shape, low)),
    ]
    return pl.pallas_call(
        forward_kernel,
        in_specs=[pl.BlockSpec(memory_space=pltpu.SMEM)] + [vmem] * 7 + [hbm] * 2,
        out_specs=tuple(spec for spec, _ in outs),
        out_shape=tuple(s for _, s in outs),
        scratch_shapes=[
            pltpu.VMEM(frames.shape, low), pltpu.VMEM(frames.shape, low), pltpu.VMEM((16, 128), full),
            pltpu.VMEM((16, 128), low), pltpu.VMEM((2, 24, 2 * width), low), pltpu.VMEM((2, 24, width), low), pltpu.VMEM((2, 48, 2 * width), low),
            pltpu.VMEM((2, 48, width), low), pltpu.VMEM((32, 16, 128), low),
            pltpu.VMEM((width, 2 * width), low), pltpu.VMEM((width, 4 * width), low), pltpu.VMEM((width, 2 * width), low),
            pltpu.VMEM((clips, width, 2 * width), low), pltpu.VMEM((128, 2 * toks), full), pltpu.VMEM((4, 2 * toks), full),
            pltpu.VMEM((pairs, 128, toks), full), pltpu.VMEM((pairs, 4, toks), full),
            pltpu.VMEM((pairs, 128, toks), low), pltpu.VMEM((pairs, 4, toks), full),
            pltpu.VMEM((pairs, 128, toks), low), pltpu.VMEM((pairs, 4, toks), full),
            pltpu.SemaphoreType.DMA((400,)), pltpu.SemaphoreType.DMA((6, 32)), pltpu.SemaphoreType.DMA((6,)),
            pltpu.SemaphoreType.DMA((2, 5)), pltpu.SemaphoreType.DMA((2, 4)), pltpu.SemaphoreType.DMA((2,)),
            pltpu.SemaphoreType.DMA((1,)),
        ],
        compiler_params=pltpu.CompilerParams(collective_id=0, has_side_effects=True, vmem_limit_bytes=60 * 2**20),
        name="fused_forward",
    )(lengths, x, vectors, up_bias, down_bias, self_w, cross_w, up_w, frames, down_w)


class Scatter:
    def __init__(self, me, grads, outs, buffers, sems, times, after):
        self.me, self.grads, self.outs, self.buffers = me, grads, outs, buffers
        self.send_sem, self.own_sem, self.pair_sem, self.plane_sem, self.line_sem, self.free_sem = sems
        self.sends = {m: [] for m in range(len(grads))}
        self.count = 0
        self.order = me.line + [me.z]
        self.tasks = []
        for m, times_of in enumerate(times):
            for time, acts in zip(times_of, self.steps(m)):
                self.tasks.append((time, m, acts))
        for late, early in after.items():
            self.tasks = [
                (time, m, ([self.wait_free] if m == late and time == times[late][0] else []) + acts
                 + ([functools.partial(self.give_free, early)] if m == early and time == times[early][-1] else []))
                for time, m, acts in self.tasks
            ]
        self.tasks.sort(key=lambda entry: entry[:2])

    def give_free(self, m):
        for copy in self.sends.pop(m):
            copy.wait_send()
        for target in self.me.peers:
            pl.semaphore_signal(self.free_sem, inc=1, device_id=target, device_id_type=MESH)

    def wait_free(self):
        pl.semaphore_wait(self.free_sem, len(self.me.peers))

    def sender(self, m, src, dst, sem, target):
        copy = pltpu.make_async_remote_copy(
            src_ref=src, dst_ref=dst, send_sem=self.send_sem.at[self.count], recv_sem=sem, device_id=target,
            device_id_type=MESH)
        self.count += 1
        self.sends[m].append(copy)
        return copy.start

    def arrival(self, dst, sem):
        return pltpu.make_async_remote_copy(
            src_ref=dst, dst_ref=dst, send_sem=self.send_sem.at[0], recv_sem=sem, device_id=self.me.mate,
            device_id_type=MESH).wait_recv

    def steps(self, m):
        me, order = self.me, self.order
        grad, out = self.grads[m], self.outs[m]
        own, pair, plane_a, plane_b, plane_c, line = self.buffers[m]
        own_sem, pair_sem, plane_sem, line_sem = self.own_sem, self.pair_sem, self.plane_sem, self.line_sem

        def adder(dst, *others):
            def act():
                total = dst[...].astype(jnp.float32)
                for other in others:
                    total = total + other[...].astype(jnp.float32)
                dst[...] = total.astype(dst.dtype)
            return act

        loads = [
            pltpu.make_async_copy(grad.at[:, p, me.core], own, own_sem.at[m, k])
            for k, p in enumerate((me.p_diag, me.p_second, me.p_first, me.p))
        ]
        begin = [loads[0].start]
        for p in (me.p_diag, me.p_first, me.p_second, me.p):
            begin.append(self.sender(m, grad.at[:, p, 1 - me.core], pair.at[:, p], pair_sem.at[m, p], me.mate))
        diag, second, first, last = (
            [loads[k].wait, self.arrival(pair.at[:, p], pair_sem.at[m, p])]
            for k, p in enumerate((me.p_diag, me.p_second, me.p_first, me.p))
        )
        for z in order:
            diag += [adder(pair.at[z, me.p_diag], own.at[z]),
                     self.sender(m, pair.at[z, me.p_diag], plane_a.at[z], plane_sem.at[m, 0, z], me.second)]
            second += [adder(pair.at[z, me.p_second], own.at[z]),
                       self.sender(m, pair.at[z, me.p_second], plane_c.at[z], plane_sem.at[m, 2, z], me.second)]
            first += [self.arrival(plane_a.at[z], plane_sem.at[m, 0, z]),
                      adder(pair.at[z, me.p_first], own.at[z], plane_a.at[z]),
                      self.sender(m, pair.at[z, me.p_first], plane_b.at[z], plane_sem.at[m, 1, z], me.first)]
        diag.append(loads[1].start)
        second.append(loads[2].start)
        first.append(loads[3].start)
        for z in me.line:
            last += [self.arrival(plane_b.at[z], plane_sem.at[m, 1, z]),
                     self.arrival(plane_c.at[z], plane_sem.at[m, 2, z]),
                     adder(pair.at[z, me.p], own.at[z], plane_b.at[z], plane_c.at[z]),
                     self.sender(m, pair.at[z, me.p], line.at[me.z], line_sem.at[m, me.z], me.on_line(z))]

        def total():
            part = own[me.z].astype(jnp.float32) + pair[me.z, me.p].astype(jnp.float32)
            out[...] = part + plane_b[me.z].astype(jnp.float32) + plane_c[me.z].astype(jnp.float32)

        def from_line(source):
            def act():
                out[...] += line[source].astype(jnp.float32)
            return act

        final = [self.arrival(plane_b.at[me.z], plane_sem.at[m, 1, me.z]),
                 self.arrival(plane_c.at[me.z], plane_sem.at[m, 2, me.z]), total]
        for source in me.line[::-1]:
            final += [self.arrival(line.at[source], line_sem.at[m, source]), from_line(source)]
        return [begin, diag, second, first, last, final]

    def run(self, entry):
        for act in entry[2]:
            act()

    def run_until(self, time):
        while self.tasks and self.tasks[0][0] <= time:
            self.run(self.tasks.pop(0))

    def take_until(self, time):
        taken = []
        while self.tasks and self.tasks[0][0] <= time:
            taken.append(self.tasks.pop(0))
        return taken

    def finish(self):
        self.run_until(10**6)
        for copies in self.sends.values():
            for copy in copies:
                copy.wait_send()


def scatter_buffers(grad):
    leads = ((4,), (4, 4), (4,), (4,), (4,), (4,))
    return [pltpu.VMEM(lead + grad.shape[1:], grad.dtype) for lead in leads]


def scatter_sems(count):
    dma = pltpu.SemaphoreType.DMA
    return [dma((20 * count,)), dma((count, 4)), dma((count, 4)), dma((count, 3, 4)), dma((count, 4)),
            pltpu.SemaphoreType.REGULAR]


def scatter_view(grad):
    return grad.reshape((4, 4, 2) + grad.shape[1:])


BACK_TIMES = (
    (0, 8, 9, 20, 32, 44),
    (1, 20, 21, 34, 46, 58),
    (45, 53, 54, 63, 70, 80),
    (66, 71, 72, 79, 86, 95),
    (70, 73, 74, 82, 89, 98),
)


def norm_rows_back(values, gain, grad):
    average = jnp.mean(values, -1, keepdims=True)
    centred = values - average
    scale = lax.rsqrt(jnp.mean(centred * centred, -1, keepdims=True) + 1e-05)
    normed = centred * scale
    inner = grad * gain
    mean_inner = jnp.mean(inner, -1, keepdims=True)
    mean_both = jnp.mean(inner * normed, -1, keepdims=True)
    result = scale * (inner - mean_inner - normed * mean_both)
    return result, jnp.sum(grad * normed, 0, keepdims=True), jnp.sum(grad, 0, keepdims=True)


def backward_kernel(*refs):
    (info_ref, x_ref, bias_ref, seg_ref, vec_ref, gac_ref, mixed_ref, cross_lse_ref, row_query_ref, after_self_ref,
     attended_ref, self_lse_ref, query_ref, kv_row_ref, normed_one_ref, normed_two_ref, rows_ref, up_bias_ref, cqo_hbm,
     ckv_hbm, self_hbm, kv_hbm, frames_hbm, up_hbm, down_hbm) = refs[:25]
    (input_grad_ref, encoder_hbm, up_out, down_out, cross_out, self_out, small_out, dkv_hbm, cross_hbm,
     self_grad_hbm) = refs[25:35]
    scratch = refs[35:]
    up_buffers, down_buffers, cross_buffers, small_buffers = (scratch[k * 6:(k + 1) * 6] for k in range(4))
    sems, scratch = scratch[24:30], scratch[30:]
    (cross_vm, kv_vm, frame_ref, turned_ref, tile_ref, stage_ref, small_ref, row_grad_ref, row_stat_ref, acc_ref,
     own_ref, give_ref, take_ref, take_query_ref, cq_ref, qkv_ref, vec_grad_ref, load_sem, mate_sems, tile_sem,
     stage_sem, frame_sem) = scratch
    group_ref = info_ref.at[:, pl.ds(0, 128)]
    me = Place()
    core = me.core
    toks, width = x_ref.shape
    frames = frames_hbm.shape[1]
    clips = kv_hbm.shape[0]
    low, full = jnp.bfloat16, jnp.float32
    halves = [pltpu.make_async_copy(cqo_hbm.at[:, pl.ds(k * width, width)], cross_vm.at[k], load_sem.at[k])
              for k in range(2)]
    kv_load = pltpu.make_async_copy(kv_hbm, kv_vm, load_sem.at[2])
    frame_loads = [
        pltpu.make_async_copy(
            frames_hbm.at[clip], frame_ref.at[:, pl.ds(clip % 2 * width, width)], frame_sem.at[clip % 2])
        for clip in range(clips)
    ]
    for copy in [halves[1], kv_load, halves[0]] + frame_loads[:2]:
        copy.start()
    me.greet()
    self_buffers = [
        ref.at[(slice(None),) * (len(ref.shape) - 1) + (pl.ds(0, 3 * width),)] for ref in up_buffers
    ]
    scatter = Scatter(
        me, (up_hbm, down_hbm, cross_hbm, self_grad_hbm, small_ref), (up_out, down_out, cross_out, self_out, small_out),
        (up_buffers, down_buffers, cross_buffers, self_buffers, small_buffers), sems, BACK_TIMES, {3: 0})
    scatter.run_until(1)

    def to_mate(src, dst, k):
        return pltpu.make_async_remote_copy(
            src_ref=src, dst_ref=dst, send_sem=mate_sems.at[0, k], recv_sem=mate_sems.at[1, k], device_id=me.mate,
            device_id_type=MESH)

    my_rows = pl.ds(pl.multiple_of(core * toks, toks), toks)
    my_cols = columns(core, toks)

    def head_rows(product, store):
        turned = product.T
        for h in range(2):
            store(h, jnp.sum(turned[h * 64:(h + 1) * 64], 0, keepdims=True))

    def tile_store(grad_hbm, slot, t):
        return pltpu.make_async_copy(tile_ref.at[slot], grad_hbm.at[:, :, :, :, columns(t, 256)], tile_sem.at[slot])

    def weight_tiles(grad_hbm, first_tile, count, tile, before=None):
        def turn(t, carry):
            slot = t % 2

            @pl.when(t >= 2)
            def _():
                tile_store(grad_hbm, slot, first_tile + t - 2).wait()

            value = tile(columns(t, 256))
            tile_ref[slot] = value.reshape(4, 4, 2, width // 32, 256).astype(low)
            tile_store(grad_hbm, slot, first_tile + t).start()
            return carry

        lax.fori_loop(0, count, turn, 0)
        for t in range(max(0, count - 2), count):
            tile_store(grad_hbm, t % 2, first_tile + t).wait()

    def product_tiles(grad_hbm, first_tile, left, right_ref):
        turned = left.T
        weight_tiles(grad_hbm, first_tile, right_ref.shape[1] // 256, lambda cols: dot(turned, right_ref[:, cols], NN))

    halves[1].wait()
    grad_cross = gac_ref[...].astype(low)
    grad_mixed = dot(grad_cross, cross_vm[1], NT).astype(low)
    row_grad_ref[my_rows] = grad_mixed
    grad_copy = to_mate(row_grad_ref.at[my_rows], row_grad_ref.at[my_rows], 0)
    grad_copy.start()
    for j in range(6):
        cols = slice(j * 128, (j + 1) * 128)
        product = grad_mixed[:, cols].astype(full) * mixed_ref[:, cols]
        row_stat_ref[j, 0:2, my_cols] = cross_lse_ref[j]

        def keep(h, row, j=j):
            row_stat_ref[j, 2 + h:3 + h, my_cols] = row

        head_rows(product, keep)
    stat_copy = to_mate(row_stat_ref.at[:, :, my_cols], row_stat_ref.at[:, :, my_cols], 1)
    stat_copy.start()
    cq_ref[...] = grad_cross
    product_tiles(cross_hbm, 9, mixed_ref[...].astype(low), cq_ref)

    def turn_frames(clip):
        frame_loads[clip].wait()
        turned_ref[clip] = frame_ref[:, clip % 2 * width:(clip % 2 + 1) * width].T

    turn_frames(0)
    frame_loads[2].start()
    turn_frames(1)
    kv_load.wait()
    scatter.run_until(5)
    grad_copy.wait()
    stat_copy.wait()

    def cross_pair(j, tick):
        def back(clip, keys_t, query, grad, lse, inner):
            weights = jnp.exp(dot(kv_vm[clip, :frames, columns(j)], query, NT) - lse)
            grad_v = dot(weights.astype(low), grad, NN)
            grad_s = (weights * (dot(kv_vm[clip, :frames, columns(j + 6)], grad, NT) - inner)).astype(low)
            return dot(keys_t, grad_s, NN), dot(grad_s, query, NN), grad_v

        keys_t = kv_vm[0, :frames, columns(j)].T
        mine = seg_ref[...] == 0
        grad_k = grad_v = None
        for h in range(2):
            tick(h)
            query, grad = one_head(row_query_ref[:, columns(j)], h), one_head(row_grad_ref[:, columns(j)], h)
            rows = slice(h * 64, (h + 1) * 64)
            acc_ref[rows], part_k, part_v = back(
                0, keys_t[rows], query, grad, jnp.where(mine, row_stat_ref[j, h:h + 1], 1e30),
                row_stat_ref[j, 2 + h:3 + h])
            grad_k = part_k if grad_k is None else grad_k + part_k
            grad_v = part_v if grad_v is None else grad_v + part_v
        kv_vm[0, :frames, columns(j)] = grad_k.astype(low)
        kv_vm[0, :frames, columns(j + 6)] = grad_v.astype(low)
        for clip in (1, 2):
            tick(clip + 1)
            in_first = group_ref[clip - 1:clip] == 0

            def chosen(ref):
                return two_heads(jnp.where(in_first, ref[:128, columns(j)], ref[384:, columns(j)]))

            def chosen_row(row):
                return jnp.where(in_first, row_stat_ref[j, row:row + 1, :128], row_stat_ref[j, row:row + 1, 384:])

            mine = jnp.where(in_first, seg_ref[:, :128], seg_ref[:, 384:]) == clip
            lse = jnp.concatenate([jnp.where(mine, chosen_row(h), 1e30) for h in range(2)], 1)
            inner = jnp.concatenate([chosen_row(2 + h) for h in range(2)], 1)
            grad_q, grad_k, grad_v = back(
                clip, kv_vm[clip, :frames, columns(j)].T, chosen(row_query_ref), chosen(row_grad_ref), lse, inner)
            for h in range(2):
                rows, part = slice(h * 64, (h + 1) * 64), slice(h * 128, (h + 1) * 128)
                for spot in (0, 3):
                    cols = slice(spot * 128, (spot + 1) * 128)
                    acc_ref[rows, cols] += jnp.where(in_first == (spot == 0), grad_q[rows, part], 0.0)
            kv_vm[clip, :frames, columns(j)] = grad_k.astype(low)
            kv_vm[clip, :frames, columns(j + 6)] = grad_v.astype(low)
        own_ref[:, columns(j)] = (acc_ref[:, my_cols] * 0.125).T
        give_ref[:, columns(j)] = (acc_ref[:, columns(1 - core, toks)] * 0.125).T.astype(low)

    loop_with(scatter, 6, 6, 4, cross_pair, (0, 0.33, 0.66, 0.83))
    query_copy = to_mate(give_ref.at[:, pl.ds(0, width)], take_query_ref, 2)
    query_copy.start()
    dkv_store = pltpu.make_async_copy(kv_vm, dkv_hbm, load_sem.at[2])
    dkv_store.start()
    vec_grad_ref[...] = rows_ref[...]
    vec_grad_ref[10:11] = sum(
        jnp.sum(kv_vm[clip, :frames, width:].astype(full), 0, keepdims=True) for clip in range(clips))
    turn_frames(2)
    scatter.run_until(37)

    def frames_tile(cols):
        total = dot(turned_ref[0], kv_vm[0, :frames, cols], NN)
        for clip in range(1, clips):
            total = total + dot(turned_ref[clip], kv_vm[clip, :frames, cols], NN)
        return total

    weight_tiles(cross_hbm, 3, 6, frames_tile)
    halves[0].wait()
    query_copy.wait()
    grad_query = (own_ref[:, :width] + take_query_ref[...].astype(full)).astype(low)
    cq_ref[...] = grad_query
    product_tiles(cross_hbm, 0, normed_two_ref[...], cq_ref)
    dkv_store.wait()
    self_loads = [
        pltpu.make_async_copy(
            self_hbm.at[:, pl.ds(k * 2 * width, 2 * width)], kv_vm.at[k], load_sem.at[2 + k]) for k in range(2)
    ]
    for copy in self_loads:
        copy.start()
    vec_grad_ref[9:10] = jnp.sum(grad_query.astype(full), 0, keepdims=True)
    grad_part, gain, shift = norm_rows_back(after_self_ref[...], vec_ref[2:3], dot(grad_query, cross_vm[0], NT))
    vec_grad_ref[2:3] = gain
    vec_grad_ref[3:4] = shift
    grad_after_self = gac_ref[...] + grad_part
    input_grad_ref[...] = grad_after_self
    grad_low = grad_after_self.astype(low)
    vec_grad_ref[8:9] = jnp.sum(grad_low.astype(full), 0, keepdims=True)
    cq_ref[...] = grad_low
    product_tiles(cross_hbm, 12, attended_ref[...].astype(low), cq_ref)
    scatter.run_until(46)
    for copy in self_loads:
        copy.wait()
    grad_attended = dot(grad_low, kv_vm[1, :width, width:], NT).astype(low)
    row_grad_ref[:toks] = grad_attended
    for j in range(6):
        cols = slice(j * 128, (j + 1) * 128)

        def keep_self(h, row, j=j):
            row_stat_ref[j, h:h + 1, :toks] = row

        head_rows(grad_attended[:, cols].astype(full) * attended_ref[:, cols], keep_self)

    def self_pair(j, tick):
        tick(0)
        cols, value_cols = columns(j), columns(j + 6)
        keys, values = kv_row_ref[:, cols], kv_row_ref[:, value_cols]
        keys_t = keys.T
        grad_k = grad_v = None
        parts = []
        for h in range(2):
            query, grad = one_head(query_ref[:, cols], h), one_head(row_grad_ref[:toks, cols], h)
            weights = jnp.exp(dot(keys, query, NT) + bias_ref[...] - self_lse_ref[j, h:h + 1])
            part = dot(weights.astype(low), grad, NN)
            grad_v = part if grad_v is None else grad_v + part
            inner = row_stat_ref[j, h:h + 1, :toks]
            grad_s = (weights * (dot(values, grad, NT) - inner)).astype(low)
            part = dot(grad_s, query, NN)
            grad_k = part if grad_k is None else grad_k + part
            parts.append(dot(keys_t[h * 64:(h + 1) * 64], grad_s, NN))
        qkv_ref[:, cols] = (jnp.concatenate(parts, 0) * 0.125).T.astype(low)
        own_ref[:, cols] = grad_k[toks:]
        own_ref[:, value_cols] = grad_v[toks:]
        give_ref[:, cols] = grad_k[:toks].astype(low)
        give_ref[:, value_cols] = grad_v[:toks].astype(low)

    loop_with(scatter, 6, 52, 1.4, self_pair)
    row_copy = to_mate(give_ref, take_ref, 3)
    row_copy.start()
    scatter.run_until(62)
    row_copy.wait()
    qkv_ref[:, width:] = (own_ref[...] + take_ref[...].astype(full)).astype(low)
    product_tiles(self_grad_hbm, 0, normed_one_ref[...], qkv_ref)
    scatter.run_until(66)
    sums = jnp.sum(qkv_ref[...].astype(full), 0, keepdims=True)
    vec_grad_ref[6:7] = sums[:, :width]
    vec_grad_ref[7:8] = sums[:, 2 * width:]
    grad_normed = dot(qkv_ref[:, :2 * width], kv_vm[0, :width], NT) + dot(
        qkv_ref[:, 2 * width:], kv_vm[1, :width, :width], NT)
    grad_part, gain, shift = norm_rows_back(x_ref[...].astype(full), vec_ref[0:1], grad_normed)
    vec_grad_ref[0:1] = gain
    vec_grad_ref[1:2] = shift
    input_grad_ref[...] += grad_part
    kv_load = pltpu.make_async_copy(dkv_hbm, kv_vm, load_sem.at[2])
    kv_load.start()
    for k in range(2):
        pltpu.make_async_copy(ckv_hbm.at[:, pl.ds(k * width, width)], cross_vm.at[k], load_sem.at[k]).start()
    small_ref[...] = jnp.zeros_like(small_ref)
    rows = vec_grad_ref[...]
    for d in range(32):
        place = (d // 8, d // 2 % 4, d % 2)
        turned_rows = rows if d == 0 else pltpu.roll(rows, width - d * 24, 1)
        small_ref[place] = turned_rows[:, :128]
        small_ref[place + (slice(13, 14),)] = up_bias_ref[d:d + 1]
    scatter.run_until(70)
    for k in range(2):
        pltpu.make_async_copy(ckv_hbm.at[:, pl.ds(k * width, width)], cross_vm.at[k], load_sem.at[k]).wait()
    kv_load.wait()
    blocks = width // 128

    def encoder_store(clip):
        rows = pl.ds(clip * frames * blocks, frames * blocks)
        return pltpu.make_async_copy(stage_ref, encoder_hbm.at[rows], stage_sem.at[0])

    for clip in range(clips):
        place = info_ref[2 + clip:3 + clip]
        for part in (slice(0, width), slice(width, 2 * width)):
            frame_ref[:, part] = jnp.where(
                place == 0, kv_vm[0, :frames, part],
                jnp.where(place == 1, kv_vm[1, :frames, part], kv_vm[2, :frames, part]))

        def encoder_tile(t, tick, clip=clip):
            tick(0)
            rows = columns(t, 256)
            value = dot(frame_ref[:, :width], cross_vm[0, rows], NT) + dot(frame_ref[:, width:], cross_vm[1, rows], NT)
            if clip > 0:
                pl.when(t == 0)(encoder_store(clip - 1).wait)
            for k in range(2):
                stage_ref[pl.ds(2 * t + k, frames, stride=blocks), 0] = value[:, k * 128:(k + 1) * 128]

        loop_with(scatter, width // 256, 71 + 3 * clip, 1, encoder_tile)
        encoder_store(clip).start()
    encoder_store(clips - 1).wait()
    scatter.finish()


def fused_backward(info, x, bias, seg, vec, gac, mixed, cross_lse, row_query, after_self, attended, self_lse, query,
                   kv_row, normed_one, normed_two, rows, up_bias, cqo_full, ckv_full, self_full, kv, frames, grad_up,
                   grad_down):
    toks, width = x.shape
    clips, count = frames.shape[:2]
    low, full = jnp.bfloat16, jnp.float32
    pairs = width // 128
    vmem, hbm = pl.BlockSpec(memory_space=pltpu.VMEM), pl.BlockSpec(memory_space=pl.ANY)
    shape = jax.ShapeDtypeStruct
    small = shape((32, 16, 128), full)
    places = (4, 4, 2, width // 32)
    cross = shape((32, width // 32, 5 * width), low)
    outs = [
        (vmem, shape((toks, width), full)), (hbm, shape((clips * count * width // 128, 1, 128), full)), (vmem, shape(grad_up.shape[1:], full)),
        (vmem, shape(grad_down.shape[1:], full)), (vmem, shape(cross.shape[1:], full)),
        (vmem, shape((width // 32, 3 * width), full)), (vmem, shape(small.shape[1:], full)), (hbm, shape(kv.shape, low)),
        (hbm, shape(places + (5 * width,), low)), (hbm, shape(places + (3 * width,), low)),
    ]
    return pl.pallas_call(
        backward_kernel,
        in_specs=[vmem] * 18 + [hbm] * 7,
        out_specs=tuple(spec for spec, _ in outs),
        out_shape=tuple(s for _, s in outs),
        scratch_shapes=scatter_buffers(grad_up) + scatter_buffers(grad_down) + scatter_buffers(cross)
        + scatter_buffers(small) + scatter_sems(5) + [
            pltpu.VMEM((2, width, width), low), pltpu.VMEM((clips, width, 2 * width), low),
            pltpu.VMEM((count, 2 * width), low), pltpu.VMEM((clips, width, count), low),
            pltpu.VMEM((2,) + places + (256,), low), pltpu.VMEM((count * width // 128, 1, 128), full),
            pltpu.VMEM((4, 4, 2, 16, 128), full), pltpu.VMEM((2 * toks, width), low),
            pltpu.VMEM((pairs, 4, 2 * toks), full), pltpu.VMEM((128, 2 * toks), full),
            pltpu.VMEM((toks, 2 * width), full), pltpu.VMEM((toks, 2 * width), low),
            pltpu.VMEM((toks, 2 * width), low), pltpu.VMEM((toks, width), low), pltpu.VMEM((toks, width), low),
            pltpu.VMEM((toks, 3 * width), low), pltpu.VMEM((16, width), full), pltpu.SemaphoreType.DMA((4,)),
            pltpu.SemaphoreType.DMA((2, 4)), pltpu.SemaphoreType.DMA((2,)), pltpu.SemaphoreType.DMA((1,)),
            pltpu.SemaphoreType.DMA((2,)),
        ],
        compiler_params=pltpu.CompilerParams(collective_id=2, has_side_effects=True, vmem_limit_bytes=63 * 2**20),
        name="fused_backward",
    )(info, x, bias, seg, vec, gac, mixed, cross_lse, row_query, after_self, attended, self_lse, query, kv_row,
      normed_one, normed_two, rows, up_bias, cqo_full, ckv_full, self_full, kv, frames, scatter_view(grad_up),
      scatter_view(grad_down))


def ffn_kernel(normed_ref, grad_ref, after_ref, vec_ref, up_ref, bias_ref, down_ref, out_ref, back_ref, grad_up_ref,
               grad_down_ref, grad_bias_ref, rows_ref, turned_ref, sum_ref, back_sum_ref):
    t = pl.program_id(0)

    @pl.when(t == 0)
    def _():
        turned_ref[...] = normed_ref[...].T
        sum_ref[...] = jnp.zeros_like(sum_ref)
        back_sum_ref[...] = jnp.zeros_like(back_sum_ref)

    grad = grad_ref[...]
    pre = dot(normed_ref[...], up_ref[...], NN) + bias_ref[...]
    below = 0.5 * (1.0 + lax.erf(pre * 0.7071067811865476))
    activated = (pre * below).astype(jnp.bfloat16)
    sum_ref[...] += dot(activated, down_ref[...], NN)
    grad_act = dot(grad, down_ref[...], NT).astype(jnp.bfloat16).astype(jnp.float32)
    density = jnp.exp(-0.5 * pre * pre) * 0.3989422804014327
    grad_pre = (grad_act * (below + pre * density)).astype(jnp.bfloat16)
    back_sum_ref[...] += dot(grad_pre, up_ref[...], NT)
    grad_up_ref[...] = dot(turned_ref[...], grad_pre, NN).astype(jnp.bfloat16)
    grad_down_ref[...] = dot(activated.T, grad, NN).astype(jnp.bfloat16)
    grad_bias_ref[...] = jnp.sum(grad_pre.astype(jnp.float32), 0, keepdims=True)

    @pl.when(t == pl.num_programs(0) - 1)
    def _():
        out_ref[...] = (after_ref[...] + sum_ref[...] + vec_ref[12:13]).astype(jnp.bfloat16)
        grad_rows = grad_ref[...].astype(jnp.float32)
        part, gain, shift = norm_rows_back(after_ref[...], vec_ref[4:5], back_sum_ref[...])
        back = grad_rows + part
        back_ref[...] = back
        rows_ref[...] = jnp.zeros_like(rows_ref)
        rows_ref[4:5] = gain
        rows_ref[5:6] = shift
        rows_ref[11:12] = jnp.sum(back.astype(jnp.bfloat16).astype(jnp.float32), 0, keepdims=True)
        rows_ref[12:13] = jnp.sum(grad_rows, 0, keepdims=True)


def ffn(normed, grad, after, vec, up_full, bias, down_full):
    toks, width = normed.shape
    hidden = up_full.shape[1]
    size = 256
    low, full = jnp.bfloat16, jnp.float32
    shape = jax.ShapeDtypeStruct
    rows = pl.BlockSpec((toks, width), lambda t: (0, 0))
    vecs = pl.BlockSpec((16, width), lambda t: (0, 0))
    up_spec = pl.BlockSpec((width, size), lambda t: (0, t))
    down_spec = pl.BlockSpec((size, width), lambda t: (t, 0))
    bias_spec = pl.BlockSpec((1, size), lambda t: (0, t))
    return pl.pallas_call(
        ffn_kernel,
        grid=(hidden // size,),
        in_specs=[rows, rows, rows, vecs, up_spec, bias_spec, down_spec],
        out_specs=[rows, rows, up_spec, down_spec, bias_spec, vecs],
        out_shape=[
            shape((toks, width), low), shape((toks, width), full), shape(up_full.shape, low),
            shape(down_full.shape, low), shape((1, hidden), full), shape((16, width), full),
        ],
        scratch_shapes=[pltpu.VMEM((width, toks), low), pltpu.VMEM((toks, width), full), pltpu.VMEM((toks, width), full)],
        compiler_params=pltpu.CompilerParams(vmem_limit_bytes=63 * 2**20),
        name="ffn",
    )(normed, grad, after, vec, up_full, bias, down_full)


def place_clips_kernel(order, in_ref, out_ref):
    frames, width = in_ref.shape[1:]
    blocks = width // 128
    for k in range(blocks):
        out_ref[pl.ds(k, frames, stride=blocks), 0] = in_ref[0, :, k * 128:(k + 1) * 128]


def place_clips(order, values):
    clips, frames, width = values.shape
    rows = frames * width // 128
    flat = pl.pallas_call(
        place_clips_kernel,
        grid_spec=pltpu.PrefetchScalarGridSpec(
            num_scalar_prefetch=1,
            grid=(clips,),
            in_specs=[pl.BlockSpec((1, frames, width), lambda k, order: (k, 0, 0))],
            out_specs=pl.BlockSpec((rows, 1, 128), lambda k, order: (order[k], 0, 0)),
        ),
        out_shape=jax.ShapeDtypeStruct((clips * rows, 1, 128), values.dtype),
        compiler_params=pltpu.CompilerParams(vmem_limit_bytes=48 * 2**20),
        name="place_clips",
    )(order, values)
    return flat.reshape(1, clips, frames, width)


def from_behind(value, axis, steps):
    count = lax.axis_size(axis)
    leading, last = (max(0, -steps), min(count, count - steps))
    return lax.ppermute(value, axis, [(source, source + steps) for source in range(leading, last)])


def layer_norm(values, gain, shift):
    average = jnp.mean(values, -1, keepdims=True)
    centred = values - average
    spread = jnp.mean(centred * centred, -1, keepdims=True)
    return centred * lax.rsqrt(spread + 1e-05) * gain + shift


def matmul(left, right):
    return jnp.dot(left, right, preferred_element_type=jnp.float32)


def swap_halves(value):
    return lax.ppermute(value, "seq", [(0, 1), (1, 0)])


def seq_halves(value, axis):
    span = value.shape[axis] // 2
    half = lax.axis_index("seq")
    mine = lax.dynamic_slice_in_dim(value, half * span, span, axis)
    other = lax.dynamic_slice_in_dim(value, (1 - half) * span, span, axis)
    return mine, other


def seq_scatter(value):
    mine, other = seq_halves(value, 0)
    return mine + swap_halves(other.astype(jnp.bfloat16)).astype(value.dtype)


def per_head(values):
    rows = values.reshape(-1, values.shape[2]).T
    return jnp.repeat(rows, HEAD_DIM, axis=1)


def head_sums(values):
    sums = jnp.sum(values.reshape(values.shape[0], -1, HEAD_DIM), -1)
    return sums.T.reshape(-1, 2, values.shape[0])


def plain_forward(
    which, layer_input, frames, mask_bias, row_segment, weights
):
    self_full, cross_full, up_full, down_full, bias_full, out_bias_full, vectors = (
        lax.all_gather(part, ("dp", "seq"), axis=0, tiled=True) for part in weights
    )
    vec = jnp.pad(
        jnp.concatenate([vectors.T, out_bias_full[None]]).astype(jnp.float32), ((0, 3), (0, 0))
    )
    model_width = layer_input.shape[1]
    cross_in = [cross_full[:, k * model_width : (k + 1) * model_width] for k in range(4)]
    ckv_full = cross_full[:, model_width : 3 * model_width]
    cqo_full = jnp.concatenate([cross_in[0], cross_in[3]], 1)
    source = layer_input.astype(jnp.float32)
    normed_one = layer_norm(source, vec[0], vec[1]).astype(jnp.bfloat16)
    proj_bias = jnp.concatenate([vec[6], jnp.zeros_like(vec[6]), vec[7]])
    qkv_low = (matmul(normed_one, self_full[:, : 3 * model_width]) + proj_bias).astype(jnp.bfloat16)
    query = qkv_low[:, :model_width] * jnp.bfloat16(0.125)
    kv_own = qkv_low[:, model_width:]
    kv_row = jnp.concatenate([from_behind(kv_own, "seq", 1), kv_own])
    attended, self_lse = self_forward(query, kv_row, mask_bias)
    attended_low = attended.astype(jnp.bfloat16)
    after_self = source + matmul(attended_low, self_full[:, 3 * model_width :]) + vec[8]
    normed_two = layer_norm(after_self, vec[2], vec[3]).astype(jnp.bfloat16)
    cross_query = (matmul(normed_two, cross_in[0]) + vec[9]).astype(jnp.bfloat16)
    cross_key = jnp.einsum(
        "cfd,de->cfe", frames, cross_in[1], preferred_element_type=jnp.float32
    ).astype(jnp.bfloat16)
    cross_value = (
        jnp.einsum("cfd,de->cfe", frames, cross_in[2], preferred_element_type=jnp.float32)
        + vec[10]
    ).astype(jnp.bfloat16)
    row_query = lax.all_gather(cross_query * jnp.bfloat16(0.125), "seq", axis=0, tiled=True)
    cross_kv = jnp.concatenate([cross_key, cross_value], 2)
    part_mixed, part_stats = cross_forward(which, row_query, cross_kv, row_segment)
    mixed_mine, mixed_other = seq_halves(part_mixed, 0)
    stats_mine, stats_other = seq_halves(part_stats, 2)
    mixed_came = swap_halves(mixed_other.astype(jnp.bfloat16))
    stats_came = swap_halves(stats_other)
    peak = jnp.maximum(stats_mine[:, :2], stats_came[:, :2])
    share_mine = stats_mine[:, 2:] * jnp.exp(stats_mine[:, :2] - peak)
    share_came = stats_came[:, 2:] * jnp.exp(stats_came[:, :2] - peak)
    total = share_mine + share_came
    cross_lse = peak + jnp.log(total)
    mixed_full = mixed_mine * per_head(share_mine / total) + mixed_came.astype(
        jnp.float32
    ) * per_head(share_came / total)
    mixed = mixed_full.astype(jnp.bfloat16)
    after_cross = after_self + matmul(mixed, cross_in[3]) + vec[11]
    normed_three = layer_norm(after_cross, vec[4], vec[5]).astype(jnp.bfloat16)
    return (
        bias_full, ckv_full, self_full, cqo_full, up_full, down_full, cross_kv, vec, normed_one, query, kv_row, attended,
        self_lse, after_self, normed_two, row_query, cross_lse, mixed_full, after_cross, normed_three,
    )


def plain_backward(
    which, layer_input, mask_bias, row_segment, vec, grad_after_cross, mixed_full, cross_lse, row_query, after_self,
    attended, self_lse, query, kv_row, cqo_full, self_full, cross_kv
):
    tok_span, model_width = layer_input.shape
    source = layer_input.astype(jnp.float32)
    grad_cross_low = grad_after_cross.astype(jnp.bfloat16)
    grad_mixed = matmul(grad_cross_low, cqo_full[:, model_width:].T).astype(jnp.bfloat16)
    row_grad = lax.all_gather(grad_mixed, "seq", axis=0, tiled=True)
    cross_inner = head_sums(grad_mixed.astype(jnp.float32) * mixed_full)
    row_stats = lax.all_gather(jnp.stack([cross_lse, cross_inner]), "seq", axis=3, tiled=True)
    part_query, grad_key, grad_value = cross_backward(
        which, row_query, cross_kv, row_segment, row_stats[0], row_stats[1], row_grad
    )
    grad_query_sum = seq_scatter(part_query).astype(jnp.bfloat16)
    grad_cq_bias = jnp.sum(grad_query_sum, 0, dtype=jnp.float32)
    grad_normed_two = matmul(grad_query_sum, cqo_full[:, :model_width].T)
    grad_cv_bias = jnp.sum(grad_value, (0, 1), dtype=jnp.float32)
    _, norm_pull_two = jax.vjp(layer_norm, after_self, vec[2], vec[3])
    grad_part, grad_gain_two, grad_shift_two = norm_pull_two(grad_normed_two)
    grad_after_self = grad_after_cross + grad_part
    grad_self_low = grad_after_self.astype(jnp.bfloat16)
    grad_self_bias = jnp.sum(grad_self_low, 0, dtype=jnp.float32)
    grad_attended = matmul(grad_self_low, self_full[:, 3 * model_width :].T).astype(jnp.bfloat16)
    self_inner = head_sums(grad_attended.astype(jnp.float32) * attended)
    grad_query, grad_key_row, grad_value_row = self_backward(
        query, kv_row, mask_bias, self_lse, self_inner, grad_attended
    )
    grad_kv = jnp.concatenate([grad_key_row, grad_value_row], 1)
    back_kv = from_behind(grad_kv[:tok_span].astype(jnp.bfloat16), "seq", -1)
    grad_qkv_low = jnp.concatenate(
        [grad_query, grad_kv[tok_span:] + back_kv.astype(jnp.float32)], 1
    ).astype(jnp.bfloat16)
    grad_qkv_bias = jnp.sum(grad_qkv_low, 0, dtype=jnp.float32)
    grad_normed_one = matmul(grad_qkv_low, self_full[:, : 3 * model_width].T)
    _, norm_pull_one = jax.vjp(layer_norm, source, vec[0], vec[1])
    grad_part, grad_gain_one, grad_shift_one = norm_pull_one(grad_normed_one)
    input_grad = grad_after_self + grad_part
    nothing = jnp.zeros_like(grad_cq_bias)
    vec_grads = jnp.stack(
        [
            grad_gain_one,
            grad_shift_one,
            grad_gain_two,
            grad_shift_two,
            nothing,
            nothing,
            grad_qkv_bias[:model_width],
            grad_qkv_bias[2 * model_width :],
            grad_self_bias,
            grad_cq_bias,
            grad_cv_bias,
        ]
        + [nothing] * 5
    )
    return (
        input_grad, grad_query_sum, grad_self_low, grad_qkv_low, vec_grads,
        jnp.concatenate([grad_key, grad_value], 2),
    )


def plain_finish(
    normed_one, grad_qkv_low, attended_low, grad_self_low, normed_two, grad_query_sum, mixed, grad_cross_low, frames,
    cross_kv_grad, ckv_full
):
    width = normed_one.shape[1]
    grads_self = jnp.concatenate([matmul(normed_one.T, grad_qkv_low), matmul(attended_low.T, grad_self_low)], 1)
    grad_ckv = jnp.einsum("cfd,cfe->de", frames, cross_kv_grad, preferred_element_type=jnp.float32)
    grads_cross = jnp.concatenate(
        [matmul(normed_two.T, grad_query_sum), grad_ckv, matmul(mixed.T, grad_cross_low)], 1
    )
    encoder_grad = jnp.einsum(
        "cfe,de->cfd", cross_kv_grad, ckv_full, preferred_element_type=jnp.float32
    )
    return encoder_grad, (grads_self, grads_cross)


def fused_device(
    layer_input,
    encoder_states,
    clip_lengths,
    out_grad,
    self_weights,
    cross_weights,
    up_weights,
    down_weights,
    up_bias,
    down_bias,
    vectors,
):
    small_blocks, ckv_full, self_full, cqo_full, up_full, down_full, cross_kv, vec, normed_one, query, kv_row, attended, \
        self_lse, after_self, normed_two, row_query, cross_lse, mixed_full, after_cross, normed_three, mask_bias, \
        row_segment, info, frames = fused_forward(
            clip_lengths, layer_input[0], vectors.T, up_bias[None], down_bias[None], self_weights, cross_weights, up_weights,
            encoder_states[0], down_weights,
        )
    bias_full = small_blocks[:, 13, : up_bias.shape[0]].reshape(-1).astype(jnp.float32)
    layer_output, grad_after_cross, grad_up, grad_down, grad_up_bias, ffn_rows = ffn(
        normed_three, out_grad[0], after_cross, vec, up_full, bias_full[None], down_full
    )
    large = [g.reshape(32, -1, g.shape[1]) for g in (grad_up, grad_down)]
    bias_rows = jnp.pad(grad_up_bias.reshape(32, -1), ((0, 0), (0, 128 - up_bias.shape[0])))
    input_grad, encoder_grad, up_share, down_share, cross_share, self_share, row, *_ = fused_backward(
        info, layer_input[0], mask_bias, row_segment, vec, grad_after_cross, mixed_full, cross_lse, row_query, after_self,
        attended, self_lse, query, kv_row, normed_one, normed_two, ffn_rows, bias_rows, cqo_full, ckv_full, self_full,
        cross_kv, frames, *large
    )
    width = layer_input.shape[2]
    self_share = jnp.concatenate([self_share, cross_share[:, 4 * width :]], 1)
    cross_share = cross_share[:, : 4 * width]
    return (
        layer_output[None], input_grad[None], encoder_grad.reshape((1,) + encoder_states.shape[1:]), self_share, cross_share,
        up_share, down_share, row[13, : up_bias.shape[0]], row[12, : down_bias.shape[0]], row[:12, : vectors.shape[0]].T,
    )


def plain_device(
    layer_input,
    encoder_states,
    clip_lengths,
    out_grad,
    self_weights,
    cross_weights,
    up_weights,
    down_weights,
    up_bias,
    down_bias,
    vectors,
):
    model_width = layer_input.shape[2]
    tok_span = layer_input.shape[1]
    seq_half = lax.axis_index("seq")
    position = seq_half * tok_span + jnp.arange(tok_span, dtype=jnp.int32)
    clip_ends = jnp.cumsum(clip_lengths[0])
    segment = jnp.sum((position[:, None] >= clip_ends[None, :]).astype(jnp.int32), 1)
    key_position = jnp.concatenate([position - tok_span, position])
    key_segment = jnp.sum((key_position[:, None] >= clip_ends[None, :]).astype(jnp.int32), 1)
    allowed = (
        (key_segment[:, None] == segment[None, :])
        & (key_position[:, None] <= position[None, :])
        & (key_position[:, None] >= 0)
    )
    mask_bias = jnp.where(allowed, 0.0, -1e30).astype(jnp.float32)
    row_position = jnp.arange(2 * tok_span, dtype=jnp.int32)
    row_segment = jnp.sum((row_position[:, None] >= clip_ends[None, :]).astype(jnp.int32), 1)[None]
    big = jnp.argmax(clip_lengths[0]).astype(jnp.int32)
    small_one = jnp.where(big == 0, 1, 0)
    small_two = jnp.where(big == 2, 1, 2)
    last_group = 2 * tok_span // 128 - 1
    order = jnp.stack([big, small_one, small_two]).astype(jnp.int32)
    row_segment = jnp.where(
        row_segment == order[0], 0, jnp.where(row_segment == order[1], 1, jnp.where(row_segment == order[2], 2, 3))
    )
    which = jnp.where(order[1:] < big, 0, last_group).astype(jnp.int32)

    frames = jnp.take(encoder_states[0], order, axis=0, mode="clip")
    (
        bias_full, ckv_full, self_full, cqo_full, up_full, down_full, cross_kv, vec, normed_one, query, kv_row, attended,
        self_lse, after_self, normed_two, row_query, cross_lse, mixed_full, after_cross, normed_three,
    ) = plain_forward(
        which, layer_input[0], frames, mask_bias, row_segment,
        (self_weights, cross_weights, up_weights, down_weights, up_bias, down_bias, vectors),
    )
    bias_full = bias_full.astype(jnp.float32)
    layer_output, grad_after_cross, grad_up, grad_down, grad_up_bias, ffn_rows = ffn(
        normed_three, out_grad[0], after_cross, vec, up_full, bias_full[None], down_full
    )
    operands = (
        layer_input[0], mask_bias, row_segment, vec, grad_after_cross, mixed_full, cross_lse, row_query, after_self,
        attended, self_lse, query, kv_row,
    )
    input_grad, grad_query_sum, grad_self_low, grad_qkv_low, vec_grads, cross_kv_grad = plain_backward(
        which, *operands, cqo_full, self_full, cross_kv
    )
    encoder_grad, large = plain_finish(
        normed_one, grad_qkv_low, attended.astype(jnp.bfloat16), grad_self_low, normed_two, grad_query_sum,
        mixed_full.astype(jnp.bfloat16), grad_after_cross.astype(jnp.bfloat16), frames, cross_kv_grad, ckv_full,
    )
    vector_grads = vec_grads + ffn_rows
    shares = tuple(
        lax.psum_scatter(part, ("dp", "seq"), scatter_dimension=0, tiled=True)
        for part in large
        + (grad_up.astype(jnp.float32), grad_down.astype(jnp.float32), grad_up_bias[0], vector_grads[12],
           vector_grads[:12].T)
    )
    return (layer_output[None], input_grad[None], place_clips(order, encoder_grad)) + shares


def solution(mesh):
    return jax.shard_map(
        fused_device if mesh.shape["dp"] == 16 else plain_device,
        mesh=mesh,
        in_specs=(
            P("dp", "seq", None),
            P("dp", None, "seq", None),
            P("dp", None),
            P("dp", "seq", None),
            P(("dp", "seq"), None),
            P(("dp", "seq"), None),
            P(("dp", "seq"), None),
            P(("dp", "seq"), None),
            P(("dp", "seq")),
            P(("dp", "seq")),
            P(("dp", "seq"), None),
        ),
        out_specs=(
            P("dp", "seq", None),
            P("dp", "seq", None),
            P("dp", None, "seq", None),
            P(("dp", "seq"), None),
            P(("dp", "seq"), None),
            P(("dp", "seq"), None),
            P(("dp", "seq"), None),
            P(("dp", "seq")),
            P(("dp", "seq")),
            P(("dp", "seq"), None),
        ),
        check_vma=False,
    )
```

```python
import functools

import jax
import jax.numpy as jnp
from jax import lax
from jax.experimental import pallas as pl
from jax.experimental.pallas import tpu as pltpu
from jax.sharding import PartitionSpec as P

HEAD_DIM = 64
CLIPS = 3
MESH = pl.DeviceIdType.MESH
NT = (((1,), (1,)), ((), ()))
NN = (((1,), (0,)), ((), ()))


def dot(left, right, dims):
    return lax.dot_general(left, right, dims, preferred_element_type=jnp.float32)


def one_head(values, h):
    lane = lax.broadcasted_iota(jnp.int32, values.shape, 1)
    return jnp.where((lane >= 64) == (h == 1), values, jnp.zeros_like(values))


def self_forward_kernel(q_ref, k_ref, v_ref, bias_ref, out_ref, lse_ref):
    keys = k_ref[...]
    values_t = v_ref[...].T
    halves = []
    for h in range(2):
        scores = dot(keys, one_head(q_ref[...], h), NT) + bias_ref[...]
        peak = jnp.max(scores, 0, keepdims=True)
        terms = jnp.exp(scores - peak)
        total = jnp.sum(terms, 0, keepdims=True)
        result = dot(values_t[h * 64:(h + 1) * 64], terms.astype(jnp.bfloat16), NN)
        halves.append(result / total)
        lse_ref[0, h:h + 1] = peak + jnp.log(total)
    out_ref[...] = jnp.concatenate(halves, 0).T.astype(out_ref.dtype)


def self_forward(q, kv, bias):
    toks, width = q.shape
    keys, pairs = kv.shape[0], width // 128
    return pl.pallas_call(
        self_forward_kernel,
        grid=(width // 128,),
        in_specs=[
            pl.BlockSpec((toks, 128), lambda j: (0, j)),
            pl.BlockSpec((keys, 128), lambda j: (0, j)),
            pl.BlockSpec((keys, 128), lambda j: (0, j + pairs)),
            pl.BlockSpec((keys, toks), lambda j: (0, 0)),
        ],
        out_specs=[
            pl.BlockSpec((toks, 128), lambda j: (0, j)),
            pl.BlockSpec((1, 2, toks), lambda j: (j, 0, 0)),
        ],
        out_shape=[
            jax.ShapeDtypeStruct((toks, width), jnp.float32),
            jax.ShapeDtypeStruct((width // 128, 2, toks), jnp.float32),
        ],
        compiler_params=pltpu.CompilerParams(vmem_limit_bytes=48 * 2**20),
        name="self_forward",
    )(q, kv, kv, bias)


def self_backward_kernel(q_ref, k_ref, v_ref, bias_ref, lse_ref, inner_ref, g_ref, dq_ref, dk_ref, dv_ref):
    keys, values = k_ref[...], v_ref[...]
    keys_t = keys.T
    grad_k = grad_v = None
    halves = []
    for h in range(2):
        query, grad = one_head(q_ref[...], h), one_head(g_ref[...], h)
        weights = jnp.exp(dot(keys, query, NT) + bias_ref[...] - lse_ref[0, h:h + 1])
        part = dot(weights.astype(jnp.bfloat16), grad, NN)
        grad_v = part if grad_v is None else grad_v + part
        grad_s = (weights * (dot(values, grad, NT) - inner_ref[0, h:h + 1])).astype(jnp.bfloat16)
        part = dot(grad_s, query, NN)
        grad_k = part if grad_k is None else grad_k + part
        halves.append(dot(keys_t[h * 64:(h + 1) * 64], grad_s, NN))
    dq_ref[...] = (jnp.concatenate(halves, 0) * 0.125).T
    dk_ref[...] = grad_k
    dv_ref[...] = grad_v


def self_backward(q, kv, bias, lse, inner, grad):
    toks, width = q.shape
    keys, pairs = kv.shape[0], width // 128
    tok_spec = pl.BlockSpec((toks, 128), lambda j: (0, j))
    key_spec = pl.BlockSpec((keys, 128), lambda j: (0, j))
    row_spec = pl.BlockSpec((1, 2, toks), lambda j: (j, 0, 0))
    return pl.pallas_call(
        self_backward_kernel,
        grid=(width // 128,),
        in_specs=[tok_spec, key_spec, pl.BlockSpec((keys, 128), lambda j: (0, j + pairs)), pl.BlockSpec((keys, toks), lambda j: (0, 0)), row_spec, row_spec, tok_spec],
        out_specs=[tok_spec, key_spec, key_spec],
        out_shape=[
            jax.ShapeDtypeStruct((toks, width), jnp.float32),
            jax.ShapeDtypeStruct((keys, width), jnp.float32),
            jax.ShapeDtypeStruct((keys, width), jnp.float32),
        ],
        compiler_params=pltpu.CompilerParams(vmem_limit_bytes=48 * 2**20),
        name="self_backward",
    )(q, kv, kv, bias, lse, inner, grad)


def cross_forward_kernel(which, q_ref, k_ref, v_ref, seg_ref, out_ref, stat_ref, acc_ref):
    def attend(clip, values_t, query, h):
        scores = dot(k_ref[clip], query, NT)
        peak = jnp.max(scores, 0, keepdims=True)
        terms = jnp.exp(scores - peak)
        total = jnp.sum(terms, 0, keepdims=True)
        result = dot(values_t[h * 64:(h + 1) * 64], terms.astype(jnp.bfloat16), NN)
        return result / total, peak, total

    values_t = v_ref[0].T
    for h in range(2):
        mine = seg_ref[...] == 0
        result, peak, total = attend(0, values_t, one_head(q_ref[...], h), h)
        acc_ref[h * 64:(h + 1) * 64] = jnp.where(mine, result, 0.0)
        stat_ref[0, h:h + 1] = jnp.where(mine, peak, 0.0)
        stat_ref[0, 2 + h:3 + h] = jnp.where(mine, total, 1.0)
    for clip in (1, 2):
        cols = pl.ds(pl.multiple_of(which[clip - 1] * 128, 128), 128)
        values_t = v_ref[clip].T
        mine = seg_ref[:, cols] == clip
        for h in range(2):
            result, peak, total = attend(clip, values_t, one_head(q_ref[cols], h), h)
            rows = slice(h * 64, (h + 1) * 64)
            acc_ref[rows, cols] = jnp.where(mine, result, acc_ref[rows, cols])
            stat_ref[0, h:h + 1, cols] = jnp.where(mine, peak, stat_ref[0, h:h + 1, cols])
            stat_ref[0, 2 + h:3 + h, cols] = jnp.where(mine, total, stat_ref[0, 2 + h:3 + h, cols])
    out_ref[...] = acc_ref[...].T


def cross_forward(which, q, kv, seg):
    toks, width = q.shape
    clips, frames = kv.shape[:2]
    pairs = width // 128
    kv_spec = pl.BlockSpec((clips, frames, 128), lambda j, w: (0, 0, j))
    v_spec = pl.BlockSpec((clips, frames, 128), lambda j, w: (0, 0, j + pairs))
    tok_spec = pl.BlockSpec((toks, 128), lambda j, w: (0, j))
    return pl.pallas_call(
        cross_forward_kernel,
        grid_spec=pltpu.PrefetchScalarGridSpec(
            num_scalar_prefetch=1,
            grid=(width // 128,),
            in_specs=[tok_spec, kv_spec, v_spec, pl.BlockSpec((1, toks), lambda j, w: (0, 0))],
            out_specs=[tok_spec, pl.BlockSpec((1, 4, toks), lambda j, w: (j, 0, 0))],
            scratch_shapes=[pltpu.VMEM((128, toks), jnp.float32)],
        ),
        out_shape=[
            jax.ShapeDtypeStruct((toks, width), jnp.float32),
            jax.ShapeDtypeStruct((width // 128, 4, toks), jnp.float32),
        ],
        compiler_params=pltpu.CompilerParams(vmem_limit_bytes=48 * 2**20),
        name="cross_forward",
    )(which, q, kv, kv, seg)


def cross_backward_kernel(which, q_ref, k_ref, v_ref, seg_ref, lse_ref, inner_ref, g_ref, dq_ref, dk_ref, dv_ref, acc_ref):
    def back(clip, keys_t, cols, h):
        query, grad = one_head(q_ref[cols], h), one_head(g_ref[cols], h)
        lse = jnp.where(seg_ref[:, cols] == clip, lse_ref[0, h:h + 1, cols], 1e30)
        weights = jnp.exp(dot(k_ref[clip], query, NT) - lse)
        grad_v = dot(weights.astype(jnp.bfloat16), grad, NN)
        grad_s = (weights * (dot(v_ref[clip], grad, NT) - inner_ref[0, h:h + 1, cols])).astype(jnp.bfloat16)
        grad_k = dot(grad_s, query, NN)
        return dot(keys_t[h * 64:(h + 1) * 64], grad_s, NN), grad_k, grad_v

    for clip in range(3):
        cols = slice(None) if clip == 0 else pl.ds(pl.multiple_of(which[clip - 1] * 128, 128), 128)
        keys_t = k_ref[clip].T
        grad_q, grad_k, grad_v = zip(*(back(clip, keys_t, cols, h) for h in range(2)))
        grad_q = jnp.concatenate(grad_q, 0)
        if clip == 0:
            acc_ref[...] = grad_q
        else:
            acc_ref[:, cols] += grad_q
        dk_ref[clip] = (grad_k[0] + grad_k[1]).astype(jnp.bfloat16)
        dv_ref[clip] = (grad_v[0] + grad_v[1]).astype(jnp.bfloat16)
    dq_ref[...] = (acc_ref[...] * 0.125).T


def cross_backward(which, q, kv, seg, lse, inner, grad):
    toks, width = q.shape
    clips, frames = kv.shape[:2]
    pairs = width // 128
    kv_spec = pl.BlockSpec((clips, frames, 128), lambda j, w: (0, 0, j))
    v_spec = pl.BlockSpec((clips, frames, 128), lambda j, w: (0, 0, j + pairs))
    tok_spec = pl.BlockSpec((toks, 128), lambda j, w: (0, j))
    row_spec = pl.BlockSpec((1, 2, toks), lambda j, w: (j, 0, 0))
    return pl.pallas_call(
        cross_backward_kernel,
        grid_spec=pltpu.PrefetchScalarGridSpec(
            num_scalar_prefetch=1,
            grid=(width // 128,),
            in_specs=[tok_spec, kv_spec, v_spec, pl.BlockSpec((1, toks), lambda j, w: (0, 0)), row_spec, row_spec, tok_spec],
            out_specs=[tok_spec, kv_spec, kv_spec],
            scratch_shapes=[pltpu.VMEM((128, toks), jnp.float32)],
        ),
        out_shape=[
            jax.ShapeDtypeStruct((toks, width), jnp.float32),
            jax.ShapeDtypeStruct((clips, frames, width), jnp.bfloat16),
            jax.ShapeDtypeStruct((clips, frames, width), jnp.bfloat16),
        ],
        compiler_params=pltpu.CompilerParams(vmem_limit_bytes=48 * 2**20),
        name="cross_backward",
    )(which, q, kv, kv, seg, lse, inner, grad)


Z = 4


class Place:
    def __init__(self):
        self.dp = lax.axis_index("dp")
        self.core = lax.axis_index("seq")
        self.z = self.dp // 4
        self.p = self.dp % 4
        x, y = self.p % 2, self.p // 2
        px, py = self.p + 1 - 2 * x, self.p + 2 - 4 * y
        self.p_first = px * (1 - self.core) + py * self.core
        self.p_second = py * (1 - self.core) + px * self.core
        self.p_diag = 3 - self.p
        base = self.z * 4
        self.first = (base + self.p_first, self.core)
        self.second = (base + self.p_second, self.core)
        self.mate = (self.dp, 1 - self.core)
        half = self.z // 2
        near = self.z + half * (3 - 2 * self.z)
        self.line = [base + half * (3 - 2 * base) for base in (3, 2, 1 - near)]
        self.peers = [self.mate, self.first, self.second] + [self.on_line(z) for z in self.line]

    def on_line(self, z):
        return (z * 4 + self.p, self.core)

    def greet(self):
        barrier = pltpu.get_barrier_semaphore()
        for target in self.peers:
            pl.semaphore_signal(barrier, inc=1, device_id=target, device_id_type=MESH)
        pl.semaphore_wait(barrier, len(self.peers))


HALF_COLS = {1: 768, 2: 1536, 3: 768, 4: 1536}


class Gather:
    def __init__(self, me, srcs, outs, send_sem, recv_sem, own_sem):
        self.me, self.srcs, self.outs = me, srcs, outs
        self.send_sem, self.recv_sem, self.own_sem = send_sem, recv_sem, own_sem
        self.sends = []
        self.tasks = []
        for m, times in enumerate(GATHER_TIMES):
            for time, task in zip(times, self.steps(m)):
                self.tasks.append((time, m, task))
        self.tasks.sort(key=lambda entry: entry[:2])

    def piece(self, m, chip, core):
        if m == 0:
            return self.outs[m].at[chip * 2 + core]
        if m == 5:
            return self.outs[m].at[pl.ds(pl.multiple_of(chip * 192 + core * 96, 96), 96)]
        rows = pl.ds(pl.multiple_of(chip * 48, 48), 48)
        return self.outs[m].at[rows, columns(core, HALF_COLS[m])]

    def sender(self, m, src, chip, target):
        copy = pltpu.make_async_remote_copy(
            src_ref=src, dst_ref=self.piece(m, chip, self.me.core), send_sem=self.send_sem.at[len(self.sends)],
            recv_sem=self.recv_sem.at[m, chip * 2 + self.me.core], device_id=target, device_id_type=MESH)
        self.sends.append(copy)
        return copy.start

    def arrival(self, m, chip, core):
        piece = self.piece(m, chip, core)
        return pltpu.make_async_remote_copy(
            src_ref=piece, dst_ref=piece, send_sem=self.send_sem.at[0],
            recv_sem=self.recv_sem.at[m, chip * 2 + core], device_id=self.me.mate, device_id_type=MESH).wait_recv

    def forward(self, m, z, p, targets):
        chip = z * 4 + p
        return [self.arrival(m, chip, self.me.core)] + [
            self.sender(m, self.piece(m, chip, self.me.core), chip, target) for target in targets
        ]

    def steps(self, m):
        me = self.me
        begin = [
            self.sender(m, self.srcs[m], me.dp, target)
            for target in [me.on_line(z) for z in me.line] + [me.first, me.second, me.mate]
        ]
        begin.append(pltpu.make_async_copy(self.srcs[m], self.piece(m, me.dp, me.core), self.own_sem.at[m]).start)
        line = []
        for z in me.line[::-1]:
            line += self.forward(m, z, me.p, [me.first, me.second, me.mate])
        beside = []
        for z in [me.z] + me.line[::-1]:
            beside += self.forward(m, z, me.p_first, [me.second, me.mate])
        rest = []
        for p in (me.p_second, me.p_diag):
            for z in [me.z] + me.line[::-1]:
                rest += self.forward(m, z, p, [me.mate])
        return [begin, line, beside, rest]

    def run(self, entry):
        for act in entry[2]:
            act()

    def run_until(self, time):
        while self.tasks and self.tasks[0][0] <= time:
            self.run(self.tasks.pop(0))

    def take_until(self, time):
        taken = []
        while self.tasks and self.tasks[0][0] <= time:
            taken.append(self.tasks.pop(0))
        return taken

    def need(self, m):
        for entry in [e for e in self.tasks if e[1] == m]:
            self.run(entry)
        self.tasks = [e for e in self.tasks if e[1] != m]
        pltpu.make_async_copy(self.srcs[m], self.piece(m, self.me.dp, self.me.core), self.own_sem.at[m]).wait()
        for chip in range(16):
            self.arrival(m, chip, 1 - self.me.core)()

    def finish(self):
        for copy in self.sends:
            copy.wait_send()


GATHER_TIMES = (
    (1, 6, 10, 15),
    (0, 5, 9, 14),
    (2, 11, 19, 27),
    (10, 20, 26, 34),
    (18, 31, 42, 54),
    (30, 48, 60, 74),
)


def loop_with(steps, count, begin, length, body, slots=(0,)):
    due = {}
    for i in range(count):
        for part, k in sorted((part, k) for k, part in enumerate(slots)):
            due[i, k] = steps.take_until(begin + length * (i + part))

    def turn(i, carry):
        def tick(k):
            for at in range(count):
                if due[at, k]:

                    def run(entries=due[at, k]):
                        for entry in entries:
                            steps.run(entry)

                    pl.when(i == at)(run)

        body(i, tick)
        return carry

    lax.fori_loop(0, count, turn, 0)


def norm_rows(values, gain, shift):
    average = jnp.mean(values, -1, keepdims=True)
    centred = values - average
    spread = jnp.mean(centred * centred, -1, keepdims=True)
    return centred * lax.rsqrt(spread + 1e-05) * gain + shift


def two_heads(values):
    return jnp.concatenate([one_head(values, 0), one_head(values, 1)], 0)


def columns(j, size=128):
    return pl.ds(pl.multiple_of(j * size, size), size)


def forward_kernel(*refs):
    (length_ref, x_ref, vectors_in, up_bias_in, down_bias_in, self_in, cross_in, up_in, frames_hbm, down_in) = refs[:10]
    (small_out, ckv_out, self_out, cqo_out, up_out, down_out, kv_out, vec_ref, normed_one_ref, query_ref, kv_row_ref,
     attended_ref, self_lse_ref, after_self_ref, normed_two_ref, row_query_ref, cross_lse_ref, mixed_ref,
     after_cross_ref, normed_three_ref, bias_ref, seg_ref, info_ref, ranked_hbm) = refs[10:34]
    (frames_in, frames_ref, small_f32, small_in, half_wide, half_narrow, pair_wide, pair_narrow, small_vm, ckv_vm, self_vm, cqo_vm, kv_vm, acc_ref, stat_ref, part_ref, part_stat_ref, give_ref,
     give_stat_ref, take_ref, take_stat_ref, send_sem, recv_sem, own_sem, half_sems, mate_sems, load_sem,
     frame_sem) = refs[34:]
    me = Place()
    core = me.core
    width = x_ref.shape[1]
    toks = x_ref.shape[0]
    frames_load = pltpu.make_async_copy(frames_hbm, frames_in, frame_sem.at[0])
    frames_load.start()
    small_f32[...] = jnp.zeros_like(small_f32)
    small_f32[:12, :vectors_in.shape[1]] = vectors_in[...].astype(jnp.float32)
    small_f32[12:13, :down_bias_in.shape[1]] = down_bias_in[...].astype(jnp.float32)
    small_f32[13:14, :up_bias_in.shape[1]] = up_bias_in[...].astype(jnp.float32)
    small_in[...] = small_f32[...].astype(jnp.bfloat16)
    me.greet()

    def to_mate(src, dst, k):
        return pltpu.make_async_remote_copy(
            src_ref=src, dst_ref=dst, send_sem=mate_sems.at[0, k], recv_sem=mate_sems.at[1, k], device_id=me.mate,
            device_id_type=MESH)

    def half_of(m, which):
        shard = (None, cross_in, self_in, cross_in, up_in)[m]
        size = HALF_COLS[m]
        begin = (0, width, 0, 0, 0)[m] + which * (0, width, size, 3 * width, size)[m]
        return shard.at[:, pl.ds(pl.multiple_of(begin, size), size)]

    buffers = {1: (half_narrow.at[0], pair_narrow.at[0]), 2: (half_wide.at[0], pair_wide.at[0]),
               3: (half_narrow.at[1], pair_narrow.at[1]), 4: (half_wide.at[1], pair_wide.at[1])}
    halves = {
        m: pltpu.make_async_remote_copy(
            src_ref=half_of(m, 1 - core), dst_ref=buffers[m][0], send_sem=half_sems.at[0, m],
            recv_sem=half_sems.at[1, m], device_id=me.mate, device_id_type=MESH)
        for m in buffers
    }
    for copy in halves.values():
        copy.start()
    sources = (small_in,) + tuple(buffers[m][1] for m in buffers) + (down_in,)
    gather = Gather(me, sources, (small_out, ckv_out, self_out, cqo_out, up_out, down_out), send_sem, recv_sem, own_sem)
    for m, (came_ref, both_ref) in buffers.items():
        halves[m].wait()
        own = half_of(m, core)[...].astype(jnp.float32)
        came = came_ref[...].astype(jnp.float32)
        both_ref[...] = jnp.concatenate(
            [jnp.where(core == 0, own, came), jnp.where(core == 0, came, own)], 0).astype(jnp.bfloat16)
        gather.run_until((0, 1, 2, 2, 2)[m])

    def fetch(src, dst, k):
        copy = pltpu.make_async_copy(src, dst, load_sem.at[k])
        copy.start()
        copy.wait()

    lengths = [length_ref[0, clip] for clip in range(3)]
    ends = [lengths[0], lengths[0] + lengths[1], lengths[0] + lengths[1] + lengths[2]]

    def clip_at(position):
        return sum((position >= end).astype(jnp.int32) for end in ends)

    def number_row(value):
        return jnp.zeros((1, width), jnp.int32) + value

    length_rows = [number_row(length) for length in lengths]
    big = jnp.where(length_rows[1] > length_rows[0], 1, 0)
    big = jnp.where(length_rows[2] > jnp.maximum(length_rows[0], length_rows[1]), 2, big)
    order = [big, jnp.where(big == 0, 1, 0), jnp.where(big == 2, 1, 2)]
    info_ref[...] = jnp.zeros_like(info_ref)
    for k in (1, 2):
        info_ref[k - 1:k] = jnp.where(order[k] < big, 0, 3)
    for clip in range(3):
        info_ref[2 + clip:3 + clip] = jnp.where(order[0] == clip, 0, jnp.where(order[1] == clip, 1, 2))
    group_ref = info_ref.at[:, pl.ds(0, 128)]
    places = clip_at(lax.broadcasted_iota(jnp.int32, (1, 2 * toks), 1))
    seg_ref[...] = jnp.where(
        places == order[0][:, :2 * toks], 0,
        jnp.where(places == order[1][:, :2 * toks], 1, jnp.where(places == order[2][:, :2 * toks], 2, 3)))
    key_at = core * toks - toks + lax.broadcasted_iota(jnp.int32, bias_ref.shape, 0)
    query_at = core * toks + lax.broadcasted_iota(jnp.int32, bias_ref.shape, 1)
    allowed = (clip_at(key_at) == clip_at(query_at)) & (key_at <= query_at) & (key_at >= 0)
    bias_ref[...] = jnp.where(allowed, 0.0, -1e30)
    frames_load.wait()
    for k in range(3):
        frames_ref[k] = jnp.where(
            order[k] == 0, frames_in[0], jnp.where(order[k] == 1, frames_in[1], frames_in[2]))
    ranked_store = pltpu.make_async_copy(frames_ref, ranked_hbm, frame_sem.at[0])
    ranked_store.start()
    gather.run_until(15)
    gather.need(0)
    fetch(small_out, small_vm, 0)
    total = jnp.zeros(vec_ref.shape, jnp.float32)
    for d in range(32):
        block = jnp.concatenate(
            [small_vm[d].astype(jnp.float32), jnp.zeros((16, width - 128), jnp.float32)], 1)
        total = total + (block if d == 0 else pltpu.roll(block, d * 24, 1))
    vec_ref[...] = total

    def vec(k):
        return vec_ref[k:k + 1]

    source = x_ref[...].astype(jnp.float32)
    normed_one_ref[...] = norm_rows(source, vec(0), vec(1)).astype(jnp.bfloat16)
    gather.need(1)
    fetch(ckv_out, ckv_vm, 0)
    clips = frames_ref.shape[0]
    tiles = 2 * width // 256

    def project(t, tick):
        tick(0)
        clip, tile = t // tiles, t % tiles
        result = dot(frames_ref[clip], ckv_vm[:, columns(tile, 256)], NN)
        is_value = (tile >= 3).astype(jnp.float32)
        shift = vec_ref[10:11, columns(tile % 3, 256)] * is_value
        kv_vm[clip, :frames_ref.shape[1], columns(tile, 256)] = (result + shift).astype(jnp.bfloat16)

    early, middle = 9, 13
    loop_with(gather, early, 20, 0.65, project)
    gather.run_until(31)
    gather.need(2)
    fetch(self_out, self_vm, 0)

    normed = normed_one_ref[...]
    own_rows = slice(toks, 2 * toks)
    kv_row_ref[own_rows, :width] = dot(normed, self_vm[:, width:2 * width], NN).astype(jnp.bfloat16)
    kv_row_ref[own_rows, width:] = (dot(normed, self_vm[:, 2 * width:3 * width], NN) + vec(7)).astype(jnp.bfloat16)
    kv_copy = to_mate(kv_row_ref.at[own_rows], kv_row_ref.at[slice(0, toks)], 0)
    kv_copy.start()
    query = (dot(normed, self_vm[:, :width], NN) + vec(6)).astype(jnp.bfloat16)
    query_ref[...] = query * jnp.bfloat16(0.125)
    lax.fori_loop(early, middle, lambda t, carry: (project(t, lambda k: None), carry)[1], 0)
    gather.run_until(35)
    kv_copy.wait()

    def self_pair(j, tick):
        tick(0)
        cols = columns(j)
        keys = kv_row_ref[:, cols]
        values_t = kv_row_ref[:, columns(j + 6)].T
        parts = []
        for h in range(2):
            scores = dot(keys, one_head(query_ref[:, cols], h), NT) + bias_ref[...]
            peak = jnp.max(scores, 0, keepdims=True)
            terms = jnp.exp(scores - peak)
            total = jnp.sum(terms, 0, keepdims=True)
            parts.append(dot(values_t[h * 64:(h + 1) * 64], terms.astype(jnp.bfloat16), NN) / total)
            self_lse_ref[j, h:h + 1] = peak + jnp.log(total)
        attended_ref[:, cols] = jnp.concatenate(parts, 0).T

    loop_with(gather, 6, 35, 1.2, self_pair)
    after_self = source + dot(attended_ref[...].astype(jnp.bfloat16), self_vm[:, 3 * width:], NN) + vec(8)
    after_self_ref[...] = after_self
    normed_two = norm_rows(after_self, vec(2), vec(3)).astype(jnp.bfloat16)
    normed_two_ref[...] = normed_two
    gather.run_until(44)
    gather.need(3)
    fetch(cqo_out, cqo_vm, 0)
    my_rows = pl.ds(pl.multiple_of(core * toks, toks), toks)
    cross_query = (dot(normed_two, cqo_vm[:, :width], NN) + vec(9)).astype(jnp.bfloat16)
    row_query_ref[my_rows] = cross_query * jnp.bfloat16(0.125)
    query_copy = to_mate(row_query_ref.at[my_rows], row_query_ref.at[my_rows], 1)
    query_copy.start()
    lax.fori_loop(middle, clips * tiles, lambda t, carry: (project(t, lambda k: None), carry)[1], 0)
    kv_store = pltpu.make_async_copy(kv_vm, kv_out, load_sem.at[1])
    kv_store.start()
    gather.run_until(48)
    query_copy.wait()

    frame_count = frames_ref.shape[1]

    def attend(clip, values_t, query, j):
        scores = dot(kv_vm[clip, :frame_count, columns(j)], query, NT)
        peak = jnp.max(scores, 0, keepdims=True)
        terms = jnp.exp(scores - peak)
        total = jnp.sum(terms, 0, keepdims=True)
        return dot(values_t, terms.astype(jnp.bfloat16), NN), peak, total

    def cross_pair(j, tick):
        values_t = kv_vm[0, :frame_count, columns(j + 6)].T
        mine = seg_ref[...] == 0
        for h in range(2):
            tick(h)
            rows = slice(h * 64, (h + 1) * 64)
            result, peak, total = attend(0, values_t[rows], one_head(row_query_ref[:, columns(j)], h), j)
            acc_ref[rows] = jnp.where(mine, result / total, 0.0)
            stat_ref[h:h + 1] = jnp.where(mine, peak, 0.0)
            stat_ref[2 + h:3 + h] = jnp.where(mine, total, 1.0)
        for clip in (1, 2):
            tick(clip + 1)
            values_t = kv_vm[clip, :frame_count, columns(j + 6)].T
            query_rows = jnp.where(
                group_ref[clip - 1:clip] == 0, row_query_ref[:128, columns(j)], row_query_ref[384:, columns(j)])
            result, peak, total = attend(clip, values_t, two_heads(query_rows), j)
            for h in range(2):
                rows, part = slice(h * 64, (h + 1) * 64), slice(h * 128, (h + 1) * 128)
                of_head = result[rows, part] / total[:, part]
                for spot in (0, 3):
                    cols = slice(spot * 128, (spot + 1) * 128)
                    mine = seg_ref[:, cols] == clip
                    acc_ref[rows, cols] = jnp.where(mine, of_head, acc_ref[rows, cols])
                    stat_ref[h:h + 1, cols] = jnp.where(mine, peak[:, part], stat_ref[h:h + 1, cols])
                    stat_ref[2 + h:3 + h, cols] = jnp.where(mine, total[:, part], stat_ref[2 + h:3 + h, cols])
        my_cols, mate_cols = columns(core, toks), columns(1 - core, toks)
        part_ref[j] = acc_ref[:, my_cols]
        part_stat_ref[j] = stat_ref[:, my_cols]
        give_ref[j] = acc_ref[:, mate_cols].astype(jnp.bfloat16)
        give_stat_ref[j] = stat_ref[:, mate_cols]

    loop_with(gather, 6, 48, 3, cross_pair, (0, 0.33, 0.66, 0.83))
    give_copy = to_mate(give_ref, take_ref, 2)
    give_copy.start()
    give_stat_copy = to_mate(give_stat_ref, take_stat_ref, 3)
    give_stat_copy.start()
    gather.run_until(1000)
    give_copy.wait()
    give_stat_copy.wait()

    def combine(j, carry):
        parts = []
        for h in range(2):
            rows = slice(h * 64, (h + 1) * 64)
            peak_a, peak_b = part_stat_ref[j, h:h + 1], take_stat_ref[j, h:h + 1]
            peak = jnp.maximum(peak_a, peak_b)
            share_a = part_stat_ref[j, 2 + h:3 + h] * jnp.exp(peak_a - peak)
            share_b = take_stat_ref[j, 2 + h:3 + h] * jnp.exp(peak_b - peak)
            total = share_a + share_b
            cross_lse_ref[j, h:h + 1] = peak + jnp.log(total)
            parts.append(part_ref[j, rows] * (share_a / total)
                         + take_ref[j, rows].astype(jnp.float32) * (share_b / total))
        mixed_ref[:, columns(j)] = jnp.concatenate(parts, 0).T
        return carry

    lax.fori_loop(0, 6, combine, 0)
    after_cross = after_self_ref[...] + dot(mixed_ref[...].astype(jnp.bfloat16), cqo_vm[:, width:], NN) + vec(11)
    after_cross_ref[...] = after_cross
    normed_three_ref[...] = norm_rows(after_cross, vec(4), vec(5)).astype(jnp.bfloat16)
    gather.run_until(1000)
    gather.need(4)
    gather.need(5)
    kv_store.wait()
    ranked_store.wait()
    gather.finish()


def fused_forward(lengths, x, vectors, up_bias, down_bias, self_w, cross_w, up_w, frames, down_w):
    toks, width = x.shape
    clips, count = frames.shape[:2]
    low, full = jnp.bfloat16, jnp.float32
    pairs = width // 128
    vmem, hbm = pl.BlockSpec(memory_space=pltpu.VMEM), pl.BlockSpec(memory_space=pl.ANY)
    shape = jax.ShapeDtypeStruct
    outs = [
        (hbm, shape((32, 16, 128), low)), (hbm, shape((width, 2 * width), low)), (hbm, shape((width, 4 * width), low)),
        (hbm, shape((width, 2 * width), low)), (hbm, shape((width, 4 * width), low)),
        (hbm, shape((4 * width, width), low)),
        (hbm, shape((clips, width, 2 * width), low)),
        (vmem, shape((16, width), full)), (vmem, shape((toks, width), low)), (vmem, shape((toks, width), low)),
        (vmem, shape((2 * toks, 2 * width), low)), (vmem, shape((toks, width), full)),
        (vmem, shape((pairs, 2, toks), full)), (vmem, shape((toks, width), full)), (vmem, shape((toks, width), low)),
        (vmem, shape((2 * toks, width), low)), (vmem, shape((pairs, 2, toks), full)), (vmem, shape((toks, width), full)),
        (vmem, shape((toks, width), full)), (vmem, shape((toks, width), low)),
        (vmem, shape((2 * toks, toks), full)), (vmem, shape((1, 2 * toks), jnp.int32)), (vmem, shape((8, width), jnp.int32)),
        (hbm, shape(frames.shape, low)),
    ]
    return pl.pallas_call(
        forward_kernel,
        in_specs=[pl.BlockSpec(memory_space=pltpu.SMEM)] + [vmem] * 7 + [hbm] * 2,
        out_specs=tuple(spec for spec, _ in outs),
        out_shape=tuple(s for _, s in outs),
        scratch_shapes=[
            pltpu.VMEM(frames.shape, low), pltpu.VMEM(frames.shape, low), pltpu.VMEM((16, 128), full),
            pltpu.VMEM((16, 128), low), pltpu.VMEM((2, 24, 2 * width), low), pltpu.VMEM((2, 24, width), low), pltpu.VMEM((2, 48, 2 * width), low),
            pltpu.VMEM((2, 48, width), low), pltpu.VMEM((32, 16, 128), low),
            pltpu.VMEM((width, 2 * width), low), pltpu.VMEM((width, 4 * width), low), pltpu.VMEM((width, 2 * width), low),
            pltpu.VMEM((clips, width, 2 * width), low), pltpu.VMEM((128, 2 * toks), full), pltpu.VMEM((4, 2 * toks), full),
            pltpu.VMEM((pairs, 128, toks), full), pltpu.VMEM((pairs, 4, toks), full),
            pltpu.VMEM((pairs, 128, toks), low), pltpu.VMEM((pairs, 4, toks), full),
            pltpu.VMEM((pairs, 128, toks), low), pltpu.VMEM((pairs, 4, toks), full),
            pltpu.SemaphoreType.DMA((400,)), pltpu.SemaphoreType.DMA((6, 32)), pltpu.SemaphoreType.DMA((6,)),
            pltpu.SemaphoreType.DMA((2, 5)), pltpu.SemaphoreType.DMA((2, 4)), pltpu.SemaphoreType.DMA((2,)),
            pltpu.SemaphoreType.DMA((1,)),
        ],
        compiler_params=pltpu.CompilerParams(collective_id=0, has_side_effects=True, vmem_limit_bytes=60 * 2**20),
        name="fused_forward",
    )(lengths, x, vectors, up_bias, down_bias, self_w, cross_w, up_w, frames, down_w)


class Scatter:
    def __init__(self, me, grads, outs, buffers, sems, times, after):
        self.me, self.grads, self.outs, self.buffers = me, grads, outs, buffers
        self.send_sem, self.own_sem, self.pair_sem, self.plane_sem, self.line_sem, self.free_sem = sems
        self.sends = {m: [] for m in range(len(grads))}
        self.count = 0
        self.order = me.line + [me.z]
        self.tasks = []
        for m, times_of in enumerate(times):
            for time, acts in zip(times_of, self.steps(m)):
                self.tasks.append((time, m, acts))
        for late, early in after.items():
            self.tasks = [
                (time, m, ([self.wait_free] if m == late and time == times[late][0] else []) + acts
                 + ([functools.partial(self.give_free, early)] if m == early and time == times[early][-1] else []))
                for time, m, acts in self.tasks
            ]
        self.tasks.sort(key=lambda entry: entry[:2])

    def give_free(self, m):
        for copy in self.sends.pop(m):
            copy.wait_send()
        for target in self.me.peers:
            pl.semaphore_signal(self.free_sem, inc=1, device_id=target, device_id_type=MESH)

    def wait_free(self):
        pl.semaphore_wait(self.free_sem, len(self.me.peers))

    def sender(self, m, src, dst, sem, target):
        copy = pltpu.make_async_remote_copy(
            src_ref=src, dst_ref=dst, send_sem=self.send_sem.at[self.count], recv_sem=sem, device_id=target,
            device_id_type=MESH)
        self.count += 1
        self.sends[m].append(copy)
        return copy.start

    def arrival(self, dst, sem):
        return pltpu.make_async_remote_copy(
            src_ref=dst, dst_ref=dst, send_sem=self.send_sem.at[0], recv_sem=sem, device_id=self.me.mate,
            device_id_type=MESH).wait_recv

    def steps(self, m):
        me, order = self.me, self.order
        grad, out = self.grads[m], self.outs[m]
        own, pair, plane_a, plane_b, plane_c, line = self.buffers[m]
        own_sem, pair_sem, plane_sem, line_sem = self.own_sem, self.pair_sem, self.plane_sem, self.line_sem

        def adder(dst, *others):
            def act():
                total = dst[...].astype(jnp.float32)
                for other in others:
                    total = total + other[...].astype(jnp.float32)
                dst[...] = total.astype(dst.dtype)
            return act

        loads = [
            pltpu.make_async_copy(grad.at[:, p, me.core], own, own_sem.at[m, k])
            for k, p in enumerate((me.p_diag, me.p_second, me.p_first, me.p))
        ]
        begin = [loads[0].start]
        for p in (me.p_diag, me.p_first, me.p_second, me.p):
            begin.append(self.sender(m, grad.at[:, p, 1 - me.core], pair.at[:, p], pair_sem.at[m, p], me.mate))
        diag, second, first, last = (
            [loads[k].wait, self.arrival(pair.at[:, p], pair_sem.at[m, p])]
            for k, p in enumerate((me.p_diag, me.p_second, me.p_first, me.p))
        )
        for z in order:
            diag += [adder(pair.at[z, me.p_diag], own.at[z]),
                     self.sender(m, pair.at[z, me.p_diag], plane_a.at[z], plane_sem.at[m, 0, z], me.second)]
            second += [adder(pair.at[z, me.p_second], own.at[z]),
                       self.sender(m, pair.at[z, me.p_second], plane_c.at[z], plane_sem.at[m, 2, z], me.second)]
            first += [self.arrival(plane_a.at[z], plane_sem.at[m, 0, z]),
                      adder(pair.at[z, me.p_first], own.at[z], plane_a.at[z]),
                      self.sender(m, pair.at[z, me.p_first], plane_b.at[z], plane_sem.at[m, 1, z], me.first)]
        diag.append(loads[1].start)
        second.append(loads[2].start)
        first.append(loads[3].start)
        for z in me.line:
            last += [self.arrival(plane_b.at[z], plane_sem.at[m, 1, z]),
                     self.arrival(plane_c.at[z], plane_sem.at[m, 2, z]),
                     adder(pair.at[z, me.p], own.at[z], plane_b.at[z], plane_c.at[z]),
                     self.sender(m, pair.at[z, me.p], line.at[me.z], line_sem.at[m, me.z], me.on_line(z))]

        def total():
            part = own[me.z].astype(jnp.float32) + pair[me.z, me.p].astype(jnp.float32)
            out[...] = part + plane_b[me.z].astype(jnp.float32) + plane_c[me.z].astype(jnp.float32)

        def from_line(source):
            def act():
                out[...] += line[source].astype(jnp.float32)
            return act

        final = [self.arrival(plane_b.at[me.z], plane_sem.at[m, 1, me.z]),
                 self.arrival(plane_c.at[me.z], plane_sem.at[m, 2, me.z]), total]
        for source in me.line[::-1]:
            final += [self.arrival(line.at[source], line_sem.at[m, source]), from_line(source)]
        return [begin, diag, second, first, last, final]

    def run(self, entry):
        for act in entry[2]:
            act()

    def run_until(self, time):
        while self.tasks and self.tasks[0][0] <= time:
            self.run(self.tasks.pop(0))

    def take_until(self, time):
        taken = []
        while self.tasks and self.tasks[0][0] <= time:
            taken.append(self.tasks.pop(0))
        return taken

    def finish(self):
        self.run_until(10**6)
        for copies in self.sends.values():
            for copy in copies:
                copy.wait_send()


def scatter_buffers(grad):
    leads = ((4,), (4, 4), (4,), (4,), (4,), (4,))
    return [pltpu.VMEM(lead + grad.shape[1:], grad.dtype) for lead in leads]


def scatter_sems(count):
    dma = pltpu.SemaphoreType.DMA
    return [dma((20 * count,)), dma((count, 4)), dma((count, 4)), dma((count, 3, 4)), dma((count, 4)),
            pltpu.SemaphoreType.REGULAR]


def scatter_view(grad):
    return grad.reshape((4, 4, 2) + grad.shape[1:])


BACK_TIMES = (
    (0, 6.5, 8, 18, 30, 43),
    (1, 17, 19, 32, 43.5, 60),
    (45, 53, 54, 63, 70, 80),
    (66, 71, 72, 79, 86, 95),
    (70, 73, 74, 82, 89, 98),
)


def norm_rows_back(values, gain, grad):
    average = jnp.mean(values, -1, keepdims=True)
    centred = values - average
    scale = lax.rsqrt(jnp.mean(centred * centred, -1, keepdims=True) + 1e-05)
    normed = centred * scale
    inner = grad * gain
    mean_inner = jnp.mean(inner, -1, keepdims=True)
    mean_both = jnp.mean(inner * normed, -1, keepdims=True)
    result = scale * (inner - mean_inner - normed * mean_both)
    return result, jnp.sum(grad * normed, 0, keepdims=True), jnp.sum(grad, 0, keepdims=True)


def backward_kernel(*refs):
    (info_ref, x_ref, bias_ref, seg_ref, vec_ref, gac_ref, mixed_ref, cross_lse_ref, row_query_ref, after_self_ref,
     attended_ref, self_lse_ref, query_ref, kv_row_ref, normed_one_ref, normed_two_ref, rows_ref, up_bias_ref, cqo_hbm,
     ckv_hbm, self_hbm, kv_hbm, frames_hbm, up_hbm, down_hbm) = refs[:25]
    (input_grad_ref, encoder_hbm, up_out, down_out, cross_out, self_out, up_bias_out, down_bias_out, vectors_out,
     dkv_hbm, cross_hbm, self_grad_hbm) = refs[25:37]
    cross_sum, small_out, *scratch = refs[37:]
    up_buffers, down_buffers, cross_buffers, small_buffers = (scratch[k * 6:(k + 1) * 6] for k in range(4))
    sems, scratch = scratch[24:30], scratch[30:]
    (cross_vm, kv_vm, frame_ref, turned_ref, tile_ref, stage_ref, small_ref, row_grad_ref, row_stat_ref, acc_ref,
     own_ref, give_ref, take_ref, take_query_ref, cq_ref, qkv_ref, vec_grad_ref, load_sem, mate_sems, tile_sem,
     stage_sem, frame_sem) = scratch
    group_ref = info_ref.at[:, pl.ds(0, 128)]
    me = Place()
    core = me.core
    toks, width = x_ref.shape
    frames = frames_hbm.shape[1]
    clips = kv_hbm.shape[0]
    low, full = jnp.bfloat16, jnp.float32
    halves = [pltpu.make_async_copy(cqo_hbm.at[:, pl.ds(k * width, width)], cross_vm.at[k], load_sem.at[k])
              for k in range(2)]
    kv_load = pltpu.make_async_copy(kv_hbm, kv_vm, load_sem.at[2])
    frame_loads = [
        pltpu.make_async_copy(
            frames_hbm.at[clip], frame_ref.at[:, pl.ds(clip % 2 * width, width)], frame_sem.at[clip % 2])
        for clip in range(clips)
    ]
    for copy in [halves[1], kv_load, halves[0]] + frame_loads[:2]:
        copy.start()
    me.greet()
    self_buffers = [
        ref.at[(slice(None),) * (len(ref.shape) - 1) + (pl.ds(0, 3 * width),)] for ref in up_buffers
    ]
    scatter = Scatter(
        me, (up_hbm, down_hbm, cross_hbm, self_grad_hbm, small_ref), (up_out, down_out, cross_sum, self_out.at[:, pl.ds(0, 3 * width)], small_out),
        (up_buffers, down_buffers, cross_buffers, self_buffers, small_buffers), sems, BACK_TIMES, {3: 0})
    scatter.run_until(1)

    def to_mate(src, dst, k):
        return pltpu.make_async_remote_copy(
            src_ref=src, dst_ref=dst, send_sem=mate_sems.at[0, k], recv_sem=mate_sems.at[1, k], device_id=me.mate,
            device_id_type=MESH)

    my_rows = pl.ds(pl.multiple_of(core * toks, toks), toks)
    my_cols = columns(core, toks)

    def head_rows(product, store):
        turned = product.T
        for h in range(2):
            store(h, jnp.sum(turned[h * 64:(h + 1) * 64], 0, keepdims=True))

    def tile_store(grad_hbm, slot, t):
        return pltpu.make_async_copy(tile_ref.at[slot], grad_hbm.at[:, :, :, :, columns(t, 256)], tile_sem.at[slot])

    def weight_tiles(grad_hbm, first_tile, count, tile, before=None):
        def turn(t, carry):
            slot = t % 2

            @pl.when(t >= 2)
            def _():
                tile_store(grad_hbm, slot, first_tile + t - 2).wait()

            value = tile(columns(t, 256))
            tile_ref[slot] = value.reshape(4, 4, 2, width // 32, 256).astype(low)
            tile_store(grad_hbm, slot, first_tile + t).start()
            return carry

        lax.fori_loop(0, count, turn, 0)
        for t in range(max(0, count - 2), count):
            tile_store(grad_hbm, t % 2, first_tile + t).wait()

    def product_tiles(grad_hbm, first_tile, left, right_ref):
        turned = left.T
        weight_tiles(grad_hbm, first_tile, right_ref.shape[1] // 256, lambda cols: dot(turned, right_ref[:, cols], NN))

    halves[1].wait()
    grad_cross = gac_ref[...].astype(low)
    grad_mixed = dot(grad_cross, cross_vm[1], NT).astype(low)
    row_grad_ref[my_rows] = grad_mixed
    grad_copy = to_mate(row_grad_ref.at[my_rows], row_grad_ref.at[my_rows], 0)
    grad_copy.start()
    for j in range(6):
        cols = slice(j * 128, (j + 1) * 128)
        product = grad_mixed[:, cols].astype(full) * mixed_ref[:, cols]
        row_stat_ref[j, 0:2, my_cols] = cross_lse_ref[j]

        def keep(h, row, j=j):
            row_stat_ref[j, 2 + h:3 + h, my_cols] = row

        head_rows(product, keep)
    stat_copy = to_mate(row_stat_ref.at[:, :, my_cols], row_stat_ref.at[:, :, my_cols], 1)
    stat_copy.start()
    cq_ref[...] = grad_cross
    product_tiles(cross_hbm, 9, mixed_ref[...].astype(low), cq_ref)

    def turn_frames(clip):
        frame_loads[clip].wait()
        turned_ref[clip] = frame_ref[:, clip % 2 * width:(clip % 2 + 1) * width].T

    turn_frames(0)
    frame_loads[2].start()
    turn_frames(1)
    kv_load.wait()
    scatter.run_until(5)
    grad_copy.wait()
    stat_copy.wait()

    def cross_pair(j, tick):
        def back(clip, keys_t, query, grad, lse, inner):
            weights = jnp.exp(dot(kv_vm[clip, :frames, columns(j)], query, NT) - lse)
            grad_v = dot(weights.astype(low), grad, NN)
            grad_s = (weights * (dot(kv_vm[clip, :frames, columns(j + 6)], grad, NT) - inner)).astype(low)
            return dot(keys_t, grad_s, NN), dot(grad_s, query, NN), grad_v

        keys_t = kv_vm[0, :frames, columns(j)].T
        mine = seg_ref[...] == 0
        grad_k = grad_v = None
        for h in range(2):
            tick(h)
            query, grad = one_head(row_query_ref[:, columns(j)], h), one_head(row_grad_ref[:, columns(j)], h)
            rows = slice(h * 64, (h + 1) * 64)
            acc_ref[rows], part_k, part_v = back(
                0, keys_t[rows], query, grad, jnp.where(mine, row_stat_ref[j, h:h + 1], 1e30),
                row_stat_ref[j, 2 + h:3 + h])
            grad_k = part_k if grad_k is None else grad_k + part_k
            grad_v = part_v if grad_v is None else grad_v + part_v
        kv_vm[0, :frames, columns(j)] = grad_k.astype(low)
        kv_vm[0, :frames, columns(j + 6)] = grad_v.astype(low)
        for clip in (1, 2):
            tick(clip + 1)
            in_first = group_ref[clip - 1:clip] == 0

            def chosen(ref):
                return two_heads(jnp.where(in_first, ref[:128, columns(j)], ref[384:, columns(j)]))

            def chosen_row(row):
                return jnp.where(in_first, row_stat_ref[j, row:row + 1, :128], row_stat_ref[j, row:row + 1, 384:])

            mine = jnp.where(in_first, seg_ref[:, :128], seg_ref[:, 384:]) == clip
            lse = jnp.concatenate([jnp.where(mine, chosen_row(h), 1e30) for h in range(2)], 1)
            inner = jnp.concatenate([chosen_row(2 + h) for h in range(2)], 1)
            grad_q, grad_k, grad_v = back(
                clip, kv_vm[clip, :frames, columns(j)].T, chosen(row_query_ref), chosen(row_grad_ref), lse, inner)
            for h in range(2):
                rows, part = slice(h * 64, (h + 1) * 64), slice(h * 128, (h + 1) * 128)
                for spot in (0, 3):
                    cols = slice(spot * 128, (spot + 1) * 128)
                    acc_ref[rows, cols] += jnp.where(in_first == (spot == 0), grad_q[rows, part], 0.0)
            kv_vm[clip, :frames, columns(j)] = grad_k.astype(low)
            kv_vm[clip, :frames, columns(j + 6)] = grad_v.astype(low)
        own_ref[:, columns(j)] = (acc_ref[:, my_cols] * 0.125).T
        give_ref[:, columns(j)] = (acc_ref[:, columns(1 - core, toks)] * 0.125).T.astype(low)

    loop_with(scatter, 6, 6, 4, cross_pair, (0, 0.33, 0.66, 0.83))
    query_copy = to_mate(give_ref.at[:, pl.ds(0, width)], take_query_ref, 2)
    query_copy.start()
    dkv_store = pltpu.make_async_copy(kv_vm, dkv_hbm, load_sem.at[2])
    dkv_store.start()
    vec_grad_ref[...] = rows_ref[...]
    vec_grad_ref[10:11] = sum(
        jnp.sum(kv_vm[clip, :frames, width:].astype(full), 0, keepdims=True) for clip in range(clips))
    turn_frames(2)
    scatter.run_until(37)

    def frames_tile(cols):
        total = dot(turned_ref[0], kv_vm[0, :frames, cols], NN)
        for clip in range(1, clips):
            total = total + dot(turned_ref[clip], kv_vm[clip, :frames, cols], NN)
        return total

    weight_tiles(cross_hbm, 3, 6, frames_tile)
    halves[0].wait()
    query_copy.wait()
    grad_query = (own_ref[:, :width] + take_query_ref[...].astype(full)).astype(low)
    cq_ref[...] = grad_query
    product_tiles(cross_hbm, 0, normed_two_ref[...], cq_ref)
    dkv_store.wait()
    self_loads = [
        pltpu.make_async_copy(
            self_hbm.at[:, pl.ds(k * 2 * width, 2 * width)], kv_vm.at[k], load_sem.at[2 + k]) for k in range(2)
    ]
    for copy in self_loads:
        copy.start()
    vec_grad_ref[9:10] = jnp.sum(grad_query.astype(full), 0, keepdims=True)
    grad_part, gain, shift = norm_rows_back(after_self_ref[...], vec_ref[2:3], dot(grad_query, cross_vm[0], NT))
    vec_grad_ref[2:3] = gain
    vec_grad_ref[3:4] = shift
    grad_after_self = gac_ref[...] + grad_part
    input_grad_ref[...] = grad_after_self
    grad_low = grad_after_self.astype(low)
    vec_grad_ref[8:9] = jnp.sum(grad_low.astype(full), 0, keepdims=True)
    cq_ref[...] = grad_low
    product_tiles(cross_hbm, 12, attended_ref[...].astype(low), cq_ref)
    scatter.run_until(46)
    for copy in self_loads:
        copy.wait()
    grad_attended = dot(grad_low, kv_vm[1, :width, width:], NT).astype(low)
    row_grad_ref[:toks] = grad_attended
    for j in range(6):
        cols = slice(j * 128, (j + 1) * 128)

        def keep_self(h, row, j=j):
            row_stat_ref[j, h:h + 1, :toks] = row

        head_rows(grad_attended[:, cols].astype(full) * attended_ref[:, cols], keep_self)

    def self_pair(j, tick):
        tick(0)
        cols, value_cols = columns(j), columns(j + 6)
        keys, values = kv_row_ref[:, cols], kv_row_ref[:, value_cols]
        keys_t = keys.T
        grad_k = grad_v = None
        parts = []
        for h in range(2):
            query, grad = one_head(query_ref[:, cols], h), one_head(row_grad_ref[:toks, cols], h)
            weights = jnp.exp(dot(keys, query, NT) + bias_ref[...] - self_lse_ref[j, h:h + 1])
            part = dot(weights.astype(low), grad, NN)
            grad_v = part if grad_v is None else grad_v + part
            inner = row_stat_ref[j, h:h + 1, :toks]
            grad_s = (weights * (dot(values, grad, NT) - inner)).astype(low)
            part = dot(grad_s, query, NN)
            grad_k = part if grad_k is None else grad_k + part
            parts.append(dot(keys_t[h * 64:(h + 1) * 64], grad_s, NN))
        qkv_ref[:, cols] = (jnp.concatenate(parts, 0) * 0.125).T.astype(low)
        own_ref[:, cols] = grad_k[toks:]
        own_ref[:, value_cols] = grad_v[toks:]
        give_ref[:, cols] = grad_k[:toks].astype(low)
        give_ref[:, value_cols] = grad_v[:toks].astype(low)

    loop_with(scatter, 6, 52, 1.4, self_pair)
    row_copy = to_mate(give_ref, take_ref, 3)
    row_copy.start()
    scatter.run_until(62)
    row_copy.wait()
    qkv_ref[:, width:] = (own_ref[...] + take_ref[...].astype(full)).astype(low)
    product_tiles(self_grad_hbm, 0, normed_one_ref[...], qkv_ref)
    scatter.run_until(66)
    sums = jnp.sum(qkv_ref[...].astype(full), 0, keepdims=True)
    vec_grad_ref[6:7] = sums[:, :width]
    vec_grad_ref[7:8] = sums[:, 2 * width:]
    grad_normed = dot(qkv_ref[:, :2 * width], kv_vm[0, :width], NT) + dot(
        qkv_ref[:, 2 * width:], kv_vm[1, :width, :width], NT)
    grad_part, gain, shift = norm_rows_back(x_ref[...].astype(full), vec_ref[0:1], grad_normed)
    vec_grad_ref[0:1] = gain
    vec_grad_ref[1:2] = shift
    input_grad_ref[...] += grad_part
    kv_load = pltpu.make_async_copy(dkv_hbm, kv_vm, load_sem.at[2])
    kv_load.start()
    for k in range(2):
        pltpu.make_async_copy(ckv_hbm.at[:, pl.ds(k * width, width)], cross_vm.at[k], load_sem.at[k]).start()
    small_ref[...] = jnp.zeros_like(small_ref)
    rows = vec_grad_ref[...]
    for d in range(32):
        place = (d // 8, d // 2 % 4, d % 2)
        turned_rows = rows if d == 0 else pltpu.roll(rows, width - d * 24, 1)
        small_ref[place] = turned_rows[:, :128]
        bias_row = up_bias_ref[...] if d == 0 else pltpu.roll(up_bias_ref[...], up_bias_ref.shape[1] * (32 - d) // 32, 1)
        small_ref[place + (slice(13, 14),)] = bias_row[:, :128]
    scatter.run_until(70)
    for k in range(2):
        pltpu.make_async_copy(ckv_hbm.at[:, pl.ds(k * width, width)], cross_vm.at[k], load_sem.at[k]).wait()
    kv_load.wait()
    blocks = width // 128

    def encoder_store(clip):
        rows = pl.ds(clip * frames * blocks, frames * blocks)
        return pltpu.make_async_copy(stage_ref, encoder_hbm.at[rows], stage_sem.at[0])

    for clip in range(clips):
        place = info_ref[2 + clip:3 + clip]
        for part in (slice(0, width), slice(width, 2 * width)):
            frame_ref[:, part] = jnp.where(
                place == 0, kv_vm[0, :frames, part],
                jnp.where(place == 1, kv_vm[1, :frames, part], kv_vm[2, :frames, part]))

        def encoder_tile(t, tick, clip=clip):
            tick(0)
            rows = columns(t, 256)
            value = dot(frame_ref[:, :width], cross_vm[0, rows], NT) + dot(frame_ref[:, width:], cross_vm[1, rows], NT)
            if clip > 0:
                pl.when(t == 0)(encoder_store(clip - 1).wait)
            for k in range(2):
                stage_ref[pl.ds(2 * t + k, frames, stride=blocks), 0] = value[:, k * 128:(k + 1) * 128]

        loop_with(scatter, width // 256, 71 + 3 * clip, 1, encoder_tile)
        encoder_store(clip).start()
    encoder_store(clips - 1).wait()
    scatter.finish()
    cross_out[...] = cross_sum[:, :4 * width]
    self_out[:, 3 * width:] = cross_sum[:, 4 * width:]
    up_bias_out[...] = small_out[13:14, :up_bias_out.shape[1]]
    down_bias_out[...] = small_out[12:13, :down_bias_out.shape[1]]
    vectors_out[...] = small_out[:12, :vectors_out.shape[1]]


def fused_backward(info, x, bias, seg, vec, gac, mixed, cross_lse, row_query, after_self, attended, self_lse, query,
                   kv_row, normed_one, normed_two, rows, up_bias, cqo_full, ckv_full, self_full, kv, frames, grad_up,
                   grad_down):
    toks, width = x.shape
    clips, count = frames.shape[:2]
    low, full = jnp.bfloat16, jnp.float32
    pairs = width // 128
    vmem, hbm = pl.BlockSpec(memory_space=pltpu.VMEM), pl.BlockSpec(memory_space=pl.ANY)
    shape = jax.ShapeDtypeStruct
    small = shape((32, 16, 128), full)
    places = (4, 4, 2, width // 32)
    cross = shape((32, width // 32, 5 * width), low)
    outs = [
        (vmem, shape((toks, width), full)), (hbm, shape((clips * count * width // 128, 1, 128), full)), (vmem, shape(grad_up.shape[1:], full)),
        (vmem, shape(grad_down.shape[1:], full)), (vmem, shape((width // 32, 4 * width), full)),
        (vmem, shape((width // 32, 4 * width), full)), (vmem, shape((1, up_bias.shape[1] // 32), full)),
        (vmem, shape((1, width // 32), full)), (vmem, shape((12, width // 32), full)), (hbm, shape(kv.shape, low)),
        (hbm, shape(places + (5 * width,), low)), (hbm, shape(places + (3 * width,), low)),
    ]
    return pl.pallas_call(
        backward_kernel,
        in_specs=[vmem] * 18 + [hbm] * 7,
        out_specs=tuple(spec for spec, _ in outs),
        out_shape=tuple(s for _, s in outs),
        scratch_shapes=[pltpu.VMEM(cross.shape[1:], full), pltpu.VMEM(small.shape[1:], full)]
        + scatter_buffers(grad_up) + scatter_buffers(grad_down) + scatter_buffers(cross)
        + scatter_buffers(small) + scatter_sems(5) + [
            pltpu.VMEM((2, width, width), low), pltpu.VMEM((clips, width, 2 * width), low),
            pltpu.VMEM((count, 2 * width), low), pltpu.VMEM((clips, width, count), low),
            pltpu.VMEM((2,) + places + (256,), low), pltpu.VMEM((count * width // 128, 1, 128), full),
            pltpu.VMEM((4, 4, 2, 16, 128), full), pltpu.VMEM((2 * toks, width), low),
            pltpu.VMEM((pairs, 4, 2 * toks), full), pltpu.VMEM((128, 2 * toks), full),
            pltpu.VMEM((toks, 2 * width), full), pltpu.VMEM((toks, 2 * width), low),
            pltpu.VMEM((toks, 2 * width), low), pltpu.VMEM((toks, width), low), pltpu.VMEM((toks, width), low),
            pltpu.VMEM((toks, 3 * width), low), pltpu.VMEM((16, width), full), pltpu.SemaphoreType.DMA((4,)),
            pltpu.SemaphoreType.DMA((2, 4)), pltpu.SemaphoreType.DMA((2,)), pltpu.SemaphoreType.DMA((1,)),
            pltpu.SemaphoreType.DMA((2,)),
        ],
        compiler_params=pltpu.CompilerParams(collective_id=2, has_side_effects=True, vmem_limit_bytes=63 * 2**20),
        name="fused_backward",
    )(info, x, bias, seg, vec, gac, mixed, cross_lse, row_query, after_self, attended, self_lse, query, kv_row,
      normed_one, normed_two, rows, up_bias, cqo_full, ckv_full, self_full, kv, frames, scatter_view(grad_up),
      scatter_view(grad_down))


def ffn_kernel(normed_ref, grad_ref, after_ref, vec_ref, up_ref, bias_ref, down_ref, out_ref, back_ref, grad_up_ref,
               grad_down_ref, grad_bias_ref, rows_ref, turned_ref, sum_ref, back_sum_ref):
    t = pl.program_id(0)

    @pl.when(t == 0)
    def _():
        turned_ref[...] = normed_ref[...].T
        sum_ref[...] = jnp.zeros_like(sum_ref)
        back_sum_ref[...] = jnp.zeros_like(back_sum_ref)

    grad = grad_ref[...]
    pre = dot(normed_ref[...], up_ref[...], NN) + bias_ref[...]
    below = 0.5 * (1.0 + lax.erf(pre * 0.7071067811865476))
    activated = (pre * below).astype(jnp.bfloat16)
    sum_ref[...] += dot(activated, down_ref[...], NN)
    grad_act = dot(grad, down_ref[...], NT).astype(jnp.bfloat16).astype(jnp.float32)
    density = jnp.exp(-0.5 * pre * pre) * 0.3989422804014327
    grad_pre = (grad_act * (below + pre * density)).astype(jnp.bfloat16)
    back_sum_ref[...] += dot(grad_pre, up_ref[...], NT)
    grad_up_ref[...] = dot(turned_ref[...], grad_pre, NN).astype(jnp.bfloat16)
    grad_down_ref[...] = dot(activated.T, grad, NN).astype(jnp.bfloat16)
    grad_bias_ref[...] = jnp.sum(grad_pre.astype(jnp.float32), 0, keepdims=True)

    @pl.when(t == pl.num_programs(0) - 1)
    def _():
        out_ref[...] = (after_ref[...] + sum_ref[...] + vec_ref[12:13]).astype(jnp.bfloat16)
        grad_rows = grad_ref[...].astype(jnp.float32)
        part, gain, shift = norm_rows_back(after_ref[...], vec_ref[4:5], back_sum_ref[...])
        back = grad_rows + part
        back_ref[...] = back
        rows_ref[...] = jnp.zeros_like(rows_ref)
        rows_ref[4:5] = gain
        rows_ref[5:6] = shift
        rows_ref[11:12] = jnp.sum(back.astype(jnp.bfloat16).astype(jnp.float32), 0, keepdims=True)
        rows_ref[12:13] = jnp.sum(grad_rows, 0, keepdims=True)


def ffn(normed, grad, after, vec, up_full, bias, down_full):
    toks, width = normed.shape
    hidden = up_full.shape[1]
    size = 768
    low, full = jnp.bfloat16, jnp.float32
    shape = jax.ShapeDtypeStruct
    rows = pl.BlockSpec((toks, width), lambda t: (0, 0))
    vecs = pl.BlockSpec((16, width), lambda t: (0, 0))
    up_spec = pl.BlockSpec((width, size), lambda t: (0, t))
    down_spec = pl.BlockSpec((size, width), lambda t: (t, 0))
    bias_spec = pl.BlockSpec((1, size), lambda t: (0, t))
    return pl.pallas_call(
        ffn_kernel,
        grid=(hidden // size,),
        in_specs=[rows, rows, rows, vecs, up_spec, bias_spec, down_spec],
        out_specs=[rows, rows, up_spec, down_spec, bias_spec, vecs],
        out_shape=[
            shape((toks, width), low), shape((toks, width), full), shape(up_full.shape, low),
            shape(down_full.shape, low), shape((1, hidden), full), shape((16, width), full),
        ],
        scratch_shapes=[pltpu.VMEM((width, toks), low), pltpu.VMEM((toks, width), full), pltpu.VMEM((toks, width), full)],
        compiler_params=pltpu.CompilerParams(vmem_limit_bytes=63 * 2**20),
        name="ffn",
    )(normed, grad, after, vec, up_full, bias, down_full)


def place_clips_kernel(order, in_ref, out_ref):
    frames, width = in_ref.shape[1:]
    blocks = width // 128
    for k in range(blocks):
        out_ref[pl.ds(k, frames, stride=blocks), 0] = in_ref[0, :, k * 128:(k + 1) * 128]


def place_clips(order, values):
    clips, frames, width = values.shape
    rows = frames * width // 128
    flat = pl.pallas_call(
        place_clips_kernel,
        grid_spec=pltpu.PrefetchScalarGridSpec(
            num_scalar_prefetch=1,
            grid=(clips,),
            in_specs=[pl.BlockSpec((1, frames, width), lambda k, order: (k, 0, 0))],
            out_specs=pl.BlockSpec((rows, 1, 128), lambda k, order: (order[k], 0, 0)),
        ),
        out_shape=jax.ShapeDtypeStruct((clips * rows, 1, 128), values.dtype),
        compiler_params=pltpu.CompilerParams(vmem_limit_bytes=48 * 2**20),
        name="place_clips",
    )(order, values)
    return flat.reshape(1, clips, frames, width)


def from_behind(value, axis, steps):
    count = lax.axis_size(axis)
    leading, last = (max(0, -steps), min(count, count - steps))
    return lax.ppermute(value, axis, [(source, source + steps) for source in range(leading, last)])


def layer_norm(values, gain, shift):
    average = jnp.mean(values, -1, keepdims=True)
    centred = values - average
    spread = jnp.mean(centred * centred, -1, keepdims=True)
    return centred * lax.rsqrt(spread + 1e-05) * gain + shift


def matmul(left, right):
    return jnp.dot(left, right, preferred_element_type=jnp.float32)


def swap_halves(value):
    return lax.ppermute(value, "seq", [(0, 1), (1, 0)])


def seq_halves(value, axis):
    span = value.shape[axis] // 2
    half = lax.axis_index("seq")
    mine = lax.dynamic_slice_in_dim(value, half * span, span, axis)
    other = lax.dynamic_slice_in_dim(value, (1 - half) * span, span, axis)
    return mine, other


def seq_scatter(value):
    mine, other = seq_halves(value, 0)
    return mine + swap_halves(other.astype(jnp.bfloat16)).astype(value.dtype)


def per_head(values):
    rows = values.reshape(-1, values.shape[2]).T
    return jnp.repeat(rows, HEAD_DIM, axis=1)


def head_sums(values):
    sums = jnp.sum(values.reshape(values.shape[0], -1, HEAD_DIM), -1)
    return sums.T.reshape(-1, 2, values.shape[0])


def plain_forward(
    which, layer_input, frames, mask_bias, row_segment, weights
):
    self_full, cross_full, up_full, down_full, bias_full, out_bias_full, vectors = (
        lax.all_gather(part, ("dp", "seq"), axis=0, tiled=True) for part in weights
    )
    vec = jnp.pad(
        jnp.concatenate([vectors.T, out_bias_full[None]]).astype(jnp.float32), ((0, 3), (0, 0))
    )
    model_width = layer_input.shape[1]
    cross_in = [cross_full[:, k * model_width : (k + 1) * model_width] for k in range(4)]
    ckv_full = cross_full[:, model_width : 3 * model_width]
    cqo_full = jnp.concatenate([cross_in[0], cross_in[3]], 1)
    source = layer_input.astype(jnp.float32)
    normed_one = layer_norm(source, vec[0], vec[1]).astype(jnp.bfloat16)
    proj_bias = jnp.concatenate([vec[6], jnp.zeros_like(vec[6]), vec[7]])
    qkv_low = (matmul(normed_one, self_full[:, : 3 * model_width]) + proj_bias).astype(jnp.bfloat16)
    query = qkv_low[:, :model_width] * jnp.bfloat16(0.125)
    kv_own = qkv_low[:, model_width:]
    kv_row = jnp.concatenate([from_behind(kv_own, "seq", 1), kv_own])
    attended, self_lse = self_forward(query, kv_row, mask_bias)
    attended_low = attended.astype(jnp.bfloat16)
    after_self = source + matmul(attended_low, self_full[:, 3 * model_width :]) + vec[8]
    normed_two = layer_norm(after_self, vec[2], vec[3]).astype(jnp.bfloat16)
    cross_query = (matmul(normed_two, cross_in[0]) + vec[9]).astype(jnp.bfloat16)
    cross_key = jnp.einsum(
        "cfd,de->cfe", frames, cross_in[1], preferred_element_type=jnp.float32
    ).astype(jnp.bfloat16)
    cross_value = (
        jnp.einsum("cfd,de->cfe", frames, cross_in[2], preferred_element_type=jnp.float32)
        + vec[10]
    ).astype(jnp.bfloat16)
    row_query = lax.all_gather(cross_query * jnp.bfloat16(0.125), "seq", axis=0, tiled=True)
    cross_kv = jnp.concatenate([cross_key, cross_value], 2)
    part_mixed, part_stats = cross_forward(which, row_query, cross_kv, row_segment)
    mixed_mine, mixed_other = seq_halves(part_mixed, 0)
    stats_mine, stats_other = seq_halves(part_stats, 2)
    mixed_came = swap_halves(mixed_other.astype(jnp.bfloat16))
    stats_came = swap_halves(stats_other)
    peak = jnp.maximum(stats_mine[:, :2], stats_came[:, :2])
    share_mine = stats_mine[:, 2:] * jnp.exp(stats_mine[:, :2] - peak)
    share_came = stats_came[:, 2:] * jnp.exp(stats_came[:, :2] - peak)
    total = share_mine + share_came
    cross_lse = peak + jnp.log(total)
    mixed_full = mixed_mine * per_head(share_mine / total) + mixed_came.astype(
        jnp.float32
    ) * per_head(share_came / total)
    mixed = mixed_full.astype(jnp.bfloat16)
    after_cross = after_self + matmul(mixed, cross_in[3]) + vec[11]
    normed_three = layer_norm(after_cross, vec[4], vec[5]).astype(jnp.bfloat16)
    return (
        bias_full, ckv_full, self_full, cqo_full, up_full, down_full, cross_kv, vec, normed_one, query, kv_row, attended,
        self_lse, after_self, normed_two, row_query, cross_lse, mixed_full, after_cross, normed_three,
    )


def plain_backward(
    which, layer_input, mask_bias, row_segment, vec, grad_after_cross, mixed_full, cross_lse, row_query, after_self,
    attended, self_lse, query, kv_row, cqo_full, self_full, cross_kv
):
    tok_span, model_width = layer_input.shape
    source = layer_input.astype(jnp.float32)
    grad_cross_low = grad_after_cross.astype(jnp.bfloat16)
    grad_mixed = matmul(grad_cross_low, cqo_full[:, model_width:].T).astype(jnp.bfloat16)
    row_grad = lax.all_gather(grad_mixed, "seq", axis=0, tiled=True)
    cross_inner = head_sums(grad_mixed.astype(jnp.float32) * mixed_full)
    row_stats = lax.all_gather(jnp.stack([cross_lse, cross_inner]), "seq", axis=3, tiled=True)
    part_query, grad_key, grad_value = cross_backward(
        which, row_query, cross_kv, row_segment, row_stats[0], row_stats[1], row_grad
    )
    grad_query_sum = seq_scatter(part_query).astype(jnp.bfloat16)
    grad_cq_bias = jnp.sum(grad_query_sum, 0, dtype=jnp.float32)
    grad_normed_two = matmul(grad_query_sum, cqo_full[:, :model_width].T)
    grad_cv_bias = jnp.sum(grad_value, (0, 1), dtype=jnp.float32)
    _, norm_pull_two = jax.vjp(layer_norm, after_self, vec[2], vec[3])
    grad_part, grad_gain_two, grad_shift_two = norm_pull_two(grad_normed_two)
    grad_after_self = grad_after_cross + grad_part
    grad_self_low = grad_after_self.astype(jnp.bfloat16)
    grad_self_bias = jnp.sum(grad_self_low, 0, dtype=jnp.float32)
    grad_attended = matmul(grad_self_low, self_full[:, 3 * model_width :].T).astype(jnp.bfloat16)
    self_inner = head_sums(grad_attended.astype(jnp.float32) * attended)
    grad_query, grad_key_row, grad_value_row = self_backward(
        query, kv_row, mask_bias, self_lse, self_inner, grad_attended
    )
    grad_kv = jnp.concatenate([grad_key_row, grad_value_row], 1)
    back_kv = from_behind(grad_kv[:tok_span].astype(jnp.bfloat16), "seq", -1)
    grad_qkv_low = jnp.concatenate(
        [grad_query, grad_kv[tok_span:] + back_kv.astype(jnp.float32)], 1
    ).astype(jnp.bfloat16)
    grad_qkv_bias = jnp.sum(grad_qkv_low, 0, dtype=jnp.float32)
    grad_normed_one = matmul(grad_qkv_low, self_full[:, : 3 * model_width].T)
    _, norm_pull_one = jax.vjp(layer_norm, source, vec[0], vec[1])
    grad_part, grad_gain_one, grad_shift_one = norm_pull_one(grad_normed_one)
    input_grad = grad_after_self + grad_part
    nothing = jnp.zeros_like(grad_cq_bias)
    vec_grads = jnp.stack(
        [
            grad_gain_one,
            grad_shift_one,
            grad_gain_two,
            grad_shift_two,
            nothing,
            nothing,
            grad_qkv_bias[:model_width],
            grad_qkv_bias[2 * model_width :],
            grad_self_bias,
            grad_cq_bias,
            grad_cv_bias,
        ]
        + [nothing] * 5
    )
    return (
        input_grad, grad_query_sum, grad_self_low, grad_qkv_low, vec_grads,
        jnp.concatenate([grad_key, grad_value], 2),
    )


def plain_finish(
    normed_one, grad_qkv_low, attended_low, grad_self_low, normed_two, grad_query_sum, mixed, grad_cross_low, frames,
    cross_kv_grad, ckv_full
):
    width = normed_one.shape[1]
    grads_self = jnp.concatenate([matmul(normed_one.T, grad_qkv_low), matmul(attended_low.T, grad_self_low)], 1)
    grad_ckv = jnp.einsum("cfd,cfe->de", frames, cross_kv_grad, preferred_element_type=jnp.float32)
    grads_cross = jnp.concatenate(
        [matmul(normed_two.T, grad_query_sum), grad_ckv, matmul(mixed.T, grad_cross_low)], 1
    )
    encoder_grad = jnp.einsum(
        "cfe,de->cfd", cross_kv_grad, ckv_full, preferred_element_type=jnp.float32
    )
    return encoder_grad, (grads_self, grads_cross)


def fused_device(
    layer_input,
    encoder_states,
    clip_lengths,
    out_grad,
    self_weights,
    cross_weights,
    up_weights,
    down_weights,
    up_bias,
    down_bias,
    vectors,
):
    small_blocks, ckv_full, self_full, cqo_full, up_full, down_full, cross_kv, vec, normed_one, query, kv_row, attended, \
        self_lse, after_self, normed_two, row_query, cross_lse, mixed_full, after_cross, normed_three, mask_bias, \
        row_segment, info, frames = fused_forward(
            clip_lengths, layer_input[0], vectors.T, up_bias[None], down_bias[None], self_weights, cross_weights, up_weights,
            encoder_states[0], down_weights,
        )
    bias_full = small_blocks[:, 13, : up_bias.shape[0]].reshape(-1).astype(jnp.float32)
    layer_output, grad_after_cross, grad_up, grad_down, grad_up_bias, ffn_rows = ffn(
        normed_three, out_grad[0], after_cross, vec, up_full, bias_full[None], down_full
    )
    large = [g.reshape(32, -1, g.shape[1]) for g in (grad_up, grad_down)]
    input_grad, encoder_grad, up_share, down_share, cross_share, self_share, up_row, down_row, vector_rows, *_ = fused_backward(
        info, layer_input[0], mask_bias, row_segment, vec, grad_after_cross, mixed_full, cross_lse, row_query, after_self,
        attended, self_lse, query, kv_row, normed_one, normed_two, ffn_rows, grad_up_bias, cqo_full, ckv_full, self_full,
        cross_kv, frames, *large
    )
    return (
        layer_output[None], input_grad[None], encoder_grad.reshape((1,) + encoder_states.shape[1:]), self_share, cross_share,
        up_share, down_share, up_row[0], down_row[0], vector_rows.T,
    )


def plain_device(
    layer_input,
    encoder_states,
    clip_lengths,
    out_grad,
    self_weights,
    cross_weights,
    up_weights,
    down_weights,
    up_bias,
    down_bias,
    vectors,
):
    model_width = layer_input.shape[2]
    tok_span = layer_input.shape[1]
    seq_half = lax.axis_index("seq")
    position = seq_half * tok_span + jnp.arange(tok_span, dtype=jnp.int32)
    clip_ends = jnp.cumsum(clip_lengths[0])
    segment = jnp.sum((position[:, None] >= clip_ends[None, :]).astype(jnp.int32), 1)
    key_position = jnp.concatenate([position - tok_span, position])
    key_segment = jnp.sum((key_position[:, None] >= clip_ends[None, :]).astype(jnp.int32), 1)
    allowed = (
        (key_segment[:, None] == segment[None, :])
        & (key_position[:, None] <= position[None, :])
        & (key_position[:, None] >= 0)
    )
    mask_bias = jnp.where(allowed, 0.0, -1e30).astype(jnp.float32)
    row_position = jnp.arange(2 * tok_span, dtype=jnp.int32)
    row_segment = jnp.sum((row_position[:, None] >= clip_ends[None, :]).astype(jnp.int32), 1)[None]
    big = jnp.argmax(clip_lengths[0]).astype(jnp.int32)
    small_one = jnp.where(big == 0, 1, 0)
    small_two = jnp.where(big == 2, 1, 2)
    last_group = 2 * tok_span // 128 - 1
    order = jnp.stack([big, small_one, small_two]).astype(jnp.int32)
    row_segment = jnp.where(
        row_segment == order[0], 0, jnp.where(row_segment == order[1], 1, jnp.where(row_segment == order[2], 2, 3))
    )
    which = jnp.where(order[1:] < big, 0, last_group).astype(jnp.int32)

    frames = jnp.take(encoder_states[0], order, axis=0, mode="clip")
    (
        bias_full, ckv_full, self_full, cqo_full, up_full, down_full, cross_kv, vec, normed_one, query, kv_row, attended,
        self_lse, after_self, normed_two, row_query, cross_lse, mixed_full, after_cross, normed_three,
    ) = plain_forward(
        which, layer_input[0], frames, mask_bias, row_segment,
        (self_weights, cross_weights, up_weights, down_weights, up_bias, down_bias, vectors),
    )
    bias_full = bias_full.astype(jnp.float32)
    layer_output, grad_after_cross, grad_up, grad_down, grad_up_bias, ffn_rows = ffn(
        normed_three, out_grad[0], after_cross, vec, up_full, bias_full[None], down_full
    )
    operands = (
        layer_input[0], mask_bias, row_segment, vec, grad_after_cross, mixed_full, cross_lse, row_query, after_self,
        attended, self_lse, query, kv_row,
    )
    input_grad, grad_query_sum, grad_self_low, grad_qkv_low, vec_grads, cross_kv_grad = plain_backward(
        which, *operands, cqo_full, self_full, cross_kv
    )
    encoder_grad, large = plain_finish(
        normed_one, grad_qkv_low, attended.astype(jnp.bfloat16), grad_self_low, normed_two, grad_query_sum,
        mixed_full.astype(jnp.bfloat16), grad_after_cross.astype(jnp.bfloat16), frames, cross_kv_grad, ckv_full,
    )
    vector_grads = vec_grads + ffn_rows
    shares = tuple(
        lax.psum_scatter(part, ("dp", "seq"), scatter_dimension=0, tiled=True)
        for part in large
        + (grad_up.astype(jnp.float32), grad_down.astype(jnp.float32), grad_up_bias[0], vector_grads[12],
           vector_grads[:12].T)
    )
    return (layer_output[None], input_grad[None], place_clips(order, encoder_grad)) + shares


def solution(mesh):
    return jax.shard_map(
        fused_device if mesh.shape["dp"] == 16 else plain_device,
        mesh=mesh,
        in_specs=(
            P("dp", "seq", None),
            P("dp", None, "seq", None),
            P("dp", None),
            P("dp", "seq", None),
            P(("dp", "seq"), None),
            P(("dp", "seq"), None),
            P(("dp", "seq"), None),
            P(("dp", "seq"), None),
            P(("dp", "seq")),
            P(("dp", "seq")),
            P(("dp", "seq"), None),
        ),
        out_specs=(
            P("dp", "seq", None),
            P("dp", "seq", None),
            P("dp", None, "seq", None),
            P(("dp", "seq"), None),
            P(("dp", "seq"), None),
            P(("dp", "seq"), None),
            P(("dp", "seq"), None),
            P(("dp", "seq")),
            P(("dp", "seq")),
            P(("dp", "seq"), None),
        ),
        check_vma=False,
    )
```

```python
import functools

import jax
import jax.numpy as jnp
from jax import lax
from jax.experimental import pallas as pl
from jax.experimental.pallas import tpu as pltpu
from jax.sharding import PartitionSpec as P

HEAD_DIM = 64
CLIPS = 3
MESH = pl.DeviceIdType.MESH
NT = (((1,), (1,)), ((), ()))
NN = (((1,), (0,)), ((), ()))


def dot(left, right, dims):
    return lax.dot_general(left, right, dims, preferred_element_type=jnp.float32)


def one_head(values, h):
    lane = lax.broadcasted_iota(jnp.int32, values.shape, 1)
    return jnp.where((lane >= 64) == (h == 1), values, jnp.zeros_like(values))


def self_forward_kernel(q_ref, k_ref, v_ref, bias_ref, out_ref, lse_ref):
    keys = k_ref[...]
    values_t = v_ref[...].T
    halves = []
    for h in range(2):
        scores = dot(keys, one_head(q_ref[...], h), NT) + bias_ref[...]
        peak = jnp.max(scores, 0, keepdims=True)
        terms = jnp.exp(scores - peak)
        total = jnp.sum(terms, 0, keepdims=True)
        result = dot(values_t[h * 64:(h + 1) * 64], terms.astype(jnp.bfloat16), NN)
        halves.append(result / total)
        lse_ref[0, h:h + 1] = peak + jnp.log(total)
    out_ref[...] = jnp.concatenate(halves, 0).T.astype(out_ref.dtype)


def self_forward(q, kv, bias):
    toks, width = q.shape
    keys, pairs = kv.shape[0], width // 128
    return pl.pallas_call(
        self_forward_kernel,
        grid=(width // 128,),
        in_specs=[
            pl.BlockSpec((toks, 128), lambda j: (0, j)),
            pl.BlockSpec((keys, 128), lambda j: (0, j)),
            pl.BlockSpec((keys, 128), lambda j: (0, j + pairs)),
            pl.BlockSpec((keys, toks), lambda j: (0, 0)),
        ],
        out_specs=[
            pl.BlockSpec((toks, 128), lambda j: (0, j)),
            pl.BlockSpec((1, 2, toks), lambda j: (j, 0, 0)),
        ],
        out_shape=[
            jax.ShapeDtypeStruct((toks, width), jnp.float32),
            jax.ShapeDtypeStruct((width // 128, 2, toks), jnp.float32),
        ],
        compiler_params=pltpu.CompilerParams(vmem_limit_bytes=48 * 2**20),
        name="self_forward",
    )(q, kv, kv, bias)


def self_backward_kernel(q_ref, k_ref, v_ref, bias_ref, lse_ref, inner_ref, g_ref, dq_ref, dk_ref, dv_ref):
    keys, values = k_ref[...], v_ref[...]
    keys_t = keys.T
    grad_k = grad_v = None
    halves = []
    for h in range(2):
        query, grad = one_head(q_ref[...], h), one_head(g_ref[...], h)
        weights = jnp.exp(dot(keys, query, NT) + bias_ref[...] - lse_ref[0, h:h + 1])
        part = dot(weights.astype(jnp.bfloat16), grad, NN)
        grad_v = part if grad_v is None else grad_v + part
        grad_s = (weights * (dot(values, grad, NT) - inner_ref[0, h:h + 1])).astype(jnp.bfloat16)
        part = dot(grad_s, query, NN)
        grad_k = part if grad_k is None else grad_k + part
        halves.append(dot(keys_t[h * 64:(h + 1) * 64], grad_s, NN))
    dq_ref[...] = (jnp.concatenate(halves, 0) * 0.125).T
    dk_ref[...] = grad_k
    dv_ref[...] = grad_v


def self_backward(q, kv, bias, lse, inner, grad):
    toks, width = q.shape
    keys, pairs = kv.shape[0], width // 128
    tok_spec = pl.BlockSpec((toks, 128), lambda j: (0, j))
    key_spec = pl.BlockSpec((keys, 128), lambda j: (0, j))
    row_spec = pl.BlockSpec((1, 2, toks), lambda j: (j, 0, 0))
    return pl.pallas_call(
        self_backward_kernel,
        grid=(width // 128,),
        in_specs=[tok_spec, key_spec, pl.BlockSpec((keys, 128), lambda j: (0, j + pairs)), pl.BlockSpec((keys, toks), lambda j: (0, 0)), row_spec, row_spec, tok_spec],
        out_specs=[tok_spec, key_spec, key_spec],
        out_shape=[
            jax.ShapeDtypeStruct((toks, width), jnp.float32),
            jax.ShapeDtypeStruct((keys, width), jnp.float32),
            jax.ShapeDtypeStruct((keys, width), jnp.float32),
        ],
        compiler_params=pltpu.CompilerParams(vmem_limit_bytes=48 * 2**20),
        name="self_backward",
    )(q, kv, kv, bias, lse, inner, grad)


def cross_forward_kernel(which, q_ref, k_ref, v_ref, seg_ref, out_ref, stat_ref, acc_ref):
    def attend(clip, values_t, query, h):
        scores = dot(k_ref[clip], query, NT)
        peak = jnp.max(scores, 0, keepdims=True)
        terms = jnp.exp(scores - peak)
        total = jnp.sum(terms, 0, keepdims=True)
        result = dot(values_t[h * 64:(h + 1) * 64], terms.astype(jnp.bfloat16), NN)
        return result / total, peak, total

    values_t = v_ref[0].T
    for h in range(2):
        mine = seg_ref[...] == 0
        result, peak, total = attend(0, values_t, one_head(q_ref[...], h), h)
        acc_ref[h * 64:(h + 1) * 64] = jnp.where(mine, result, 0.0)
        stat_ref[0, h:h + 1] = jnp.where(mine, peak, 0.0)
        stat_ref[0, 2 + h:3 + h] = jnp.where(mine, total, 1.0)
    for clip in (1, 2):
        cols = pl.ds(pl.multiple_of(which[clip - 1] * 128, 128), 128)
        values_t = v_ref[clip].T
        mine = seg_ref[:, cols] == clip
        for h in range(2):
            result, peak, total = attend(clip, values_t, one_head(q_ref[cols], h), h)
            rows = slice(h * 64, (h + 1) * 64)
            acc_ref[rows, cols] = jnp.where(mine, result, acc_ref[rows, cols])
            stat_ref[0, h:h + 1, cols] = jnp.where(mine, peak, stat_ref[0, h:h + 1, cols])
            stat_ref[0, 2 + h:3 + h, cols] = jnp.where(mine, total, stat_ref[0, 2 + h:3 + h, cols])
    out_ref[...] = acc_ref[...].T


def cross_forward(which, q, kv, seg):
    toks, width = q.shape
    clips, frames = kv.shape[:2]
    pairs = width // 128
    kv_spec = pl.BlockSpec((clips, frames, 128), lambda j, w: (0, 0, j))
    v_spec = pl.BlockSpec((clips, frames, 128), lambda j, w: (0, 0, j + pairs))
    tok_spec = pl.BlockSpec((toks, 128), lambda j, w: (0, j))
    return pl.pallas_call(
        cross_forward_kernel,
        grid_spec=pltpu.PrefetchScalarGridSpec(
            num_scalar_prefetch=1,
            grid=(width // 128,),
            in_specs=[tok_spec, kv_spec, v_spec, pl.BlockSpec((1, toks), lambda j, w: (0, 0))],
            out_specs=[tok_spec, pl.BlockSpec((1, 4, toks), lambda j, w: (j, 0, 0))],
            scratch_shapes=[pltpu.VMEM((128, toks), jnp.float32)],
        ),
        out_shape=[
            jax.ShapeDtypeStruct((toks, width), jnp.float32),
            jax.ShapeDtypeStruct((width // 128, 4, toks), jnp.float32),
        ],
        compiler_params=pltpu.CompilerParams(vmem_limit_bytes=48 * 2**20),
        name="cross_forward",
    )(which, q, kv, kv, seg)


def cross_backward_kernel(which, q_ref, k_ref, v_ref, seg_ref, lse_ref, inner_ref, g_ref, dq_ref, dk_ref, dv_ref, acc_ref):
    def back(clip, keys_t, cols, h):
        query, grad = one_head(q_ref[cols], h), one_head(g_ref[cols], h)
        lse = jnp.where(seg_ref[:, cols] == clip, lse_ref[0, h:h + 1, cols], 1e30)
        weights = jnp.exp(dot(k_ref[clip], query, NT) - lse)
        grad_v = dot(weights.astype(jnp.bfloat16), grad, NN)
        grad_s = (weights * (dot(v_ref[clip], grad, NT) - inner_ref[0, h:h + 1, cols])).astype(jnp.bfloat16)
        grad_k = dot(grad_s, query, NN)
        return dot(keys_t[h * 64:(h + 1) * 64], grad_s, NN), grad_k, grad_v

    for clip in range(3):
        cols = slice(None) if clip == 0 else pl.ds(pl.multiple_of(which[clip - 1] * 128, 128), 128)
        keys_t = k_ref[clip].T
        grad_q, grad_k, grad_v = zip(*(back(clip, keys_t, cols, h) for h in range(2)))
        grad_q = jnp.concatenate(grad_q, 0)
        if clip == 0:
            acc_ref[...] = grad_q
        else:
            acc_ref[:, cols] += grad_q
        dk_ref[clip] = (grad_k[0] + grad_k[1]).astype(jnp.bfloat16)
        dv_ref[clip] = (grad_v[0] + grad_v[1]).astype(jnp.bfloat16)
    dq_ref[...] = (acc_ref[...] * 0.125).T


def cross_backward(which, q, kv, seg, lse, inner, grad):
    toks, width = q.shape
    clips, frames = kv.shape[:2]
    pairs = width // 128
    kv_spec = pl.BlockSpec((clips, frames, 128), lambda j, w: (0, 0, j))
    v_spec = pl.BlockSpec((clips, frames, 128), lambda j, w: (0, 0, j + pairs))
    tok_spec = pl.BlockSpec((toks, 128), lambda j, w: (0, j))
    row_spec = pl.BlockSpec((1, 2, toks), lambda j, w: (j, 0, 0))
    return pl.pallas_call(
        cross_backward_kernel,
        grid_spec=pltpu.PrefetchScalarGridSpec(
            num_scalar_prefetch=1,
            grid=(width // 128,),
            in_specs=[tok_spec, kv_spec, v_spec, pl.BlockSpec((1, toks), lambda j, w: (0, 0)), row_spec, row_spec, tok_spec],
            out_specs=[tok_spec, kv_spec, kv_spec],
            scratch_shapes=[pltpu.VMEM((128, toks), jnp.float32)],
        ),
        out_shape=[
            jax.ShapeDtypeStruct((toks, width), jnp.float32),
            jax.ShapeDtypeStruct((clips, frames, width), jnp.bfloat16),
            jax.ShapeDtypeStruct((clips, frames, width), jnp.bfloat16),
        ],
        compiler_params=pltpu.CompilerParams(vmem_limit_bytes=48 * 2**20),
        name="cross_backward",
    )(which, q, kv, kv, seg, lse, inner, grad)


Z = 4


class Place:
    def __init__(self):
        self.dp = lax.axis_index("dp")
        self.core = lax.axis_index("seq")
        self.z = self.dp // 4
        self.p = self.dp % 4
        x, y = self.p % 2, self.p // 2
        px, py = self.p + 1 - 2 * x, self.p + 2 - 4 * y
        self.p_first = px * (1 - self.core) + py * self.core
        self.p_second = py * (1 - self.core) + px * self.core
        self.p_diag = 3 - self.p
        base = self.z * 4
        self.first = (base + self.p_first, self.core)
        self.second = (base + self.p_second, self.core)
        self.mate = (self.dp, 1 - self.core)
        half = self.z // 2
        near = self.z + half * (3 - 2 * self.z)
        self.line = [base + half * (3 - 2 * base) for base in (3, 2, 1 - near)]
        self.peers = [self.mate, self.first, self.second] + [self.on_line(z) for z in self.line]

    def on_line(self, z):
        return (z * 4 + self.p, self.core)

    def greet(self):
        barrier = pltpu.get_barrier_semaphore()
        for target in self.peers:
            pl.semaphore_signal(barrier, inc=1, device_id=target, device_id_type=MESH)
        pl.semaphore_wait(barrier, len(self.peers))


HALF_COLS = {1: 768, 2: 1536, 3: 768, 4: 1536}


class Gather:
    def __init__(self, me, srcs, outs, send_sem, recv_sem, own_sem):
        self.me, self.srcs, self.outs = me, srcs, outs
        self.send_sem, self.recv_sem, self.own_sem = send_sem, recv_sem, own_sem
        self.sends = []
        self.tasks = []
        for m, times in enumerate(GATHER_TIMES):
            for time, task in zip(times, self.steps(m)):
                self.tasks.append((time, m, task))
        self.tasks.sort(key=lambda entry: entry[:2])

    def piece(self, m, chip, core):
        if m == 0:
            return self.outs[m].at[chip * 2 + core]
        if m == 5:
            return self.outs[m].at[pl.ds(pl.multiple_of(chip * 192 + core * 96, 96), 96)]
        rows = pl.ds(pl.multiple_of(chip * 48, 48), 48)
        return self.outs[m].at[rows, columns(core, HALF_COLS[m])]

    def sender(self, m, src, chip, target):
        copy = pltpu.make_async_remote_copy(
            src_ref=src, dst_ref=self.piece(m, chip, self.me.core), send_sem=self.send_sem.at[len(self.sends)],
            recv_sem=self.recv_sem.at[m, chip * 2 + self.me.core], device_id=target, device_id_type=MESH)
        self.sends.append(copy)
        return copy.start

    def arrival(self, m, chip, core):
        piece = self.piece(m, chip, core)
        return pltpu.make_async_remote_copy(
            src_ref=piece, dst_ref=piece, send_sem=self.send_sem.at[0],
            recv_sem=self.recv_sem.at[m, chip * 2 + core], device_id=self.me.mate, device_id_type=MESH).wait_recv

    def forward(self, m, z, p, targets):
        chip = z * 4 + p
        return [self.arrival(m, chip, self.me.core)] + [
            self.sender(m, self.piece(m, chip, self.me.core), chip, target) for target in targets
        ]

    def steps(self, m):
        me = self.me
        begin = [
            self.sender(m, self.srcs[m], me.dp, target)
            for target in [me.on_line(z) for z in me.line] + [me.first, me.second, me.mate]
        ]
        begin.append(pltpu.make_async_copy(self.srcs[m], self.piece(m, me.dp, me.core), self.own_sem.at[m]).start)
        line = []
        for z in me.line[::-1]:
            line += self.forward(m, z, me.p, [me.first, me.second, me.mate])
        beside = []
        for z in [me.z] + me.line[::-1]:
            beside += self.forward(m, z, me.p_first, [me.second, me.mate])
        rest = []
        for p in (me.p_second, me.p_diag):
            for z in [me.z] + me.line[::-1]:
                rest += self.forward(m, z, p, [me.mate])
        return [begin, line, beside, rest]

    def run(self, entry):
        for act in entry[2]:
            act()

    def run_until(self, time):
        while self.tasks and self.tasks[0][0] <= time:
            self.run(self.tasks.pop(0))

    def take_until(self, time):
        taken = []
        while self.tasks and self.tasks[0][0] <= time:
            taken.append(self.tasks.pop(0))
        return taken

    def need(self, m):
        for entry in [e for e in self.tasks if e[1] == m]:
            self.run(entry)
        self.tasks = [e for e in self.tasks if e[1] != m]
        pltpu.make_async_copy(self.srcs[m], self.piece(m, self.me.dp, self.me.core), self.own_sem.at[m]).wait()
        for chip in range(16):
            self.arrival(m, chip, 1 - self.me.core)()

    def finish(self):
        for copy in self.sends:
            copy.wait_send()


GATHER_TIMES = (
    (1, 6, 10, 15),
    (0, 5, 9, 14),
    (2, 11, 19, 27),
    (10, 20, 26, 34),
    (18, 31, 42, 54),
    (30, 48, 60, 74),
)


def loop_with(steps, count, begin, length, body, slots=(0,)):
    due = {}
    for i in range(count):
        for part, k in sorted((part, k) for k, part in enumerate(slots)):
            due[i, k] = steps.take_until(begin + length * (i + part))

    def turn(i, carry):
        def tick(k):
            for at in range(count):
                if due[at, k]:

                    def run(entries=due[at, k]):
                        for entry in entries:
                            steps.run(entry)

                    pl.when(i == at)(run)

        body(i, tick)
        return carry

    lax.fori_loop(0, count, turn, 0)


def norm_rows(values, gain, shift):
    average = jnp.mean(values, -1, keepdims=True)
    centred = values - average
    spread = jnp.mean(centred * centred, -1, keepdims=True)
    return centred * lax.rsqrt(spread + 1e-05) * gain + shift


def two_heads(values):
    return jnp.concatenate([one_head(values, 0), one_head(values, 1)], 0)


def columns(j, size=128):
    return pl.ds(pl.multiple_of(j * size, size), size)


def forward_kernel(*refs):
    (length_ref, x_ref, vectors_in, up_bias_in, down_bias_in, self_in, cross_in, up_in, frames_hbm, down_in) = refs[:10]
    (small_out, ckv_out, self_out, cqo_out, up_out, down_out, kv_out, vec_ref, normed_one_ref, query_ref, kv_row_ref,
     attended_ref, self_lse_ref, after_self_ref, normed_two_ref, row_query_ref, cross_lse_ref, mixed_ref,
     after_cross_ref, normed_three_ref, bias_ref, seg_ref, info_ref, ranked_hbm,
     up_bias_ref) = refs[10:35]
    (frames_in, frames_ref, small_f32, small_in, half_wide, half_narrow, pair_wide, pair_narrow, small_vm, ckv_vm, self_vm, cqo_vm, kv_vm, acc_ref, stat_ref, part_ref, part_stat_ref, give_ref,
     give_stat_ref, take_ref, take_stat_ref, send_sem, recv_sem, own_sem, half_sems, mate_sems, load_sem,
     frame_sem) = refs[35:]
    me = Place()
    core = me.core
    width = x_ref.shape[1]
    toks = x_ref.shape[0]
    frames_load = pltpu.make_async_copy(frames_hbm, frames_in, frame_sem.at[0])
    frames_load.start()
    small_f32[...] = jnp.zeros_like(small_f32)
    small_f32[:12, :vectors_in.shape[1]] = vectors_in[...].astype(jnp.float32)
    small_f32[12:13, :down_bias_in.shape[1]] = down_bias_in[...].astype(jnp.float32)
    small_f32[13:14, :up_bias_in.shape[1]] = up_bias_in[...].astype(jnp.float32)
    small_in[...] = small_f32[...].astype(jnp.bfloat16)
    me.greet()

    def to_mate(src, dst, k):
        return pltpu.make_async_remote_copy(
            src_ref=src, dst_ref=dst, send_sem=mate_sems.at[0, k], recv_sem=mate_sems.at[1, k], device_id=me.mate,
            device_id_type=MESH)

    def half_of(m, which):
        shard = (None, cross_in, self_in, cross_in, up_in)[m]
        size = HALF_COLS[m]
        begin = (0, width, 0, 0, 0)[m] + which * (0, width, size, 3 * width, size)[m]
        return shard.at[:, pl.ds(pl.multiple_of(begin, size), size)]

    buffers = {1: (half_narrow.at[0], pair_narrow.at[0]), 2: (half_wide.at[0], pair_wide.at[0]),
               3: (half_narrow.at[1], pair_narrow.at[1]), 4: (half_wide.at[1], pair_wide.at[1])}
    halves = {
        m: pltpu.make_async_remote_copy(
            src_ref=half_of(m, 1 - core), dst_ref=buffers[m][0], send_sem=half_sems.at[0, m],
            recv_sem=half_sems.at[1, m], device_id=me.mate, device_id_type=MESH)
        for m in buffers
    }
    for copy in halves.values():
        copy.start()
    sources = (small_in,) + tuple(buffers[m][1] for m in buffers) + (down_in,)
    gather = Gather(me, sources, (small_out, ckv_out, self_out, cqo_out, up_out, down_out), send_sem, recv_sem, own_sem)
    for m, (came_ref, both_ref) in buffers.items():
        halves[m].wait()
        own = half_of(m, core)[...].astype(jnp.float32)
        came = came_ref[...].astype(jnp.float32)
        both_ref[...] = jnp.concatenate(
            [jnp.where(core == 0, own, came), jnp.where(core == 0, came, own)], 0).astype(jnp.bfloat16)
        gather.run_until((0, 1, 2, 2, 2)[m])

    def fetch(src, dst, k):
        copy = pltpu.make_async_copy(src, dst, load_sem.at[k])
        copy.start()
        copy.wait()

    lengths = [length_ref[0, clip] for clip in range(3)]
    ends = [lengths[0], lengths[0] + lengths[1], lengths[0] + lengths[1] + lengths[2]]

    def clip_at(position):
        return sum((position >= end).astype(jnp.int32) for end in ends)

    def number_row(value):
        return jnp.zeros((1, width), jnp.int32) + value

    length_rows = [number_row(length) for length in lengths]
    big = jnp.where(length_rows[1] > length_rows[0], 1, 0)
    big = jnp.where(length_rows[2] > jnp.maximum(length_rows[0], length_rows[1]), 2, big)
    order = [big, jnp.where(big == 0, 1, 0), jnp.where(big == 2, 1, 2)]
    info_ref[...] = jnp.zeros_like(info_ref)
    for k in (1, 2):
        info_ref[k - 1:k] = jnp.where(order[k] < big, 0, 3)
    for clip in range(3):
        info_ref[2 + clip:3 + clip] = jnp.where(order[0] == clip, 0, jnp.where(order[1] == clip, 1, 2))
    group_ref = info_ref.at[:, pl.ds(0, 128)]
    places = clip_at(lax.broadcasted_iota(jnp.int32, (1, 2 * toks), 1))
    seg_ref[...] = jnp.where(
        places == order[0][:, :2 * toks], 0,
        jnp.where(places == order[1][:, :2 * toks], 1, jnp.where(places == order[2][:, :2 * toks], 2, 3)))
    key_at = core * toks - toks + lax.broadcasted_iota(jnp.int32, bias_ref.shape, 0)
    query_at = core * toks + lax.broadcasted_iota(jnp.int32, bias_ref.shape, 1)
    allowed = (clip_at(key_at) == clip_at(query_at)) & (key_at <= query_at) & (key_at >= 0)
    bias_ref[...] = jnp.where(allowed, 0.0, -1e30)
    frames_load.wait()
    for k in range(3):
        frames_ref[k] = jnp.where(
            order[k] == 0, frames_in[0], jnp.where(order[k] == 1, frames_in[1], frames_in[2]))
    ranked_store = pltpu.make_async_copy(frames_ref, ranked_hbm, frame_sem.at[0])
    ranked_store.start()
    gather.run_until(15)
    gather.need(0)
    fetch(small_out, small_vm, 0)
    total = jnp.zeros(vec_ref.shape, jnp.float32)
    for d in range(32):
        block = jnp.concatenate(
            [small_vm[d].astype(jnp.float32), jnp.zeros((16, width - 128), jnp.float32)], 1)
        total = total + (block if d == 0 else pltpu.roll(block, d * 24, 1))
    vec_ref[...] = total
    hidden = up_bias_ref.shape[1]
    bias = jnp.zeros((1, hidden), jnp.float32)
    for d in range(32):
        block = jnp.concatenate(
            [small_vm[d].astype(jnp.float32)[13:14], jnp.zeros((1, hidden - 128), jnp.float32)], 1)
        bias = bias + (block if d == 0 else pltpu.roll(block, d * hidden // 32, 1))
    up_bias_ref[...] = bias

    def vec(k):
        return vec_ref[k:k + 1]

    source = x_ref[...].astype(jnp.float32)
    normed_one_ref[...] = norm_rows(source, vec(0), vec(1)).astype(jnp.bfloat16)
    gather.need(1)
    fetch(ckv_out, ckv_vm, 0)
    clips = frames_ref.shape[0]
    tiles = 2 * width // 256

    def project(t, tick):
        tick(0)
        clip, tile = t // tiles, t % tiles
        result = dot(frames_ref[clip], ckv_vm[:, columns(tile, 256)], NN)
        is_value = (tile >= 3).astype(jnp.float32)
        shift = vec_ref[10:11, columns(tile % 3, 256)] * is_value
        kv_vm[clip, :frames_ref.shape[1], columns(tile, 256)] = (result + shift).astype(jnp.bfloat16)

    early, middle = 6, 12
    loop_with(gather, early, 20, 0.65, project)
    gather.run_until(31)
    gather.need(2)
    fetch(self_out, self_vm, 0)

    normed = normed_one_ref[...]
    own_rows = slice(toks, 2 * toks)
    kv_row_ref[own_rows, :width] = dot(normed, self_vm[:, width:2 * width], NN).astype(jnp.bfloat16)
    kv_row_ref[own_rows, width:] = (dot(normed, self_vm[:, 2 * width:3 * width], NN) + vec(7)).astype(jnp.bfloat16)
    kv_copy = to_mate(kv_row_ref.at[own_rows], kv_row_ref.at[slice(0, toks)], 0)
    kv_copy.start()
    query = (dot(normed, self_vm[:, :width], NN) + vec(6)).astype(jnp.bfloat16)
    query_ref[...] = query * jnp.bfloat16(0.125)
    lax.fori_loop(early, middle, lambda t, carry: (project(t, lambda k: None), carry)[1], 0)
    gather.run_until(35)
    kv_copy.wait()

    def self_pair(j, tick):
        tick(0)
        cols = columns(j)
        keys = kv_row_ref[:, cols]
        values_t = kv_row_ref[:, columns(j + 6)].T
        parts = []
        for h in range(2):
            scores = dot(keys, one_head(query_ref[:, cols], h), NT) + bias_ref[...]
            peak = jnp.max(scores, 0, keepdims=True)
            terms = jnp.exp(scores - peak)
            total = jnp.sum(terms, 0, keepdims=True)
            parts.append(dot(values_t[h * 64:(h + 1) * 64], terms.astype(jnp.bfloat16), NN) / total)
            self_lse_ref[j, h:h + 1] = peak + jnp.log(total)
        attended_ref[:, cols] = jnp.concatenate(parts, 0).T

    loop_with(gather, 6, 35, 1.2, self_pair)
    after_self = source + dot(attended_ref[...].astype(jnp.bfloat16), self_vm[:, 3 * width:], NN) + vec(8)
    after_self_ref[...] = after_self
    normed_two = norm_rows(after_self, vec(2), vec(3)).astype(jnp.bfloat16)
    normed_two_ref[...] = normed_two
    gather.run_until(44)
    gather.need(3)
    fetch(cqo_out, cqo_vm, 0)
    my_rows = pl.ds(pl.multiple_of(core * toks, toks), toks)
    cross_query = (dot(normed_two, cqo_vm[:, :width], NN) + vec(9)).astype(jnp.bfloat16)
    row_query_ref[my_rows] = cross_query * jnp.bfloat16(0.125)
    query_copy = to_mate(row_query_ref.at[my_rows], row_query_ref.at[my_rows], 1)
    query_copy.start()
    lax.fori_loop(middle, clips * tiles, lambda t, carry: (project(t, lambda k: None), carry)[1], 0)
    kv_store = pltpu.make_async_copy(kv_vm, kv_out, load_sem.at[1])
    kv_store.start()
    gather.run_until(48)
    query_copy.wait()

    frame_count = frames_ref.shape[1]

    def attend(clip, values_t, query, j):
        scores = dot(kv_vm[clip, :frame_count, columns(j)], query, NT)
        peak = jnp.max(scores, 0, keepdims=True)
        terms = jnp.exp(scores - peak)
        total = jnp.sum(terms, 0, keepdims=True)
        return dot(values_t, terms.astype(jnp.bfloat16), NN), peak, total

    def cross_pair(j, tick):
        values_t = kv_vm[0, :frame_count, columns(j + 6)].T
        mine = seg_ref[...] == 0
        for h in range(2):
            tick(h)
            rows = slice(h * 64, (h + 1) * 64)
            result, peak, total = attend(0, values_t[rows], one_head(row_query_ref[:, columns(j)], h), j)
            acc_ref[rows] = jnp.where(mine, result / total, 0.0)
            stat_ref[h:h + 1] = jnp.where(mine, peak, 0.0)
            stat_ref[2 + h:3 + h] = jnp.where(mine, total, 1.0)
        for clip in (1, 2):
            tick(clip + 1)
            values_t = kv_vm[clip, :frame_count, columns(j + 6)].T
            query_rows = jnp.where(
                group_ref[clip - 1:clip] == 0, row_query_ref[:128, columns(j)], row_query_ref[384:, columns(j)])
            result, peak, total = attend(clip, values_t, two_heads(query_rows), j)
            for h in range(2):
                rows, part = slice(h * 64, (h + 1) * 64), slice(h * 128, (h + 1) * 128)
                of_head = result[rows, part] / total[:, part]
                for spot in (0, 3):
                    cols = slice(spot * 128, (spot + 1) * 128)
                    mine = seg_ref[:, cols] == clip
                    acc_ref[rows, cols] = jnp.where(mine, of_head, acc_ref[rows, cols])
                    stat_ref[h:h + 1, cols] = jnp.where(mine, peak[:, part], stat_ref[h:h + 1, cols])
                    stat_ref[2 + h:3 + h, cols] = jnp.where(mine, total[:, part], stat_ref[2 + h:3 + h, cols])
        my_cols, mate_cols = columns(core, toks), columns(1 - core, toks)
        part_ref[j] = acc_ref[:, my_cols]
        part_stat_ref[j] = stat_ref[:, my_cols]
        give_ref[j] = acc_ref[:, mate_cols].astype(jnp.bfloat16)
        give_stat_ref[j] = stat_ref[:, mate_cols]

    loop_with(gather, 6, 48, 3, cross_pair, (0, 0.33, 0.66, 0.83))
    give_copy = to_mate(give_ref, take_ref, 2)
    give_copy.start()
    give_stat_copy = to_mate(give_stat_ref, take_stat_ref, 3)
    give_stat_copy.start()
    gather.run_until(1000)
    give_copy.wait()
    give_stat_copy.wait()

    def combine(j, carry):
        parts = []
        for h in range(2):
            rows = slice(h * 64, (h + 1) * 64)
            peak_a, peak_b = part_stat_ref[j, h:h + 1], take_stat_ref[j, h:h + 1]
            peak = jnp.maximum(peak_a, peak_b)
            share_a = part_stat_ref[j, 2 + h:3 + h] * jnp.exp(peak_a - peak)
            share_b = take_stat_ref[j, 2 + h:3 + h] * jnp.exp(peak_b - peak)
            total = share_a + share_b
            cross_lse_ref[j, h:h + 1] = peak + jnp.log(total)
            parts.append(part_ref[j, rows] * (share_a / total)
                         + take_ref[j, rows].astype(jnp.float32) * (share_b / total))
        mixed_ref[:, columns(j)] = jnp.concatenate(parts, 0).T
        return carry

    lax.fori_loop(0, 6, combine, 0)
    after_cross = after_self_ref[...] + dot(mixed_ref[...].astype(jnp.bfloat16), cqo_vm[:, width:], NN) + vec(11)
    after_cross_ref[...] = after_cross
    normed_three_ref[...] = norm_rows(after_cross, vec(4), vec(5)).astype(jnp.bfloat16)
    gather.run_until(1000)
    gather.need(4)
    gather.need(5)
    kv_store.wait()
    ranked_store.wait()
    gather.finish()


def fused_forward(lengths, x, vectors, up_bias, down_bias, self_w, cross_w, up_w, frames, down_w):
    toks, width = x.shape
    clips, count = frames.shape[:2]
    low, full = jnp.bfloat16, jnp.float32
    pairs = width // 128
    vmem, hbm = pl.BlockSpec(memory_space=pltpu.VMEM), pl.BlockSpec(memory_space=pl.ANY)
    shape = jax.ShapeDtypeStruct
    outs = [
        (hbm, shape((32, 16, 128), low)), (hbm, shape((width, 2 * width), low)), (hbm, shape((width, 4 * width), low)),
        (hbm, shape((width, 2 * width), low)), (hbm, shape((width, 4 * width), low)),
        (hbm, shape((4 * width, width), low)),
        (hbm, shape((clips, width, 2 * width), low)),
        (vmem, shape((16, width), full)), (vmem, shape((toks, width), low)), (vmem, shape((toks, width), low)),
        (vmem, shape((2 * toks, 2 * width), low)), (vmem, shape((toks, width), full)),
        (vmem, shape((pairs, 2, toks), full)), (vmem, shape((toks, width), full)), (vmem, shape((toks, width), low)),
        (vmem, shape((2 * toks, width), low)), (vmem, shape((pairs, 2, toks), full)), (vmem, shape((toks, width), full)),
        (vmem, shape((toks, width), full)), (vmem, shape((toks, width), low)),
        (vmem, shape((2 * toks, toks), full)), (vmem, shape((1, 2 * toks), jnp.int32)), (vmem, shape((8, width), jnp.int32)),
        (hbm, shape(frames.shape, low)), (vmem, shape((1, 4 * width), full)),
    ]
    return pl.pallas_call(
        forward_kernel,
        in_specs=[pl.BlockSpec(memory_space=pltpu.SMEM)] + [vmem] * 7 + [hbm] * 2,
        out_specs=tuple(spec for spec, _ in outs),
        out_shape=tuple(s for _, s in outs),
        scratch_shapes=[
            pltpu.VMEM(frames.shape, low), pltpu.VMEM(frames.shape, low), pltpu.VMEM((16, 128), full),
            pltpu.VMEM((16, 128), low), pltpu.VMEM((2, 24, 2 * width), low), pltpu.VMEM((2, 24, width), low), pltpu.VMEM((2, 48, 2 * width), low),
            pltpu.VMEM((2, 48, width), low), pltpu.VMEM((32, 16, 128), low),
            pltpu.VMEM((width, 2 * width), low), pltpu.VMEM((width, 4 * width), low), pltpu.VMEM((width, 2 * width), low),
            pltpu.VMEM((clips, width, 2 * width), low), pltpu.VMEM((128, 2 * toks), full), pltpu.VMEM((4, 2 * toks), full),
            pltpu.VMEM((pairs, 128, toks), full), pltpu.VMEM((pairs, 4, toks), full),
            pltpu.VMEM((pairs, 128, toks), low), pltpu.VMEM((pairs, 4, toks), full),
            pltpu.VMEM((pairs, 128, toks), low), pltpu.VMEM((pairs, 4, toks), full),
            pltpu.SemaphoreType.DMA((400,)), pltpu.SemaphoreType.DMA((6, 32)), pltpu.SemaphoreType.DMA((6,)),
            pltpu.SemaphoreType.DMA((2, 5)), pltpu.SemaphoreType.DMA((2, 4)), pltpu.SemaphoreType.DMA((2,)),
            pltpu.SemaphoreType.DMA((1,)),
        ],
        compiler_params=pltpu.CompilerParams(collective_id=0, has_side_effects=True, vmem_limit_bytes=60 * 2**20),
        name="fused_forward",
    )(lengths, x, vectors, up_bias, down_bias, self_w, cross_w, up_w, frames, down_w)


class Scatter:
    def __init__(self, me, grads, outs, buffers, sems, times, after):
        self.me, self.grads, self.outs, self.buffers = me, grads, outs, buffers
        self.send_sem, self.own_sem, self.pair_sem, self.plane_sem, self.line_sem, self.free_sem = sems
        self.sends = {m: [] for m in range(len(grads))}
        self.count = 0
        self.order = me.line + [me.z]
        self.tasks = []
        for m, times_of in enumerate(times):
            for time, acts in zip(times_of, self.steps(m)):
                self.tasks.append((time, m, acts))
        for late, early in after.items():
            self.tasks = [
                (time, m, ([self.wait_free] if m == late and time == times[late][0] else []) + acts
                 + ([functools.partial(self.give_free, early)] if m == early and time == times[early][-1] else []))
                for time, m, acts in self.tasks
            ]
        self.tasks.sort(key=lambda entry: entry[:2])

    def give_free(self, m):
        for copy in self.sends.pop(m):
            copy.wait_send()
        for target in self.me.peers:
            pl.semaphore_signal(self.free_sem, inc=1, device_id=target, device_id_type=MESH)

    def wait_free(self):
        pl.semaphore_wait(self.free_sem, len(self.me.peers))

    def sender(self, m, src, dst, sem, target):
        copy = pltpu.make_async_remote_copy(
            src_ref=src, dst_ref=dst, send_sem=self.send_sem.at[self.count], recv_sem=sem, device_id=target,
            device_id_type=MESH)
        self.count += 1
        self.sends[m].append(copy)
        return copy.start

    def arrival(self, dst, sem):
        return pltpu.make_async_remote_copy(
            src_ref=dst, dst_ref=dst, send_sem=self.send_sem.at[0], recv_sem=sem, device_id=self.me.mate,
            device_id_type=MESH).wait_recv

    def steps(self, m):
        me, order = self.me, self.order
        grad, out = self.grads[m], self.outs[m]
        own, pair, plane_a, plane_b, plane_c, line = self.buffers[m]
        own_sem, pair_sem, plane_sem, line_sem = self.own_sem, self.pair_sem, self.plane_sem, self.line_sem

        def adder(dst, *others):
            def act():
                total = dst[...].astype(jnp.float32)
                for other in others:
                    total = total + other[...].astype(jnp.float32)
                dst[...] = total.astype(dst.dtype)
            return act

        loads = [
            pltpu.make_async_copy(grad.at[:, p, me.core], own, own_sem.at[m, k])
            for k, p in enumerate((me.p_diag, me.p_second, me.p_first, me.p))
        ]
        begin = [loads[0].start]
        for p in (me.p_diag, me.p_first, me.p_second, me.p):
            begin.append(self.sender(m, grad.at[:, p, 1 - me.core], pair.at[:, p], pair_sem.at[m, p], me.mate))
        diag, second, first, last = (
            [loads[k].wait, self.arrival(pair.at[:, p], pair_sem.at[m, p])]
            for k, p in enumerate((me.p_diag, me.p_second, me.p_first, me.p))
        )
        for z in order:
            diag += [adder(pair.at[z, me.p_diag], own.at[z]),
                     self.sender(m, pair.at[z, me.p_diag], plane_a.at[z], plane_sem.at[m, 0, z], me.second)]
            second += [adder(pair.at[z, me.p_second], own.at[z]),
                       self.sender(m, pair.at[z, me.p_second], plane_c.at[z], plane_sem.at[m, 2, z], me.second)]
            first += [self.arrival(plane_a.at[z], plane_sem.at[m, 0, z]),
                      adder(pair.at[z, me.p_first], own.at[z], plane_a.at[z]),
                      self.sender(m, pair.at[z, me.p_first], plane_b.at[z], plane_sem.at[m, 1, z], me.first)]
        diag.append(loads[1].start)
        second.append(loads[2].start)
        first.append(loads[3].start)
        for z in me.line:
            last += [self.arrival(plane_b.at[z], plane_sem.at[m, 1, z]),
                     self.arrival(plane_c.at[z], plane_sem.at[m, 2, z]),
                     adder(pair.at[z, me.p], own.at[z], plane_b.at[z], plane_c.at[z]),
                     self.sender(m, pair.at[z, me.p], line.at[me.z], line_sem.at[m, me.z], me.on_line(z))]

        def total():
            part = own[me.z].astype(jnp.float32) + pair[me.z, me.p].astype(jnp.float32)
            out[...] = part + plane_b[me.z].astype(jnp.float32) + plane_c[me.z].astype(jnp.float32)

        def from_line(source):
            def act():
                out[...] += line[source].astype(jnp.float32)
            return act

        final = [self.arrival(plane_b.at[me.z], plane_sem.at[m, 1, me.z]),
                 self.arrival(plane_c.at[me.z], plane_sem.at[m, 2, me.z]), total]
        for source in me.line[::-1]:
            final += [self.arrival(line.at[source], line_sem.at[m, source]), from_line(source)]
        return [begin, diag, second, first, last, final]

    def run(self, entry):
        for act in entry[2]:
            act()

    def run_until(self, time):
        while self.tasks and self.tasks[0][0] <= time:
            self.run(self.tasks.pop(0))

    def take_until(self, time):
        taken = []
        while self.tasks and self.tasks[0][0] <= time:
            taken.append(self.tasks.pop(0))
        return taken

    def finish(self):
        self.run_until(10**6)
        for copies in self.sends.values():
            for copy in copies:
                copy.wait_send()


def scatter_buffers(grad):
    leads = ((4,), (4, 4), (4,), (4,), (4,), (4,))
    return [pltpu.VMEM(lead + grad.shape[1:], grad.dtype) for lead in leads]


def scatter_sems(count):
    dma = pltpu.SemaphoreType.DMA
    return [dma((20 * count,)), dma((count, 4)), dma((count, 4)), dma((count, 3, 4)), dma((count, 4)),
            pltpu.SemaphoreType.REGULAR]


def scatter_view(grad):
    return grad.reshape((4, 4, 2) + grad.shape[1:])


BACK_TIMES = (
    (0, 6.5, 8, 18, 30, 43),
    (1, 17, 19, 32, 43.5, 60),
    (45, 53, 54, 63, 70, 80),
    (66, 71, 72, 79, 86, 95),
    (70, 73, 74, 82, 89, 98),
)


def norm_rows_back(values, gain, grad):
    average = jnp.mean(values, -1, keepdims=True)
    centred = values - average
    scale = lax.rsqrt(jnp.mean(centred * centred, -1, keepdims=True) + 1e-05)
    normed = centred * scale
    inner = grad * gain
    mean_inner = jnp.mean(inner, -1, keepdims=True)
    mean_both = jnp.mean(inner * normed, -1, keepdims=True)
    result = scale * (inner - mean_inner - normed * mean_both)
    return result, jnp.sum(grad * normed, 0, keepdims=True), jnp.sum(grad, 0, keepdims=True)


def backward_kernel(*refs):
    (info_ref, x_ref, bias_ref, seg_ref, vec_ref, gac_ref, mixed_ref, cross_lse_ref, row_query_ref, after_self_ref,
     attended_ref, self_lse_ref, query_ref, kv_row_ref, normed_one_ref, normed_two_ref, rows_ref, up_bias_ref, cqo_hbm,
     ckv_hbm, self_hbm, kv_hbm, frames_hbm, up_hbm, down_hbm) = refs[:25]
    (input_grad_ref, encoder_hbm, up_out, down_out, cross_out, self_out, up_bias_out, down_bias_out, vectors_out,
     dkv_hbm, cross_hbm, self_grad_hbm) = refs[25:37]
    cross_sum, small_out, *scratch = refs[37:]
    up_buffers, down_buffers, cross_buffers, small_buffers = (scratch[k * 6:(k + 1) * 6] for k in range(4))
    sems, scratch = scratch[24:30], scratch[30:]
    (cross_vm, kv_vm, frame_ref, turned_ref, tile_ref, stage_ref, small_ref, row_grad_ref, row_stat_ref, acc_ref,
     own_ref, give_ref, take_ref, take_query_ref, cq_ref, qkv_ref, vec_grad_ref, load_sem, mate_sems, tile_sem,
     stage_sem, frame_sem) = scratch
    group_ref = info_ref.at[:, pl.ds(0, 128)]
    me = Place()
    core = me.core
    toks, width = x_ref.shape
    frames = frames_hbm.shape[1]
    clips = kv_hbm.shape[0]
    low, full = jnp.bfloat16, jnp.float32
    halves = [pltpu.make_async_copy(cqo_hbm.at[:, pl.ds(k * width, width)], cross_vm.at[k], load_sem.at[k])
              for k in range(2)]
    kv_load = pltpu.make_async_copy(kv_hbm, kv_vm, load_sem.at[2])
    frame_loads = [
        pltpu.make_async_copy(
            frames_hbm.at[clip], frame_ref.at[:, pl.ds(clip % 2 * width, width)], frame_sem.at[clip % 2])
        for clip in range(clips)
    ]
    for copy in [halves[1], kv_load, halves[0]] + frame_loads[:2]:
        copy.start()
    me.greet()
    self_buffers = [
        ref.at[(slice(None),) * (len(ref.shape) - 1) + (pl.ds(0, 3 * width),)] for ref in up_buffers
    ]
    scatter = Scatter(
        me, (up_hbm, down_hbm, cross_hbm, self_grad_hbm, small_ref), (up_out, down_out, cross_sum, self_out.at[:, pl.ds(0, 3 * width)], small_out),
        (up_buffers, down_buffers, cross_buffers, self_buffers, small_buffers), sems, BACK_TIMES, {3: 0})
    scatter.run_until(1)

    def to_mate(src, dst, k):
        return pltpu.make_async_remote_copy(
            src_ref=src, dst_ref=dst, send_sem=mate_sems.at[0, k], recv_sem=mate_sems.at[1, k], device_id=me.mate,
            device_id_type=MESH)

    my_rows = pl.ds(pl.multiple_of(core * toks, toks), toks)
    my_cols = columns(core, toks)

    def head_rows(product, store):
        turned = product.T
        for h in range(2):
            store(h, jnp.sum(turned[h * 64:(h + 1) * 64], 0, keepdims=True))

    def tile_store(grad_hbm, slot, t):
        return pltpu.make_async_copy(tile_ref.at[slot], grad_hbm.at[:, :, :, :, columns(t, 256)], tile_sem.at[slot])

    def weight_tiles(grad_hbm, first_tile, count, tile, before=None):
        def turn(t, carry):
            slot = t % 2

            @pl.when(t >= 2)
            def _():
                tile_store(grad_hbm, slot, first_tile + t - 2).wait()

            value = tile(columns(t, 256))
            tile_ref[slot] = value.reshape(4, 4, 2, width // 32, 256).astype(low)
            tile_store(grad_hbm, slot, first_tile + t).start()
            return carry

        lax.fori_loop(0, count, turn, 0)
        for t in range(max(0, count - 2), count):
            tile_store(grad_hbm, t % 2, first_tile + t).wait()

    def product_tiles(grad_hbm, first_tile, left, right_ref):
        turned = left.T
        weight_tiles(grad_hbm, first_tile, right_ref.shape[1] // 256, lambda cols: dot(turned, right_ref[:, cols], NN))

    halves[1].wait()
    grad_cross = gac_ref[...].astype(low)
    grad_mixed = dot(grad_cross, cross_vm[1], NT).astype(low)
    row_grad_ref[my_rows] = grad_mixed
    grad_copy = to_mate(row_grad_ref.at[my_rows], row_grad_ref.at[my_rows], 0)
    grad_copy.start()
    for j in range(6):
        cols = slice(j * 128, (j + 1) * 128)
        product = grad_mixed[:, cols].astype(full) * mixed_ref[:, cols]
        row_stat_ref[j, 0:2, my_cols] = cross_lse_ref[j]

        def keep(h, row, j=j):
            row_stat_ref[j, 2 + h:3 + h, my_cols] = row

        head_rows(product, keep)
    stat_copy = to_mate(row_stat_ref.at[:, :, my_cols], row_stat_ref.at[:, :, my_cols], 1)
    stat_copy.start()
    cq_ref[...] = grad_cross
    product_tiles(cross_hbm, 9, mixed_ref[...].astype(low), cq_ref)

    def turn_frames(clip):
        frame_loads[clip].wait()
        turned_ref[clip] = frame_ref[:, clip % 2 * width:(clip % 2 + 1) * width].T

    turn_frames(0)
    frame_loads[2].start()
    turn_frames(1)
    kv_load.wait()
    scatter.run_until(5)
    grad_copy.wait()
    stat_copy.wait()

    def cross_pair(j, tick):
        def back(clip, keys_t, query, grad, lse, inner):
            weights = jnp.exp(dot(kv_vm[clip, :frames, columns(j)], query, NT) - lse)
            grad_v = dot(weights.astype(low), grad, NN)
            grad_s = (weights * (dot(kv_vm[clip, :frames, columns(j + 6)], grad, NT) - inner)).astype(low)
            return dot(keys_t, grad_s, NN), dot(grad_s, query, NN), grad_v

        keys_t = kv_vm[0, :frames, columns(j)].T
        mine = seg_ref[...] == 0
        grad_k = grad_v = None
        for h in range(2):
            tick(h)
            query, grad = one_head(row_query_ref[:, columns(j)], h), one_head(row_grad_ref[:, columns(j)], h)
            rows = slice(h * 64, (h + 1) * 64)
            acc_ref[rows], part_k, part_v = back(
                0, keys_t[rows], query, grad, jnp.where(mine, row_stat_ref[j, h:h + 1], 1e30),
                row_stat_ref[j, 2 + h:3 + h])
            grad_k = part_k if grad_k is None else grad_k + part_k
            grad_v = part_v if grad_v is None else grad_v + part_v
        kv_vm[0, :frames, columns(j)] = grad_k.astype(low)
        kv_vm[0, :frames, columns(j + 6)] = grad_v.astype(low)
        for clip in (1, 2):
            tick(clip + 1)
            in_first = group_ref[clip - 1:clip] == 0

            def chosen(ref):
                return two_heads(jnp.where(in_first, ref[:128, columns(j)], ref[384:, columns(j)]))

            def chosen_row(row):
                return jnp.where(in_first, row_stat_ref[j, row:row + 1, :128], row_stat_ref[j, row:row + 1, 384:])

            mine = jnp.where(in_first, seg_ref[:, :128], seg_ref[:, 384:]) == clip
            lse = jnp.concatenate([jnp.where(mine, chosen_row(h), 1e30) for h in range(2)], 1)
            inner = jnp.concatenate([chosen_row(2 + h) for h in range(2)], 1)
            grad_q, grad_k, grad_v = back(
                clip, kv_vm[clip, :frames, columns(j)].T, chosen(row_query_ref), chosen(row_grad_ref), lse, inner)
            for h in range(2):
                rows, part = slice(h * 64, (h + 1) * 64), slice(h * 128, (h + 1) * 128)
                for spot in (0, 3):
                    cols = slice(spot * 128, (spot + 1) * 128)
                    acc_ref[rows, cols] += jnp.where(in_first == (spot == 0), grad_q[rows, part], 0.0)
            kv_vm[clip, :frames, columns(j)] = grad_k.astype(low)
            kv_vm[clip, :frames, columns(j + 6)] = grad_v.astype(low)
        own_ref[:, columns(j)] = (acc_ref[:, my_cols] * 0.125).T
        give_ref[:, columns(j)] = (acc_ref[:, columns(1 - core, toks)] * 0.125).T.astype(low)

    loop_with(scatter, 6, 6, 4, cross_pair, (0, 0.33, 0.66, 0.83))
    query_copy = to_mate(give_ref.at[:, pl.ds(0, width)], take_query_ref, 2)
    query_copy.start()
    dkv_store = pltpu.make_async_copy(kv_vm, dkv_hbm, load_sem.at[2])
    dkv_store.start()
    vec_grad_ref[...] = rows_ref[...]
    vec_grad_ref[10:11] = sum(
        jnp.sum(kv_vm[clip, :frames, width:].astype(full), 0, keepdims=True) for clip in range(clips))
    turn_frames(2)
    scatter.run_until(37)

    def frames_tile(cols):
        total = dot(turned_ref[0], kv_vm[0, :frames, cols], NN)
        for clip in range(1, clips):
            total = total + dot(turned_ref[clip], kv_vm[clip, :frames, cols], NN)
        return total

    weight_tiles(cross_hbm, 3, 6, frames_tile)
    halves[0].wait()
    query_copy.wait()
    grad_query = (own_ref[:, :width] + take_query_ref[...].astype(full)).astype(low)
    cq_ref[...] = grad_query
    product_tiles(cross_hbm, 0, normed_two_ref[...], cq_ref)
    dkv_store.wait()
    self_loads = [
        pltpu.make_async_copy(
            self_hbm.at[:, pl.ds(k * 2 * width, 2 * width)], kv_vm.at[k], load_sem.at[2 + k]) for k in range(2)
    ]
    for copy in self_loads:
        copy.start()
    vec_grad_ref[9:10] = jnp.sum(grad_query.astype(full), 0, keepdims=True)
    grad_part, gain, shift = norm_rows_back(after_self_ref[...], vec_ref[2:3], dot(grad_query, cross_vm[0], NT))
    vec_grad_ref[2:3] = gain
    vec_grad_ref[3:4] = shift
    grad_after_self = gac_ref[...] + grad_part
    input_grad_ref[...] = grad_after_self
    grad_low = grad_after_self.astype(low)
    vec_grad_ref[8:9] = jnp.sum(grad_low.astype(full), 0, keepdims=True)
    cq_ref[...] = grad_low
    product_tiles(cross_hbm, 12, attended_ref[...].astype(low), cq_ref)
    scatter.run_until(46)
    for copy in self_loads:
        copy.wait()
    grad_attended = dot(grad_low, kv_vm[1, :width, width:], NT).astype(low)
    row_grad_ref[:toks] = grad_attended
    for j in range(6):
        cols = slice(j * 128, (j + 1) * 128)

        def keep_self(h, row, j=j):
            row_stat_ref[j, h:h + 1, :toks] = row

        head_rows(grad_attended[:, cols].astype(full) * attended_ref[:, cols], keep_self)

    def self_pair(j, tick):
        tick(0)
        cols, value_cols = columns(j), columns(j + 6)
        keys, values = kv_row_ref[:, cols], kv_row_ref[:, value_cols]
        keys_t = keys.T
        grad_k = grad_v = None
        parts = []
        for h in range(2):
            query, grad = one_head(query_ref[:, cols], h), one_head(row_grad_ref[:toks, cols], h)
            weights = jnp.exp(dot(keys, query, NT) + bias_ref[...] - self_lse_ref[j, h:h + 1])
            part = dot(weights.astype(low), grad, NN)
            grad_v = part if grad_v is None else grad_v + part
            inner = row_stat_ref[j, h:h + 1, :toks]
            grad_s = (weights * (dot(values, grad, NT) - inner)).astype(low)
            part = dot(grad_s, query, NN)
            grad_k = part if grad_k is None else grad_k + part
            parts.append(dot(keys_t[h * 64:(h + 1) * 64], grad_s, NN))
        qkv_ref[:, cols] = (jnp.concatenate(parts, 0) * 0.125).T.astype(low)
        own_ref[:, cols] = grad_k[toks:]
        own_ref[:, value_cols] = grad_v[toks:]
        give_ref[:, cols] = grad_k[:toks].astype(low)
        give_ref[:, value_cols] = grad_v[:toks].astype(low)

    loop_with(scatter, 6, 52, 1.4, self_pair)
    row_copy = to_mate(give_ref, take_ref, 3)
    row_copy.start()
    scatter.run_until(62)
    row_copy.wait()
    qkv_ref[:, width:] = (own_ref[...] + take_ref[...].astype(full)).astype(low)
    product_tiles(self_grad_hbm, 0, normed_one_ref[...], qkv_ref)
    scatter.run_until(66)
    sums = jnp.sum(qkv_ref[...].astype(full), 0, keepdims=True)
    vec_grad_ref[6:7] = sums[:, :width]
    vec_grad_ref[7:8] = sums[:, 2 * width:]
    grad_normed = dot(qkv_ref[:, :2 * width], kv_vm[0, :width], NT) + dot(
        qkv_ref[:, 2 * width:], kv_vm[1, :width, :width], NT)
    grad_part, gain, shift = norm_rows_back(x_ref[...].astype(full), vec_ref[0:1], grad_normed)
    vec_grad_ref[0:1] = gain
    vec_grad_ref[1:2] = shift
    input_grad_ref[...] += grad_part
    kv_load = pltpu.make_async_copy(dkv_hbm, kv_vm, load_sem.at[2])
    kv_load.start()
    for k in range(2):
        pltpu.make_async_copy(ckv_hbm.at[:, pl.ds(k * width, width)], cross_vm.at[k], load_sem.at[k]).start()
    small_ref[...] = jnp.zeros_like(small_ref)
    rows = vec_grad_ref[...]
    for d in range(32):
        place = (d // 8, d // 2 % 4, d % 2)
        turned_rows = rows if d == 0 else pltpu.roll(rows, width - d * 24, 1)
        small_ref[place] = turned_rows[:, :128]
        bias_row = up_bias_ref[...] if d == 0 else pltpu.roll(up_bias_ref[...], up_bias_ref.shape[1] * (32 - d) // 32, 1)
        small_ref[place + (slice(13, 14),)] = bias_row[:, :128]
    scatter.run_until(70)
    for k in range(2):
        pltpu.make_async_copy(ckv_hbm.at[:, pl.ds(k * width, width)], cross_vm.at[k], load_sem.at[k]).wait()
    kv_load.wait()
    blocks = width // 128

    def encoder_store(clip):
        rows = pl.ds(clip * frames * blocks, frames * blocks)
        return pltpu.make_async_copy(stage_ref, encoder_hbm.at[rows], stage_sem.at[0])

    for clip in range(clips):
        place = info_ref[2 + clip:3 + clip]
        for part in (slice(0, width), slice(width, 2 * width)):
            frame_ref[:, part] = jnp.where(
                place == 0, kv_vm[0, :frames, part],
                jnp.where(place == 1, kv_vm[1, :frames, part], kv_vm[2, :frames, part]))

        def encoder_tile(t, tick, clip=clip):
            tick(0)
            rows = columns(t, 256)
            value = dot(frame_ref[:, :width], cross_vm[0, rows], NT) + dot(frame_ref[:, width:], cross_vm[1, rows], NT)
            if clip > 0:
                pl.when(t == 0)(encoder_store(clip - 1).wait)
            for k in range(2):
                stage_ref[pl.ds(2 * t + k, frames, stride=blocks), 0] = value[:, k * 128:(k + 1) * 128]

        loop_with(scatter, width // 256, 71 + 3 * clip, 1, encoder_tile)
        encoder_store(clip).start()
    encoder_store(clips - 1).wait()
    scatter.finish()
    cross_out[...] = cross_sum[:, :4 * width]
    self_out[:, 3 * width:] = cross_sum[:, 4 * width:]
    up_bias_out[...] = small_out[13:14, :up_bias_out.shape[1]]
    down_bias_out[...] = small_out[12:13, :down_bias_out.shape[1]]
    vectors_out[...] = small_out[:12, :vectors_out.shape[1]]


def fused_backward(info, x, bias, seg, vec, gac, mixed, cross_lse, row_query, after_self, attended, self_lse, query,
                   kv_row, normed_one, normed_two, rows, up_bias, cqo_full, ckv_full, self_full, kv, frames, grad_up,
                   grad_down):
    toks, width = x.shape
    clips, count = frames.shape[:2]
    low, full = jnp.bfloat16, jnp.float32
    pairs = width // 128
    vmem, hbm = pl.BlockSpec(memory_space=pltpu.VMEM), pl.BlockSpec(memory_space=pl.ANY)
    shape = jax.ShapeDtypeStruct
    small = shape((32, 16, 128), full)
    places = (4, 4, 2, width // 32)
    cross = shape((32, width // 32, 5 * width), low)
    outs = [
        (vmem, shape((toks, width), full)), (hbm, shape((clips * count * width // 128, 1, 128), full)), (vmem, shape(grad_up.shape[1:], full)),
        (vmem, shape(grad_down.shape[1:], full)), (vmem, shape((width // 32, 4 * width), full)),
        (vmem, shape((width // 32, 4 * width), full)), (vmem, shape((1, up_bias.shape[1] // 32), full)),
        (vmem, shape((1, width // 32), full)), (vmem, shape((12, width // 32), full)), (hbm, shape(kv.shape, low)),
        (hbm, shape(places + (5 * width,), low)), (hbm, shape(places + (3 * width,), low)),
    ]
    return pl.pallas_call(
        backward_kernel,
        in_specs=[vmem] * 18 + [hbm] * 7,
        out_specs=tuple(spec for spec, _ in outs),
        out_shape=tuple(s for _, s in outs),
        scratch_shapes=[pltpu.VMEM(cross.shape[1:], full), pltpu.VMEM(small.shape[1:], full)]
        + scatter_buffers(grad_up) + scatter_buffers(grad_down) + scatter_buffers(cross)
        + scatter_buffers(small) + scatter_sems(5) + [
            pltpu.VMEM((2, width, width), low), pltpu.VMEM((clips, width, 2 * width), low),
            pltpu.VMEM((count, 2 * width), low), pltpu.VMEM((clips, width, count), low),
            pltpu.VMEM((2,) + places + (256,), low), pltpu.VMEM((count * width // 128, 1, 128), full),
            pltpu.VMEM((4, 4, 2, 16, 128), full), pltpu.VMEM((2 * toks, width), low),
            pltpu.VMEM((pairs, 4, 2 * toks), full), pltpu.VMEM((128, 2 * toks), full),
            pltpu.VMEM((toks, 2 * width), full), pltpu.VMEM((toks, 2 * width), low),
            pltpu.VMEM((toks, 2 * width), low), pltpu.VMEM((toks, width), low), pltpu.VMEM((toks, width), low),
            pltpu.VMEM((toks, 3 * width), low), pltpu.VMEM((16, width), full), pltpu.SemaphoreType.DMA((4,)),
            pltpu.SemaphoreType.DMA((2, 4)), pltpu.SemaphoreType.DMA((2,)), pltpu.SemaphoreType.DMA((1,)),
            pltpu.SemaphoreType.DMA((2,)),
        ],
        compiler_params=pltpu.CompilerParams(collective_id=2, has_side_effects=True, vmem_limit_bytes=63 * 2**20),
        name="fused_backward",
    )(info, x, bias, seg, vec, gac, mixed, cross_lse, row_query, after_self, attended, self_lse, query, kv_row,
      normed_one, normed_two, rows, up_bias, cqo_full, ckv_full, self_full, kv, frames, scatter_view(grad_up),
      scatter_view(grad_down))


def ffn_kernel(normed_ref, grad_ref, after_ref, vec_ref, up_ref, bias_ref, down_ref, out_ref, back_ref, grad_up_ref,
               grad_down_ref, grad_bias_ref, rows_ref, turned_ref, sum_ref, back_sum_ref):
    t = pl.program_id(0)

    @pl.when(t == 0)
    def _():
        turned_ref[...] = normed_ref[...].T
        sum_ref[...] = jnp.zeros_like(sum_ref)
        back_sum_ref[...] = jnp.zeros_like(back_sum_ref)

    grad = grad_ref[...]
    pre = dot(normed_ref[...], up_ref[...], NN) + bias_ref[...]
    below = 0.5 * (1.0 + lax.erf(pre * 0.7071067811865476))
    activated = (pre * below).astype(jnp.bfloat16)
    sum_ref[...] += dot(activated, down_ref[...], NN)
    grad_act = dot(grad, down_ref[...], NT).astype(jnp.bfloat16).astype(jnp.float32)
    density = jnp.exp(-0.5 * pre * pre) * 0.3989422804014327
    grad_pre = (grad_act * (below + pre * density)).astype(jnp.bfloat16)
    back_sum_ref[...] += dot(grad_pre, up_ref[...], NT)
    grad_up_ref[...] = dot(turned_ref[...], grad_pre, NN).astype(jnp.bfloat16)
    grad_down_ref[...] = dot(activated.T, grad, NN).astype(jnp.bfloat16)
    grad_bias_ref[...] = jnp.sum(grad_pre.astype(jnp.float32), 0, keepdims=True)

    @pl.when(t == pl.num_programs(0) - 1)
    def _():
        out_ref[...] = (after_ref[...] + sum_ref[...] + vec_ref[12:13]).astype(jnp.bfloat16)
        grad_rows = grad_ref[...].astype(jnp.float32)
        part, gain, shift = norm_rows_back(after_ref[...], vec_ref[4:5], back_sum_ref[...])
        back = grad_rows + part
        back_ref[...] = back
        rows_ref[...] = jnp.zeros_like(rows_ref)
        rows_ref[4:5] = gain
        rows_ref[5:6] = shift
        rows_ref[11:12] = jnp.sum(back.astype(jnp.bfloat16).astype(jnp.float32), 0, keepdims=True)
        rows_ref[12:13] = jnp.sum(grad_rows, 0, keepdims=True)


def ffn(normed, grad, after, vec, up_full, bias, down_full):
    toks, width = normed.shape
    hidden = up_full.shape[1]
    size = 768
    low, full = jnp.bfloat16, jnp.float32
    shape = jax.ShapeDtypeStruct
    rows = pl.BlockSpec((toks, width), lambda t: (0, 0))
    vecs = pl.BlockSpec((16, width), lambda t: (0, 0))
    up_spec = pl.BlockSpec((width, size), lambda t: (0, t))
    down_spec = pl.BlockSpec((size, width), lambda t: (t, 0))
    bias_spec = pl.BlockSpec((1, size), lambda t: (0, t))
    return pl.pallas_call(
        ffn_kernel,
        grid=(hidden // size,),
        in_specs=[rows, rows, rows, vecs, up_spec, bias_spec, down_spec],
        out_specs=[rows, rows, up_spec, down_spec, bias_spec, vecs],
        out_shape=[
            shape((toks, width), low), shape((toks, width), full), shape(up_full.shape, low),
            shape(down_full.shape, low), shape((1, hidden), full), shape((16, width), full),
        ],
        scratch_shapes=[pltpu.VMEM((width, toks), low), pltpu.VMEM((toks, width), full), pltpu.VMEM((toks, width), full)],
        compiler_params=pltpu.CompilerParams(vmem_limit_bytes=63 * 2**20),
        name="ffn",
    )(normed, grad, after, vec, up_full, bias, down_full)


def place_clips_kernel(order, in_ref, out_ref):
    frames, width = in_ref.shape[1:]
    blocks = width // 128
    for k in range(blocks):
        out_ref[pl.ds(k, frames, stride=blocks), 0] = in_ref[0, :, k * 128:(k + 1) * 128]


def place_clips(order, values):
    clips, frames, width = values.shape
    rows = frames * width // 128
    flat = pl.pallas_call(
        place_clips_kernel,
        grid_spec=pltpu.PrefetchScalarGridSpec(
            num_scalar_prefetch=1,
            grid=(clips,),
            in_specs=[pl.BlockSpec((1, frames, width), lambda k, order: (k, 0, 0))],
            out_specs=pl.BlockSpec((rows, 1, 128), lambda k, order: (order[k], 0, 0)),
        ),
        out_shape=jax.ShapeDtypeStruct((clips * rows, 1, 128), values.dtype),
        compiler_params=pltpu.CompilerParams(vmem_limit_bytes=48 * 2**20),
        name="place_clips",
    )(order, values)
    return flat.reshape(1, clips, frames, width)


def from_behind(value, axis, steps):
    count = lax.axis_size(axis)
    leading, last = (max(0, -steps), min(count, count - steps))
    return lax.ppermute(value, axis, [(source, source + steps) for source in range(leading, last)])


def layer_norm(values, gain, shift):
    average = jnp.mean(values, -1, keepdims=True)
    centred = values - average
    spread = jnp.mean(centred * centred, -1, keepdims=True)
    return centred * lax.rsqrt(spread + 1e-05) * gain + shift


def matmul(left, right):
    return jnp.dot(left, right, preferred_element_type=jnp.float32)


def swap_halves(value):
    return lax.ppermute(value, "seq", [(0, 1), (1, 0)])


def seq_halves(value, axis):
    span = value.shape[axis] // 2
    half = lax.axis_index("seq")
    mine = lax.dynamic_slice_in_dim(value, half * span, span, axis)
    other = lax.dynamic_slice_in_dim(value, (1 - half) * span, span, axis)
    return mine, other


def seq_scatter(value):
    mine, other = seq_halves(value, 0)
    return mine + swap_halves(other.astype(jnp.bfloat16)).astype(value.dtype)


def per_head(values):
    rows = values.reshape(-1, values.shape[2]).T
    return jnp.repeat(rows, HEAD_DIM, axis=1)


def head_sums(values):
    sums = jnp.sum(values.reshape(values.shape[0], -1, HEAD_DIM), -1)
    return sums.T.reshape(-1, 2, values.shape[0])


def plain_forward(
    which, layer_input, frames, mask_bias, row_segment, weights
):
    self_full, cross_full, up_full, down_full, bias_full, out_bias_full, vectors = (
        lax.all_gather(part, ("dp", "seq"), axis=0, tiled=True) for part in weights
    )
    vec = jnp.pad(
        jnp.concatenate([vectors.T, out_bias_full[None]]).astype(jnp.float32), ((0, 3), (0, 0))
    )
    model_width = layer_input.shape[1]
    cross_in = [cross_full[:, k * model_width : (k + 1) * model_width] for k in range(4)]
    ckv_full = cross_full[:, model_width : 3 * model_width]
    cqo_full = jnp.concatenate([cross_in[0], cross_in[3]], 1)
    source = layer_input.astype(jnp.float32)
    normed_one = layer_norm(source, vec[0], vec[1]).astype(jnp.bfloat16)
    proj_bias = jnp.concatenate([vec[6], jnp.zeros_like(vec[6]), vec[7]])
    qkv_low = (matmul(normed_one, self_full[:, : 3 * model_width]) + proj_bias).astype(jnp.bfloat16)
    query = qkv_low[:, :model_width] * jnp.bfloat16(0.125)
    kv_own = qkv_low[:, model_width:]
    kv_row = jnp.concatenate([from_behind(kv_own, "seq", 1), kv_own])
    attended, self_lse = self_forward(query, kv_row, mask_bias)
    attended_low = attended.astype(jnp.bfloat16)
    after_self = source + matmul(attended_low, self_full[:, 3 * model_width :]) + vec[8]
    normed_two = layer_norm(after_self, vec[2], vec[3]).astype(jnp.bfloat16)
    cross_query = (matmul(normed_two, cross_in[0]) + vec[9]).astype(jnp.bfloat16)
    cross_key = jnp.einsum(
        "cfd,de->cfe", frames, cross_in[1], preferred_element_type=jnp.float32
    ).astype(jnp.bfloat16)
    cross_value = (
        jnp.einsum("cfd,de->cfe", frames, cross_in[2], preferred_element_type=jnp.float32)
        + vec[10]
    ).astype(jnp.bfloat16)
    row_query = lax.all_gather(cross_query * jnp.bfloat16(0.125), "seq", axis=0, tiled=True)
    cross_kv = jnp.concatenate([cross_key, cross_value], 2)
    part_mixed, part_stats = cross_forward(which, row_query, cross_kv, row_segment)
    mixed_mine, mixed_other = seq_halves(part_mixed, 0)
    stats_mine, stats_other = seq_halves(part_stats, 2)
    mixed_came = swap_halves(mixed_other.astype(jnp.bfloat16))
    stats_came = swap_halves(stats_other)
    peak = jnp.maximum(stats_mine[:, :2], stats_came[:, :2])
    share_mine = stats_mine[:, 2:] * jnp.exp(stats_mine[:, :2] - peak)
    share_came = stats_came[:, 2:] * jnp.exp(stats_came[:, :2] - peak)
    total = share_mine + share_came
    cross_lse = peak + jnp.log(total)
    mixed_full = mixed_mine * per_head(share_mine / total) + mixed_came.astype(
        jnp.float32
    ) * per_head(share_came / total)
    mixed = mixed_full.astype(jnp.bfloat16)
    after_cross = after_self + matmul(mixed, cross_in[3]) + vec[11]
    normed_three = layer_norm(after_cross, vec[4], vec[5]).astype(jnp.bfloat16)
    return (
        bias_full, ckv_full, self_full, cqo_full, up_full, down_full, cross_kv, vec, normed_one, query, kv_row, attended,
        self_lse, after_self, normed_two, row_query, cross_lse, mixed_full, after_cross, normed_three,
    )


def plain_backward(
    which, layer_input, mask_bias, row_segment, vec, grad_after_cross, mixed_full, cross_lse, row_query, after_self,
    attended, self_lse, query, kv_row, cqo_full, self_full, cross_kv
):
    tok_span, model_width = layer_input.shape
    source = layer_input.astype(jnp.float32)
    grad_cross_low = grad_after_cross.astype(jnp.bfloat16)
    grad_mixed = matmul(grad_cross_low, cqo_full[:, model_width:].T).astype(jnp.bfloat16)
    row_grad = lax.all_gather(grad_mixed, "seq", axis=0, tiled=True)
    cross_inner = head_sums(grad_mixed.astype(jnp.float32) * mixed_full)
    row_stats = lax.all_gather(jnp.stack([cross_lse, cross_inner]), "seq", axis=3, tiled=True)
    part_query, grad_key, grad_value = cross_backward(
        which, row_query, cross_kv, row_segment, row_stats[0], row_stats[1], row_grad
    )
    grad_query_sum = seq_scatter(part_query).astype(jnp.bfloat16)
    grad_cq_bias = jnp.sum(grad_query_sum, 0, dtype=jnp.float32)
    grad_normed_two = matmul(grad_query_sum, cqo_full[:, :model_width].T)
    grad_cv_bias = jnp.sum(grad_value, (0, 1), dtype=jnp.float32)
    _, norm_pull_two = jax.vjp(layer_norm, after_self, vec[2], vec[3])
    grad_part, grad_gain_two, grad_shift_two = norm_pull_two(grad_normed_two)
    grad_after_self = grad_after_cross + grad_part
    grad_self_low = grad_after_self.astype(jnp.bfloat16)
    grad_self_bias = jnp.sum(grad_self_low, 0, dtype=jnp.float32)
    grad_attended = matmul(grad_self_low, self_full[:, 3 * model_width :].T).astype(jnp.bfloat16)
    self_inner = head_sums(grad_attended.astype(jnp.float32) * attended)
    grad_query, grad_key_row, grad_value_row = self_backward(
        query, kv_row, mask_bias, self_lse, self_inner, grad_attended
    )
    grad_kv = jnp.concatenate([grad_key_row, grad_value_row], 1)
    back_kv = from_behind(grad_kv[:tok_span].astype(jnp.bfloat16), "seq", -1)
    grad_qkv_low = jnp.concatenate(
        [grad_query, grad_kv[tok_span:] + back_kv.astype(jnp.float32)], 1
    ).astype(jnp.bfloat16)
    grad_qkv_bias = jnp.sum(grad_qkv_low, 0, dtype=jnp.float32)
    grad_normed_one = matmul(grad_qkv_low, self_full[:, : 3 * model_width].T)
    _, norm_pull_one = jax.vjp(layer_norm, source, vec[0], vec[1])
    grad_part, grad_gain_one, grad_shift_one = norm_pull_one(grad_normed_one)
    input_grad = grad_after_self + grad_part
    nothing = jnp.zeros_like(grad_cq_bias)
    vec_grads = jnp.stack(
        [
            grad_gain_one,
            grad_shift_one,
            grad_gain_two,
            grad_shift_two,
            nothing,
            nothing,
            grad_qkv_bias[:model_width],
            grad_qkv_bias[2 * model_width :],
            grad_self_bias,
            grad_cq_bias,
            grad_cv_bias,
        ]
        + [nothing] * 5
    )
    return (
        input_grad, grad_query_sum, grad_self_low, grad_qkv_low, vec_grads,
        jnp.concatenate([grad_key, grad_value], 2),
    )


def plain_finish(
    normed_one, grad_qkv_low, attended_low, grad_self_low, normed_two, grad_query_sum, mixed, grad_cross_low, frames,
    cross_kv_grad, ckv_full
):
    width = normed_one.shape[1]
    grads_self = jnp.concatenate([matmul(normed_one.T, grad_qkv_low), matmul(attended_low.T, grad_self_low)], 1)
    grad_ckv = jnp.einsum("cfd,cfe->de", frames, cross_kv_grad, preferred_element_type=jnp.float32)
    grads_cross = jnp.concatenate(
        [matmul(normed_two.T, grad_query_sum), grad_ckv, matmul(mixed.T, grad_cross_low)], 1
    )
    encoder_grad = jnp.einsum(
        "cfe,de->cfd", cross_kv_grad, ckv_full, preferred_element_type=jnp.float32
    )
    return encoder_grad, (grads_self, grads_cross)


def fused_device(
    layer_input,
    encoder_states,
    clip_lengths,
    out_grad,
    self_weights,
    cross_weights,
    up_weights,
    down_weights,
    up_bias,
    down_bias,
    vectors,
):
    _, ckv_full, self_full, cqo_full, up_full, down_full, cross_kv, vec, normed_one, query, kv_row, attended, \
        self_lse, after_self, normed_two, row_query, cross_lse, mixed_full, after_cross, normed_three, mask_bias, \
        row_segment, info, frames, bias_row = fused_forward(
            clip_lengths, layer_input[0], vectors.T, up_bias[None], down_bias[None], self_weights, cross_weights, up_weights,
            encoder_states[0], down_weights,
        )
    layer_output, grad_after_cross, grad_up, grad_down, grad_up_bias, ffn_rows = ffn(
        normed_three, out_grad[0], after_cross, vec, up_full, bias_row, down_full
    )
    large = [g.reshape(32, -1, g.shape[1]) for g in (grad_up, grad_down)]
    input_grad, encoder_grad, up_share, down_share, cross_share, self_share, up_row, down_row, vector_rows, *_ = fused_backward(
        info, layer_input[0], mask_bias, row_segment, vec, grad_after_cross, mixed_full, cross_lse, row_query, after_self,
        attended, self_lse, query, kv_row, normed_one, normed_two, ffn_rows, grad_up_bias, cqo_full, ckv_full, self_full,
        cross_kv, frames, *large
    )
    return (
        layer_output[None], input_grad[None], encoder_grad.reshape((1,) + encoder_states.shape[1:]), self_share, cross_share,
        up_share, down_share, up_row[0], down_row[0], vector_rows.T,
    )


def plain_device(
    layer_input,
    encoder_states,
    clip_lengths,
    out_grad,
    self_weights,
    cross_weights,
    up_weights,
    down_weights,
    up_bias,
    down_bias,
    vectors,
):
    model_width = layer_input.shape[2]
    tok_span = layer_input.shape[1]
    seq_half = lax.axis_index("seq")
    position = seq_half * tok_span + jnp.arange(tok_span, dtype=jnp.int32)
    clip_ends = jnp.cumsum(clip_lengths[0])
    segment = jnp.sum((position[:, None] >= clip_ends[None, :]).astype(jnp.int32), 1)
    key_position = jnp.concatenate([position - tok_span, position])
    key_segment = jnp.sum((key_position[:, None] >= clip_ends[None, :]).astype(jnp.int32), 1)
    allowed = (
        (key_segment[:, None] == segment[None, :])
        & (key_position[:, None] <= position[None, :])
        & (key_position[:, None] >= 0)
    )
    mask_bias = jnp.where(allowed, 0.0, -1e30).astype(jnp.float32)
    row_position = jnp.arange(2 * tok_span, dtype=jnp.int32)
    row_segment = jnp.sum((row_position[:, None] >= clip_ends[None, :]).astype(jnp.int32), 1)[None]
    big = jnp.argmax(clip_lengths[0]).astype(jnp.int32)
    small_one = jnp.where(big == 0, 1, 0)
    small_two = jnp.where(big == 2, 1, 2)
    last_group = 2 * tok_span // 128 - 1
    order = jnp.stack([big, small_one, small_two]).astype(jnp.int32)
    row_segment = jnp.where(
        row_segment == order[0], 0, jnp.where(row_segment == order[1], 1, jnp.where(row_segment == order[2], 2, 3))
    )
    which = jnp.where(order[1:] < big, 0, last_group).astype(jnp.int32)

    frames = jnp.take(encoder_states[0], order, axis=0, mode="clip")
    (
        bias_full, ckv_full, self_full, cqo_full, up_full, down_full, cross_kv, vec, normed_one, query, kv_row, attended,
        self_lse, after_self, normed_two, row_query, cross_lse, mixed_full, after_cross, normed_three,
    ) = plain_forward(
        which, layer_input[0], frames, mask_bias, row_segment,
        (self_weights, cross_weights, up_weights, down_weights, up_bias, down_bias, vectors),
    )
    bias_full = bias_full.astype(jnp.float32)
    layer_output, grad_after_cross, grad_up, grad_down, grad_up_bias, ffn_rows = ffn(
        normed_three, out_grad[0], after_cross, vec, up_full, bias_full[None], down_full
    )
    operands = (
        layer_input[0], mask_bias, row_segment, vec, grad_after_cross, mixed_full, cross_lse, row_query, after_self,
        attended, self_lse, query, kv_row,
    )
    input_grad, grad_query_sum, grad_self_low, grad_qkv_low, vec_grads, cross_kv_grad = plain_backward(
        which, *operands, cqo_full, self_full, cross_kv
    )
    encoder_grad, large = plain_finish(
        normed_one, grad_qkv_low, attended.astype(jnp.bfloat16), grad_self_low, normed_two, grad_query_sum,
        mixed_full.astype(jnp.bfloat16), grad_after_cross.astype(jnp.bfloat16), frames, cross_kv_grad, ckv_full,
    )
    vector_grads = vec_grads + ffn_rows
    shares = tuple(
        lax.psum_scatter(part, ("dp", "seq"), scatter_dimension=0, tiled=True)
        for part in large
        + (grad_up.astype(jnp.float32), grad_down.astype(jnp.float32), grad_up_bias[0], vector_grads[12],
           vector_grads[:12].T)
    )
    return (layer_output[None], input_grad[None], place_clips(order, encoder_grad)) + shares


def solution(mesh):
    return jax.shard_map(
        fused_device if mesh.shape["dp"] == 16 else plain_device,
        mesh=mesh,
        in_specs=(
            P("dp", "seq", None),
            P("dp", None, "seq", None),
            P("dp", None),
            P("dp", "seq", None),
            P(("dp", "seq"), None),
            P(("dp", "seq"), None),
            P(("dp", "seq"), None),
            P(("dp", "seq"), None),
            P(("dp", "seq")),
            P(("dp", "seq")),
            P(("dp", "seq"), None),
        ),
        out_specs=(
            P("dp", "seq", None),
            P("dp", "seq", None),
            P("dp", None, "seq", None),
            P(("dp", "seq"), None),
            P(("dp", "seq"), None),
            P(("dp", "seq"), None),
            P(("dp", "seq"), None),
            P(("dp", "seq")),
            P(("dp", "seq")),
            P(("dp", "seq"), None),
        ),
        check_vma=False,
    )
```
